32 devices in a mesh: gx: 8 (over z, core), gy: 4 (over y, x).
Axes of the slice: x: 2, y: 2, z: 4, core: 2. Of those that a mesh axis runs over, the one named last changes fastest.
Arguments:
- feature: bfloat16 [6, 64, 192, 512], P(None, None, 'gx', 'gy'), may hold values from -6 to 6
- widths: int32 [8], replicated, may hold values from 8 to 24, as said below
- dw_weight: float32 [27, 64], replicated, may hold values from -1.25 to 1.25
- dw_bias: float32 [64], replicated, may hold values from -3 to 3
- pw_weight: bfloat16 [64, 64], replicated, may hold values from -0.75 to 0.75
- pw_bias: float32 [64], replicated, may hold values from -3 to 3
- lift_weight: float32 [64, 3], replicated, may hold values from -3 to 3
- coarse: float32 [3, 8, 32], P(None, 'gy'), may hold values from -6 to 6
Outputs:
- block_out: bfloat16 [2, 64, 192, 512], P(None, None, 'gx', 'gy')
The draws below stay inside these ranges and needn't reach their ends.
Inputs may be any that keep to these rules, and one draw needn't show every extreme that they name: The widths sum to 128; some slab has width exactly 24 and some exactly 8.
All inputs are finite; a program needn't handle non-finite values.
Results may differ from the reference program's by a relative error of at most 0.0031.
Values may be sent and summed in bfloat16 or wider, within the bound.
No kernel may reach another device: no remote copies, remote signals or barrier semaphores. Data moves between devices by JAX's collectives and lax.ppermute only.
A program may use at most 64 MiB of HBM per device.

```python
import jax
import jax.numpy as jnp
from jax import lax

C = 64
XW = 16
ZOUT = 2
CF = 16
ZIN = 6
XMAX = 24
NY = 512
NCX = 8
NCY = 32
N_GX = 8


def draw_widths(key, part):
    first = jax.random.fold_in(key, 11)
    second = jax.random.fold_in(key, 23)
    spread = jax.random.randint(first, (N_GX // 2,), 0, XMAX - XW + 1).astype(jnp.int32)
    spread = spread.at[0].set(XMAX - XW)
    paired = jnp.stack([XW + spread, XW - spread], axis=1).reshape(N_GX)
    order = jax.random.permutation(second, N_GX)
    return paired[order].astype(jnp.int32)


def levels(own_key, extent, cuts, low, top_value):
    level = 1.0
    for position, shards_of in cuts:
        heights = jax.random.uniform(jax.random.fold_in(jax.random.fold_in(own_key, 6), position), (shards_of,), jnp.float32, low / len(cuts), top_value / len(cuts))
        level = level * jnp.repeat(jnp.exp(heights), extent[position] // shards_of).reshape((-1,) + (1,) * (len(extent) - 1 - position))
    return level


def bell_draw(own_key, dims, scale, most, shards=(), held_as=jnp.bfloat16):
    gain = levels(own_key, dims, shards, -0.22, 0.18) if shards else 1.0
    result = jax.random.normal(own_key, dims, jnp.float32) * scale * gain
    return jnp.minimum(jnp.maximum(result, -most), most).astype(held_as)


def setup_inputs(seed: int = 0) -> dict:
    splits = jax.random.split(jax.random.key(seed), 9)
    feature = bell_draw(splits[0], (ZIN, C, N_GX * XMAX, NY), 1.0, 6.0, ((2, 8), (3, 4)))
    widths = draw_widths(jax.random.fold_in(splits[8], 71), 0)
    dw_weight = bell_draw(splits[2], (27, C), 27 ** -0.5, 1.25, (), jnp.float32)
    dw_bias = bell_draw(splits[3], (C,), 0.5, 3.0, (), jnp.float32)
    pw_weight = bell_draw(splits[4], (C, C), C ** -0.5, 0.75)
    pw_bias = bell_draw(splits[5], (C,), 0.5, 3.0, (), jnp.float32)
    lift_weight = bell_draw(splits[6], (C, 3), 0.5, 3.0, (), jnp.float32)
    coarse = bell_draw(splits[7], (3, NCX, NCY), 1.0, 6.0, ((1, 4),), jnp.float32)
    return dict(feature=feature, widths=widths, dw_weight=dw_weight, dw_bias=dw_bias, pw_weight=pw_weight, pw_bias=pw_bias, lift_weight=lift_weight, coarse=coarse)


def reference(feature, widths, dw_weight, dw_bias, pw_weight, pw_bias, lift_weight, coarse):
    total = XW * N_GX
    starts = (jnp.cumsum(widths) - widths).astype(jnp.int32)
    places = jnp.arange(total, dtype=jnp.int32)
    owner = (jnp.sum((starts[None, :] <= places[:, None]).astype(jnp.int32), axis=1) - 1).astype(jnp.int32)
    source = (owner * XMAX + places - starts[owner]).astype(jnp.int32)
    field = jnp.take(feature, source, axis=2)
    depth = jnp.zeros((ZOUT, C, total, NY), jnp.float32) + dw_bias[None, :, None, None]
    for dz in (-1, 0, 1):
        plane = field[2 + 2 * dz:2 + 2 * dz + ZOUT].astype(jnp.float32)
        for dx in (-1, 0, 1):
            for dy in (-1, 0, 1):
                tap = 9 * (dz + 1) + 3 * (dx + 1) + (dy + 1)
                moved = jnp.roll(plane, (-2 * dx, -2 * dy), axis=(2, 3))
                depth = depth + dw_weight[tap][None, :, None, None] * moved
    depth = depth.astype(jnp.bfloat16)
    mixed = jnp.einsum("oc,zcxy->zoxy", pw_weight.astype(jnp.float32), depth.astype(jnp.float32))
    mixed = mixed + pw_bias[None, :, None, None]
    active = jnp.where(mixed > 0, mixed, 0.2 * mixed)
    xcells = jnp.arange(total, dtype=jnp.int32) // CF
    ycells = jnp.arange(NY, dtype=jnp.int32) // CF
    upsampled = jnp.take(jnp.take(coarse, xcells, axis=1), ycells, axis=2)
    lifted = jnp.einsum("ck,kxy->cxy", lift_weight, upsampled, precision=lax.Precision.HIGHEST)
    value = field[2:2 + ZOUT].astype(jnp.float32) + active + lifted[None]
    slots = jnp.arange(N_GX * XMAX, dtype=jnp.int32)
    slab = slots // XMAX
    inner = slots % XMAX
    valid = inner < widths[slab]
    target = jnp.clip(starts[slab] + inner, 0, total - 1).astype(jnp.int32)
    placed = jnp.take(value, target, axis=2)
    return jnp.where(valid[None, None, :, None], placed, 0.0).astype(jnp.bfloat16)
```

```python
import functools

import jax
import jax.numpy as jnp
from jax import lax
from jax.experimental import pallas as pl
from jax.experimental.pallas import tpu as pltpu
from jax.sharding import PartitionSpec as P

XW = 16
ZOUT = 2
CF = 16
ROWS = 8
PAD = 8
F32 = jnp.float32
BF16 = jnp.bfloat16
VMEM_BYTES = 48 * 1024 * 1024


def lane_iota(shape):
    return lax.broadcasted_iota(jnp.int32, shape, len(shape) - 1)


def row_iota(shape):
    return lax.broadcasted_iota(jnp.int32, shape, len(shape) - 2)


def pack_kernel(
    widths, feature, planes, top, bottom, left, right, left_top, left_bottom, right_top, right_bottom,
    cells, pairs, edges, corners, sems,
):
    width = widths[lax.axis_index("gx")]
    count, channels, slots, tile = feature.shape

    def copy_of(z):
        return pltpu.make_async_copy(feature.at[z], planes.at[z], sems.at[z])

    for z in range(count):
        copy_of(z).start()
    corners[...] = jnp.zeros_like(corners)
    half = lane_iota((slots, tile)) // 2
    for z in range(count):
        copy_of(z).wait()
        cells[...] = planes[z].astype(F32).reshape(channels * slots, tile)
        for side, begin in ((0, 0), (1, width - 2)):
            for r in range(2):
                picked = cells[pl.ds(begin + r, channels, stride=slots), :]
                place = (z // ZOUT) * channels * 4 + (z % ZOUT) * 2 + r
                pairs[side, pl.ds(place, channels, stride=4), :] = picked
        low = jnp.zeros((slots, tile), F32)
        high = jnp.zeros((slots, tile), F32)
        for c in range(channels):
            moved = cells[c * slots : (c + 1) * slots, :]
            if c:
                moved = pltpu.roll(moved, 2 * c, 1)
            low = jnp.where(half == c, moved, low)
            high = jnp.where(half == (c - 1) % channels, moved, high)
        high = pltpu.roll(high, 2, 1)
        left[z] = low.astype(BF16)
        right[z] = high.astype(BF16)
        edges[0] = low
        edges[1] = high
        for side in range(2):
            corners[side, 0, 2 * z : 2 * z + 2, :] = edges[side, 0:2, :]
            corners[side, 1, 2 * z : 2 * z + 2, :] = edges[side, pl.ds(width - 2, 2), :]
    top[...] = pairs[0].astype(BF16)
    bottom[...] = pairs[1].astype(BF16)
    left_top[...] = corners[0, 0].astype(BF16)
    left_bottom[...] = corners[0, 1].astype(BF16)
    right_top[...] = corners[1, 0].astype(BF16)
    right_bottom[...] = corners[1, 1].astype(BF16)


def tap_of(m, dx, dy):
    return 9 * m + 3 * (dx + 1) + (dy + 1)


def shifted_sum(centre, before, after):
    lane = lane_iota(centre.shape)
    tile = centre.shape[-1]
    before = jnp.where(lane < 2, 0.0, pltpu.roll(before, 2, 1))
    after = jnp.where(lane >= tile - 2, 0.0, pltpu.roll(after, tile - 2, 1))
    return centre + before + after


def inner_kernel(widths, taps, bias, planes, mix, depth, spread, lane_taps, padded):
    width = widths[lax.axis_index("gx")]
    count, channels, slots, tile = planes.shape
    valid = row_iota((slots, tile)) < width

    def widen(c, carry):
        for z in range(count):
            padded[z, c, 0:PAD, :] = jnp.zeros((PAD, tile), F32)
            padded[z, c, PAD : PAD + slots, :] = jnp.where(valid, planes[z, c].astype(F32), 0.0)
            padded[z, c, PAD + slots : 2 * PAD + slots, :] = jnp.zeros((PAD, tile), F32)
        return carry

    lax.fori_loop(0, channels, widen, 0)

    def convolve(c, carry):
        for out in range(ZOUT):
            for b in range(slots // ROWS):
                sums = [None, None, None]
                for m in range(3):
                    for dx in (-1, 0, 1):
                        rows = padded[out + 2 * m, c, pl.ds(PAD + 2 * dx + ROWS * b, ROWS), :]
                        for dy in (-1, 0, 1):
                            term = taps[tap_of(m, dx, dy), c] * rows
                            held = sums[dy + 1]
                            sums[dy + 1] = term if held is None else held + term
                total = shifted_sum(sums[1], sums[0], sums[2]) + bias[c]
                depth[out, c, ROWS * b : ROWS * (b + 1), :] = total
        return carry

    lax.fori_loop(0, channels, convolve, 0)
    size = channels * ROWS
    tall = (size, channels)
    wide = (channels, size)
    column = lane_iota(tall) * ROWS
    row = row_iota(tall)
    grow = ((row >= column) & (row < column + ROWS)).astype(BF16)
    row = row_iota(wide) * ROWS
    column = lane_iota(wide)
    stretch = ((column >= row) & (column < row + ROWS)).astype(BF16)
    repeated = jnp.dot(grow, mix[...], preferred_element_type=F32).astype(BF16)
    repeated = jnp.dot(repeated, stretch, preferred_element_type=F32)
    square = (size, size)
    same = (row_iota(square) & (ROWS - 1)) == (lane_iota(square) & (ROWS - 1))
    spread[...] = jnp.where(same, repeated, 0.0).astype(BF16)


def finish_kernel(
    widths, taps, pw_bias, lift, planes, spread, lane_taps, lower, upper, from_left, from_right,
    lower_left, upper_left, lower_right, upper_right, coarse, depth_in,
    out, depth,
    rims, rows8, halo, sides, mixed_in, block, sems,
):
    slab = lax.axis_index("gx")
    count, channels, slots, tile = planes.shape
    width = widths[slab]
    slabs = widths.shape[0]
    total = XW * slabs
    start = jnp.int32(0)
    for d in range(slabs):
        start = start + jnp.where(d < slab, widths[d], 0)
    valid = row_iota((slots, tile)) < width

    for side, strip, low, high in (
        (0, from_left, lower_left, upper_left),
        (1, from_right, lower_right, upper_right),
    ):
        rims[0:16, :] = low[...].astype(F32)
        rims[16:32, :] = high[...].astype(F32)
        for z in range(count):
            halo[z, PAD : PAD + slots, :] = jnp.where(valid, strip[z].astype(F32), 0.0)
            halo[z, PAD + slots : 2 * PAD + slots, :] = jnp.zeros((PAD, tile), F32)
            halo[z, PAD - 2 : PAD, :] = rims[2 * z : 2 * z + 2, :]
            halo[z, pl.ds(PAD + width, 2), :] = rims[16 + 2 * z : 18 + 2 * z, :]
        dy = 2 * side - 1
        for o in range(ZOUT):
            held = jnp.zeros((slots, tile), F32)
            for m in range(3):
                for dx in (-1, 0, 1):
                    tap = tap_of(m, dx, dy)
                    held = held + lane_taps[tap : tap + 1, :] * halo[o + 2 * m, PAD + 2 * dx : PAD + 2 * dx + slots, :]
            sides[side, o] = held

    groups = lower.shape[0] // 4
    for side, strip in ((0, lower), (1, upper)):
        rims[...] = strip[...].astype(F32)
        for q in range(4):
            rows8[pl.ds(4 * side + q, groups, stride=8), :] = rims[pl.ds(q, groups, stride=4), :]
    first = row_iota((8, tile)) < 4

    def attach(c, carry):
        sums = [None, None, None]
        for m in range(3):
            rows = rows8[pl.ds(pl.multiple_of((m * channels + c) * 8, 8), 8), :]
            for dy in (-1, 0, 1):
                weight = jnp.where(first, taps[tap_of(m, -1, dy), c], taps[tap_of(m, 1, dy), c])
                held = sums[dy + 1]
                sums[dy + 1] = weight * rows if held is None else held + weight * rows
        added = shifted_sum(sums[1], sums[0], sums[2])
        for o in range(ZOUT):
            depth[o, c, 0:2, :] = depth_in[o, c, 0:2, :] + added[2 * o : 2 * o + 2, :]
            depth[o, c, pl.ds(width - 2, 2), :] = depth_in[o, c, pl.ds(width - 2, 2), :] + added[4 + 2 * o : 6 + 2 * o, :]
        return carry

    lax.fori_loop(0, channels, attach, 0)

    lane = lane_iota((ROWS, tile))

    def gather(pair, carry):
        for o in range(ZOUT):
            for b in range(slots // ROWS):
                both = []
                for k in range(2):
                    c = 2 * pair + k
                    at = slice(ROWS * b, ROWS * (b + 1))
                    before = pltpu.roll(sides[0, o, at, :], tile - 2 * c, 1)
                    after = pltpu.roll(sides[1, o, at, :], tile - 2 - 2 * c, 1)
                    edge = jnp.where(lane < 2, before, jnp.where(lane >= tile - 2, after, 0.0))
                    both.append(depth[o, c, at, :] + edge)
                both = jnp.concatenate(both, axis=0).astype(BF16)
                at = pl.ds(pl.multiple_of(pair * 2 * ROWS, 2 * ROWS), 2 * ROWS)
                mixed_in[b, at, o * tile : (o + 1) * tile] = both
        return carry

    lax.fori_loop(0, channels // 2, gather, 0)

    _, ncx, ncy = coarse.shape
    shape = (ncy, tile)
    cell = row_iota(shape) * CF
    place = lane_iota(shape) + lax.axis_index("gy") * tile
    along_y = ((place >= cell) & (place < cell + CF)).astype(F32)
    shape = (slots, ncx)
    cell = lane_iota(shape) * CF
    place = row_iota(shape) + start
    place = jnp.where(place >= total, place - total, place)
    along_x = ((place >= cell) & (place < cell + CF)).astype(F32)
    lifted = []
    for k in range(coarse.shape[0]):
        wide = jnp.dot(coarse[k], along_y, precision=lax.Precision.HIGHEST, preferred_element_type=F32)
        lifted.append(jnp.dot(along_x, wide, precision=lax.Precision.HIGHEST, preferred_element_type=F32))

    chunk = 16
    copies = []
    for part in range(channels // chunk):
        rows = slice(part * chunk * ROWS, (part + 1) * chunk * ROWS)
        mixed = [
            jnp.dot(spread[rows, :], mixed_in[b], preferred_element_type=F32) for b in range(slots // ROWS)
        ]
        for k in range(chunk):
            o = part * chunk + k
            lift_o = lift[o, 0] * lifted[0] + lift[o, 1] * lifted[1] + lift[o, 2] * lifted[2]
            for z in range(ZOUT):
                value = jnp.concatenate(
                    [m[k * ROWS : (k + 1) * ROWS, z * tile : (z + 1) * tile] for m in mixed], axis=0
                )
                value = value + pw_bias[o]
                value = jnp.where(value > 0, value, 0.2 * value) + lift_o
                value = value + planes[2 + z, o].astype(F32)
                block[z, o] = jnp.where(valid, value, 0.0).astype(BF16)
        for z in range(ZOUT):
            part_of = pl.ds(part * chunk, chunk)
            copy = pltpu.make_async_copy(block.at[z, part_of], out.at[z, part_of], sems.at[part, z])
            copy.start()
            copies.append(copy)
    for copy in copies:
        copy.wait()


def shards(feature, widths, dw_weight, dw_bias, pw_weight, pw_bias, lift_weight, coarse):
    planes, channels, slots, tile = feature.shape
    nx, ny = lax.axis_size("gx"), lax.axis_size("gy")
    smem = pl.BlockSpec(memory_space=pltpu.SMEM)
    vmem = pl.BlockSpec(memory_space=pltpu.VMEM)
    anywhere = pl.BlockSpec(memory_space=pl.ANY)
    params = pltpu.CompilerParams(vmem_limit_bytes=VMEM_BYTES)
    shape = jax.ShapeDtypeStruct
    message = planes // ZOUT * channels * 4
    strip = shape((planes, slots, tile), BF16)
    corner = shape((16, tile), BF16)
    held, top, bottom, left, right, left_top, left_bottom, right_top, right_bottom = pl.pallas_call(
        pack_kernel,
        out_shape=(
            pltpu.VMEM(feature.shape, BF16),
            shape((message, tile), BF16),
            shape((message, tile), BF16),
            strip,
            strip,
            corner,
            corner,
            corner,
            corner,
        ),
        in_specs=[smem, anywhere],
        out_specs=(vmem,) * 9,
        scratch_shapes=[
            pltpu.VMEM((channels * slots, tile), F32),
            pltpu.VMEM((2, message, tile), F32),
            pltpu.VMEM((2, slots, tile), F32),
            pltpu.VMEM((2, 2, 16, tile), F32),
            pltpu.SemaphoreType.DMA((planes,)),
        ],
        compiler_params=params,
    )(widths, feature)

    def sent(array, by_x, by_y):
        route = [
            (x * ny + y, (x + by_x) % nx * ny + (y + by_y) % ny) for x in range(nx) for y in range(ny)
        ]
        return lax.ppermute(array, ("gx", "gy"), route)

    lower = sent(bottom, 1, 0)
    upper = sent(top, -1, 0)
    from_left = sent(right, 0, 1)
    from_right = sent(left, 0, -1)
    lower_left = sent(right_bottom, 1, 1)
    upper_left = sent(right_top, -1, 1)
    lower_right = sent(left_bottom, 1, -1)
    upper_right = sent(left_top, -1, -1)
    every = lax.all_gather(coarse, "gy", axis=1, tiled=True)
    lane_taps = jnp.repeat(dw_weight, 2, axis=1)
    size = channels * ROWS
    depth, spread = pl.pallas_call(
        lambda w, t, b, f, m, d, s, p: inner_kernel(w, t, b, f, m, d, s, None, p),
        out_shape=(pltpu.VMEM((ZOUT, channels, slots, tile), F32), pltpu.VMEM((size, size), BF16)),
        in_specs=[smem, smem, smem, vmem, vmem],
        out_specs=(vmem, vmem),
        scratch_shapes=[pltpu.VMEM((planes, channels, slots + 2 * PAD, tile), F32)],
        compiler_params=params,
        cost_estimate=pl.CostEstimate(flops=10**9, bytes_accessed=3 * 10**6, transcendentals=0),
    )(widths, dw_weight, dw_bias, held, pw_weight)
    out, _ = pl.pallas_call(
        finish_kernel,
        out_shape=(
            shape((ZOUT, channels, slots, tile), BF16),
            pltpu.VMEM((ZOUT, channels, slots, tile), F32),
        ),
        in_specs=[smem, smem, smem, smem] + [vmem] * 13,
        out_specs=(anywhere, vmem),
        scratch_shapes=[
            pltpu.VMEM((message, tile), F32),
            pltpu.VMEM((2 * message, tile), F32),
            pltpu.VMEM((planes, slots + 2 * PAD, tile), F32),
            pltpu.VMEM((2, ZOUT, slots, tile), F32),
            pltpu.VMEM((slots // ROWS, size, ZOUT * tile), BF16),
            pltpu.VMEM((ZOUT, channels, slots, tile), BF16),
            pltpu.SemaphoreType.DMA((channels // 16, ZOUT)),
        ],
        input_output_aliases={16: 1},
        compiler_params=params,
    )(
        widths, dw_weight, pw_bias, lift_weight, held, spread, lane_taps, lower, upper, from_left, from_right,
        lower_left, upper_left, lower_right, upper_right, every, depth,
    )
    return out


def solution(mesh):
    placed = (P(None, None, "gx", "gy"), P(), P(), P(), P(), P(), P(), P(None, "gy", None))
    return jax.shard_map(
        shards, mesh=mesh, in_specs=placed, out_specs=P(None, None, "gx", "gy"), check_vma=False
    )
```

```python
import jax
import jax.numpy as jnp
from jax import lax
from jax.experimental import pallas as pl
from jax.experimental.pallas import tpu as pltpu
from jax.sharding import PartitionSpec as P

XW = 16
ZOUT = 2
CF = 16
ROWS = 8
OUTER = 32
F32 = jnp.float32
BF16 = jnp.bfloat16
VMEM_BYTES = 48 * 1024 * 1024


def lane_iota(shape):
    return lax.broadcasted_iota(jnp.int32, shape, len(shape) - 1)


def row_iota(shape):
    return lax.broadcasted_iota(jnp.int32, shape, len(shape) - 2)


def tap_of(m, dx, dy):
    return 9 * m + 3 * (dx + 1) + (dy + 1)


def is_even(axis):
    return lax.rem(lax.axis_index(axis), 2) == 0


def pack_kernel(widths, feature, taps, planes, band, first, second, tap_rows, masks, sems):
    width = widths[lax.axis_index("gx")]
    count, channels, slots, tile = feature.shape
    depth = 3 * slots
    lanes = band.shape[2]

    def copy_of(z):
        return pltpu.make_async_copy(feature.at[z], planes.at[z], sems.at[z])

    for z in range(count):
        copy_of(z).start()

    shape = (taps.shape[0], lanes)
    lane = lane_iota(shape)
    segment = sum((lane >= slots * i).astype(jnp.int32) for i in range(1, 6))
    high = taps[...].astype(BF16)
    low = (taps[...] - high.astype(F32)).astype(BF16)
    over_taps = (((0,), (0,)), ((), ()))
    for k in range(9):
        row = row_iota(shape)
        in_high = ((row == 9 * segment + k) & (lane < depth)).astype(BF16)
        in_low = ((row == 9 * (segment - 3) + k) & (lane >= depth) & (lane < 2 * depth)).astype(BF16)
        tap_rows[k] = lax.dot_general(high, in_high, over_taps, preferred_element_type=F32) + lax.dot_general(
            low, in_low, over_taps, preferred_element_type=F32
        )
    shape = (OUTER, lanes)
    lane = lane_iota(shape)
    segment = sum((lane >= slots * i).astype(jnp.int32) for i in range(1, 6))
    source = lane - slots * segment
    row = row_iota(shape)
    target = jnp.where(row < slots, row, jnp.where(row < slots + 2, row - slots - 2, row - slots - 2 + width))
    target = jnp.where(row < slots + 4, target, 4 * OUTER)
    known = (lane < 2 * depth) & (source < width)
    for dx in (-1, 0, 1):
        masks[dx + 1] = ((source == target + 2 * dx) & known).astype(F32)

    def build(c, carry):
        for dy in (-1, 0, 1):
            total = None
            for dx in (-1, 0, 1):
                term = masks[dx + 1] * tap_rows[3 * (dx + 1) + dy + 1, pl.ds(c, 1), :]
                total = term if total is None else total + term
            band[c, OUTER * (dy + 1) : OUTER * (dy + 2), :] = total.astype(BF16)
        return carry

    lax.fori_loop(0, channels, build, 0, unroll=2)

    lane = lane_iota((slots, tile))
    even = is_even("gy")

    def merged(z, level, c):
        if level == 0:
            return planes[z, c].astype(F32)
        step = tile >> level
        one = merged(z, level - 1, c)
        other = pltpu.roll(merged(z, level - 1, c + step // 2), step, 1)
        if step > 2:
            return jnp.where(((lane + step // 2) & step) != 0, other, one)
        return jnp.where((lane & 2) != 0, other, one), jnp.where((lane & 2) != 0, one, other)

    for z in range(count):
        copy_of(z).wait()
        left, right = merged(z, channels.bit_length() - 1, 0)
        right = pltpu.roll(right, 2, 1)
        first[z] = jnp.where(even, right, left).astype(BF16)
        second[z] = jnp.where(even, left, right).astype(BF16)


def shifted_sum(centre, before, after):
    lane = lane_iota(centre.shape)
    tile = centre.shape[-1]
    before = jnp.where(lane < 2, 0.0, pltpu.roll(before, 2, 1))
    after = jnp.where(lane >= tile - 2, 0.0, pltpu.roll(after, tile - 2, 1))
    return centre + before + after


def conv_kernel(bias, planes, band, depth):
    count, channels, slots, tile = planes.shape
    inside = row_iota((OUTER, tile)) < slots

    def convolve(c, carry):
        cells = jnp.concatenate(
            [
                jnp.concatenate([planes[z + ZOUT * m, c] for m in range(3)] * 2, axis=0)
                for z in range(ZOUT)
            ],
            axis=1,
        )
        sums = jnp.dot(band[c][:, : cells.shape[0]], cells, preferred_element_type=F32)
        for z in range(ZOUT):
            part = [sums[OUTER * k : OUTER * (k + 1), z * tile : (z + 1) * tile] for k in range(3)]
            total = shifted_sum(part[1], part[0], part[2])
            at = pl.ds(pl.multiple_of(c * OUTER, OUTER), OUTER)
            depth[z, at, :] = total + jnp.where(inside, bias[c], 0.0)
        return carry

    lax.fori_loop(0, channels, convolve, 0, unroll=4)


def rim_kernel(widths, taps, first, second, depth, edge, near, far, strips, held, beyond, tail):
    width = widths[lax.axis_index("gx")]
    count, slots, tile = first.shape
    channels = taps.shape[1]
    pad = 8
    wide = 2 * tile

    shape = (wide, wide)
    row = row_iota(shape)
    own = row & (tile - 1)
    from_right = (row < tile) == is_even("gy")
    target = ((own >> 1) << 2) + (own & 1) + jnp.where(from_right, 0, 2)
    spread = (lane_iota(shape) == target).astype(BF16)
    both = jnp.concatenate(
        [first[...].reshape(count * slots, tile), second[...].reshape(count * slots, tile)], axis=1
    )
    both = jnp.dot(both, spread, preferred_element_type=F32)
    valid = row_iota((slots, wide)) < width
    for z in range(count):
        strips[z, 0:pad, :] = jnp.zeros((pad, wide), F32)
        strips[z, pad : pad + slots, :] = jnp.where(valid, both[z * slots : (z + 1) * slots, :], 0.0)
        strips[z, pad + slots : 2 * pad + slots, :] = jnp.zeros((pad, wide), F32)
    shape = (channels, wide)
    spread = ((lane_iota(shape) >> 2) == row_iota(shape)).astype(F32)
    along = jnp.dot(taps[...], spread, precision=lax.Precision.HIGHEST, preferred_element_type=F32)
    on_left = (lane_iota((1, wide)) & 2) != 0
    size = slots + 4
    for z in range(ZOUT):
        total = None
        for m in range(3):
            for dx in (-1, 0, 1):
                before, after = tap_of(m, dx, -1), tap_of(m, dx, 1)
                weight = jnp.where(on_left, along[before : before + 1, :], along[after : after + 1, :])
                begin = pad - 4 + 2 * dx
                term = weight * strips[z + ZOUT * m, begin : begin + slots + 8, :]
                total = term if total is None else total + term
        for h in range(2):
            held[h] = total[:, h * tile : (h + 1) * tile]
            edge[z, h] = held[h, 4 : 4 + slots, :]
            beyond[z, h, 0:2, :] = held[h, 2:4, :]
            beyond[z, h, 2:4, :] = held[h, pl.ds(4 + width, 2), :]
            beyond[z, h, 4:8, :] = jnp.zeros((4, tile), F32)

    lane = lane_iota((ROWS, tile))
    per_tile = tile // 4
    for z in range(ZOUT):
        for c in range(channels):
            cells = pltpu.roll(beyond[z, c // per_tile], (tile - 2 - 4 * (c % per_tile)) % tile, 1)
            cells = jnp.where((lane < 2) | (lane >= tile - 2), cells, 0.0)
            at = slice(c * OUTER + slots, (c + 1) * OUTER)
            row = (z * channels + c) * ROWS
            tail[row : row + ROWS, :] = depth[z, at, :] + cells
    even = is_even("gx")
    rows = ZOUT * channels
    for r in range(2):
        to_lower = tail[pl.ds(r, rows, stride=ROWS), :]
        to_upper = tail[pl.ds(2 + r, rows, stride=ROWS), :]
        at = slice(r * rows, (r + 1) * rows)
        near[at, :] = jnp.where(even, to_upper, to_lower).astype(BF16)
        far[at, :] = jnp.where(even, to_lower, to_upper).astype(BF16)


def settle_kernel(widths, mix, coarse, edge, depth_in, depth, spread, lifted):
    slab = lax.axis_index("gx")
    slabs = widths.shape[0]
    channels = mix.shape[0]
    _, _, slots, tile = edge.shape
    lane = lane_iota((slots, tile))
    per_tile = tile // 4
    for z in range(ZOUT):
        for c in range(channels):
            cells = pltpu.roll(edge[z, c // per_tile], (tile - 2 - 4 * (c % per_tile)) % tile, 1)
            cells = jnp.where((lane < 2) | (lane >= tile - 2), cells, 0.0)
            at = slice(c * OUTER, c * OUTER + slots)
            depth[z, at, :] = depth_in[z, at, :] + cells

    size = channels * ROWS
    tall = (size, channels)
    flat = (channels, size)
    grow = ((row_iota(tall) >> 3) == lane_iota(tall)).astype(BF16)
    stretch = ((lane_iota(flat) >> 3) == row_iota(flat)).astype(BF16)
    repeated = jnp.dot(grow, mix[...], preferred_element_type=F32).astype(BF16)
    repeated = jnp.dot(repeated, stretch, preferred_element_type=F32)
    square = (size, size)
    same = (row_iota(square) & (ROWS - 1)) == (lane_iota(square) & (ROWS - 1))
    spread[...] = jnp.where(same, repeated, 0.0).astype(BF16)

    total = XW * slabs
    start = jnp.int32(0)
    for d in range(slabs):
        start = start + jnp.where(d < slab, widths[d], 0)
    parts, ncx, own = coarse.shape
    shape = (own, tile)
    cell = row_iota(shape) * CF
    place = lane_iota(shape)
    along_y = ((place >= cell) & (place < cell + CF)).astype(F32)
    shape = (slots, ncx)
    cell = lane_iota(shape) * CF
    place = row_iota(shape) + start
    place = jnp.where(place >= total, place - total, place)
    along_x = ((place >= cell) & (place < cell + CF)).astype(F32)
    for k in range(parts):
        across = jnp.dot(coarse[k], along_y, precision=lax.Precision.HIGHEST, preferred_element_type=F32)
        lifted[k] = jnp.dot(along_x, across, precision=lax.Precision.HIGHEST, preferred_element_type=F32)


def finish_kernel(widths, pw_bias, lift, planes, spread, lifted, near, far, depth_in, out, depth, mixed_in, block, sems):
    slab = lax.axis_index("gx")
    width = widths[slab]
    count, channels, slots, tile = planes.shape
    even = is_even("gx")
    rows = ZOUT * channels
    for arrived, at_top in ((near, jnp.logical_not(even)), (far, even)):
        begin = jnp.where(at_top, 0, width - 2)
        for r in range(2):
            for z in range(ZOUT):
                at = pl.ds(begin + r, channels, stride=OUTER)
                begin_row = r * rows + z * channels
                depth[z, at, :] = depth_in[z, at, :] + arrived[begin_row : begin_row + channels, :].astype(F32)
    for c in range(0, channels, 2):
        for z in range(ZOUT):
            for b in range(slots // ROWS):
                both = [depth[z, (c + k) * OUTER + ROWS * b : (c + k) * OUTER + ROWS * (b + 1), :] for k in range(2)]
                both = jnp.concatenate(both, axis=0).astype(BF16)
                mixed_in[b, c * ROWS : (c + 2) * ROWS, z * tile : (z + 1) * tile] = both

    valid = row_iota((slots, tile)) < width
    chunk = 16
    copies = []
    for part in range(channels // chunk):
        picked = slice(part * chunk * ROWS, (part + 1) * chunk * ROWS)
        mixed = [
            jnp.dot(spread[picked, :], mixed_in[b], preferred_element_type=F32) for b in range(slots // ROWS)
        ]
        for k in range(chunk):
            o = part * chunk + k
            lift_o = lift[o, 0] * lifted[0] + lift[o, 1] * lifted[1] + lift[o, 2] * lifted[2]
            for z in range(ZOUT):
                value = jnp.concatenate(
                    [m[k * ROWS : (k + 1) * ROWS, z * tile : (z + 1) * tile] for m in mixed], axis=0
                )
                value = value + pw_bias[o]
                value = jnp.maximum(value, 0.2 * value) + lift_o
                value = value + planes[2 + z, o].astype(F32)
                block[z, o] = jnp.where(valid, value, 0.0).astype(BF16)
        for z in range(ZOUT):
            part_of = pl.ds(part * chunk, chunk)
            copy = pltpu.make_async_copy(block.at[z, part_of], out.at[z, part_of], sems.at[part, z])
            copy.start()
            copies.append(copy)
    for copy in copies:
        copy.wait()


def shards(feature, widths, dw_weight, dw_bias, pw_weight, pw_bias, lift_weight, coarse):
    planes, channels, slots, tile = feature.shape
    smem = pl.BlockSpec(memory_space=pltpu.SMEM)
    vmem = pl.BlockSpec(memory_space=pltpu.VMEM)
    hbm = pl.BlockSpec(memory_space=pltpu.HBM)
    params = pltpu.CompilerParams(vmem_limit_bytes=VMEM_BYTES)
    shape = jax.ShapeDtypeStruct
    strip = shape((planes, slots, tile), BF16)
    depth_shape = pltpu.VMEM((ZOUT, channels * OUTER, tile), F32)
    message = shape((2 * ZOUT * channels, tile), BF16)
    size = channels * ROWS

    def swapped(array, axis, first):
        count = lax.axis_size(axis)
        pairs = []
        for i in range(first, count + first, 2):
            a, b = i % count, (i + 1) % count
            pairs += [(a, b), (b, a)]
        return lax.ppermute(array, axis, pairs)

    local = lax.all_to_all(coarse, "gy", split_axis=2, concat_axis=1, tiled=True)
    held, band, first, second = pl.pallas_call(
        pack_kernel,
        out_shape=(
            pltpu.VMEM(feature.shape, BF16),
            pltpu.VMEM((channels, 3 * OUTER, 2 * tile), BF16),
            strip,
            strip,
        ),
        in_specs=[smem, hbm, vmem],
        out_specs=(vmem,) * 4,
        scratch_shapes=[
            pltpu.VMEM((9, channels, 2 * tile), F32),
            pltpu.VMEM((3, OUTER, 2 * tile), F32),
            pltpu.SemaphoreType.DMA((planes,)),
        ],
        compiler_params=params,
    )(widths, feature, dw_weight)
    first = swapped(first, "gy", 0)
    second = swapped(second, "gy", 1)
    depth = pl.pallas_call(
        conv_kernel,
        out_shape=depth_shape,
        in_specs=[smem, vmem, vmem],
        out_specs=vmem,
        compiler_params=params,
        cost_estimate=pl.CostEstimate(flops=10**9, bytes_accessed=10**6, transcendentals=0),
    )(dw_bias, held, band)
    edge, near, far = pl.pallas_call(
        rim_kernel,
        out_shape=(pltpu.VMEM((ZOUT, 2, slots, tile), F32), message, message),
        in_specs=[smem] + [vmem] * 4,
        out_specs=(vmem,) * 3,
        scratch_shapes=[
            pltpu.VMEM((planes, slots + 16, 2 * tile), F32),
            pltpu.VMEM((2, slots + 8, tile), F32),
            pltpu.VMEM((ZOUT, 2, ROWS, tile), F32),
            pltpu.VMEM((ZOUT * channels * ROWS, tile), F32),
        ],
        compiler_params=params,
    )(widths, dw_weight, first, second, depth)
    near = swapped(near, "gx", 0)
    far = swapped(far, "gx", 1)
    depth, spread, lifted = pl.pallas_call(
        settle_kernel,
        out_shape=(depth_shape, pltpu.VMEM((size, size), BF16), pltpu.VMEM((3, slots, tile), F32)),
        in_specs=[smem] + [vmem] * 4,
        out_specs=(vmem,) * 3,
        input_output_aliases={4: 0},
        compiler_params=params,
        cost_estimate=pl.CostEstimate(flops=10**9, bytes_accessed=10**6, transcendentals=0),
    )(widths, pw_weight, local, edge, depth)
    out, _ = pl.pallas_call(
        finish_kernel,
        out_shape=(shape((ZOUT, channels, slots, tile), BF16), depth_shape),
        in_specs=[smem, smem, smem] + [vmem] * 6,
        out_specs=(hbm, vmem),
        scratch_shapes=[
            pltpu.VMEM((slots // ROWS, size, ZOUT * tile), BF16),
            pltpu.VMEM((ZOUT, channels, slots, tile), BF16),
            pltpu.SemaphoreType.DMA((channels // 16, ZOUT)),
        ],
        input_output_aliases={8: 1},
        compiler_params=params,
    )(widths, pw_bias, lift_weight, held, spread, lifted, near, far, depth)
    return out


def solution(mesh):
    placed = (P(None, None, "gx", "gy"), P(), P(), P(), P(), P(), P(), P(None, "gy", None))
    return jax.shard_map(
        shards, mesh=mesh, in_specs=placed, out_specs=P(None, None, "gx", "gy"), check_vma=False
    )
```

```python
import functools

import jax
import jax.numpy as jnp
from jax import lax
from jax.experimental import pallas as pl
from jax.experimental.pallas import tpu as pltpu
from jax.sharding import PartitionSpec as P

XW = 16
ZOUT = 2
CF = 16
ROWS = 8
OUTER = 32
F32 = jnp.float32
BF16 = jnp.bfloat16
VMEM_BYTES = 14 * 1024 * 1024


def lane_iota(shape):
    return lax.broadcasted_iota(jnp.int32, shape, len(shape) - 1)


def row_iota(shape):
    return lax.broadcasted_iota(jnp.int32, shape, len(shape) - 2)


def tap_of(m, dx, dy):
    return 9 * m + 3 * (dx + 1) + (dy + 1)


def is_even(axis):
    return lax.rem(lax.axis_index(axis), 2) == 0


def pack_kernel(
    widths_in, feature, taps_in, coarse_in,
    planes, band, first, second,
    tap_rows, widths, taps, coarse, tail, sems, small_sems,
):
    count, channels, slots, tile = feature.shape
    depth = 3 * slots
    lanes = band.shape[2]

    def copy_of(z):
        return pltpu.make_async_copy(feature.at[z], planes.at[z], sems.at[z])

    small = [
        pltpu.make_async_copy(source, target, small_sems.at[i])
        for i, (source, target) in enumerate(((taps_in, taps), (widths_in, widths), (coarse_in, coarse)))
    ]
    for copy in small:
        copy.start()
    for z in range(count):
        copy_of(z).start()
    for copy in small:
        copy.wait()
    width = widths[lax.axis_index("gx")]

    shape = (taps.shape[0], lanes)
    lane = lane_iota(shape)
    segment = sum((lane >= slots * i).astype(jnp.int32) for i in range(1, 6))
    high = taps[...].astype(BF16)
    low = (taps[...] - high.astype(F32)).astype(BF16)
    over_taps = (((0,), (0,)), ((), ()))
    for k in range(9):
        row = row_iota(shape)
        in_high = ((row == 9 * segment + k) & (lane < depth)).astype(BF16)
        in_low = ((row == 9 * (segment - 3) + k) & (lane >= depth) & (lane < 2 * depth)).astype(BF16)
        tap_rows[k] = lax.dot_general(high, in_high, over_taps, preferred_element_type=F32) + lax.dot_general(
            low, in_low, over_taps, preferred_element_type=F32
        )
    shape = (OUTER, lanes)
    lane = lane_iota(shape)
    segment = sum((lane >= slots * i).astype(jnp.int32) for i in range(1, 6))
    source = lane - slots * segment
    row = row_iota(shape)
    target = jnp.where(row < slots, row, jnp.where(row < slots + 2, row - slots - 2, row - slots - 2 + width))
    target = jnp.where(row < slots + 4, target, 4 * OUTER)
    known = (lane < 2 * depth) & (source < width)
    masks = [((source == target + 2 * dx) & known).astype(BF16) for dx in (-1, 0, 1)]

    def build(c, carry):
        for dy in (-1, 0, 1):
            total = None
            for dx in (-1, 0, 1):
                weights = tap_rows[3 * (dx + 1) + dy + 1, pl.ds(c, 1), :]
                weights = jnp.broadcast_to(weights, (OUTER // 2, lanes)).astype(BF16)
                term = masks[dx + 1] * jnp.concatenate([weights, weights], axis=0)
                total = term if total is None else total + term
            band[c, OUTER * (dy + 1) : OUTER * (dy + 2), :] = total
        return carry

    lax.fori_loop(0, channels, build, 0, unroll=4)

    parts, own_rows, ncy = coarse.shape
    tail[...] = jnp.zeros_like(tail)
    for k in range(parts):
        rest = coarse[k]
        for p in range(3):
            term = rest.astype(BF16).astype(F32)
            rest = rest - term
            at = (p * parts + k) * own_rows
            tail[at : at + own_rows, 0:ncy] = term
    for message in (first, second):
        message[count * slots :, :] = tail[...].astype(BF16)

    lane = lane_iota((slots, tile))
    even = is_even("gy")

    def merged(z, level, c):
        if level == 0:
            return planes[z, c].astype(F32)
        step = tile >> level
        one = merged(z, level - 1, c)
        other = pltpu.roll(merged(z, level - 1, c + step // 2), step, 1)
        if step > 2:
            return jnp.where(((lane + step // 2) & step) != 0, other, one)
        return jnp.where((lane & 2) != 0, other, one), jnp.where((lane & 2) != 0, one, other)

    for z in range(0, count, 2):
        columns = []
        for k in range(2):
            copy_of(z + k).wait()
            left, right = merged(z + k, channels.bit_length() - 1, 0)
            columns.append((left, pltpu.roll(right, 2, 1)))
        left = jnp.concatenate([columns[0][0], columns[1][0]], axis=0)
        right = jnp.concatenate([columns[0][1], columns[1][1]], axis=0)
        at = slice(z * slots, (z + 2) * slots)
        first[at, :] = jnp.where(even, right, left).astype(BF16)
        second[at, :] = jnp.where(even, left, right).astype(BF16)


def shifted_sum(centre, before, after):
    lane = lane_iota(centre.shape)
    tile = centre.shape[-1]
    before = jnp.where(lane < 2, 0.0, pltpu.roll(before, 2, 1))
    after = jnp.where(lane >= tile - 2, 0.0, pltpu.roll(after, tile - 2, 1))
    return centre + before + after


def conv_kernel(bias, planes, band, depth):
    count, channels, slots, tile = planes.shape
    inside = row_iota((OUTER, tile)) < slots

    def convolve(c, carry):
        cells = jnp.concatenate(
            [
                jnp.concatenate([planes[z + ZOUT * m, c].astype(F32) for m in range(3)] * 2, axis=0).astype(BF16)
                for z in range(ZOUT)
            ],
            axis=1,
        )
        sums = jnp.dot(band[c][:, : cells.shape[0]], cells, preferred_element_type=F32)
        for z in range(ZOUT):
            part = [sums[OUTER * k : OUTER * (k + 1), z * tile : (z + 1) * tile] for k in range(3)]
            total = shifted_sum(part[1], part[0], part[2])
            at = pl.ds(pl.multiple_of(c * OUTER, OUTER), OUTER)
            depth[z, at, :] = total + jnp.where(inside, bias[c], 0.0)
        return carry

    lax.fori_loop(0, channels, convolve, 0, unroll=4)


def rim_kernel(widths, taps, first, second, depth, edge, near, far, strips, held, beyond, tail):
    width = widths[lax.axis_index("gx")]
    count, slots = 3 * ZOUT, edge.shape[2]
    tile = first.shape[1]
    channels = taps.shape[1]
    pad = 8
    wide = 2 * tile

    shape = (wide, wide)
    row = row_iota(shape)
    own = row & (tile - 1)
    from_right = (row < tile) == is_even("gy")
    target = ((own >> 1) << 2) + (own & 1) + jnp.where(from_right, 0, 2)
    spread = (lane_iota(shape) == target).astype(BF16)
    both = jnp.concatenate([first[: count * slots, :], second[: count * slots, :]], axis=1)
    both = jnp.dot(both, spread, preferred_element_type=F32)
    valid = row_iota((slots, wide)) < width
    for z in range(count):
        strips[z, 0:pad, :] = jnp.zeros((pad, wide), F32)
        strips[z, pad : pad + slots, :] = jnp.where(valid, both[z * slots : (z + 1) * slots, :], 0.0)
        strips[z, pad + slots : 2 * pad + slots, :] = jnp.zeros((pad, wide), F32)
    shape = (channels, wide)
    spread = ((lane_iota(shape) >> 2) == row_iota(shape)).astype(F32)
    along = jnp.dot(taps[...], spread, precision=lax.Precision.HIGHEST, preferred_element_type=F32)
    on_left = (lane_iota((1, wide)) & 2) != 0
    size = slots + 4
    for z in range(ZOUT):
        total = None
        for m in range(3):
            for dx in (-1, 0, 1):
                before, after = tap_of(m, dx, -1), tap_of(m, dx, 1)
                weight = jnp.where(on_left, along[before : before + 1, :], along[after : after + 1, :])
                begin = pad - 4 + 2 * dx
                term = weight * strips[z + ZOUT * m, begin : begin + slots + 8, :]
                total = term if total is None else total + term
        for h in range(2):
            held[h] = total[:, h * tile : (h + 1) * tile]
            edge[z, h] = held[h, 4 : 4 + slots, :]
            beyond[z, h, 0:2, :] = held[h, 2:4, :]
            beyond[z, h, 2:4, :] = held[h, pl.ds(4 + width, 2), :]
            beyond[z, h, 4:8, :] = jnp.zeros((4, tile), F32)

    lane = lane_iota((ROWS, tile))
    per_tile = tile // 4
    for z in range(ZOUT):
        for c in range(channels):
            cells = pltpu.roll(beyond[z, c // per_tile], (tile - 2 - 4 * (c % per_tile)) % tile, 1)
            cells = jnp.where((lane < 2) | (lane >= tile - 2), cells, 0.0)
            at = slice(c * OUTER + slots, (c + 1) * OUTER)
            row = (z * channels + c) * ROWS
            tail[row : row + ROWS, :] = depth[z, at, :] + cells
    even = is_even("gx")
    rows = ZOUT * channels
    for r in range(2):
        to_lower = tail[pl.ds(r, rows, stride=ROWS), :]
        to_upper = tail[pl.ds(2 + r, rows, stride=ROWS), :]
        at = slice(r * rows, (r + 1) * rows)
        near[at, :] = jnp.where(even, to_upper, to_lower).astype(BF16)
        far[at, :] = jnp.where(even, to_lower, to_upper).astype(BF16)


def settle_kernel(gathered, widths, lift, mix, planes, *refs):
    if gathered:
        coarse, edge, depth_in, depth, spread, base = refs
        parts, ncx, ncy = coarse.shape
    else:
        first, second, own_block, opposite, edge, depth_in, depth, spread, base, cells = refs
        parts, own_rows, ncy = own_block.shape
        ncx = 4 * own_rows
    slab = lax.axis_index("gx")
    here = lax.axis_index("gy")
    slabs = widths.shape[0]
    channels = mix.shape[0]
    _, _, slots, tile = edge.shape
    lane = lane_iota((slots, tile))
    per_tile = tile // 4
    for z in range(ZOUT):
        for c in range(channels):
            cells_of = pltpu.roll(edge[z, c // per_tile], (tile - 2 - 4 * (c % per_tile)) % tile, 1)
            cells_of = jnp.where((lane < 2) | (lane >= tile - 2), cells_of, 0.0)
            at = slice(c * OUTER, c * OUTER + slots)
            depth[z, at, :] = depth_in[z, at, :] + cells_of

    size = channels * ROWS
    tall = (size, channels)
    flat = (channels, size)
    grow = ((row_iota(tall) >> 3) == lane_iota(tall)).astype(BF16)
    stretch = ((lane_iota(flat) >> 3) == row_iota(flat)).astype(BF16)
    repeated = jnp.dot(grow, mix[...], preferred_element_type=F32).astype(BF16)
    repeated = jnp.dot(repeated, stretch, preferred_element_type=F32)
    square = (size, size)
    same = (row_iota(square) & (ROWS - 1)) == (lane_iota(square) & (ROWS - 1))
    spread[...] = jnp.where(same, repeated, 0.0).astype(BF16)

    total = XW * slabs
    start = jnp.int32(0)
    for d in range(slabs):
        start = start + jnp.where(d < slab, widths[d], 0)
    shape = (ncy, tile)
    cell = row_iota(shape) * CF
    place = lane_iota(shape) + here * tile
    along_y = ((place >= cell) & (place < cell + CF)).astype(F32)
    shape = (slots, ncx)
    cell = lane_iota(shape)
    if not gathered:
        even = is_even("gy")
        after, before = lax.rem(here + 1, 4), lax.rem(here + 3, 4)
        owners = (here, jnp.where(even, after, before), jnp.where(even, before, after), lax.rem(here + 2, 4))
        index = cell
        cell = jnp.zeros(shape, jnp.int32)
        for i, owner in enumerate(owners):
            inside = (index >= i * own_rows) & (index < (i + 1) * own_rows)
            cell = jnp.where(inside, index + (owner - i) * own_rows, cell)
        cells[...] = jnp.zeros_like(cells)
        for k in range(parts):
            cells[k, 0:own_rows, 0:ncy] = own_block[k]
            cells[k, 3 * own_rows : ncx, 0:ncy] = opposite[k]
        strip = slots * planes.shape[0]
        for i, message in ((1, first), (2, second)):
            terms = message[strip:, 0:ncy].astype(F32)
            count = parts * own_rows
            sums = terms[0:count] + terms[count : 2 * count] + terms[2 * count : 3 * count]
            for k in range(parts):
                cells[k, i * own_rows : (i + 1) * own_rows, :] = sums[k * own_rows : (k + 1) * own_rows]
    cell = cell * CF
    place = row_iota(shape) + start
    place = jnp.where(place >= total, place - total, place)
    along_x = ((place >= cell) & (place < cell + CF)).astype(F32)
    lifted = []
    for k in range(parts):
        block = coarse[k] if gathered else cells[k]
        across = jnp.dot(block, along_y, precision=lax.Precision.HIGHEST, preferred_element_type=F32)
        lifted.append(jnp.dot(along_x, across, precision=lax.Precision.HIGHEST, preferred_element_type=F32))
    for o in range(channels):
        lift_o = lift[o, 0] * lifted[0] + lift[o, 1] * lifted[1] + lift[o, 2] * lifted[2]
        for z in range(ZOUT):
            base[z, o] = planes[2 + z, o].astype(F32) + lift_o


def finish_kernel(widths, pw_bias, base, spread, near, far, depth_in, out, depth, mixed_in, mixed, block, sems):
    slab = lax.axis_index("gx")
    width = widths[slab]
    _, channels, slots, tile = base.shape
    even = is_even("gx")
    rows = ZOUT * channels
    for arrived, at_top in ((near, jnp.logical_not(even)), (far, even)):
        begin = jnp.where(at_top, 0, width - 2)
        for r in range(2):
            for z in range(ZOUT):
                at = pl.ds(begin + r, channels, stride=OUTER)
                begin_row = r * rows + z * channels
                depth[z, at, :] = depth_in[z, at, :] + arrived[begin_row : begin_row + channels, :].astype(F32)
    for b in range(slots // ROWS):
        for c in range(0, channels, 2):
            for z in range(ZOUT):
                both = [depth[z, (c + k) * OUTER + ROWS * b : (c + k) * OUTER + ROWS * (b + 1), :] for k in range(2)]
                both = jnp.concatenate(both, axis=0).astype(BF16)
                mixed_in[b, c * ROWS : (c + 2) * ROWS, z * tile : (z + 1) * tile] = both
        mixed[b] = jnp.dot(spread[...], mixed_in[b], preferred_element_type=F32)

    valid = row_iota((slots, tile)) < width
    chunk = 16
    copies = []
    for part in range(channels // chunk):
        for k in range(chunk):
            o = part * chunk + k
            for z in range(ZOUT):
                value = jnp.concatenate(
                    [
                        mixed[b, o * ROWS : (o + 1) * ROWS, z * tile : (z + 1) * tile]
                        for b in range(slots // ROWS)
                    ],
                    axis=0,
                )
                value = value + pw_bias[o]
                value = jnp.maximum(value, 0.2 * value) + base[z, o]
                block[z, o] = jnp.where(valid, value, 0.0).astype(BF16)
        for z in range(ZOUT):
            part_of = pl.ds(part * chunk, chunk)
            copy = pltpu.make_async_copy(block.at[z, part_of], out.at[z, part_of], sems.at[part, z])
            copy.start()
            copies.append(copy)
    for copy in copies:
        copy.wait()


def shards(feature, widths, dw_weight, dw_bias, pw_weight, pw_bias, lift_weight, coarse):
    planes, channels, slots, tile = feature.shape
    ny = lax.axis_size("gy")
    parts, own_rows, ncy = coarse.shape
    gathered = ny != 4
    smem = pl.BlockSpec(memory_space=pltpu.SMEM)
    vmem = pl.BlockSpec(memory_space=pltpu.VMEM)
    hbm = pl.BlockSpec(memory_space=pltpu.HBM)
    params = pltpu.CompilerParams(vmem_limit_bytes=VMEM_BYTES)
    shape = jax.ShapeDtypeStruct
    strip = shape((planes * slots + 32, tile), BF16)
    depth_shape = pltpu.VMEM((ZOUT, channels * OUTER, tile), F32)
    base_shape = pltpu.VMEM((ZOUT, channels, slots, tile), F32)
    message = shape((2 * ZOUT * channels, tile), BF16)
    size = channels * ROWS

    def swapped(array, axis, first):
        count = lax.axis_size(axis)
        pairs = []
        for i in range(first, count + first, 2):
            a, b = i % count, (i + 1) % count
            pairs += [(a, b), (b, a)]
        return lax.ppermute(array, axis, pairs)

    if gathered:
        every = lax.all_gather(coarse, "gy", axis=1, tiled=True)
    else:
        opposite = lax.ppermute(coarse, "gy", [(i, (i + 2) % 4) for i in range(4)])
    held, band, first, second = pl.pallas_call(
        pack_kernel,
        out_shape=(
            pltpu.VMEM(feature.shape, BF16),
            pltpu.VMEM((channels, 3 * OUTER, 2 * tile), BF16),
            strip,
            strip,
        ),
        in_specs=[hbm] * 4,
        out_specs=(vmem,) * 4,
        scratch_shapes=[
            pltpu.VMEM((9, channels, 2 * tile), F32),
            pltpu.SMEM(widths.shape, jnp.int32),
            pltpu.VMEM(dw_weight.shape, F32),
            pltpu.VMEM(coarse.shape, F32),
            pltpu.VMEM((32, tile), F32),
            pltpu.SemaphoreType.DMA((planes,)),
            pltpu.SemaphoreType.DMA((3,)),
        ],
        compiler_params=params,
    )(widths, feature, dw_weight, coarse)
    first = swapped(first, "gy", 0)
    second = swapped(second, "gy", 1)
    depth = pl.pallas_call(
        conv_kernel,
        out_shape=depth_shape,
        in_specs=[smem, vmem, vmem],
        out_specs=vmem,
        compiler_params=params,
        cost_estimate=pl.CostEstimate(flops=10**9, bytes_accessed=10**6, transcendentals=0),
    )(dw_bias, held, band)
    edge, near, far = pl.pallas_call(
        rim_kernel,
        out_shape=(pltpu.VMEM((ZOUT, 2, slots, tile), F32), message, message),
        in_specs=[smem] + [vmem] * 4,
        out_specs=(vmem,) * 3,
        scratch_shapes=[
            pltpu.VMEM((planes, slots + 16, 2 * tile), F32),
            pltpu.VMEM((2, slots + 8, tile), F32),
            pltpu.VMEM((ZOUT, 2, ROWS, tile), F32),
            pltpu.VMEM((ZOUT * channels * ROWS, tile), F32),
        ],
        compiler_params=params,
    )(widths, dw_weight, first, second, depth)
    near = swapped(near, "gx", 0)
    far = swapped(far, "gx", 1)
    rows = (every,) if gathered else (first, second, coarse, opposite)
    depth, spread, base = pl.pallas_call(
        functools.partial(settle_kernel, gathered),
        out_shape=(depth_shape, pltpu.VMEM((size, size), BF16), base_shape),
        in_specs=[smem, smem] + [vmem] * (4 + len(rows)),
        out_specs=(vmem,) * 3,
        scratch_shapes=[] if gathered else [pltpu.VMEM((parts, 4 * own_rows, ncy), F32)],
        input_output_aliases={5 + len(rows): 0},
        compiler_params=params,
        cost_estimate=pl.CostEstimate(flops=10**9, bytes_accessed=10**6, transcendentals=0),
    )(widths, lift_weight, pw_weight, held, *rows, edge, depth)
    out, _ = pl.pallas_call(
        finish_kernel,
        out_shape=(shape((ZOUT, channels, slots, tile), BF16), depth_shape),
        in_specs=[smem, smem] + [vmem] * 5,
        out_specs=(hbm, vmem),
        scratch_shapes=[
            pltpu.VMEM((slots // ROWS, size, ZOUT * tile), BF16),
            pltpu.VMEM((slots // ROWS, size, ZOUT * tile), F32),
            pltpu.VMEM((ZOUT, channels, slots, tile), BF16),
            pltpu.SemaphoreType.DMA((channels // 16, ZOUT)),
        ],
        input_output_aliases={6: 1},
        compiler_params=params,
    )(widths, pw_bias, base, spread, near, far, depth)
    return out


def solution(mesh):
    placed = (P(None, None, "gx", "gy"), P(), P(), P(), P(), P(), P(), P(None, "gy", None))
    return jax.shard_map(
        shards, mesh=mesh, in_specs=placed, out_specs=P(None, None, "gx", "gy"), check_vma=False
    )
```

```python
import functools

import jax
import jax.numpy as jnp
from jax import lax
from jax.experimental import pallas as pl
from jax.experimental.pallas import tpu as pltpu
from jax.sharding import PartitionSpec as P

XW = 16
ZOUT = 2
CF = 16
ROWS = 8
FIRST_LANE = 10
DW_BIAS, PW_BIAS, LIFT = 27, 28, 29
F32 = jnp.float32
BF16 = jnp.bfloat16
VMEM_BYTES = 14 * 1024 * 1024


def lane_iota(shape):
    return lax.broadcasted_iota(jnp.int32, shape, len(shape) - 1)


def row_iota(shape):
    return lax.broadcasted_iota(jnp.int32, shape, len(shape) - 2)


def tap_of(m, dx, dy):
    return 9 * m + 3 * (dx + 1) + (dy + 1)


def is_even(axis):
    return lax.rem(lax.axis_index(axis), 2) == 0


def pack_kernel(
    feature, widths_in, taps_in, dw_bias_in, pw_bias_in, lift_in, coarse_in,
    cells, weights, first, second,
    planes, widths, taps, dw_bias, pw_bias, lift, coarse, stacked, tail, sems, small_sems,
):
    count, channels, slots, tile = feature.shape

    def copy_of(z):
        return pltpu.make_async_copy(feature.at[z], planes.at[z], sems.at[z])

    small = [
        pltpu.make_async_copy(source, target, small_sems.at[i])
        for i, (source, target) in enumerate(
            (
                (widths_in, widths),
                (taps_in, taps),
                (dw_bias_in, dw_bias),
                (pw_bias_in, pw_bias),
                (lift_in, lift),
                (coarse_in, coarse),
            )
        )
    ]
    for copy in small:
        copy.start()
    for z in range(count):
        copy_of(z).start()
    for copy in small:
        copy.wait()
    width = widths[lax.axis_index("gx")]

    stacked[0:DW_BIAS, :] = taps[...]
    stacked[DW_BIAS : DW_BIAS + 1, :] = dw_bias[...]
    stacked[PW_BIAS : PW_BIAS + 1, :] = pw_bias[...]
    stacked[LIFT : LIFT + 3, :] = lift[...]
    turned = jnp.transpose(stacked[...])
    for t in range(stacked.shape[0]):
        weights[t] = jnp.broadcast_to(turned[:, t : t + 1], (channels, tile))

    parts, own_rows, ncy = coarse.shape
    tail[...] = jnp.zeros_like(tail)
    for k in range(parts):
        rest = coarse[k]
        for p in range(3):
            term = rest.astype(BF16).astype(F32)
            rest = rest - term
            at = (p * parts + k) * own_rows
            tail[at : at + own_rows, 0:ncy] = term
    strip = count // 2 * channels
    for message in (first, second):
        message[strip:, :] = tail[...].astype(BF16)

    valid = row_iota((slots, tile)) < width
    block = 16
    lane = lane_iota((block, tile))
    on_right = (lane & 2) != 0
    even = is_even("gy")

    for z in range(0, count, 2):
        for k in range(2):
            copy_of(z + k).wait()
            for c in range(channels):
                cells[z + k, c * slots : (c + 1) * slots, :] = jnp.where(valid, planes[z + k, c].astype(F32), 0.0)
        for c in range(0, channels, block):
            one = edge_columns(cells, z, c, block, slots, lane)
            two = pltpu.roll(edge_columns(cells, z + 1, c, block, slots, lane), 2, 1)
            left = jnp.where(on_right, two, one)
            right = jnp.where(on_right, one, two)
            at = slice(z // 2 * channels + c, z // 2 * channels + c + block)
            first[at, :] = jnp.where(even, right, left).astype(BF16)
            second[at, :] = jnp.where(even, left, right).astype(BF16)


def edge_columns(cells, z, c, block, slots, lane):
    def merged(x, stride):
        if x >= slots:
            return None
        if 4 * stride == lane.shape[1]:
            return cells[z, pl.ds(c * slots + x, block, stride=slots), :]
        one = merged(x, 2 * stride)
        other = merged(x + stride, 2 * stride)
        if other is None:
            return one
        other = pltpu.roll(other, 4 * stride, 1)
        return jnp.where(((lane + 2 * stride) & (4 * stride)) != 0, other, one)

    return merged(0, 1)


def conv_kernel(cells, weights, depth):
    channels, tile = weights.shape[1:]
    slots = cells.shape[1] // channels
    lane = lane_iota((ROWS, tile))

    def convolve(b, carry):
        at = pl.ds(pl.multiple_of(b * ROWS, ROWS), ROWS)
        tap = [weights[t, at, :] for t in range(27)]
        for z in range(ZOUT):
            for parity in range(2):
                sums = {}
                for x in range(parity, slots + 2, 2):
                    if x < slots:
                        rows = [cells[z + ZOUT * m, pl.ds(b * (ROWS * slots) + x, ROWS, stride=slots), :] for m in range(3)]
                        for m in range(3):
                            for dx in (1, 0, -1):
                                for dy in (-1, 0, 1):
                                    term = tap[tap_of(m, dx, dy)] * rows[m]
                                    key = (x - 2 * dx, dy)
                                    sums[key] = sums[key] + term if key in sums else term
                    done = [x - 2] if x < slots else [x - 2, x]
                    for out in done:
                        before, centre, after = (sums.pop((out, dy)) for dy in (-1, 0, 1))
                        before = jnp.where(lane < 2, 0.0, pltpu.roll(before, 2, 1))
                        after = jnp.where(lane >= tile - 2, 0.0, pltpu.roll(after, tile - 2, 1))
                        depth[z, out + 2, at, :] = centre + before + after
        return carry

    lax.fori_loop(0, channels // ROWS, convolve, 0)


def edge_term(edge, z, shift):
    cells = pltpu.roll(edge[z], shift, 1)
    lane = lane_iota(cells.shape)
    return jnp.where((lane < 2) | (lane >= cells.shape[1] - 2), cells, 0.0)


def edge_shift(x, tile):
    shift = tile - 2 - FIRST_LANE - 4 * x
    if isinstance(x, int):
        return shift % tile
    return lax.rem(shift + tile, tile)


def rim_kernel(widths, weights, first, second, depth, edge, near, far):
    width = widths[lax.axis_index("gx")]
    channels, tile = weights.shape[1:]
    even = is_even("gy")
    lane = lane_iota((channels, tile))
    inside = (lane >= FIRST_LANE) & (lane < FIRST_LANE + 4 * width)
    on_right = ((lane - FIRST_LANE) & 2) == 0
    halo = []
    for pair in range(3):
        at = slice(pair * channels, (pair + 1) * channels)
        one, two = first[at, :].astype(F32), second[at, :].astype(F32)
        right = jnp.where(even, one, two)
        left = jnp.where(even, two, one)
        for k in range(2):
            right_k = pltpu.roll(right, FIRST_LANE - 2 * k, 1)
            left_k = pltpu.roll(left, FIRST_LANE + 4 - 2 * k, 1)
            halo.append(jnp.where(inside, jnp.where(on_right, right_k, left_k), 0.0))
    for z in range(ZOUT):
        total = None
        for m in range(3):
            for dx in (-1, 0, 1):
                weight = jnp.where(on_right, weights[tap_of(m, dx, 1)], weights[tap_of(m, dx, -1)])
                rows = halo[z + ZOUT * m]
                if dx:
                    rows = pltpu.roll(rows, (-8 * dx) % tile, 1)
                total = weight * rows if total is None else total + weight * rows
        edge[z] = total
    even = is_even("gx")
    for z in range(ZOUT):
        for r in range(2):
            to_lower = depth[z, r] + edge_term(edge, z, edge_shift(r - 2, tile))
            to_upper = depth[z, width + 2 + r] + edge_term(edge, z, edge_shift(width + r, tile))
            at = slice((2 * z + r) * channels, (2 * z + r + 1) * channels)
            near[at, :] = jnp.where(even, to_upper, to_lower).astype(BF16)
            far[at, :] = jnp.where(even, to_lower, to_upper).astype(BF16)


def slab_start(widths):
    slab = lax.axis_index("gx")
    start = jnp.int32(0)
    for d in range(widths.shape[0]):
        start = start + jnp.where(d < slab, widths[d], 0)
    return start


def depth_row(weights, depth, edge, z, x, tile):
    return depth[z, x + 2] + weights[DW_BIAS] + edge_term(edge, z, edge_shift(x, tile))


def finished_row(weights, cells, lifted, phase, width, mixed, z, x):
    channels = weights.shape[1]
    slots = cells.shape[1] // channels
    mixed = mixed + weights[PW_BIAS]
    active = jnp.maximum(mixed, 0.2 * mixed)
    field = cells[2 + z, pl.ds(x, channels, stride=slots), :]
    value = active + (field + lifted[lax.div(phase + x, CF)])
    return jnp.where(x < width, value, 0.0)


def mix_kernel(gathered, widths, mix, cells, weights, depth, edge, *refs):
    if gathered:
        coarse, value, lifted, mixer, across = refs
        parts, ncx, ncy = coarse.shape
    else:
        first, second, own_block, opposite, value, lifted, mixer, across, blocks = refs
        parts, own_rows, ncy = own_block.shape
        ncx = 4 * own_rows
    width = widths[lax.axis_index("gx")]
    here = lax.axis_index("gy")
    start = slab_start(widths)
    phase = lax.rem(start, CF)
    channels, tile = weights.shape[1:]
    slots = cells.shape[1] // channels

    if not gathered:
        even = is_even("gy")
        after, before = lax.rem(here + 1, 4), lax.rem(here + 3, 4)
        count = parts * own_rows
        strip = 3 * channels
        for message, owner in (
            (first, jnp.where(even, after, before)),
            (second, jnp.where(even, before, after)),
        ):
            terms = message[strip:, 0:ncy].astype(F32)
            sums = terms[0:count] + terms[count : 2 * count] + terms[2 * count : 3 * count]
            for k in range(parts):
                blocks[k, pl.ds(owner * own_rows, own_rows), :] = sums[k * own_rows : (k + 1) * own_rows]
        for block, owner in ((own_block, here), (opposite, lax.rem(here + 2, 4))):
            for k in range(parts):
                blocks[k, pl.ds(owner * own_rows, own_rows), :] = block[k]
    shape = (ncy, tile)
    cell = row_iota(shape) * CF
    place = lane_iota(shape) + here * tile
    along_y = ((place >= cell) & (place < cell + CF)).astype(F32)
    for k in range(parts):
        block = coarse[k] if gathered else blocks[k]
        across[k] = jnp.dot(block, along_y, precision=lax.Precision.HIGHEST, preferred_element_type=F32)
    for i in range(3):
        cell = lax.rem(lax.div(start, CF) + i, ncx)
        total = None
        for k in range(parts):
            term = weights[LIFT + k] * across[k, pl.ds(cell, 1), :]
            total = term if total is None else total + term
        lifted[i] = total

    group = 4
    wide = jnp.concatenate([mix[...]] * group, axis=1)
    wide = jnp.concatenate([wide] * group, axis=0)
    size = group * channels
    row, column = row_iota((size, size)), lane_iota((size, size))
    same = sum(
        ((row >= i * channels) & (row < (i + 1) * channels) & (column >= i * channels) & (column < (i + 1) * channels)).astype(F32)
        for i in range(group)
    )
    mixer[...] = jnp.where(same > 0, wide.astype(F32), 0.0).astype(BF16)

    for x in range(0, slots, group):
        depths = [
            jnp.concatenate([depth_row(weights, depth, edge, z, x + i, tile) for i in range(group)], axis=0).astype(BF16)
            for z in range(ZOUT)
        ]
        mixed = jnp.dot(mixer[...], jnp.concatenate(depths, axis=1), preferred_element_type=F32)
        for i in range(group):
            for z in range(ZOUT):
                part = mixed[i * channels : (i + 1) * channels, z * tile : (z + 1) * tile]
                value[z, pl.ds(x + i, channels, stride=slots), :] = finished_row(
                    weights, cells, lifted, phase, width, part, z, x + i
                )


def finish_kernel(widths, cells, weights, depth, edge, lifted, mixer, near, far, value_in, out, value, block, sems):
    width = widths[lax.axis_index("gx")]
    phase = lax.rem(slab_start(widths), CF)
    channels, tile = weights.shape[1:]
    slots = cells.shape[1] // channels
    even = is_even("gx")
    at_top = jnp.where(even, far[...].astype(F32), near[...].astype(F32))
    at_end = jnp.where(even, near[...].astype(F32), far[...].astype(F32))
    rows = (0, 1, width - 2, width - 1)
    depths = []
    for z in range(ZOUT):
        parts = []
        for i, x in enumerate(rows):
            arrived = at_top if i < 2 else at_end
            begin = (2 * z + i % 2) * channels
            parts.append(depth_row(weights, depth, edge, z, x, tile) + arrived[begin : begin + channels, :])
        depths.append(jnp.concatenate(parts, axis=0).astype(BF16))
    mixed = jnp.dot(mixer[...], jnp.concatenate(depths, axis=1), preferred_element_type=F32)
    for i, x in enumerate(rows):
        for z in range(ZOUT):
            part = mixed[i * channels : (i + 1) * channels, z * tile : (z + 1) * tile]
            value[z, pl.ds(x, channels, stride=slots), :] = finished_row(
                weights, cells, lifted, phase, width, part, z, x
            )
    chunk = 16
    copies = []
    for z in range(ZOUT):
        for part in range(channels // chunk):
            for o in range(part * chunk, (part + 1) * chunk):
                block[z, o] = value[z, o * slots : (o + 1) * slots, :].astype(BF16)
            part_of = pl.ds(part * chunk, chunk)
            copy = pltpu.make_async_copy(block.at[z, part_of], out.at[z, part_of], sems.at[part, z])
            copy.start()
            copies.append(copy)
    for copy in copies:
        copy.wait()


def shards(feature, widths, dw_weight, dw_bias, pw_weight, pw_bias, lift_weight, coarse):
    planes, channels, slots, tile = feature.shape
    ny = lax.axis_size("gy")
    parts, own_rows, ncy = coarse.shape
    gathered = ny != 4
    ncx = ny * own_rows
    smem = pl.BlockSpec(memory_space=pltpu.SMEM)
    vmem = pl.BlockSpec(memory_space=pltpu.VMEM)
    hbm = pl.BlockSpec(memory_space=pltpu.HBM)
    params = pltpu.CompilerParams(vmem_limit_bytes=VMEM_BYTES)
    shape = jax.ShapeDtypeStruct
    strip = shape((planes // 2 * channels + 32, tile), BF16)
    cells_shape = pltpu.VMEM((planes, channels * slots, tile), F32)
    value_shape = pltpu.VMEM((ZOUT, channels * slots, tile), F32)
    message = shape((2 * ZOUT * channels, tile), BF16)

    def swapped(array, axis, first):
        count = lax.axis_size(axis)
        pairs = []
        for i in range(first, count + first, 2):
            a, b = i % count, (i + 1) % count
            pairs += [(a, b), (b, a)]
        return lax.ppermute(array, axis, pairs)

    def pinned(array):
        return pltpu.with_memory_space_constraint(array, pltpu.HBM)

    if gathered:
        every = lax.all_gather(coarse, "gy", axis=1, tiled=True)
    else:
        opposite = lax.ppermute(coarse, "gy", [(i, (i + 2) % 4) for i in range(4)])
    small = (
        widths,
        dw_weight,
        dw_bias.reshape(1, channels),
        pw_bias.reshape(1, channels),
        lift_weight.T,
        coarse,
    )
    cells, weights, first, second = pl.pallas_call(
        pack_kernel,
        out_shape=(cells_shape, pltpu.VMEM((32, channels, tile), F32), strip, strip),
        in_specs=[hbm] * 7,
        out_specs=(vmem,) * 4,
        scratch_shapes=[
            pltpu.VMEM(feature.shape, BF16),
            pltpu.SMEM(widths.shape, jnp.int32),
            pltpu.VMEM(dw_weight.shape, F32),
            pltpu.VMEM((1, channels), F32),
            pltpu.VMEM((1, channels), F32),
            pltpu.VMEM((parts, channels), F32),
            pltpu.VMEM(coarse.shape, F32),
            pltpu.VMEM((32, channels), F32),
            pltpu.VMEM((32, tile), F32),
            pltpu.SemaphoreType.DMA((planes,)),
            pltpu.SemaphoreType.DMA((len(small),)),
        ],
        compiler_params=params,
    )(pinned(feature), *(pinned(array) for array in small))
    first = swapped(first, "gy", 0)
    second = swapped(second, "gy", 1)
    depth = pl.pallas_call(
        conv_kernel,
        out_shape=pltpu.VMEM((ZOUT, slots + 4, channels, tile), F32),
        in_specs=[vmem, vmem],
        out_specs=vmem,
        compiler_params=params,
        cost_estimate=pl.CostEstimate(flops=10**9, bytes_accessed=10**6, transcendentals=0),
    )(cells, weights)
    edge, near, far = pl.pallas_call(
        rim_kernel,
        out_shape=(pltpu.VMEM((ZOUT, channels, tile), F32), message, message),
        in_specs=[smem] + [vmem] * 4,
        out_specs=(vmem,) * 3,
        compiler_params=params,
    )(widths, weights, first, second, depth)
    near = swapped(near, "gx", 0)
    far = swapped(far, "gx", 1)
    blocks = (every,) if gathered else (first, second, coarse, opposite)
    value, lifted, mixer = pl.pallas_call(
        functools.partial(mix_kernel, gathered),
        out_shape=(
            value_shape,
            pltpu.VMEM((3, channels, tile), F32),
            pltpu.VMEM((4 * channels, 4 * channels), BF16),
        ),
        in_specs=[smem] + [vmem] * (5 + len(blocks)),
        out_specs=(vmem,) * 3,
        scratch_shapes=[pltpu.VMEM((parts, ncx, tile), F32)]
        + ([] if gathered else [pltpu.VMEM((parts, ncx, ncy), F32)]),
        compiler_params=params,
        cost_estimate=pl.CostEstimate(flops=10**9, bytes_accessed=10**6, transcendentals=0),
    )(widths, pw_weight, cells, weights, depth, edge, *blocks)
    out, _ = pl.pallas_call(
        finish_kernel,
        out_shape=(shape((ZOUT, channels, slots, tile), BF16), value_shape),
        in_specs=[smem] + [vmem] * 9,
        out_specs=(hbm, vmem),
        scratch_shapes=[
            pltpu.VMEM((ZOUT, channels, slots, tile), BF16),
            pltpu.SemaphoreType.DMA((channels // 16, ZOUT)),
        ],
        input_output_aliases={9: 1},
        compiler_params=params,
    )(widths, cells, weights, depth, edge, lifted, mixer, near, far, value)
    return out


def solution(mesh):
    placed = (P(None, None, "gx", "gy"), P(), P(), P(), P(), P(), P(), P(None, "gy", None))
    return jax.shard_map(
        shards, mesh=mesh, in_specs=placed, out_specs=P(None, None, "gx", "gy"), check_vma=False
    )
```

```python
import functools

import jax
import jax.numpy as jnp
from jax import lax
from jax.experimental import pallas as pl
from jax.experimental.pallas import tpu as pltpu
from jax.sharding import PartitionSpec as P

XW = 16
ZOUT = 2
CF = 16
ROWS = 8
SPLIT = 4
CHUNK = 16
DW_BIAS, PW_BIAS, LIFT = 27, 28, 29
F32 = jnp.float32
BF16 = jnp.bfloat16
VMEM_BYTES = 14 * 1024 * 1024


def lane_iota(shape):
    return lax.broadcasted_iota(jnp.int32, shape, len(shape) - 1)


def row_iota(shape):
    return lax.broadcasted_iota(jnp.int32, shape, len(shape) - 2)


def tap_of(m, dx, dy):
    return 9 * m + 3 * (dx + 1) + (dy + 1)


def is_even(axis):
    return lax.rem(lax.axis_index(axis), 2) == 0


def pack_kernel(
    feature, widths_in, taps_in, dw_bias_in, pw_bias_in, lift_in, coarse_in,
    planes, weights, first, second,
    widths, taps, dw_bias, pw_bias, lift, coarse, stacked, tail, picked, sems, small_sems,
):
    count, channels, slots, tile = feature.shape
    chunks = range(0, channels, CHUNK)

    def copy_of(c):
        at = pl.ds(c, CHUNK)
        return pltpu.make_async_copy(feature.at[:, at], planes.at[:, at], sems.at[c // CHUNK])

    small = [
        pltpu.make_async_copy(source, target, small_sems.at[i])
        for i, (source, target) in enumerate(
            (
                (widths_in, widths),
                (taps_in, taps),
                (dw_bias_in, dw_bias),
                (pw_bias_in, pw_bias),
                (lift_in, lift),
                (coarse_in, coarse),
            )
        )
    ]
    for copy in small:
        copy.start()
    for c in chunks:
        copy_of(c).start()

    shape = (tile, tile)
    lane, row = lane_iota(shape), row_iota(shape)
    column = jnp.where((lane & 3) < 2, tile - 2 + (lane & 3), (lane & 3) - 2)
    plane = (lane & 31) >> 2
    picks = jnp.concatenate(
        [((row == column) & (plane == z)).astype(F32) for z in range(count)], axis=0
    ).astype(BF16)

    for copy in small:
        copy.wait()
    width = widths[lax.axis_index("gx")]
    stacked[0:DW_BIAS, :] = taps[...]
    stacked[DW_BIAS : DW_BIAS + 1, :] = dw_bias[...]
    stacked[PW_BIAS : PW_BIAS + 1, :] = pw_bias[...]
    stacked[LIFT : LIFT + 3, :] = lift[...]
    turned = jnp.transpose(stacked[...])
    for t in range(stacked.shape[0]):
        weights[t] = jnp.broadcast_to(turned[:, t : t + 1], (channels, tile))

    parts, own_rows, ncy = coarse.shape
    tail[...] = jnp.zeros_like(tail)
    if 3 * ncy <= tile:
        for k in range(parts):
            rest = coarse[k]
            for p in range(3):
                term = rest.astype(BF16).astype(F32)
                rest = rest - term
                tail[k * own_rows : (k + 1) * own_rows, p * ncy : (p + 1) * ncy] = term
    for message in (first, second):
        message[channels:, :] = tail[...].astype(BF16)

    shape = (channels, tile)
    lane = lane_iota(shape)
    member = (lane & 31) >> 3
    on_left = (lane & 2) != 0
    scale = []
    for dx in (-1, 0, 1):
        total = None
        for m in range(3):
            weight = jnp.where(on_left, weights[tap_of(m, dx, 1)], weights[tap_of(m, dx, -1)])
            total = weight if total is None else jnp.where(member == m, weight, total)
        scale.append(total)

    for c in chunks:
        copy_of(c).wait()
        rows = [
            jnp.concatenate([planes[z, c + k].astype(F32) for k in range(CHUNK)], axis=0).astype(BF16)
            for z in range(count)
        ]
        picked[c * slots : (c + CHUNK) * slots, :] = jnp.dot(
            jnp.concatenate(rows, axis=1), picks, preferred_element_type=F32
        )

    groups = slots // 4
    held, moved = {}, {}
    for q in range(groups):
        rows = [picked[pl.ds(4 * q + i, channels, stride=slots), :] for i in range(4)]
        rows = jnp.where(
            lane < 64, jnp.where(lane < 32, rows[0], rows[1]), jnp.where(lane < 96, rows[2], rows[3])
        )
        held[q] = jnp.where(4 * q + (lane >> 5) < width, rows, 0.0)
    for q in range(-1, groups):
        low = held.get(q + 1, jnp.zeros(shape, F32))
        high = held.get(q, jnp.zeros(shape, F32))
        moved[q] = pltpu.roll(jnp.where(lane < 64, low, high), 64, 1)
    sums = []
    for q in range(-1, groups + 1):
        total = None
        for weight, rows in ((scale[0], moved.get(q - 1)), (scale[1], held.get(q)), (scale[2], moved.get(q))):
            if rows is not None:
                total = weight * rows if total is None else total + weight * rows
        sums.append(total + pltpu.roll(total, tile - 8, 1) + pltpu.roll(total, tile - 16, 1))
    packed = []
    for half in range(2):
        total = sums[4 * half]
        for k in range(1, 4):
            total = jnp.where(((lane >> 3) & 3) == k, pltpu.roll(sums[4 * half + k], 8 * k, 1), total)
        packed.append(total)
    left = jnp.where(on_left, packed[0], pltpu.roll(packed[1], tile - 2, 1))
    right = jnp.where(on_left, pltpu.roll(packed[1], 2, 1), packed[0])
    even = is_even("gy")
    first[0:channels, :] = jnp.where(even, right, left).astype(BF16)
    second[0:channels, :] = jnp.where(even, left, right).astype(BF16)


def shifted_sum(before, centre, after):
    lane = lane_iota(centre.shape)
    tile = centre.shape[-1]
    before = jnp.where(lane < 2, 0.0, pltpu.roll(before, 2, 1))
    after = jnp.where(lane >= tile - 2, 0.0, pltpu.roll(after, tile - 2, 1))
    return centre + before + after


def convolve_block(cells, weights, depth, b, first_block):
    channels = weights.shape[1]
    slots = cells.shape[1] // channels
    at = pl.ds(pl.multiple_of(b * ROWS, ROWS), ROWS)
    to = pl.ds(pl.multiple_of((b - first_block) * ROWS, ROWS), ROWS)
    tap = [weights[t, at, :] for t in range(27)]
    for z in range(ZOUT):
        for parity in range(2):
            sums = {}
            for x in range(parity, slots, 2):
                rows = [cells[z + ZOUT * m, pl.ds(b * (ROWS * slots) + x, ROWS, stride=slots), :] for m in range(3)]
                for m in range(3):
                    for dx in (1, 0, -1):
                        out = x - 2 * dx
                        if 0 <= out < slots:
                            for dy in (-1, 0, 1):
                                term = tap[tap_of(m, dx, dy)] * rows[m]
                                key = (out, dy)
                                sums[key] = sums[key] + term if key in sums else term
                for out in [x - 2] if x + 2 < slots else [x - 2, x]:
                    if out >= 0:
                        depth[z, out, to, :] = shifted_sum(*(sums.pop((out, dy)) for dy in (-1, 0, 1)))


def conv_kernel(widths, planes, weights, cells, depth, rims):
    width = widths[lax.axis_index("gx")]
    count, channels, slots, tile = planes.shape
    valid = row_iota((slots, tile)) < width

    def outer_rows(b, carry):
        for z in range(count):
            for k in range(ROWS):
                at = pl.ds(pl.multiple_of((b * ROWS + k) * slots, ROWS), slots)
                cells[z, at, :] = jnp.where(valid, planes[z, b * ROWS + k].astype(F32), 0.0)
        at = pl.ds(pl.multiple_of(b * ROWS, ROWS), ROWS)
        for i, (x, dx) in enumerate(((0, 1), (1, 1), (width - 2, -1), (width - 1, -1))):
            for z in range(ZOUT):
                rows = [cells[z + ZOUT * m, pl.ds(b * (ROWS * slots) + x, ROWS, stride=slots), :] for m in range(3)]
                parts = [
                    sum(weights[tap_of(m, dx, dy), at, :] * rows[m] for m in range(3)) for dy in (-1, 0, 1)
                ]
                rims[z, i, at, :] = shifted_sum(*parts)
        return carry

    lax.fori_loop(0, channels // ROWS, outer_rows, 0)

    def convolve(b, carry):
        convolve_block(cells, weights, depth, b, 0)
        return carry

    lax.fori_loop(0, SPLIT, convolve, 0)


def edge_term(edge, z, x):
    tile = edge.shape[2]
    group = x // 4 + 1 if isinstance(x, int) else lax.div(x, 4) + 1
    at = x % 4 if isinstance(x, int) else lax.rem(x, 4)
    begin = 32 * at + 8 * (group & 3) + 4 * z
    cells = pltpu.roll(edge[group >> 2], tile - 2 - begin, 1)
    lane = lane_iota(cells.shape)
    return jnp.where((lane < 2) | (lane >= tile - 2), cells, 0.0)


def rim_kernel(widths, first, second, rims, edge, near, far):
    width = widths[lax.axis_index("gx")]
    _, _, channels, tile = rims.shape
    even = is_even("gy")
    one, two = first[0:channels, :].astype(F32), second[0:channels, :].astype(F32)
    right = jnp.where(even, one, two)
    left = jnp.where(even, two, one)
    on_left = (lane_iota((channels, tile)) & 2) != 0
    edge[0] = jnp.where(on_left, pltpu.roll(left, 2, 1), pltpu.roll(right, tile - 2, 1))
    edge[1] = jnp.where(on_left, left, right)
    even = is_even("gx")
    for z in range(ZOUT):
        for r in range(2):
            to_lower = rims[z, r] + edge_term(edge, z, r - 2)
            to_upper = rims[z, 2 + r] + edge_term(edge, z, width + r)
            at = slice((2 * z + r) * channels, (2 * z + r + 1) * channels)
            near[at, :] = jnp.where(even, to_upper, to_lower).astype(BF16)
            far[at, :] = jnp.where(even, to_lower, to_upper).astype(BF16)


def slab_start(widths):
    slab = lax.axis_index("gx")
    start = jnp.int32(0)
    for d in range(widths.shape[0]):
        start = start + jnp.where(d < slab, widths[d], 0)
    return start


def depth_row(weights, depths, edge, z, x):
    own = jnp.concatenate([depth[z, x] for depth in depths], axis=0)
    return own + weights[DW_BIAS] + edge_term(edge, z, x)


def finished_row(weights, cells, lifted, phase, width, mixed, z, x):
    channels = weights.shape[1]
    slots = cells.shape[1] // channels
    mixed = mixed + weights[PW_BIAS]
    active = jnp.maximum(mixed, 0.2 * mixed)
    field = cells[2 + z, pl.ds(x, channels, stride=slots), :]
    value = active + (field + lifted[lax.div(phase + x, CF)])
    return jnp.where(x < width, value, 0.0)


def mix_kernel(gathered, widths, mix, cells, weights, depth, edge, *refs):
    if gathered:
        coarse, value, rest, lifted, mixer, across = refs
        parts, ncx, ncy = coarse.shape
    else:
        first, second, own_block, opposite, value, rest, lifted, mixer, across, blocks = refs
        parts, own_rows, ncy = own_block.shape
        ncx = 4 * own_rows
    width = widths[lax.axis_index("gx")]
    here = lax.axis_index("gy")
    start = slab_start(widths)
    phase = lax.rem(start, CF)
    channels, tile = weights.shape[1:]
    slots = cells.shape[1] // channels

    def convolve(b, carry):
        convolve_block(cells, weights, rest, b, SPLIT)
        return carry

    lax.fori_loop(SPLIT, channels // ROWS, convolve, 0)

    if not gathered:
        even = is_even("gy")
        after, before = lax.rem(here + 1, 4), lax.rem(here + 3, 4)
        count = parts * own_rows
        for message, owner in (
            (first, jnp.where(even, after, before)),
            (second, jnp.where(even, before, after)),
        ):
            terms = message[channels:, :].astype(F32)[0:count, :]
            sums = terms[:, 0:ncy] + terms[:, ncy : 2 * ncy] + terms[:, 2 * ncy : 3 * ncy]
            for k in range(parts):
                blocks[k, pl.ds(owner * own_rows, own_rows), :] = sums[k * own_rows : (k + 1) * own_rows]
        for block, owner in ((own_block, here), (opposite, lax.rem(here + 2, 4))):
            for k in range(parts):
                blocks[k, pl.ds(owner * own_rows, own_rows), :] = block[k]
    shape = (ncy, tile)
    cell = row_iota(shape) * CF
    place = lane_iota(shape) + here * tile
    along_y = ((place >= cell) & (place < cell + CF)).astype(F32)
    for k in range(parts):
        block = coarse[k] if gathered else blocks[k]
        across[k] = jnp.dot(block, along_y, precision=lax.Precision.HIGHEST, preferred_element_type=F32)
    for i in range(3):
        cell = lax.rem(lax.div(start, CF) + i, ncx)
        total = None
        for k in range(parts):
            term = weights[LIFT + k] * across[k, pl.ds(cell, 1), :]
            total = term if total is None else total + term
        lifted[i] = total

    group = 4
    wide = jnp.concatenate([mix[...]] * group, axis=1)
    wide = jnp.concatenate([wide] * group, axis=0)
    size = group * channels
    row, column = row_iota((size, size)), lane_iota((size, size))
    same = sum(
        ((row >= i * channels) & (row < (i + 1) * channels) & (column >= i * channels) & (column < (i + 1) * channels)).astype(F32)
        for i in range(group)
    )
    mixer[...] = jnp.where(same > 0, wide.astype(F32), 0.0).astype(BF16)

    for x in range(0, slots, group):
        depths = [
            jnp.concatenate([depth_row(weights, (depth, rest), edge, z, x + i) for i in range(group)], axis=0).astype(BF16)
            for z in range(ZOUT)
        ]
        mixed = jnp.dot(mixer[...], jnp.concatenate(depths, axis=1), preferred_element_type=F32)
        for i in range(group):
            for z in range(ZOUT):
                part = mixed[i * channels : (i + 1) * channels, z * tile : (z + 1) * tile]
                value[z, pl.ds(x + i, channels, stride=slots), :] = finished_row(
                    weights, cells, lifted, phase, width, part, z, x + i
                )


def finish_kernel(widths, cells, weights, depth, rest, edge, lifted, mixer, near, far, value_in, out, value, block, sems):
    width = widths[lax.axis_index("gx")]
    phase = lax.rem(slab_start(widths), CF)
    channels, tile = weights.shape[1:]
    slots = cells.shape[1] // channels
    even = is_even("gx")
    at_top = jnp.where(even, far[...].astype(F32), near[...].astype(F32))
    at_end = jnp.where(even, near[...].astype(F32), far[...].astype(F32))
    rows = (0, 1, width - 2, width - 1)
    depths = []
    for z in range(ZOUT):
        parts = []
        for i, x in enumerate(rows):
            arrived = at_top if i < 2 else at_end
            begin = (2 * z + i % 2) * channels
            parts.append(depth_row(weights, (depth, rest), edge, z, x) + arrived[begin : begin + channels, :])
        depths.append(jnp.concatenate(parts, axis=0).astype(BF16))
    mixed = jnp.dot(mixer[...], jnp.concatenate(depths, axis=1), preferred_element_type=F32)
    for i, x in enumerate(rows):
        for z in range(ZOUT):
            part = mixed[i * channels : (i + 1) * channels, z * tile : (z + 1) * tile]
            value[z, pl.ds(x, channels, stride=slots), :] = finished_row(
                weights, cells, lifted, phase, width, part, z, x
            )
    chunk = 16
    copies = []
    for z in range(ZOUT):
        for part in range(channels // chunk):
            for o in range(part * chunk, (part + 1) * chunk):
                block[z, o] = value[z, o * slots : (o + 1) * slots, :].astype(BF16)
            part_of = pl.ds(part * chunk, chunk)
            copy = pltpu.make_async_copy(block.at[z, part_of], out.at[z, part_of], sems.at[part, z])
            copy.start()
            copies.append(copy)
    for copy in copies:
        copy.wait()


def shards(feature, widths, dw_weight, dw_bias, pw_weight, pw_bias, lift_weight, coarse):
    planes, channels, slots, tile = feature.shape
    ny = lax.axis_size("gy")
    parts, own_rows, ncy = coarse.shape
    gathered = ny != 4
    ncx = ny * own_rows
    smem = pl.BlockSpec(memory_space=pltpu.SMEM)
    vmem = pl.BlockSpec(memory_space=pltpu.VMEM)
    hbm = pl.BlockSpec(memory_space=pltpu.HBM)
    params = pltpu.CompilerParams(vmem_limit_bytes=VMEM_BYTES)
    shape = jax.ShapeDtypeStruct
    strip = shape((channels + 16, tile), BF16)
    cells_shape = pltpu.VMEM((planes, channels * slots, tile), F32)
    value_shape = pltpu.VMEM((ZOUT, channels * slots, tile), F32)
    message = shape((2 * ZOUT * channels, tile), BF16)

    def swapped(array, axis, first):
        count = lax.axis_size(axis)
        pairs = []
        for i in range(first, count + first, 2):
            a, b = i % count, (i + 1) % count
            pairs += [(a, b), (b, a)]
        return lax.ppermute(array, axis, pairs)

    def pinned(array):
        return pltpu.with_memory_space_constraint(array, pltpu.HBM)

    if gathered:
        every = lax.all_gather(coarse, "gy", axis=1, tiled=True)
    else:
        opposite = lax.ppermute(coarse, "gy", [(i, (i + 2) % 4) for i in range(4)])
    small = (
        widths,
        dw_weight,
        dw_bias.reshape(1, channels),
        pw_bias.reshape(1, channels),
        lift_weight.T,
        coarse,
    )
    held, weights, first, second = pl.pallas_call(
        pack_kernel,
        out_shape=(pltpu.VMEM(feature.shape, BF16), pltpu.VMEM((32, channels, tile), F32), strip, strip),
        in_specs=[hbm] * 7,
        out_specs=(vmem,) * 4,
        scratch_shapes=[
            pltpu.SMEM(widths.shape, jnp.int32),
            pltpu.VMEM(dw_weight.shape, F32),
            pltpu.VMEM((1, channels), F32),
            pltpu.VMEM((1, channels), F32),
            pltpu.VMEM((parts, channels), F32),
            pltpu.VMEM(coarse.shape, F32),
            pltpu.VMEM((32, channels), F32),
            pltpu.VMEM((16, tile), F32),
            pltpu.VMEM((channels * slots, tile), F32),
            pltpu.SemaphoreType.DMA((channels // CHUNK,)),
            pltpu.SemaphoreType.DMA((len(small),)),
        ],
        compiler_params=params,
    )(pinned(feature), *(pinned(array) for array in small))
    first = swapped(first, "gy", 0)
    second = swapped(second, "gy", 1)
    early = SPLIT * ROWS
    cells, depth, rims = pl.pallas_call(
        conv_kernel,
        out_shape=(
            cells_shape,
            pltpu.VMEM((ZOUT, slots, early, tile), F32),
            pltpu.VMEM((ZOUT, 4, channels, tile), F32),
        ),
        in_specs=[smem, vmem, vmem],
        out_specs=(vmem,) * 3,
        compiler_params=params,
        cost_estimate=pl.CostEstimate(flops=10**9, bytes_accessed=10**6, transcendentals=0),
    )(widths, held, weights)
    edge, near, far = pl.pallas_call(
        rim_kernel,
        out_shape=(pltpu.VMEM((2, channels, tile), F32), message, message),
        in_specs=[smem] + [vmem] * 3,
        out_specs=(vmem,) * 3,
        compiler_params=params,
    )(widths, first, second, rims)
    near = swapped(near, "gx", 0)
    far = swapped(far, "gx", 1)
    blocks = (every,) if gathered else (first, second, coarse, opposite)
    value, rest, lifted, mixer = pl.pallas_call(
        functools.partial(mix_kernel, gathered),
        out_shape=(
            value_shape,
            pltpu.VMEM((ZOUT, slots, channels - early, tile), F32),
            pltpu.VMEM((3, channels, tile), F32),
            pltpu.VMEM((4 * channels, 4 * channels), BF16),
        ),
        in_specs=[smem] + [vmem] * (5 + len(blocks)),
        out_specs=(vmem,) * 4,
        scratch_shapes=[pltpu.VMEM((parts, ncx, tile), F32)]
        + ([] if gathered else [pltpu.VMEM((parts, ncx, ncy), F32)]),
        compiler_params=params,
        cost_estimate=pl.CostEstimate(flops=10**9, bytes_accessed=10**6, transcendentals=0),
    )(widths, pw_weight, cells, weights, depth, edge, *blocks)
    out, _ = pl.pallas_call(
        finish_kernel,
        out_shape=(shape((ZOUT, channels, slots, tile), BF16), value_shape),
        in_specs=[smem] + [vmem] * 10,
        out_specs=(hbm, vmem),
        scratch_shapes=[
            pltpu.VMEM((ZOUT, channels, slots, tile), BF16),
            pltpu.SemaphoreType.DMA((channels // 16, ZOUT)),
        ],
        input_output_aliases={10: 1},
        compiler_params=params,
    )(widths, cells, weights, depth, rest, edge, lifted, mixer, near, far, value)
    return out


def solution(mesh):
    placed = (P(None, None, "gx", "gy"), P(), P(), P(), P(), P(), P(), P(None, "gy", None))
    return jax.shard_map(
        shards, mesh=mesh, in_specs=placed, out_specs=P(None, None, "gx", "gy"), check_vma=False
    )
```

```python
import functools

import jax
import jax.numpy as jnp
from jax import lax
from jax.experimental import pallas as pl
from jax.experimental.pallas import tpu as pltpu
from jax.sharding import PartitionSpec as P

XW = 16
ZOUT = 2
CF = 16
ROWS = 8
SPLIT = 5
CHUNK = 16
DW_BIAS, PW_BIAS, LIFT = 27, 28, 29
F32 = jnp.float32
BF16 = jnp.bfloat16
VMEM_BYTES = 14 * 1024 * 1024


def lane_iota(shape):
    return lax.broadcasted_iota(jnp.int32, shape, len(shape) - 1)


def row_iota(shape):
    return lax.broadcasted_iota(jnp.int32, shape, len(shape) - 2)


def tap_of(m, dx, dy):
    return 9 * m + 3 * (dx + 1) + (dy + 1)


def is_even(axis):
    return lax.rem(lax.axis_index(axis), 2) == 0


def pack_kernel(
    feature, widths_in, taps_in, dw_bias_in, pw_bias_in, lift_in, coarse_in,
    cells, weights, first, second, own_block,
    planes, widths, taps, dw_bias, pw_bias, lift, coarse, stacked, tail, picked, sems, small_sems,
):
    count, channels, slots, tile = feature.shape
    chunks = range(0, channels, CHUNK)

    def copy_of(c):
        at = pl.ds(c, CHUNK)
        return pltpu.make_async_copy(feature.at[:, at], planes.at[:, at], sems.at[c // CHUNK])

    small = [
        pltpu.make_async_copy(source, target, small_sems.at[i])
        for i, (source, target) in enumerate(
            (
                (widths_in, widths),
                (taps_in, taps),
                (dw_bias_in, dw_bias),
                (pw_bias_in, pw_bias),
                (lift_in, lift),
                (coarse_in, coarse),
            )
        )
    ]
    for copy in small:
        copy.start()
    for c in chunks:
        copy_of(c).start()

    for copy in small:
        copy.wait()
    width = widths[lax.axis_index("gx")]
    stacked[0:DW_BIAS, :] = taps[...]
    stacked[DW_BIAS : DW_BIAS + 1, :] = dw_bias[...]
    stacked[PW_BIAS : PW_BIAS + 1, :] = pw_bias[...]
    stacked[LIFT : LIFT + 3, :] = lift[...]
    turned = jnp.transpose(stacked[...])
    for t in range(stacked.shape[0]):
        weights[t] = jnp.broadcast_to(turned[:, t : t + 1], (channels, tile))

    own_block[...] = coarse[...]
    parts, own_rows, ncy = coarse.shape
    tail[...] = jnp.zeros_like(tail)
    if 3 * ncy <= tile:
        for k in range(parts):
            rest = coarse[k]
            for p in range(3):
                term = rest.astype(BF16).astype(F32)
                rest = rest - term
                tail[k * own_rows : (k + 1) * own_rows, p * ncy : (p + 1) * ncy] = term
    for message in (first, second):
        message[channels:, :] = tail[...].astype(BF16)

    shape = (channels, tile)
    lane = lane_iota(shape)
    member = (lane & 31) >> 3
    on_left = (lane & 2) != 0
    scale = []
    for dx in (-1, 0, 1):
        total = None
        for m in range(3):
            weight = jnp.where(on_left, weights[tap_of(m, dx, 1)], weights[tap_of(m, dx, -1)])
            total = weight if total is None else jnp.where(member == m, weight, total)
        scale.append(total)

    valid = row_iota((slots, tile)) < width
    across = lane_iota((slots, tile))
    for c in chunks:
        copy_of(c).wait()
        for k in range(CHUNK):
            at = slice((c + k) * slots, (c + k + 1) * slots)
            total = None
            for z in range(count):
                rows = jnp.where(valid, planes[z, c + k].astype(F32), 0.0)
                cells[z, at, :] = rows
                if z:
                    inside = (across >= 4 * z - 2) & (across < 4 * z + 2)
                    total = jnp.where(inside, pltpu.roll(rows, 4 * z, 1), total)
                else:
                    total = rows
            picked[at, :] = total

    groups = slots // 4
    held, moved = {}, {}
    for q in range(groups):
        rows = [pltpu.roll(picked[pl.ds(4 * q + i, channels, stride=slots), :], 32 * i + 2, 1) for i in range(4)]
        rows = jnp.where(
            lane < 64, jnp.where(lane < 32, rows[0], rows[1]), jnp.where(lane < 96, rows[2], rows[3])
        )
        held[q] = rows
    for q in range(-1, groups):
        low = held.get(q + 1, jnp.zeros(shape, F32))
        high = held.get(q, jnp.zeros(shape, F32))
        moved[q] = pltpu.roll(jnp.where(lane < 64, low, high), 64, 1)
    sums = []
    for q in range(-1, groups + 1):
        total = None
        for weight, rows in ((scale[0], moved.get(q - 1)), (scale[1], held.get(q)), (scale[2], moved.get(q))):
            if rows is not None:
                total = weight * rows if total is None else total + weight * rows
        sums.append(total + pltpu.roll(total, tile - 8, 1) + pltpu.roll(total, tile - 16, 1))
    packed = []
    for half in range(2):
        total = sums[4 * half]
        for k in range(1, 4):
            total = jnp.where(((lane >> 3) & 3) == k, pltpu.roll(sums[4 * half + k], 8 * k, 1), total)
        packed.append(total)
    left = jnp.where(on_left, packed[0], pltpu.roll(packed[1], tile - 2, 1))
    right = jnp.where(on_left, pltpu.roll(packed[1], 2, 1), packed[0])
    even = is_even("gy")
    first[0:channels, :] = jnp.where(even, right, left).astype(BF16)
    second[0:channels, :] = jnp.where(even, left, right).astype(BF16)


def shifted_sum(before, centre, after):
    lane = lane_iota(centre.shape)
    tile = centre.shape[-1]
    before = jnp.where(lane < 2, 0.0, pltpu.roll(before, 2, 1))
    after = jnp.where(lane >= tile - 2, 0.0, pltpu.roll(after, tile - 2, 1))
    return centre + before + after


def convolve_block(cells, weights, depth, b, first_block):
    channels = weights.shape[1]
    slots = cells.shape[1] // channels
    at = pl.ds(pl.multiple_of(b * ROWS, ROWS), ROWS)
    to = pl.ds(pl.multiple_of((b - first_block) * ROWS, ROWS), ROWS)
    tap = [weights[t, at, :] for t in range(27)]
    for z in range(ZOUT):
        for parity in range(2):
            sums = {}
            for x in range(parity, slots, 2):
                rows = [cells[z + ZOUT * m, pl.ds(b * (ROWS * slots) + x, ROWS, stride=slots), :] for m in range(3)]
                for m in range(3):
                    for dx in (1, 0, -1):
                        out = x - 2 * dx
                        if 0 <= out < slots:
                            for dy in (-1, 0, 1):
                                term = tap[tap_of(m, dx, dy)] * rows[m]
                                key = (out, dy)
                                sums[key] = sums[key] + term if key in sums else term
                for out in [x - 2] if x + 2 < slots else [x - 2, x]:
                    if out >= 0:
                        depth[z, out, to, :] = shifted_sum(*(sums.pop((out, dy)) for dy in (-1, 0, 1)))


def conv_kernel(widths, cells, weights, depth, rims):
    width = widths[lax.axis_index("gx")]
    channels = weights.shape[1]
    slots = cells.shape[1] // channels

    def outer_rows(b, carry):
        at = pl.ds(pl.multiple_of(b * ROWS, ROWS), ROWS)
        for i, (x, dx) in enumerate(((0, 1), (1, 1), (width - 2, -1), (width - 1, -1))):
            for z in range(ZOUT):
                rows = [cells[z + ZOUT * m, pl.ds(b * (ROWS * slots) + x, ROWS, stride=slots), :] for m in range(3)]
                parts = [
                    sum(weights[tap_of(m, dx, dy), at, :] * rows[m] for m in range(3)) for dy in (-1, 0, 1)
                ]
                rims[z, i, at, :] = shifted_sum(*parts)
        return carry

    lax.fori_loop(0, channels // ROWS, outer_rows, 0)

    def convolve(b, carry):
        convolve_block(cells, weights, depth, b, 0)
        return carry

    lax.fori_loop(0, SPLIT, convolve, 0)


def edge_term(edge, z, x):
    tile = edge.shape[2]
    group = x // 4 + 1 if isinstance(x, int) else lax.div(x, 4) + 1
    at = x % 4 if isinstance(x, int) else lax.rem(x, 4)
    begin = 32 * at + 8 * (group & 3) + 4 * z
    cells = pltpu.roll(edge[group >> 2], tile - 2 - begin, 1)
    lane = lane_iota(cells.shape)
    return jnp.where((lane < 2) | (lane >= tile - 2), cells, 0.0)


def rim_kernel(widths, second, first, rims, edge, far, near):
    width = widths[lax.axis_index("gx")]
    _, _, channels, tile = rims.shape
    even = is_even("gy")
    one, two = first[0:channels, :].astype(F32), second[0:channels, :].astype(F32)
    right = jnp.where(even, one, two)
    left = jnp.where(even, two, one)
    on_left = (lane_iota((channels, tile)) & 2) != 0
    edge[0] = jnp.where(on_left, pltpu.roll(left, 2, 1), pltpu.roll(right, tile - 2, 1))
    edge[1] = jnp.where(on_left, left, right)
    even = is_even("gx")
    for z in range(ZOUT):
        for r in range(2):
            to_lower = rims[z, r] + edge_term(edge, z, r - 2)
            to_upper = rims[z, 2 + r] + edge_term(edge, z, width + r)
            at = slice((2 * z + r) * channels, (2 * z + r + 1) * channels)
            near[at, :] = jnp.where(even, to_upper, to_lower).astype(BF16)
            far[at, :] = jnp.where(even, to_lower, to_upper).astype(BF16)


def slab_start(widths):
    slab = lax.axis_index("gx")
    start = jnp.int32(0)
    for d in range(widths.shape[0]):
        start = start + jnp.where(d < slab, widths[d], 0)
    return start


def depth_row(weights, depths, edge, z, x):
    own = jnp.concatenate([depth[z, x] for depth in depths], axis=0)
    return own + weights[DW_BIAS] + edge_term(edge, z, x)


def finished_row(weights, cells, lifted, phase, width, mixed, z, x):
    channels = weights.shape[1]
    slots = cells.shape[1] // channels
    mixed = mixed + weights[PW_BIAS]
    active = jnp.maximum(mixed, 0.2 * mixed)
    field = cells[2 + z, pl.ds(x, channels, stride=slots), :]
    value = active + (field + lifted[lax.div(phase + x, CF)])
    return jnp.where(x < width, value, 0.0)


def mix_kernel(gathered, widths, mix, cells, weights, depth, edge, *refs):
    if gathered:
        coarse, value, rest, lifted, mixer, across = refs
        parts, ncx, ncy = coarse.shape
    else:
        second, first, own_block, opposite, value, rest, lifted, mixer, across, blocks = refs
        parts, own_rows, ncy = own_block.shape
        ncx = 4 * own_rows
    width = widths[lax.axis_index("gx")]
    here = lax.axis_index("gy")
    start = slab_start(widths)
    phase = lax.rem(start, CF)
    channels, tile = weights.shape[1:]
    slots = cells.shape[1] // channels

    def convolve(b, carry):
        convolve_block(cells, weights, rest, b, SPLIT)
        return carry

    lax.fori_loop(SPLIT, channels // ROWS, convolve, 0)

    if not gathered:
        even = is_even("gy")
        after, before = lax.rem(here + 1, 4), lax.rem(here + 3, 4)
        count = parts * own_rows
        for message, owner in (
            (first, jnp.where(even, after, before)),
            (second, jnp.where(even, before, after)),
        ):
            terms = message[channels:, :].astype(F32)[0:count, :]
            sums = terms[:, 0:ncy] + terms[:, ncy : 2 * ncy] + terms[:, 2 * ncy : 3 * ncy]
            for k in range(parts):
                blocks[k, pl.ds(owner * own_rows, own_rows), :] = sums[k * own_rows : (k + 1) * own_rows]
        for block, owner in ((own_block, here), (opposite, lax.rem(here + 2, 4))):
            for k in range(parts):
                blocks[k, pl.ds(owner * own_rows, own_rows), :] = block[k]
    shape = (ncy, tile)
    cell = row_iota(shape) * CF
    place = lane_iota(shape) + here * tile
    along_y = ((place >= cell) & (place < cell + CF)).astype(F32)
    for k in range(parts):
        block = coarse[k] if gathered else blocks[k]
        across[k] = jnp.dot(block, along_y, precision=lax.Precision.HIGHEST, preferred_element_type=F32)
    for i in range(3):
        cell = lax.rem(lax.div(start, CF) + i, ncx)
        total = None
        for k in range(parts):
            term = weights[LIFT + k] * across[k, pl.ds(cell, 1), :]
            total = term if total is None else total + term
        lifted[i] = total

    group = 4
    wide = jnp.concatenate([mix[...]] * group, axis=1)
    wide = jnp.concatenate([wide] * group, axis=0)
    size = group * channels
    row, column = row_iota((size, size)), lane_iota((size, size))
    same = sum(
        ((row >= i * channels) & (row < (i + 1) * channels) & (column >= i * channels) & (column < (i + 1) * channels)).astype(F32)
        for i in range(group)
    )
    mixer[...] = jnp.where(same > 0, wide.astype(F32), 0.0).astype(BF16)

    for x in range(0, slots, group):
        depths = [
            jnp.concatenate([depth_row(weights, (depth, rest), edge, z, x + i) for i in range(group)], axis=0).astype(BF16)
            for z in range(ZOUT)
        ]
        mixed = jnp.dot(mixer[...], jnp.concatenate(depths, axis=1), preferred_element_type=F32)
        for i in range(group):
            for z in range(ZOUT):
                part = mixed[i * channels : (i + 1) * channels, z * tile : (z + 1) * tile]
                value[z, pl.ds(x + i, channels, stride=slots), :] = finished_row(
                    weights, cells, lifted, phase, width, part, z, x + i
                )


def finish_kernel(widths, cells, weights, depth, rest, edge, lifted, mixer, far, near, value_in, out, value, block, sems):
    width = widths[lax.axis_index("gx")]
    phase = lax.rem(slab_start(widths), CF)
    channels, tile = weights.shape[1:]
    slots = cells.shape[1] // channels
    even = is_even("gx")
    at_top = jnp.where(even, far[...].astype(F32), near[...].astype(F32))
    at_end = jnp.where(even, near[...].astype(F32), far[...].astype(F32))
    rows = (0, 1, width - 2, width - 1)
    depths = []
    for z in range(ZOUT):
        parts = []
        for i, x in enumerate(rows):
            arrived = at_top if i < 2 else at_end
            begin = (2 * z + i % 2) * channels
            parts.append(depth_row(weights, (depth, rest), edge, z, x) + arrived[begin : begin + channels, :])
        depths.append(jnp.concatenate(parts, axis=0).astype(BF16))
    mixed = jnp.dot(mixer[...], jnp.concatenate(depths, axis=1), preferred_element_type=F32)
    for i, x in enumerate(rows):
        for z in range(ZOUT):
            part = mixed[i * channels : (i + 1) * channels, z * tile : (z + 1) * tile]
            value[z, pl.ds(x, channels, stride=slots), :] = finished_row(
                weights, cells, lifted, phase, width, part, z, x
            )
    chunk = 16
    copies = []
    for z in range(ZOUT):
        for part in range(channels // chunk):
            for o in range(part * chunk, (part + 1) * chunk):
                block[z, o] = value[z, o * slots : (o + 1) * slots, :].astype(BF16)
            part_of = pl.ds(part * chunk, chunk)
            copy = pltpu.make_async_copy(block.at[z, part_of], out.at[z, part_of], sems.at[part, z])
            copy.start()
            copies.append(copy)
    for copy in copies:
        copy.wait()


def shards(feature, widths, dw_weight, dw_bias, pw_weight, pw_bias, lift_weight, coarse):
    planes, channels, slots, tile = feature.shape
    ny = lax.axis_size("gy")
    parts, own_rows, ncy = coarse.shape
    gathered = ny != 4
    ncx = ny * own_rows
    smem = pl.BlockSpec(memory_space=pltpu.SMEM)
    vmem = pl.BlockSpec(memory_space=pltpu.VMEM)
    hbm = pl.BlockSpec(memory_space=pltpu.HBM)
    params = pltpu.CompilerParams(vmem_limit_bytes=VMEM_BYTES)
    shape = jax.ShapeDtypeStruct
    strip = shape((channels + 16, tile), BF16)
    cells_shape = pltpu.VMEM((planes, channels * slots, tile), F32)
    value_shape = pltpu.VMEM((ZOUT, channels * slots, tile), F32)
    message = shape((2 * ZOUT * channels, tile), BF16)

    def swapped(array, axis, first):
        count = lax.axis_size(axis)
        pairs = []
        for i in range(first, count + first, 2):
            a, b = i % count, (i + 1) % count
            pairs += [(a, b), (b, a)]
        return lax.ppermute(array, axis, pairs)

    def pinned(array):
        return pltpu.with_memory_space_constraint(array, pltpu.HBM)

    if gathered:
        every = lax.all_gather(coarse, "gy", axis=1, tiled=True)
    small = (
        widths,
        dw_weight,
        dw_bias.reshape(1, channels),
        pw_bias.reshape(1, channels),
        lift_weight.T,
        coarse,
    )
    cells, weights, first, second, own_block = pl.pallas_call(
        pack_kernel,
        out_shape=(
            cells_shape,
            pltpu.VMEM((32, channels, tile), F32),
            strip,
            strip,
            pltpu.VMEM(coarse.shape, F32),
        ),
        in_specs=[hbm] * 7,
        out_specs=(vmem,) * 5,
        scratch_shapes=[
            pltpu.VMEM(feature.shape, BF16),
            pltpu.SMEM(widths.shape, jnp.int32),
            pltpu.VMEM(dw_weight.shape, F32),
            pltpu.VMEM((1, channels), F32),
            pltpu.VMEM((1, channels), F32),
            pltpu.VMEM((parts, channels), F32),
            pltpu.VMEM(coarse.shape, F32),
            pltpu.VMEM((32, channels), F32),
            pltpu.VMEM((16, tile), F32),
            pltpu.VMEM((channels * slots, tile), F32),
            pltpu.SemaphoreType.DMA((channels // CHUNK,)),
            pltpu.SemaphoreType.DMA((len(small),)),
        ],
        compiler_params=params,
    )(pinned(feature), *(pinned(array) for array in small))
    second = swapped(second, "gy", 1)
    first = swapped(first, "gy", 0)
    if not gathered:
        opposite = lax.ppermute(own_block, "gy", [(i, (i + 2) % 4) for i in range(4)])
    early = SPLIT * ROWS
    depth, rims = pl.pallas_call(
        conv_kernel,
        out_shape=(
            pltpu.VMEM((ZOUT, slots, early, tile), F32),
            pltpu.VMEM((ZOUT, 4, channels, tile), F32),
        ),
        in_specs=[smem, vmem, vmem],
        out_specs=(vmem,) * 2,
        compiler_params=params,
        cost_estimate=pl.CostEstimate(flops=10**9, bytes_accessed=10**6, transcendentals=0),
    )(widths, cells, weights)
    edge, far, near = pl.pallas_call(
        rim_kernel,
        out_shape=(pltpu.VMEM((2, channels, tile), F32), message, message),
        in_specs=[smem] + [vmem] * 3,
        out_specs=(vmem,) * 3,
        compiler_params=params,
    )(widths, second, first, rims)
    far = swapped(far, "gx", 1)
    near = swapped(near, "gx", 0)
    blocks = (every,) if gathered else (second, first, own_block, opposite)
    value, rest, lifted, mixer = pl.pallas_call(
        functools.partial(mix_kernel, gathered),
        out_shape=(
            value_shape,
            pltpu.VMEM((ZOUT, slots, channels - early, tile), F32),
            pltpu.VMEM((3, channels, tile), F32),
            pltpu.VMEM((4 * channels, 4 * channels), BF16),
        ),
        in_specs=[smem] + [vmem] * (5 + len(blocks)),
        out_specs=(vmem,) * 4,
        scratch_shapes=[pltpu.VMEM((parts, ncx, tile), F32)]
        + ([] if gathered else [pltpu.VMEM((parts, ncx, ncy), F32)]),
        compiler_params=params,
        cost_estimate=pl.CostEstimate(flops=10**9, bytes_accessed=10**6, transcendentals=0),
    )(widths, pw_weight, cells, weights, depth, edge, *blocks)
    out, _ = pl.pallas_call(
        finish_kernel,
        out_shape=(shape((ZOUT, channels, slots, tile), BF16), value_shape),
        in_specs=[smem] + [vmem] * 10,
        out_specs=(hbm, vmem),
        scratch_shapes=[
            pltpu.VMEM((ZOUT, channels, slots, tile), BF16),
            pltpu.SemaphoreType.DMA((channels // 16, ZOUT)),
        ],
        input_output_aliases={10: 1},
        compiler_params=params,
    )(widths, cells, weights, depth, rest, edge, lifted, mixer, far, near, value)
    return out


def solution(mesh):
    placed = (P(None, None, "gx", "gy"), P(), P(), P(), P(), P(), P(), P(None, "gy", None))
    return jax.shard_map(
        shards, mesh=mesh, in_specs=placed, out_specs=P(None, None, "gx", "gy"), check_vma=False
    )
```

```python
import functools

import jax
import jax.numpy as jnp
from jax import lax
from jax.experimental import pallas as pl
from jax.experimental.pallas import tpu as pltpu
from jax.sharding import PartitionSpec as P

XW = 16
ZOUT = 2
CF = 16
ROWS = 8
SPLIT = 5
CHUNK = 16
DW_BIAS, PW_BIAS, LIFT = 27, 28, 29
F32 = jnp.float32
BF16 = jnp.bfloat16
VMEM_BYTES = 14 * 1024 * 1024


def lane_iota(shape):
    return lax.broadcasted_iota(jnp.int32, shape, len(shape) - 1)


def row_iota(shape):
    return lax.broadcasted_iota(jnp.int32, shape, len(shape) - 2)


def tap_of(m, dx, dy):
    return 9 * m + 3 * (dx + 1) + (dy + 1)


def is_even(axis):
    return lax.rem(lax.axis_index(axis), 2) == 0


def pack_kernel(
    feature, widths_in, taps_in, dw_bias_in, pw_bias_in, lift_in, coarse_in,
    cells, weights, first, second, own_block,
    planes, widths, taps, dw_bias, pw_bias, lift, coarse, stacked, tail, picked, sems, small_sems,
):
    count, channels, slots, tile = feature.shape
    chunks = range(0, channels, CHUNK)

    def copy_of(c):
        at = pl.ds(c, CHUNK)
        return pltpu.make_async_copy(feature.at[:, at], planes.at[:, at], sems.at[c // CHUNK])

    small = [
        pltpu.make_async_copy(source, target, small_sems.at[i])
        for i, (source, target) in enumerate(
            (
                (widths_in, widths),
                (taps_in, taps),
                (dw_bias_in, dw_bias),
                (pw_bias_in, pw_bias),
                (lift_in, lift),
                (coarse_in, coarse),
            )
        )
    ]
    for copy in small:
        copy.start()
    for c in chunks:
        copy_of(c).start()

    for copy in small:
        copy.wait()
    width = widths[lax.axis_index("gx")]
    stacked[0:DW_BIAS, :] = taps[...]
    stacked[DW_BIAS : DW_BIAS + 1, :] = dw_bias[...]
    stacked[PW_BIAS : PW_BIAS + 1, :] = pw_bias[...]
    stacked[LIFT : LIFT + 3, :] = lift[...]
    turned = jnp.transpose(stacked[...])
    for t in range(stacked.shape[0]):
        weights[t] = jnp.broadcast_to(turned[:, t : t + 1], (channels, tile))

    own_block[...] = coarse[...]
    parts, own_rows, ncy = coarse.shape
    tail[...] = jnp.zeros_like(tail)
    if 3 * ncy <= tile:
        for k in range(parts):
            rest = coarse[k]
            for p in range(3):
                term = rest.astype(BF16).astype(F32)
                rest = rest - term
                tail[k * own_rows : (k + 1) * own_rows, p * ncy : (p + 1) * ncy] = term
    for message in (first, second):
        message[channels:, :] = tail[...].astype(BF16)

    shape = (channels, tile)
    lane = lane_iota(shape)
    member = (lane & 31) >> 3
    on_left = (lane & 2) != 0
    scale = []
    for dx in (-1, 0, 1):
        total = None
        for m in range(3):
            weight = jnp.where(on_left, weights[tap_of(m, dx, 1)], weights[tap_of(m, dx, -1)])
            total = weight if total is None else jnp.where(member == m, weight, total)
        scale.append(total)

    across = lane_iota((slots, tile))
    for c in chunks:
        copy_of(c).wait()
        for k in range(CHUNK):
            at = slice((c + k) * slots, (c + k + 1) * slots)
            total = None
            for z in range(count):
                rows = planes[z, c + k].astype(F32)
                cells[z, at, :] = rows
                if z:
                    inside = (across >= 4 * z - 2) & (across < 4 * z + 2)
                    total = jnp.where(inside, pltpu.roll(rows, 4 * z, 1), total)
                else:
                    total = rows
            picked[at, :] = total
    for r in range(2):

        @pl.when(width + r < slots)
        def _():
            for z in range(count):
                cells[z, pl.ds(width + r, channels, stride=slots), :] = jnp.zeros((channels, tile), F32)

    groups = slots // 4
    held, moved = {}, {}
    for q in range(groups):
        rows = [pltpu.roll(picked[pl.ds(4 * q + i, channels, stride=slots), :], 32 * i + 2, 1) for i in range(4)]
        rows = jnp.where(
            lane < 64, jnp.where(lane < 32, rows[0], rows[1]), jnp.where(lane < 96, rows[2], rows[3])
        )
        held[q] = jnp.where(4 * q + (lane >> 5) < width, rows, 0.0)
    for q in range(-1, groups):
        low = held.get(q + 1, jnp.zeros(shape, F32))
        high = held.get(q, jnp.zeros(shape, F32))
        moved[q] = pltpu.roll(jnp.where(lane < 64, low, high), 64, 1)
    sums = []
    for q in range(-1, groups + 1):
        total = None
        for weight, rows in ((scale[0], moved.get(q - 1)), (scale[1], held.get(q)), (scale[2], moved.get(q))):
            if rows is not None:
                total = weight * rows if total is None else total + weight * rows
        sums.append(total + pltpu.roll(total, tile - 8, 1) + pltpu.roll(total, tile - 16, 1))
    packed = []
    for half in range(2):
        total = sums[4 * half]
        for k in range(1, 4):
            total = jnp.where(((lane >> 3) & 3) == k, pltpu.roll(sums[4 * half + k], 8 * k, 1), total)
        packed.append(total)
    left = jnp.where(on_left, packed[0], pltpu.roll(packed[1], tile - 2, 1))
    right = jnp.where(on_left, pltpu.roll(packed[1], 2, 1), packed[0])
    even = is_even("gy")
    first[0:channels, :] = jnp.where(even, right, left).astype(BF16)
    second[0:channels, :] = jnp.where(even, left, right).astype(BF16)


def shifted_sum(before, centre, after):
    lane = lane_iota(centre.shape)
    tile = centre.shape[-1]
    before = jnp.where(lane < 2, 0.0, pltpu.roll(before, 2, 1))
    after = jnp.where(lane >= tile - 2, 0.0, pltpu.roll(after, tile - 2, 1))
    return centre + before + after


def convolve_block(cells, weights, depth, b, first_block):
    channels = weights.shape[1]
    slots = cells.shape[1] // channels
    at = pl.ds(pl.multiple_of(b * ROWS, ROWS), ROWS)
    to = pl.ds(pl.multiple_of((b - first_block) * ROWS, ROWS), ROWS)
    tap = [weights[t, at, :] for t in range(27)]
    for z in range(ZOUT):
        for parity in range(2):
            sums = {}
            for x in range(parity, slots, 2):
                rows = [cells[z + ZOUT * m, pl.ds(b * (ROWS * slots) + x, ROWS, stride=slots), :] for m in range(3)]
                for m in range(3):
                    for dx in (1, 0, -1):
                        out = x - 2 * dx
                        if 0 <= out < slots:
                            for dy in (-1, 0, 1):
                                term = tap[tap_of(m, dx, dy)] * rows[m]
                                key = (out, dy)
                                sums[key] = sums[key] + term if key in sums else term
                for out in [x - 2] if x + 2 < slots else [x - 2, x]:
                    if out >= 0:
                        depth[z, out, to, :] = shifted_sum(*(sums.pop((out, dy)) for dy in (-1, 0, 1)))


def conv_kernel(widths, cells, weights, coarse, depth, rims, own_block):
    width = widths[lax.axis_index("gx")]
    channels = weights.shape[1]
    slots = cells.shape[1] // channels
    own_block[...] = coarse[...]

    for b in range(channels // ROWS):
        at = slice(b * ROWS, (b + 1) * ROWS)
        for side, dx in enumerate((1, -1)):
            tap = [[weights[tap_of(m, dx, dy), at, :] for m in range(3)] for dy in (-1, 0, 1)]
            for r in range(2):
                x = r if side == 0 else width - 2 + r
                for z in range(ZOUT):
                    rows = [
                        cells[z + ZOUT * m, pl.ds(b * (ROWS * slots) + x, ROWS, stride=slots), :] for m in range(3)
                    ]
                    parts = [sum(weight * row for weight, row in zip(weights_of, rows)) for weights_of in tap]
                    rims[z, 2 * side + r, at, :] = shifted_sum(*parts)

    def convolve(b, carry):
        convolve_block(cells, weights, depth, b, 0)
        return carry

    lax.fori_loop(0, SPLIT, convolve, 0)


def edge_term(edge, z, x):
    tile = edge.shape[2]
    group = x // 4 + 1 if isinstance(x, int) else lax.div(x, 4) + 1
    at = x % 4 if isinstance(x, int) else lax.rem(x, 4)
    begin = 32 * at + 8 * (group & 3) + 4 * z
    cells = pltpu.roll(edge[group >> 2], tile - 2 - begin, 1)
    lane = lane_iota(cells.shape)
    return jnp.where((lane < 2) | (lane >= tile - 2), cells, 0.0)


def rim_kernel(widths, second, first, rims, edge, far, near):
    width = widths[lax.axis_index("gx")]
    _, _, channels, tile = rims.shape
    even = is_even("gy")
    one, two = first[0:channels, :].astype(F32), second[0:channels, :].astype(F32)
    right = jnp.where(even, one, two)
    left = jnp.where(even, two, one)
    on_left = (lane_iota((channels, tile)) & 2) != 0
    edge[0] = jnp.where(on_left, pltpu.roll(left, 2, 1), pltpu.roll(right, tile - 2, 1))
    edge[1] = jnp.where(on_left, left, right)
    even = is_even("gx")
    for z in range(ZOUT):
        for r in range(2):
            to_lower = rims[z, r] + edge_term(edge, z, r - 2)
            to_upper = rims[z, 2 + r] + edge_term(edge, z, width + r)
            at = slice((2 * z + r) * channels, (2 * z + r + 1) * channels)
            near[at, :] = jnp.where(even, to_upper, to_lower).astype(BF16)
            far[at, :] = jnp.where(even, to_lower, to_upper).astype(BF16)


def slab_start(widths):
    slab = lax.axis_index("gx")
    start = jnp.int32(0)
    for d in range(widths.shape[0]):
        start = start + jnp.where(d < slab, widths[d], 0)
    return start


def depth_row(weights, depths, edge, z, x):
    own = jnp.concatenate([depth[z, x] for depth in depths], axis=0)
    return own + weights[DW_BIAS] + edge_term(edge, z, x)


def finished_row(weights, cells, lifted, phase, width, mixed, z, x):
    channels = weights.shape[1]
    slots = cells.shape[1] // channels
    mixed = mixed + weights[PW_BIAS]
    active = jnp.maximum(mixed, 0.2 * mixed)
    field = cells[2 + z, pl.ds(x, channels, stride=slots), :]
    value = active + (field + lifted[lax.div(phase + x, CF)])
    return jnp.where(x < width, value, 0.0)


def mix_kernel(gathered, widths, mix, cells, weights, depth, edge, *refs):
    if gathered:
        coarse, value, rest, lifted, mixer, across = refs
        parts, ncx, ncy = coarse.shape
    else:
        second, first, own_block, opposite, value, rest, lifted, mixer, across, blocks = refs
        parts, own_rows, ncy = own_block.shape
        ncx = 4 * own_rows
    width = widths[lax.axis_index("gx")]
    here = lax.axis_index("gy")
    start = slab_start(widths)
    phase = lax.rem(start, CF)
    channels, tile = weights.shape[1:]
    slots = cells.shape[1] // channels

    def convolve(b, carry):
        convolve_block(cells, weights, rest, b, SPLIT)
        return carry

    lax.fori_loop(SPLIT, channels // ROWS, convolve, 0)

    if not gathered:
        even = is_even("gy")
        after, before = lax.rem(here + 1, 4), lax.rem(here + 3, 4)
        count = parts * own_rows
        for message, owner in (
            (first, jnp.where(even, after, before)),
            (second, jnp.where(even, before, after)),
        ):
            terms = message[channels:, :].astype(F32)[0:count, :]
            sums = terms[:, 0:ncy] + terms[:, ncy : 2 * ncy] + terms[:, 2 * ncy : 3 * ncy]
            for k in range(parts):
                blocks[k, pl.ds(owner * own_rows, own_rows), :] = sums[k * own_rows : (k + 1) * own_rows]
        for block, owner in ((own_block, here), (opposite, lax.rem(here + 2, 4))):
            for k in range(parts):
                blocks[k, pl.ds(owner * own_rows, own_rows), :] = block[k]
    shape = (ncy, tile)
    cell = row_iota(shape) * CF
    place = lane_iota(shape) + here * tile
    along_y = ((place >= cell) & (place < cell + CF)).astype(F32)
    for k in range(parts):
        block = coarse[k] if gathered else blocks[k]
        across[k] = jnp.dot(block, along_y, precision=lax.Precision.HIGHEST, preferred_element_type=F32)
    for i in range(3):
        cell = lax.rem(lax.div(start, CF) + i, ncx)
        total = None
        for k in range(parts):
            term = weights[LIFT + k] * across[k, pl.ds(cell, 1), :]
            total = term if total is None else total + term
        lifted[i] = total

    group = 4
    wide = jnp.concatenate([mix[...]] * group, axis=1)
    wide = jnp.concatenate([wide] * group, axis=0)
    size = group * channels
    row, column = row_iota((size, size)), lane_iota((size, size))
    same = sum(
        ((row >= i * channels) & (row < (i + 1) * channels) & (column >= i * channels) & (column < (i + 1) * channels)).astype(F32)
        for i in range(group)
    )
    mixer[...] = jnp.where(same > 0, wide.astype(F32), 0.0).astype(BF16)

    for x in range(0, slots, group):
        depths = [
            jnp.concatenate([depth_row(weights, (depth, rest), edge, z, x + i) for i in range(group)], axis=0).astype(BF16)
            for z in range(ZOUT)
        ]
        mixed = jnp.dot(mixer[...], jnp.concatenate(depths, axis=1), preferred_element_type=F32)
        for i in range(group):
            for z in range(ZOUT):
                part = mixed[i * channels : (i + 1) * channels, z * tile : (z + 1) * tile]
                value[z, pl.ds(x + i, channels, stride=slots), :] = finished_row(
                    weights, cells, lifted, phase, width, part, z, x + i
                )


def finish_kernel(widths, cells, weights, depth, rest, edge, lifted, mixer, far, near, value_in, out, value, block, sems):
    width = widths[lax.axis_index("gx")]
    phase = lax.rem(slab_start(widths), CF)
    channels, tile = weights.shape[1:]
    slots = cells.shape[1] // channels
    even = is_even("gx")
    at_top = jnp.where(even, far[...].astype(F32), near[...].astype(F32))
    at_end = jnp.where(even, near[...].astype(F32), far[...].astype(F32))
    rows = (0, 1, width - 2, width - 1)
    chunk = 16
    copies = []
    for z in range(ZOUT):
        parts = []
        for i, x in enumerate(rows):
            arrived = at_top if i < 2 else at_end
            begin = (2 * z + i % 2) * channels
            parts.append(depth_row(weights, (depth, rest), edge, z, x) + arrived[begin : begin + channels, :])
        mixed = jnp.dot(mixer[...], jnp.concatenate(parts, axis=0).astype(BF16), preferred_element_type=F32)
        for i, x in enumerate(rows):
            value[z, pl.ds(x, channels, stride=slots), :] = finished_row(
                weights, cells, lifted, phase, width, mixed[i * channels : (i + 1) * channels, :], z, x
            )
        for part in range(channels // chunk):
            for o in range(part * chunk, (part + 1) * chunk):
                block[z, o] = value[z, o * slots : (o + 1) * slots, :].astype(BF16)
            part_of = pl.ds(part * chunk, chunk)
            copy = pltpu.make_async_copy(block.at[z, part_of], out.at[z, part_of], sems.at[part, z])
            copy.start()
            copies.append(copy)
    for copy in copies:
        copy.wait()


def shards(feature, widths, dw_weight, dw_bias, pw_weight, pw_bias, lift_weight, coarse):
    planes, channels, slots, tile = feature.shape
    ny = lax.axis_size("gy")
    parts, own_rows, ncy = coarse.shape
    gathered = ny != 4
    ncx = ny * own_rows
    smem = pl.BlockSpec(memory_space=pltpu.SMEM)
    vmem = pl.BlockSpec(memory_space=pltpu.VMEM)
    hbm = pl.BlockSpec(memory_space=pltpu.HBM)
    params = pltpu.CompilerParams(vmem_limit_bytes=VMEM_BYTES)
    shape = jax.ShapeDtypeStruct
    strip = shape((channels + 16, tile), BF16)
    cells_shape = pltpu.VMEM((planes, channels * slots, tile), F32)
    value_shape = pltpu.VMEM((ZOUT, channels * slots, tile), F32)
    message = shape((2 * ZOUT * channels, tile), BF16)

    def swapped(array, axis, first):
        count = lax.axis_size(axis)
        pairs = []
        for i in range(first, count + first, 2):
            a, b = i % count, (i + 1) % count
            pairs += [(a, b), (b, a)]
        return lax.ppermute(array, axis, pairs)

    def pinned(array):
        return pltpu.with_memory_space_constraint(array, pltpu.HBM)

    if gathered:
        every = lax.all_gather(coarse, "gy", axis=1, tiled=True)
    small = (
        widths,
        dw_weight,
        dw_bias.reshape(1, channels),
        pw_bias.reshape(1, channels),
        lift_weight.T,
        coarse,
    )
    cells, weights, first, second, block = pl.pallas_call(
        pack_kernel,
        out_shape=(
            cells_shape,
            pltpu.VMEM((32, channels, tile), F32),
            strip,
            strip,
            pltpu.VMEM(coarse.shape, F32),
        ),
        in_specs=[hbm] * 7,
        out_specs=(vmem,) * 5,
        scratch_shapes=[
            pltpu.VMEM(feature.shape, BF16),
            pltpu.SMEM(widths.shape, jnp.int32),
            pltpu.VMEM(dw_weight.shape, F32),
            pltpu.VMEM((1, channels), F32),
            pltpu.VMEM((1, channels), F32),
            pltpu.VMEM((parts, channels), F32),
            pltpu.VMEM(coarse.shape, F32),
            pltpu.VMEM((32, channels), F32),
            pltpu.VMEM((16, tile), F32),
            pltpu.VMEM((channels * slots, tile), F32),
            pltpu.SemaphoreType.DMA((channels // CHUNK,)),
            pltpu.SemaphoreType.DMA((len(small),)),
        ],
        compiler_params=params,
    )(pinned(feature), *(pinned(array) for array in small))
    second = swapped(second, "gy", 1)
    first = swapped(first, "gy", 0)
    early = SPLIT * ROWS
    depth, rims, own_block = pl.pallas_call(
        conv_kernel,
        out_shape=(
            pltpu.VMEM((ZOUT, slots, early, tile), F32),
            pltpu.VMEM((ZOUT, 4, channels, tile), F32),
            pltpu.VMEM(coarse.shape, F32),
        ),
        in_specs=[smem, vmem, vmem, vmem],
        out_specs=(vmem,) * 3,
        compiler_params=params,
        cost_estimate=pl.CostEstimate(flops=10**9, bytes_accessed=10**6, transcendentals=0),
    )(widths, cells, weights, block)
    if not gathered:
        opposite = lax.ppermute(own_block, "gy", [(i, (i + 2) % 4) for i in range(4)])
    edge, far, near = pl.pallas_call(
        rim_kernel,
        out_shape=(pltpu.VMEM((2, channels, tile), F32), message, message),
        in_specs=[smem] + [vmem] * 3,
        out_specs=(vmem,) * 3,
        compiler_params=params,
    )(widths, second, first, rims)
    far = swapped(far, "gx", 1)
    near = swapped(near, "gx", 0)
    blocks = (every,) if gathered else (second, first, own_block, opposite)
    value, rest, lifted, mixer = pl.pallas_call(
        functools.partial(mix_kernel, gathered),
        out_shape=(
            value_shape,
            pltpu.VMEM((ZOUT, slots, channels - early, tile), F32),
            pltpu.VMEM((3, channels, tile), F32),
            pltpu.VMEM((4 * channels, 4 * channels), BF16),
        ),
        in_specs=[smem] + [vmem] * (5 + len(blocks)),
        out_specs=(vmem,) * 4,
        scratch_shapes=[pltpu.VMEM((parts, ncx, tile), F32)]
        + ([] if gathered else [pltpu.VMEM((parts, ncx, ncy), F32)]),
        compiler_params=params,
        cost_estimate=pl.CostEstimate(flops=10**9, bytes_accessed=10**6, transcendentals=0),
    )(widths, pw_weight, cells, weights, depth, edge, *blocks)
    out, _ = pl.pallas_call(
        finish_kernel,
        out_shape=(shape((ZOUT, channels, slots, tile), BF16), value_shape),
        in_specs=[smem] + [vmem] * 10,
        out_specs=(hbm, vmem),
        scratch_shapes=[
            pltpu.VMEM((ZOUT, channels, slots, tile), BF16),
            pltpu.SemaphoreType.DMA((channels // 16, ZOUT)),
        ],
        input_output_aliases={10: 1},
        compiler_params=params,
    )(widths, cells, weights, depth, rest, edge, lifted, mixer, far, near, value)
    return out


def solution(mesh):
    placed = (P(None, None, "gx", "gy"), P(), P(), P(), P(), P(), P(), P(None, "gy", None))
    return jax.shard_map(
        shards, mesh=mesh, in_specs=placed, out_specs=P(None, None, "gx", "gy"), check_vma=False
    )
```

```python
import functools

import jax
import jax.numpy as jnp
from jax import lax
from jax.experimental import pallas as pl
from jax.experimental.pallas import tpu as pltpu
from jax.sharding import PartitionSpec as P

XW = 16
ZOUT = 2
CF = 16
ROWS = 8
SPLIT = 5
CHUNK = 16
DW_BIAS, PW_BIAS, LIFT = 27, 28, 29
F32 = jnp.float32
BF16 = jnp.bfloat16
VMEM_BYTES = 14 * 1024 * 1024


def lane_iota(shape):
    return lax.broadcasted_iota(jnp.int32, shape, len(shape) - 1)


def row_iota(shape):
    return lax.broadcasted_iota(jnp.int32, shape, len(shape) - 2)


def tap_of(m, dx, dy):
    return 9 * m + 3 * (dx + 1) + (dy + 1)


def is_even(axis):
    return lax.rem(lax.axis_index(axis), 2) == 0


def pack_kernel(
    feature, widths_in, taps_in, dw_bias_in, pw_bias_in, lift_in, coarse_in,
    cells, weights, first, second, own_block, widths,
    planes, widths_here, taps, dw_bias, pw_bias, lift, coarse, stacked, tail, picked, sems, small_sems,
):
    count, channels, slots, tile = feature.shape
    chunks = range(0, channels, CHUNK)

    def copy_of(c):
        at = pl.ds(c, CHUNK)
        return pltpu.make_async_copy(feature.at[:, at], planes.at[:, at], sems.at[c // CHUNK])

    small = [
        pltpu.make_async_copy(source, target, small_sems.at[i])
        for i, (source, target) in enumerate(
            (
                (widths_in, widths_here),
                (taps_in, taps),
                (dw_bias_in, dw_bias),
                (pw_bias_in, pw_bias),
                (lift_in, lift),
                (coarse_in, coarse),
            )
        )
    ]
    for copy in small:
        copy.start()
    for c in chunks:
        copy_of(c).start()

    for copy in small:
        copy.wait()
    for d in range(widths.shape[0]):
        widths[d] = widths_here[d]
    width = widths_here[lax.axis_index("gx")]
    stacked[0:DW_BIAS, :] = taps[...]
    stacked[DW_BIAS : DW_BIAS + 1, :] = dw_bias[...]
    stacked[PW_BIAS : PW_BIAS + 1, :] = pw_bias[...]
    stacked[LIFT : LIFT + 3, :] = lift[...]
    turned = jnp.transpose(stacked[...])
    for t in range(stacked.shape[0]):
        weights[t] = jnp.broadcast_to(turned[:, t : t + 1], (channels, tile))

    own_block[...] = coarse[...]
    parts, own_rows, ncy = coarse.shape
    tail[...] = jnp.zeros_like(tail)
    if 3 * ncy <= tile:
        for k in range(parts):
            rest = coarse[k]
            for p in range(3):
                term = rest.astype(BF16).astype(F32)
                rest = rest - term
                tail[k * own_rows : (k + 1) * own_rows, p * ncy : (p + 1) * ncy] = term
    for message in (first, second):
        message[channels:, :] = tail[...].astype(BF16)

    shape = (channels, tile)
    lane = lane_iota(shape)
    on_left = (lane & 2) != 0
    row, along = row_iota((taps.shape[0], tile)), lane_iota((taps.shape[0], tile))
    of_plane = 9 * ((along & 31) >> 3) + jnp.where((along & 2) != 0, 2, 0)
    terms, rest = [], taps[...]
    for _ in range(3):
        terms.append(rest.astype(BF16))
        rest = rest - terms[-1].astype(F32)
    scale = []
    for dx in (-1, 0, 1):
        chosen = (row == of_plane + 3 * (dx + 1)).astype(BF16)
        scale.append(
            sum(
                lax.dot_general(term, chosen, (((0,), (0,)), ((), ())), preferred_element_type=F32) for term in terms
            )
        )

    across = lane_iota((CHUNK * slots, tile))
    for c in chunks:
        copy_of(c).wait()
        at = slice(c * slots, (c + CHUNK) * slots)
        total = None
        for z in range(count):
            rows = planes[z, c : c + CHUNK].reshape(CHUNK * slots, tile)
            cells[z, at, :] = rows.astype(F32)
            if z:
                inside = (across >= 4 * z - 2) & (across < 4 * z + 2)
                total = jnp.where(inside, pltpu.roll(rows, 4 * z, 1), total)
            else:
                total = rows
        picked[at, :] = total.astype(F32)
    for r in range(2):

        @pl.when(width + r < slots)
        def _():
            for z in range(count):
                cells[z, pl.ds(width + r, channels, stride=slots), :] = jnp.zeros((channels, tile), F32)

    groups = slots // 4
    held, moved = {}, {}
    for q in range(groups):
        rows = [pltpu.roll(picked[pl.ds(4 * q + i, channels, stride=slots), :], 32 * i + 2, 1) for i in range(4)]
        rows = jnp.where(
            lane < 64, jnp.where(lane < 32, rows[0], rows[1]), jnp.where(lane < 96, rows[2], rows[3])
        )
        held[q] = jnp.where(4 * q + (lane >> 5) < width, rows, 0.0)
    for q in range(-1, groups):
        low = held.get(q + 1, jnp.zeros(shape, F32))
        high = held.get(q, jnp.zeros(shape, F32))
        moved[q] = pltpu.roll(jnp.where(lane < 64, low, high), 64, 1)
    sums = []
    for q in range(-1, groups + 1):
        total = None
        for weight, rows in ((scale[0], moved.get(q - 1)), (scale[1], held.get(q)), (scale[2], moved.get(q))):
            if rows is not None:
                total = weight * rows if total is None else total + weight * rows
        sums.append(total + pltpu.roll(total, tile - 8, 1) + pltpu.roll(total, tile - 16, 1))
    packed = []
    for half in range(2):
        total = sums[4 * half]
        for k in range(1, 4):
            total = jnp.where(((lane >> 3) & 3) == k, pltpu.roll(sums[4 * half + k], 8 * k, 1), total)
        packed.append(total)
    left = jnp.where(on_left, packed[0], pltpu.roll(packed[1], tile - 2, 1))
    right = jnp.where(on_left, pltpu.roll(packed[1], 2, 1), packed[0])
    even = is_even("gy")
    first[0:channels, :] = jnp.where(even, right, left).astype(BF16)
    second[0:channels, :] = jnp.where(even, left, right).astype(BF16)


def shifted_sum(before, centre, after):
    lane = lane_iota(centre.shape)
    tile = centre.shape[-1]
    before = jnp.where(lane < 2, 0.0, pltpu.roll(before, 2, 1))
    after = jnp.where(lane >= tile - 2, 0.0, pltpu.roll(after, tile - 2, 1))
    return centre + before + after


def convolve_block(cells, weights, depth, b, first_block):
    channels = weights.shape[1]
    slots = cells.shape[1] // channels
    at = pl.ds(pl.multiple_of(b * ROWS, ROWS), ROWS)
    to = pl.ds(pl.multiple_of((b - first_block) * ROWS, ROWS), ROWS)
    tap = [weights[t, at, :] for t in range(27)]
    for z in range(ZOUT):
        for parity in range(2):
            sums = {}
            for x in range(parity, slots, 2):
                rows = [cells[z + ZOUT * m, pl.ds(b * (ROWS * slots) + x, ROWS, stride=slots), :] for m in range(3)]
                for m in range(3):
                    for dx in (1, 0, -1):
                        out = x - 2 * dx
                        if 0 <= out < slots:
                            for dy in (-1, 0, 1):
                                term = tap[tap_of(m, dx, dy)] * rows[m]
                                key = (out, dy)
                                sums[key] = sums[key] + term if key in sums else term
                for out in [x - 2] if x + 2 < slots else [x - 2, x]:
                    if out >= 0:
                        depth[z, out, to, :] = shifted_sum(*(sums.pop((out, dy)) for dy in (-1, 0, 1)))


def conv_kernel(widths, cells, weights, coarse, depth, rims, own_block):
    width = widths[lax.axis_index("gx")]
    channels = weights.shape[1]
    slots = cells.shape[1] // channels
    own_block[...] = coarse[...]

    for b in range(channels // ROWS):
        at = slice(b * ROWS, (b + 1) * ROWS)
        for side, dx in enumerate((1, -1)):
            tap = [[weights[tap_of(m, dx, dy), at, :] for m in range(3)] for dy in (-1, 0, 1)]
            for r in range(2):
                x = r if side == 0 else width - 2 + r
                for z in range(ZOUT):
                    rows = [
                        cells[z + ZOUT * m, pl.ds(b * (ROWS * slots) + x, ROWS, stride=slots), :] for m in range(3)
                    ]
                    parts = [sum(weight * row for weight, row in zip(weights_of, rows)) for weights_of in tap]
                    rims[z, 2 * side + r, at, :] = shifted_sum(*parts)

    def convolve(b, carry):
        convolve_block(cells, weights, depth, b, 0)
        return carry

    lax.fori_loop(0, SPLIT, convolve, 0)


def edge_term(edge, z, x):
    tile = edge.shape[2]
    group = x // 4 + 1 if isinstance(x, int) else lax.div(x, 4) + 1
    at = x % 4 if isinstance(x, int) else lax.rem(x, 4)
    begin = 32 * at + 8 * (group & 3) + 4 * z
    cells = pltpu.roll(edge[group >> 2], tile - 2 - begin, 1)
    lane = lane_iota(cells.shape)
    return jnp.where((lane < 2) | (lane >= tile - 2), cells, 0.0)


def rim_kernel(widths, second, first, rims, edge, far, near):
    width = widths[lax.axis_index("gx")]
    _, _, channels, tile = rims.shape
    even = is_even("gy")
    one, two = first[0:channels, :].astype(F32), second[0:channels, :].astype(F32)
    right = jnp.where(even, one, two)
    left = jnp.where(even, two, one)
    on_left = (lane_iota((channels, tile)) & 2) != 0
    edge[0] = jnp.where(on_left, pltpu.roll(left, 2, 1), pltpu.roll(right, tile - 2, 1))
    edge[1] = jnp.where(on_left, left, right)
    even = is_even("gx")
    for z in range(ZOUT):
        for r in range(2):
            to_lower = rims[z, r] + edge_term(edge, z, r - 2)
            to_upper = rims[z, 2 + r] + edge_term(edge, z, width + r)
            at = slice((2 * z + r) * channels, (2 * z + r + 1) * channels)
            near[at, :] = jnp.where(even, to_upper, to_lower).astype(BF16)
            far[at, :] = jnp.where(even, to_lower, to_upper).astype(BF16)


def slab_start(widths):
    slab = lax.axis_index("gx")
    start = jnp.int32(0)
    for d in range(widths.shape[0]):
        start = start + jnp.where(d < slab, widths[d], 0)
    return start


def depth_row(weights, depths, edge, z, x):
    own = jnp.concatenate([depth[z, x] for depth in depths], axis=0)
    return own + weights[DW_BIAS] + edge_term(edge, z, x)


def finished_row(weights, cells, lifted, phase, width, mixed, z, x):
    channels = weights.shape[1]
    slots = cells.shape[1] // channels
    mixed = mixed + weights[PW_BIAS]
    active = jnp.maximum(mixed, 0.2 * mixed)
    field = cells[2 + z, pl.ds(x, channels, stride=slots), :]
    value = active + (field + lifted[lax.div(phase + x, CF)])
    return jnp.where(x < width, value, 0.0)


def mix_kernel(gathered, widths, mix, cells, weights, depth, edge, *refs):
    if gathered:
        coarse, value, rest, lifted, mixer, across = refs
        parts, ncx, ncy = coarse.shape
    else:
        second, first, own_block, opposite, value, rest, lifted, mixer, across, blocks = refs
        parts, own_rows, ncy = own_block.shape
        ncx = 4 * own_rows
    width = widths[lax.axis_index("gx")]
    here = lax.axis_index("gy")
    start = slab_start(widths)
    phase = lax.rem(start, CF)
    channels, tile = weights.shape[1:]
    slots = cells.shape[1] // channels

    def convolve(b, carry):
        convolve_block(cells, weights, rest, b, SPLIT)
        return carry

    lax.fori_loop(SPLIT, channels // ROWS, convolve, 0)

    if not gathered:
        even = is_even("gy")
        after, before = lax.rem(here + 1, 4), lax.rem(here + 3, 4)
        count = parts * own_rows
        for message, owner in (
            (first, jnp.where(even, after, before)),
            (second, jnp.where(even, before, after)),
        ):
            terms = message[channels:, :].astype(F32)[0:count, :]
            sums = terms[:, 0:ncy] + terms[:, ncy : 2 * ncy] + terms[:, 2 * ncy : 3 * ncy]
            for k in range(parts):
                blocks[k, pl.ds(owner * own_rows, own_rows), :] = sums[k * own_rows : (k + 1) * own_rows]
        for block, owner in ((own_block, here), (opposite, lax.rem(here + 2, 4))):
            for k in range(parts):
                blocks[k, pl.ds(owner * own_rows, own_rows), :] = block[k]
    shape = (ncy, tile)
    cell = row_iota(shape) * CF
    place = lane_iota(shape) + here * tile
    along_y = ((place >= cell) & (place < cell + CF)).astype(F32)
    for k in range(parts):
        block = coarse[k] if gathered else blocks[k]
        across[k] = jnp.dot(block, along_y, precision=lax.Precision.HIGHEST, preferred_element_type=F32)
    for i in range(3):
        cell = lax.rem(lax.div(start, CF) + i, ncx)
        total = None
        for k in range(parts):
            term = weights[LIFT + k] * across[k, pl.ds(cell, 1), :]
            total = term if total is None else total + term
        lifted[i] = total

    group = 4
    wide = jnp.concatenate([mix[...]] * group, axis=1)
    wide = jnp.concatenate([wide] * group, axis=0)
    size = group * channels
    row, column = row_iota((size, size)), lane_iota((size, size))
    same = sum(
        ((row >= i * channels) & (row < (i + 1) * channels) & (column >= i * channels) & (column < (i + 1) * channels)).astype(F32)
        for i in range(group)
    )
    mixer[...] = jnp.where(same > 0, wide.astype(F32), 0.0).astype(BF16)

    for x in range(0, slots, group):
        depths = [
            jnp.concatenate([depth_row(weights, (depth, rest), edge, z, x + i) for i in range(group)], axis=0).astype(BF16)
            for z in range(ZOUT)
        ]
        mixed = jnp.dot(mixer[...], jnp.concatenate(depths, axis=1), preferred_element_type=F32)
        for i in range(group):
            for z in range(ZOUT):
                part = mixed[i * channels : (i + 1) * channels, z * tile : (z + 1) * tile]
                value[z, pl.ds(x + i, channels, stride=slots), :] = finished_row(
                    weights, cells, lifted, phase, width, part, z, x + i
                )


def finish_kernel(widths, cells, weights, depth, rest, edge, lifted, mixer, far, near, value_in, out, value, block, sems):
    width = widths[lax.axis_index("gx")]
    phase = lax.rem(slab_start(widths), CF)
    channels, tile = weights.shape[1:]
    slots = cells.shape[1] // channels
    even = is_even("gx")
    at_top = jnp.where(even, far[...].astype(F32), near[...].astype(F32))
    at_end = jnp.where(even, near[...].astype(F32), far[...].astype(F32))
    rows = (0, 1, width - 2, width - 1)
    chunk = 16
    copies = []
    for z in range(ZOUT):
        parts = []
        for i, x in enumerate(rows):
            arrived = at_top if i < 2 else at_end
            begin = (2 * z + i % 2) * channels
            parts.append(depth_row(weights, (depth, rest), edge, z, x) + arrived[begin : begin + channels, :])
        mixed = jnp.dot(mixer[...], jnp.concatenate(parts, axis=0).astype(BF16), preferred_element_type=F32)
        for i, x in enumerate(rows):
            value[z, pl.ds(x, channels, stride=slots), :] = finished_row(
                weights, cells, lifted, phase, width, mixed[i * channels : (i + 1) * channels, :], z, x
            )
        for part in range(channels // chunk):
            for o in range(part * chunk, (part + 1) * chunk):
                block[z, o] = value[z, o * slots : (o + 1) * slots, :].astype(BF16)
            part_of = pl.ds(part * chunk, chunk)
            copy = pltpu.make_async_copy(block.at[z, part_of], out.at[z, part_of], sems.at[part, z])
            copy.start()
            copies.append(copy)
    for copy in copies:
        copy.wait()


def shards(feature, widths, dw_weight, dw_bias, pw_weight, pw_bias, lift_weight, coarse):
    planes, channels, slots, tile = feature.shape
    ny = lax.axis_size("gy")
    parts, own_rows, ncy = coarse.shape
    gathered = ny != 4
    ncx = ny * own_rows
    smem = pl.BlockSpec(memory_space=pltpu.SMEM)
    vmem = pl.BlockSpec(memory_space=pltpu.VMEM)
    hbm = pl.BlockSpec(memory_space=pltpu.HBM)
    params = pltpu.CompilerParams(vmem_limit_bytes=VMEM_BYTES)
    shape = jax.ShapeDtypeStruct
    strip = shape((channels + 16, tile), BF16)
    cells_shape = pltpu.VMEM((planes, channels * slots, tile), F32)
    value_shape = pltpu.VMEM((ZOUT, channels * slots, tile), F32)
    message = shape((2 * ZOUT * channels, tile), BF16)

    def swapped(array, axis, first):
        count = lax.axis_size(axis)
        pairs = []
        for i in range(first, count + first, 2):
            a, b = i % count, (i + 1) % count
            pairs += [(a, b), (b, a)]
        return lax.ppermute(array, axis, pairs)

    def pinned(array):
        return pltpu.with_memory_space_constraint(array, pltpu.HBM)

    if gathered:
        every = lax.all_gather(coarse, "gy", axis=1, tiled=True)
    small = (
        widths,
        dw_weight,
        dw_bias.reshape(1, channels),
        pw_bias.reshape(1, channels),
        lift_weight.T,
        coarse,
    )
    cells, weights, first, second, block, slab_widths = pl.pallas_call(
        pack_kernel,
        out_shape=(
            cells_shape,
            pltpu.VMEM((32, channels, tile), F32),
            strip,
            strip,
            pltpu.VMEM(coarse.shape, F32),
            pltpu.SMEM(widths.shape, jnp.int32),
        ),
        in_specs=[hbm] * 7,
        out_specs=(vmem,) * 5 + (smem,),
        scratch_shapes=[
            pltpu.VMEM(feature.shape, BF16),
            pltpu.SMEM(widths.shape, jnp.int32),
            pltpu.VMEM(dw_weight.shape, F32),
            pltpu.VMEM((1, channels), F32),
            pltpu.VMEM((1, channels), F32),
            pltpu.VMEM((parts, channels), F32),
            pltpu.VMEM(coarse.shape, F32),
            pltpu.VMEM((32, channels), F32),
            pltpu.VMEM((16, tile), F32),
            pltpu.VMEM((channels * slots, tile), F32),
            pltpu.SemaphoreType.DMA((channels // CHUNK,)),
            pltpu.SemaphoreType.DMA((len(small),)),
        ],
        compiler_params=params,
    )(pinned(feature), *(pinned(array) for array in small))
    second = swapped(second, "gy", 1)
    first = swapped(first, "gy", 0)
    early = SPLIT * ROWS
    depth, rims, own_block = pl.pallas_call(
        conv_kernel,
        out_shape=(
            pltpu.VMEM((ZOUT, slots, early, tile), F32),
            pltpu.VMEM((ZOUT, 4, channels, tile), F32),
            pltpu.VMEM(coarse.shape, F32),
        ),
        in_specs=[smem, vmem, vmem, vmem],
        out_specs=(vmem,) * 3,
        compiler_params=params,
        cost_estimate=pl.CostEstimate(flops=10**9, bytes_accessed=10**6, transcendentals=0),
    )(slab_widths, cells, weights, block)
    if not gathered:
        opposite = lax.ppermute(own_block, "gy", [(i, (i + 2) % 4) for i in range(4)])
    edge, far, near = pl.pallas_call(
        rim_kernel,
        out_shape=(pltpu.VMEM((2, channels, tile), F32), message, message),
        in_specs=[smem] + [vmem] * 3,
        out_specs=(vmem,) * 3,
        compiler_params=params,
    )(slab_widths, second, first, rims)
    far = swapped(far, "gx", 1)
    near = swapped(near, "gx", 0)
    blocks = (every,) if gathered else (second, first, own_block, opposite)
    value, rest, lifted, mixer = pl.pallas_call(
        functools.partial(mix_kernel, gathered),
        out_shape=(
            value_shape,
            pltpu.VMEM((ZOUT, slots, channels - early, tile), F32),
            pltpu.VMEM((3, channels, tile), F32),
            pltpu.VMEM((4 * channels, 4 * channels), BF16),
        ),
        in_specs=[smem] + [vmem] * (5 + len(blocks)),
        out_specs=(vmem,) * 4,
        scratch_shapes=[pltpu.VMEM((parts, ncx, tile), F32)]
        + ([] if gathered else [pltpu.VMEM((parts, ncx, ncy), F32)]),
        compiler_params=params,
        cost_estimate=pl.CostEstimate(flops=10**9, bytes_accessed=10**6, transcendentals=0),
    )(slab_widths, pw_weight, cells, weights, depth, edge, *blocks)
    out, _ = pl.pallas_call(
        finish_kernel,
        out_shape=(shape((ZOUT, channels, slots, tile), BF16), value_shape),
        in_specs=[smem] + [vmem] * 10,
        out_specs=(hbm, vmem),
        scratch_shapes=[
            pltpu.VMEM((ZOUT, channels, slots, tile), BF16),
            pltpu.SemaphoreType.DMA((channels // 16, ZOUT)),
        ],
        input_output_aliases={10: 1},
        compiler_params=params,
    )(slab_widths, cells, weights, depth, rest, edge, lifted, mixer, far, near, value)
    return out


def solution(mesh):
    placed = (P(None, None, "gx", "gy"), P(), P(), P(), P(), P(), P(), P(None, "gy", None))
    return jax.shard_map(
        shards, mesh=mesh, in_specs=placed, out_specs=P(None, None, "gx", "gy"), check_vma=False
    )
```

```python
import functools

import jax
import jax.numpy as jnp
from jax import lax
from jax.experimental import pallas as pl
from jax.experimental.pallas import tpu as pltpu
from jax.sharding import PartitionSpec as P

XW = 16
ZOUT = 2
CF = 16
ROWS = 8
SPLIT = 5
CHUNK = 16
DW_BIAS, PW_BIAS, LIFT = 27, 28, 29
F32 = jnp.float32
BF16 = jnp.bfloat16
VMEM_BYTES = 14 * 1024 * 1024


def lane_iota(shape):
    return lax.broadcasted_iota(jnp.int32, shape, len(shape) - 1)


def row_iota(shape):
    return lax.broadcasted_iota(jnp.int32, shape, len(shape) - 2)


def tap_of(m, dx, dy):
    return 9 * m + 3 * (dx + 1) + (dy + 1)


def is_even(axis):
    return lax.rem(lax.axis_index(axis), 2) == 0


def pack_kernel(
    feature, widths_in, taps_in, dw_bias_in, pw_bias_in, lift_in, coarse_in,
    cells, first, second, stacked, own_block, widths,
    planes, widths_here, taps, dw_bias, pw_bias, lift, coarse, tail, picked, sems, small_sems,
):
    count, channels, slots, tile = feature.shape
    chunks = range(0, channels, CHUNK)

    def copy_of(z, c):
        at = pl.ds(c, CHUNK)
        return pltpu.make_async_copy(feature.at[z, at], planes.at[z, at], sems.at[z, c // CHUNK])

    small = [
        pltpu.make_async_copy(source, target, small_sems.at[i])
        for i, (source, target) in enumerate(
            (
                (widths_in, widths_here),
                (taps_in, taps),
                (dw_bias_in, dw_bias),
                (pw_bias_in, pw_bias),
                (lift_in, lift),
                (coarse_in, coarse),
            )
        )
    ]
    for copy in small:
        copy.start()
    for c in chunks:
        for z in range(count):
            copy_of(z, c).start()
    for copy in small:
        copy.wait()
    for d in range(widths.shape[0]):
        widths[d] = widths_here[d]
    width = widths_here[lax.axis_index("gx")]
    stacked[0:DW_BIAS, :] = taps[...]
    stacked[DW_BIAS : DW_BIAS + 1, :] = dw_bias[...]
    stacked[PW_BIAS : PW_BIAS + 1, :] = pw_bias[...]
    stacked[LIFT : LIFT + 3, :] = lift[...]

    own_block[...] = coarse[...]
    parts, own_rows, ncy = coarse.shape
    tail[...] = jnp.zeros_like(tail)
    if 3 * ncy <= tile:
        for k in range(parts):
            rest = coarse[k]
            for p in range(3):
                term = rest.astype(BF16).astype(F32)
                rest = rest - term
                tail[k * own_rows : (k + 1) * own_rows, p * ncy : (p + 1) * ncy] = term
    for message in (first, second):
        message[channels:, :] = tail[...].astype(BF16)

    row, along = row_iota((taps.shape[0], tile)), lane_iota((taps.shape[0], tile))
    of_plane = 9 * ((along & 31) >> 3) + jnp.where((along & 2) != 0, 2, 0)
    terms, rest = [], taps[...]
    for _ in range(3):
        terms.append(rest.astype(BF16))
        rest = rest - terms[-1].astype(F32)
    scale = []
    for dx in (-1, 0, 1):
        chosen = (row == of_plane + 3 * (dx + 1)).astype(BF16)
        scale.append(
            sum(
                lax.dot_general(term, chosen, (((0,), (0,)), ((), ())), preferred_element_type=F32) for term in terms
            )
        )

    across = lane_iota((CHUNK * slots, tile))
    shape = (CHUNK, tile)
    lane = lane_iota(shape)
    on_left = (lane & 2) != 0
    even = is_even("gy")
    groups = slots // 4
    for c in chunks:
        at = slice(c * slots, (c + CHUNK) * slots)
        total = None
        for z in range(count):
            copy_of(z, c).wait()
            rows = planes[z, c : c + CHUNK].reshape(CHUNK * slots, tile)
            cells[z, at, :] = rows.astype(F32)
            if z:
                inside = (across >= 4 * z - 2) & (across < 4 * z + 2)
                total = jnp.where(inside, pltpu.roll(rows, 4 * z, 1), total)
            else:
                total = rows
        picked[at, :] = total.astype(F32)

        held, moved = {}, {}
        for q in range(groups):
            rows = [
                pltpu.roll(picked[pl.ds(c * slots + 4 * q + i, CHUNK, stride=slots), :], 32 * i + 2, 1)
                for i in range(4)
            ]
            rows = jnp.where(
                lane < 64, jnp.where(lane < 32, rows[0], rows[1]), jnp.where(lane < 96, rows[2], rows[3])
            )
            held[q] = jnp.where(4 * q + (lane >> 5) < width, rows, 0.0)
        for q in range(-1, groups):
            low = held.get(q + 1, jnp.zeros(shape, F32))
            high = held.get(q, jnp.zeros(shape, F32))
            moved[q] = pltpu.roll(jnp.where(lane < 64, low, high), 64, 1)
        sums = []
        for q in range(-1, groups + 1):
            total = None
            for weight, rows in ((scale[0], moved.get(q - 1)), (scale[1], held.get(q)), (scale[2], moved.get(q))):
                if rows is not None:
                    term = weight[c : c + CHUNK, :] * rows
                    total = term if total is None else total + term
            sums.append(total + pltpu.roll(total, tile - 8, 1) + pltpu.roll(total, tile - 16, 1))
        packed = []
        for half in range(2):
            total = sums[4 * half]
            for k in range(1, 4):
                total = jnp.where(((lane >> 3) & 3) == k, pltpu.roll(sums[4 * half + k], 8 * k, 1), total)
            packed.append(total)
        left = jnp.where(on_left, packed[0], pltpu.roll(packed[1], tile - 2, 1))
        right = jnp.where(on_left, pltpu.roll(packed[1], 2, 1), packed[0])
        first[c : c + CHUNK, :] = jnp.where(even, right, left).astype(BF16)
        second[c : c + CHUNK, :] = jnp.where(even, left, right).astype(BF16)


def shifted_sum(before, centre, after):
    lane = lane_iota(centre.shape)
    tile = centre.shape[-1]
    before = jnp.where(lane < 2, 0.0, pltpu.roll(before, 2, 1))
    after = jnp.where(lane >= tile - 2, 0.0, pltpu.roll(after, tile - 2, 1))
    return centre + before + after


def convolve_block(cells, weights, depth, b, first_block):
    channels = weights.shape[1]
    slots = cells.shape[1] // channels
    at = pl.ds(pl.multiple_of(b * ROWS, ROWS), ROWS)
    to = pl.ds(pl.multiple_of((b - first_block) * ROWS, ROWS), ROWS)
    tap = [weights[t, at, :] for t in range(27)]
    for z in range(ZOUT):
        for parity in range(2):
            sums = {}
            for x in range(parity, slots, 2):
                rows = [cells[z + ZOUT * m, pl.ds(b * (ROWS * slots) + x, ROWS, stride=slots), :] for m in range(3)]
                for m in range(3):
                    for dx in (1, 0, -1):
                        out = x - 2 * dx
                        if 0 <= out < slots:
                            for dy in (-1, 0, 1):
                                term = tap[tap_of(m, dx, dy)] * rows[m]
                                key = (out, dy)
                                sums[key] = sums[key] + term if key in sums else term
                for out in [x - 2] if x + 2 < slots else [x - 2, x]:
                    if out >= 0:
                        depth[z, out, to, :] = shifted_sum(*(sums.pop((out, dy)) for dy in (-1, 0, 1)))


def conv_kernel(widths, stacked, coarse, cells_in, cells, weights, depth, rims, own_block):
    width = widths[lax.axis_index("gx")]
    channels, tile = weights.shape[1:]
    slots = cells.shape[1] // channels
    own_block[...] = coarse[...]
    turned = jnp.transpose(stacked[...])
    for t in range(stacked.shape[0]):
        weights[t] = jnp.broadcast_to(turned[:, t : t + 1], (channels, tile))
    for r in range(2):

        @pl.when(width + r < slots)
        def _():
            for z in range(cells.shape[0]):
                cells[z, pl.ds(width + r, channels, stride=slots), :] = jnp.zeros((channels, tile), F32)

    for b in range(channels // ROWS):
        at = slice(b * ROWS, (b + 1) * ROWS)
        for side, dx in enumerate((1, -1)):
            tap = [[weights[tap_of(m, dx, dy), at, :] for m in range(3)] for dy in (-1, 0, 1)]
            for r in range(2):
                x = r if side == 0 else width - 2 + r
                for z in range(ZOUT):
                    rows = [
                        cells[z + ZOUT * m, pl.ds(b * (ROWS * slots) + x, ROWS, stride=slots), :] for m in range(3)
                    ]
                    parts = [sum(weight * row for weight, row in zip(weights_of, rows)) for weights_of in tap]
                    rims[z, 2 * side + r, at, :] = shifted_sum(*parts)

    def convolve(b, carry):
        convolve_block(cells, weights, depth, b, 0)
        return carry

    lax.fori_loop(0, SPLIT, convolve, 0)


def edge_term(edge, z, x):
    tile = edge.shape[2]
    group = x // 4 + 1 if isinstance(x, int) else lax.div(x, 4) + 1
    at = x % 4 if isinstance(x, int) else lax.rem(x, 4)
    begin = 32 * at + 8 * (group & 3) + 4 * z
    cells = pltpu.roll(edge[group >> 2], tile - 2 - begin, 1)
    lane = lane_iota(cells.shape)
    return jnp.where((lane < 2) | (lane >= tile - 2), cells, 0.0)


def rim_kernel(widths, second, first, rims, edge, far, near):
    width = widths[lax.axis_index("gx")]
    _, _, channels, tile = rims.shape
    even = is_even("gy")
    one, two = first[0:channels, :].astype(F32), second[0:channels, :].astype(F32)
    right = jnp.where(even, one, two)
    left = jnp.where(even, two, one)
    on_left = (lane_iota((channels, tile)) & 2) != 0
    edge[0] = jnp.where(on_left, pltpu.roll(left, 2, 1), pltpu.roll(right, tile - 2, 1))
    edge[1] = jnp.where(on_left, left, right)
    even = is_even("gx")
    for z in range(ZOUT):
        for r in range(2):
            to_lower = rims[z, r] + edge_term(edge, z, r - 2)
            to_upper = rims[z, 2 + r] + edge_term(edge, z, width + r)
            at = slice((2 * z + r) * channels, (2 * z + r + 1) * channels)
            near[at, :] = jnp.where(even, to_upper, to_lower).astype(BF16)
            far[at, :] = jnp.where(even, to_lower, to_upper).astype(BF16)


def slab_start(widths):
    slab = lax.axis_index("gx")
    start = jnp.int32(0)
    for d in range(widths.shape[0]):
        start = start + jnp.where(d < slab, widths[d], 0)
    return start


def depth_row(weights, depths, edge, z, x):
    own = jnp.concatenate([depth[z, x] for depth in depths], axis=0)
    return own + weights[DW_BIAS] + edge_term(edge, z, x)


def base_row(cells, lifted, phase, z, x):
    channels = lifted.shape[1]
    slots = cells.shape[1] // channels
    return cells[2 + z, pl.ds(x, channels, stride=slots), :] + lifted[lax.div(phase + x, CF)]


def active(weights, mixed):
    mixed = mixed + weights[PW_BIAS]
    return jnp.maximum(mixed, 0.2 * mixed)


def mix_kernel(gathered, widths, mix, cells, weights, depth, edge, *refs):
    if gathered:
        coarse, value, ends, bases, mixer, rest, lifted, across = refs
        parts, ncx, ncy = coarse.shape
    else:
        second, first, own_block, opposite, value, ends, bases, mixer, rest, lifted, across, blocks = refs
        parts, own_rows, ncy = own_block.shape
        ncx = 4 * own_rows
    width = widths[lax.axis_index("gx")]
    here = lax.axis_index("gy")
    start = slab_start(widths)
    phase = lax.rem(start, CF)
    channels, tile = weights.shape[1:]
    slots = cells.shape[1] // channels

    def convolve(b, carry):
        convolve_block(cells, weights, rest, b, SPLIT)
        return carry

    lax.fori_loop(SPLIT, channels // ROWS, convolve, 0)

    if not gathered:
        even = is_even("gy")
        after, before = lax.rem(here + 1, 4), lax.rem(here + 3, 4)
        count = parts * own_rows
        for message, owner in (
            (first, jnp.where(even, after, before)),
            (second, jnp.where(even, before, after)),
        ):
            terms = message[channels:, :].astype(F32)[0:count, :]
            sums = terms[:, 0:ncy] + terms[:, ncy : 2 * ncy] + terms[:, 2 * ncy : 3 * ncy]
            for k in range(parts):
                blocks[k, pl.ds(owner * own_rows, own_rows), :] = sums[k * own_rows : (k + 1) * own_rows]
        for block, owner in ((own_block, here), (opposite, lax.rem(here + 2, 4))):
            for k in range(parts):
                blocks[k, pl.ds(owner * own_rows, own_rows), :] = block[k]
    shape = (ncy, tile)
    cell = row_iota(shape) * CF
    place = lane_iota(shape) + here * tile
    along_y = ((place >= cell) & (place < cell + CF)).astype(F32)
    for k in range(parts):
        block = coarse[k] if gathered else blocks[k]
        across[k] = jnp.dot(block, along_y, precision=lax.Precision.HIGHEST, preferred_element_type=F32)
    for i in range(3):
        cell = lax.rem(lax.div(start, CF) + i, ncx)
        total = None
        for k in range(parts):
            term = weights[LIFT + k] * across[k, pl.ds(cell, 1), :]
            total = term if total is None else total + term
        lifted[i] = total

    group = 4
    wide = jnp.concatenate([mix[...]] * group, axis=1)
    wide = jnp.concatenate([wide] * group, axis=0)
    size = group * channels
    row, column = row_iota((size, size)), lane_iota((size, size))
    same = sum(
        ((row >= i * channels) & (row < (i + 1) * channels) & (column >= i * channels) & (column < (i + 1) * channels)).astype(F32)
        for i in range(group)
    )
    mixer[...] = jnp.where(same > 0, wide.astype(F32), 0.0).astype(BF16)

    for x in range(0, slots, group):
        depths = [
            jnp.concatenate([depth_row(weights, (depth, rest), edge, z, x + i) for i in range(group)], axis=0).astype(BF16)
            for z in range(ZOUT)
        ]
        mixed = jnp.dot(mixer[...], jnp.concatenate(depths, axis=1), preferred_element_type=F32)
        for i in range(group):
            for z in range(ZOUT):
                part = mixed[i * channels : (i + 1) * channels, z * tile : (z + 1) * tile]
                part = active(weights, part) + base_row(cells, lifted, phase, z, x + i)
                value[z, pl.ds(x + i, channels, stride=slots), :] = jnp.where(x + i < width, part, 0.0)
    for z in range(ZOUT):
        for i, x in enumerate((0, 1, width - 2, width - 1)):
            ends[z, i * channels : (i + 1) * channels, :] = depth_row(weights, (depth, rest), edge, z, x)
            bases[z, i * channels : (i + 1) * channels, :] = base_row(cells, lifted, phase, z, x)


def finish_kernel(widths, weights, ends, bases, mixer, far, near, value_in, out, value, block, sems):
    width = widths[lax.axis_index("gx")]
    channels = weights.shape[1]
    slots = block.shape[2]
    even = is_even("gx")
    half = 2 * channels
    copies = []
    for z in range(ZOUT):
        at = slice(z * half, (z + 1) * half)
        one, two = far[at, :].astype(F32), near[at, :].astype(F32)
        arrived = jnp.concatenate([jnp.where(even, one, two), jnp.where(even, two, one)], axis=0)
        mixed = jnp.dot(mixer[...], (ends[z] + arrived).astype(BF16), preferred_element_type=F32)
        for i, x in enumerate((0, 1, width - 2, width - 1)):
            at = slice(i * channels, (i + 1) * channels)
            value[z, pl.ds(x, channels, stride=slots), :] = active(weights, mixed[at, :]) + bases[z, at, :]
        for part in range(channels // CHUNK):
            for o in range(part * CHUNK, (part + 1) * CHUNK):
                block[z, o] = value[z, o * slots : (o + 1) * slots, :].astype(BF16)
            part_of = pl.ds(part * CHUNK, CHUNK)
            copy = pltpu.make_async_copy(block.at[z, part_of], out.at[z, part_of], sems.at[part, z])
            copy.start()
            copies.append(copy)
    for copy in copies:
        copy.wait()


def shards(feature, widths, dw_weight, dw_bias, pw_weight, pw_bias, lift_weight, coarse):
    planes, channels, slots, tile = feature.shape
    ny = lax.axis_size("gy")
    parts, own_rows, ncy = coarse.shape
    gathered = ny != 4
    ncx = ny * own_rows
    smem = pl.BlockSpec(memory_space=pltpu.SMEM)
    vmem = pl.BlockSpec(memory_space=pltpu.VMEM)
    hbm = pl.BlockSpec(memory_space=pltpu.HBM)
    params = pltpu.CompilerParams(vmem_limit_bytes=VMEM_BYTES)
    shape = jax.ShapeDtypeStruct
    strip = shape((channels + 16, tile), BF16)
    cells_shape = pltpu.VMEM((planes, channels * slots, tile), F32)
    value_shape = pltpu.VMEM((ZOUT, channels * slots, tile), F32)
    message = shape((2 * ZOUT * channels, tile), BF16)

    def swapped(array, axis, first):
        count = lax.axis_size(axis)
        pairs = []
        for i in range(first, count + first, 2):
            a, b = i % count, (i + 1) % count
            pairs += [(a, b), (b, a)]
        return lax.ppermute(array, axis, pairs)

    def pinned(array):
        return pltpu.with_memory_space_constraint(array, pltpu.HBM)

    if gathered:
        every = lax.all_gather(coarse, "gy", axis=1, tiled=True)
    small = (
        widths,
        dw_weight,
        dw_bias.reshape(1, channels),
        pw_bias.reshape(1, channels),
        lift_weight.T,
        coarse,
    )
    cells, first, second, stacked, block, slab_widths = pl.pallas_call(
        pack_kernel,
        out_shape=(
            cells_shape,
            strip,
            strip,
            pltpu.VMEM((32, channels), F32),
            pltpu.VMEM(coarse.shape, F32),
            pltpu.SMEM(widths.shape, jnp.int32),
        ),
        in_specs=[hbm] * 7,
        out_specs=(vmem,) * 5 + (smem,),
        scratch_shapes=[
            pltpu.VMEM(feature.shape, BF16),
            pltpu.SMEM(widths.shape, jnp.int32),
            pltpu.VMEM(dw_weight.shape, F32),
            pltpu.VMEM((1, channels), F32),
            pltpu.VMEM((1, channels), F32),
            pltpu.VMEM((parts, channels), F32),
            pltpu.VMEM(coarse.shape, F32),
            pltpu.VMEM((16, tile), F32),
            pltpu.VMEM((channels * slots, tile), F32),
            pltpu.SemaphoreType.DMA((planes, channels // CHUNK)),
            pltpu.SemaphoreType.DMA((len(small),)),
        ],
        compiler_params=params,
    )(pinned(feature), *(pinned(array) for array in small))
    second = swapped(second, "gy", 1)
    first = swapped(first, "gy", 0)
    early = SPLIT * ROWS
    cells, weights, depth, rims, own_block = pl.pallas_call(
        conv_kernel,
        out_shape=(
            cells_shape,
            pltpu.VMEM((32, channels, tile), F32),
            pltpu.VMEM((ZOUT, slots, early, tile), F32),
            pltpu.VMEM((ZOUT, 4, channels, tile), F32),
            pltpu.VMEM(coarse.shape, F32),
        ),
        in_specs=[smem] + [vmem] * 3,
        out_specs=(vmem,) * 5,
        input_output_aliases={3: 0},
        compiler_params=params,
        cost_estimate=pl.CostEstimate(flops=10**9, bytes_accessed=10**6, transcendentals=0),
    )(slab_widths, stacked, block, cells)
    if not gathered:
        opposite = lax.ppermute(own_block, "gy", [(i, (i + 2) % 4) for i in range(4)])
    edge, far, near = pl.pallas_call(
        rim_kernel,
        out_shape=(pltpu.VMEM((2, channels, tile), F32), message, message),
        in_specs=[smem] + [vmem] * 3,
        out_specs=(vmem,) * 3,
        compiler_params=params,
    )(slab_widths, second, first, rims)
    far = swapped(far, "gx", 1)
    near = swapped(near, "gx", 0)
    blocks = (every,) if gathered else (second, first, own_block, opposite)
    ends_shape = pltpu.VMEM((ZOUT, 4 * channels, tile), F32)
    value, ends, bases, mixer = pl.pallas_call(
        functools.partial(mix_kernel, gathered),
        out_shape=(value_shape, ends_shape, ends_shape, pltpu.VMEM((4 * channels, 4 * channels), BF16)),
        in_specs=[smem] + [vmem] * (5 + len(blocks)),
        out_specs=(vmem,) * 4,
        scratch_shapes=[
            pltpu.VMEM((ZOUT, slots, channels - early, tile), F32),
            pltpu.VMEM((3, channels, tile), F32),
            pltpu.VMEM((parts, ncx, tile), F32),
        ]
        + ([] if gathered else [pltpu.VMEM((parts, ncx, ncy), F32)]),
        compiler_params=params,
        cost_estimate=pl.CostEstimate(flops=10**9, bytes_accessed=10**6, transcendentals=0),
    )(slab_widths, pw_weight, cells, weights, depth, edge, *blocks)
    out, _ = pl.pallas_call(
        finish_kernel,
        out_shape=(shape((ZOUT, channels, slots, tile), BF16), value_shape),
        in_specs=[smem] + [vmem] * 7,
        out_specs=(hbm, vmem),
        scratch_shapes=[
            pltpu.VMEM((ZOUT, channels, slots, tile), BF16),
            pltpu.SemaphoreType.DMA((channels // CHUNK, ZOUT)),
        ],
        input_output_aliases={7: 1},
        compiler_params=params,
    )(slab_widths, weights, ends, bases, mixer, far, near, value)
    return out


def solution(mesh):
    placed = (P(None, None, "gx", "gy"), P(), P(), P(), P(), P(), P(), P(None, "gy", None))
    return jax.shard_map(
        shards, mesh=mesh, in_specs=placed, out_specs=P(None, None, "gx", "gy"), check_vma=False
    )
```

```python
import functools

import jax
import jax.numpy as jnp
from jax import lax
from jax.experimental import pallas as pl
from jax.experimental.pallas import tpu as pltpu
from jax.sharding import PartitionSpec as P

XW = 16
ZOUT = 2
CF = 16
ROWS = 8
SPLIT = 5
CHUNK = 16
DW_BIAS, PW_BIAS, LIFT = 27, 28, 29
F32 = jnp.float32
BF16 = jnp.bfloat16
VMEM_BYTES = 14 * 1024 * 1024


def lane_iota(shape):
    return lax.broadcasted_iota(jnp.int32, shape, len(shape) - 1)


def row_iota(shape):
    return lax.broadcasted_iota(jnp.int32, shape, len(shape) - 2)


def tap_of(m, dx, dy):
    return 9 * m + 3 * (dx + 1) + (dy + 1)


def is_even(axis):
    return lax.rem(lax.axis_index(axis), 2) == 0


def pack_kernel(
    feature, widths_in, taps_in, dw_bias_in, pw_bias_in, lift_in, coarse_in,
    cells, weights, first, second, own_block, widths,
    planes, widths_here, taps, dw_bias, pw_bias, lift, coarse, stacked, tail, picked, sems, small_sems,
):
    count, channels, slots, tile = feature.shape
    chunks = range(0, channels, CHUNK)

    def copy_of(c):
        at = pl.ds(c, CHUNK)
        return pltpu.make_async_copy(feature.at[:, at], planes.at[:, at], sems.at[c // CHUNK])

    small = [
        pltpu.make_async_copy(source, target, small_sems.at[i])
        for i, (source, target) in enumerate(
            (
                (widths_in, widths_here),
                (taps_in, taps),
                (dw_bias_in, dw_bias),
                (pw_bias_in, pw_bias),
                (lift_in, lift),
                (coarse_in, coarse),
            )
        )
    ]
    for copy in small:
        copy.start()
    for c in chunks:
        copy_of(c).start()
    for copy in small:
        copy.wait()
    for d in range(widths.shape[0]):
        widths[d] = widths_here[d]
    width = widths_here[lax.axis_index("gx")]
    stacked[0:DW_BIAS, :] = taps[...]
    stacked[DW_BIAS : DW_BIAS + 1, :] = dw_bias[...]
    stacked[PW_BIAS : PW_BIAS + 1, :] = pw_bias[...]
    stacked[LIFT : LIFT + 3, :] = lift[...]

    own_block[...] = coarse[...]
    parts, own_rows, ncy = coarse.shape
    tail[...] = jnp.zeros_like(tail)
    if 3 * ncy <= tile:
        for k in range(parts):
            rest = coarse[k]
            for p in range(3):
                term = rest.astype(BF16).astype(F32)
                rest = rest - term
                tail[k * own_rows : (k + 1) * own_rows, p * ncy : (p + 1) * ncy] = term
    for message in (first, second):
        message[channels:, :] = tail[...].astype(BF16)

    row, along = row_iota((taps.shape[0], tile)), lane_iota((taps.shape[0], tile))
    by_side = jnp.where((along & 2) != 0, 2, 0)
    terms, rest = [], taps[...]
    for _ in range(3):
        terms.append(rest.astype(BF16))
        rest = rest - terms[-1].astype(F32)
    chosen = jnp.concatenate(
        [(row == tap_of(m, dx, -1) + by_side).astype(BF16) for m in range(3) for dx in (-1, 0, 1)], axis=1
    )
    scale = sum(lax.dot_general(term, chosen, (((0,), (0,)), ((), ())), preferred_element_type=F32) for term in terms)
    turned = jnp.transpose(stacked[...])
    for t in range(stacked.shape[0]):
        weights[t] = jnp.broadcast_to(turned[:, t : t + 1], (channels, tile))

    lane, row = lane_iota((slots, tile)), row_iota((slots, tile))
    mine = (lane >> 3) == (row & 15)
    in_even, in_odd = mine & ((lane & 4) == 0), mine & ((lane & 4) != 0)
    shape = (2 * CHUNK, CHUNK * slots)
    row, column = row_iota(shape), lane_iota(shape)
    begin = (row & (CHUNK - 1)) * slots
    low = jnp.where(row < CHUNK, begin, begin + 16)
    high = jnp.where(row < CHUNK, begin + 16, begin + slots)
    gather = ((column >= low) & (column < high)).astype(BF16)
    shape = (CHUNK, tile)
    for c in chunks:
        copy_of(c).wait()
        spread = []
        for m in range(3):
            rows = []
            for k in range(c, c + CHUNK):
                both = []
                for z in range(ZOUT):
                    plane = planes[ZOUT * m + z, k].astype(F32)
                    cells[ZOUT * m + z, k * slots : (k + 1) * slots, :] = plane
                    both.append(
                        jnp.concatenate(
                            [
                                pltpu.roll(plane[x : x + ROWS], (2 + 4 * z + 8 * x) % tile, 1, stride=8, stride_axis=0)
                                for x in range(0, slots, ROWS)
                            ],
                            axis=0,
                        )
                    )
                rows.append(jnp.where(in_even, both[0], jnp.where(in_odd, both[1], 0.0)))
            spread.append(jnp.concatenate(rows, axis=0).astype(BF16))
        sums = jnp.dot(gather, jnp.concatenate(spread, axis=1), preferred_element_type=F32)
        for half in range(2):
            inside = 16 * half + (lane_iota(shape) >> 3) < width
            for m in range(3):
                part = sums[half * CHUNK : (half + 1) * CHUNK, m * tile : (m + 1) * tile]
                picked[m, half, c : c + CHUNK, :] = jnp.where(inside, part, 0.0)

    shape = (channels, tile)
    lane = lane_iota(shape)
    on_left = (lane & 2) != 0
    packed = [None, None]
    for m in range(3):
        low, high = picked[m, 0], picked[m, 1]
        moved = {
            -1: tuple(
                pltpu.roll(jnp.where(lane < tile - 16, one, two), 16, 1) for one, two in ((low, high), (high, low))
            ),
            0: (low, high),
            1: tuple(
                pltpu.roll(jnp.where(lane >= 16, one, two), tile - 16, 1) for one, two in ((low, high), (high, low))
            ),
        }
        for dx in (-1, 0, 1):
            begin = (3 * m + dx + 1) * tile
            for half in range(2):
                term = scale[:, begin : begin + tile] * moved[dx][half]
                packed[half] = term if packed[half] is None else packed[half] + term
    left = jnp.where(on_left, packed[0], pltpu.roll(packed[1], tile - 2, 1))
    right = jnp.where(on_left, pltpu.roll(packed[1], 2, 1), packed[0])
    even = is_even("gy")
    first[0:channels, :] = jnp.where(even, right, left).astype(BF16)
    second[0:channels, :] = jnp.where(even, left, right).astype(BF16)


def shifted_sum(before, centre, after):
    lane = lane_iota(centre.shape)
    tile = centre.shape[-1]
    before = jnp.where(lane < 2, 0.0, pltpu.roll(before, 2, 1))
    after = jnp.where(lane >= tile - 2, 0.0, pltpu.roll(after, tile - 2, 1))
    return centre + before + after


def convolve_block(cells, weights, depth, b, first_block):
    channels = weights.shape[1]
    slots = cells.shape[1] // channels
    at = pl.ds(pl.multiple_of(b * ROWS, ROWS), ROWS)
    to = pl.ds(pl.multiple_of((b - first_block) * ROWS, ROWS), ROWS)
    tap = [weights[t, at, :] for t in range(27)]
    for z in range(ZOUT):
        for parity in range(2):
            sums = {}
            for x in range(parity, slots, 2):
                rows = [cells[z + ZOUT * m, pl.ds(b * (ROWS * slots) + x, ROWS, stride=slots), :] for m in range(3)]
                for m in range(3):
                    for dx in (1, 0, -1):
                        out = x - 2 * dx
                        if 0 <= out < slots:
                            for dy in (-1, 0, 1):
                                term = tap[tap_of(m, dx, dy)] * rows[m]
                                key = (out, dy)
                                sums[key] = sums[key] + term if key in sums else term
                for out in [x - 2] if x + 2 < slots else [x - 2, x]:
                    if out >= 0:
                        depth[z, out, to, :] = shifted_sum(*(sums.pop((out, dy)) for dy in (-1, 0, 1)))


def conv_kernel(widths, weights, coarse, cells_in, cells, depth, rims, own_block):
    width = widths[lax.axis_index("gx")]
    channels, tile = weights.shape[1:]
    slots = cells.shape[1] // channels
    own_block[...] = coarse[...]
    for r in range(2):

        @pl.when(width + r < slots)
        def _():
            for z in range(cells.shape[0]):
                cells[z, pl.ds(width + r, channels, stride=slots), :] = jnp.zeros((channels, tile), F32)

    for b in range(channels // ROWS):
        at = slice(b * ROWS, (b + 1) * ROWS)
        for side, dx in enumerate((1, -1)):
            tap = [[weights[tap_of(m, dx, dy), at, :] for m in range(3)] for dy in (-1, 0, 1)]
            for r in range(2):
                x = r if side == 0 else width - 2 + r
                for z in range(ZOUT):
                    rows = [
                        cells[z + ZOUT * m, pl.ds(b * (ROWS * slots) + x, ROWS, stride=slots), :] for m in range(3)
                    ]
                    parts = [sum(weight * row for weight, row in zip(weights_of, rows)) for weights_of in tap]
                    rims[z, 2 * side + r, at, :] = shifted_sum(*parts)

    def convolve(b, carry):
        convolve_block(cells, weights, depth, b, 0)
        return carry

    lax.fori_loop(0, SPLIT, convolve, 0)


def edge_term(edge, z, x):
    tile = edge.shape[2]
    begin = 8 * (x & 15) + 4 * z
    cells = pltpu.roll(edge[(x >> 4) & 1], (tile - 2 - begin) & (tile - 1), 1)
    lane = lane_iota(cells.shape)
    return jnp.where((lane < 2) | (lane >= tile - 2), cells, 0.0)


def rim_kernel(widths, second, first, rims, edge, far, near):
    width = widths[lax.axis_index("gx")]
    _, _, channels, tile = rims.shape
    even = is_even("gy")
    one, two = first[0:channels, :].astype(F32), second[0:channels, :].astype(F32)
    right = jnp.where(even, one, two)
    left = jnp.where(even, two, one)
    on_left = (lane_iota((channels, tile)) & 2) != 0
    edge[0] = jnp.where(on_left, pltpu.roll(left, 2, 1), pltpu.roll(right, tile - 2, 1))
    edge[1] = jnp.where(on_left, left, right)
    even = is_even("gx")
    for z in range(ZOUT):
        for r in range(2):
            to_lower = rims[z, r] + edge_term(edge, z, r - 2)
            to_upper = rims[z, 2 + r] + edge_term(edge, z, width + r)
            at = slice((2 * z + r) * channels, (2 * z + r + 1) * channels)
            near[at, :] = jnp.where(even, to_upper, to_lower).astype(BF16)
            far[at, :] = jnp.where(even, to_lower, to_upper).astype(BF16)


def slab_start(widths):
    slab = lax.axis_index("gx")
    start = jnp.int32(0)
    for d in range(widths.shape[0]):
        start = start + jnp.where(d < slab, widths[d], 0)
    return start


def depth_row(weights, depths, edge, z, x):
    own = jnp.concatenate([depth[z, x] for depth in depths], axis=0)
    return own + weights[DW_BIAS] + edge_term(edge, z, x)


def base_row(cells, lifted, phase, z, x):
    channels = lifted.shape[1]
    slots = cells.shape[1] // channels
    return cells[2 + z, pl.ds(x, channels, stride=slots), :] + lifted[lax.div(phase + x, CF)]


def active(weights, mixed):
    mixed = mixed + weights[PW_BIAS]
    return jnp.maximum(mixed, 0.2 * mixed)


def mix_kernel(gathered, widths, mix, cells, weights, depth, edge, *refs):
    if gathered:
        coarse, value, ends, bases, mixer, rest, lifted, across = refs
        parts, ncx, ncy = coarse.shape
    else:
        second, first, own_block, opposite, value, ends, bases, mixer, rest, lifted, across, blocks = refs
        parts, own_rows, ncy = own_block.shape
        ncx = 4 * own_rows
    width = widths[lax.axis_index("gx")]
    here = lax.axis_index("gy")
    start = slab_start(widths)
    phase = lax.rem(start, CF)
    channels, tile = weights.shape[1:]
    slots = cells.shape[1] // channels

    def convolve(b, carry):
        convolve_block(cells, weights, rest, b, SPLIT)
        return carry

    lax.fori_loop(SPLIT, channels // ROWS, convolve, 0)

    if not gathered:
        even = is_even("gy")
        after, before = lax.rem(here + 1, 4), lax.rem(here + 3, 4)
        count = parts * own_rows
        for message, owner in (
            (first, jnp.where(even, after, before)),
            (second, jnp.where(even, before, after)),
        ):
            terms = message[channels:, :].astype(F32)[0:count, :]
            sums = terms[:, 0:ncy] + terms[:, ncy : 2 * ncy] + terms[:, 2 * ncy : 3 * ncy]
            for k in range(parts):
                blocks[k, pl.ds(owner * own_rows, own_rows), :] = sums[k * own_rows : (k + 1) * own_rows]
        for block, owner in ((own_block, here), (opposite, lax.rem(here + 2, 4))):
            for k in range(parts):
                blocks[k, pl.ds(owner * own_rows, own_rows), :] = block[k]
    shape = (ncy, tile)
    cell = row_iota(shape) * CF
    place = lane_iota(shape) + here * tile
    along_y = ((place >= cell) & (place < cell + CF)).astype(F32)
    for k in range(parts):
        block = coarse[k] if gathered else blocks[k]
        across[k] = jnp.dot(block, along_y, precision=lax.Precision.HIGHEST, preferred_element_type=F32)
    for i in range(3):
        cell = lax.rem(lax.div(start, CF) + i, ncx)
        total = None
        for k in range(parts):
            term = weights[LIFT + k] * across[k, pl.ds(cell, 1), :]
            total = term if total is None else total + term
        lifted[i] = total

    group = 4
    wide = jnp.concatenate([mix[...]] * group, axis=1)
    wide = jnp.concatenate([wide] * group, axis=0)
    size = group * channels
    row, column = row_iota((size, size)), lane_iota((size, size))
    same = sum(
        ((row >= i * channels) & (row < (i + 1) * channels) & (column >= i * channels) & (column < (i + 1) * channels)).astype(F32)
        for i in range(group)
    )
    mixer[...] = jnp.where(same > 0, wide.astype(F32), 0.0).astype(BF16)

    for x in range(0, slots, group):
        depths = [
            jnp.concatenate([depth_row(weights, (depth, rest), edge, z, x + i) for i in range(group)], axis=0).astype(BF16)
            for z in range(ZOUT)
        ]
        mixed = jnp.dot(mixer[...], jnp.concatenate(depths, axis=1), preferred_element_type=F32)
        for i in range(group):
            for z in range(ZOUT):
                part = mixed[i * channels : (i + 1) * channels, z * tile : (z + 1) * tile]
                part = active(weights, part) + base_row(cells, lifted, phase, z, x + i)
                value[z, pl.ds(x + i, channels, stride=slots), :] = jnp.where(x + i < width, part, 0.0)
    for z in range(ZOUT):
        for i, x in enumerate((0, 1, width - 2, width - 1)):
            ends[z, i * channels : (i + 1) * channels, :] = depth_row(weights, (depth, rest), edge, z, x)
            bases[z, i * channels : (i + 1) * channels, :] = base_row(cells, lifted, phase, z, x)


def finish_kernel(widths, weights, ends, bases, mixer, far, near, value_in, out, value, block, sems):
    width = widths[lax.axis_index("gx")]
    channels = weights.shape[1]
    slots = block.shape[2]
    even = is_even("gx")
    half = 2 * channels
    copies = []
    for z in range(ZOUT):
        at = slice(z * half, (z + 1) * half)
        one, two = far[at, :].astype(F32), near[at, :].astype(F32)
        arrived = jnp.concatenate([jnp.where(even, one, two), jnp.where(even, two, one)], axis=0)
        mixed = jnp.dot(mixer[...], (ends[z] + arrived).astype(BF16), preferred_element_type=F32)
        for i, x in enumerate((0, 1, width - 2, width - 1)):
            at = slice(i * channels, (i + 1) * channels)
            value[z, pl.ds(x, channels, stride=slots), :] = active(weights, mixed[at, :]) + bases[z, at, :]
        for part in range(channels // CHUNK):
            for o in range(part * CHUNK, (part + 1) * CHUNK):
                block[z, o] = value[z, o * slots : (o + 1) * slots, :].astype(BF16)
            part_of = pl.ds(part * CHUNK, CHUNK)
            copy = pltpu.make_async_copy(block.at[z, part_of], out.at[z, part_of], sems.at[part, z])
            copy.start()
            copies.append(copy)
    for copy in copies:
        copy.wait()


def shards(feature, widths, dw_weight, dw_bias, pw_weight, pw_bias, lift_weight, coarse):
    planes, channels, slots, tile = feature.shape
    ny = lax.axis_size("gy")
    parts, own_rows, ncy = coarse.shape
    gathered = ny != 4
    ncx = ny * own_rows
    smem = pl.BlockSpec(memory_space=pltpu.SMEM)
    vmem = pl.BlockSpec(memory_space=pltpu.VMEM)
    hbm = pl.BlockSpec(memory_space=pltpu.HBM)
    params = pltpu.CompilerParams(vmem_limit_bytes=VMEM_BYTES)
    shape = jax.ShapeDtypeStruct
    strip = shape((channels + 16, tile), BF16)
    cells_shape = pltpu.VMEM((planes, channels * slots, tile), F32)
    value_shape = pltpu.VMEM((ZOUT, channels * slots, tile), F32)
    message = shape((2 * ZOUT * channels, tile), BF16)

    def swapped(array, axis, first):
        count = lax.axis_size(axis)
        pairs = []
        for i in range(first, count + first, 2):
            a, b = i % count, (i + 1) % count
            pairs += [(a, b), (b, a)]
        return lax.ppermute(array, axis, pairs)

    def pinned(array):
        return pltpu.with_memory_space_constraint(array, pltpu.HBM)

    if gathered:
        every = lax.all_gather(coarse, "gy", axis=1, tiled=True)
    small = (
        widths,
        dw_weight,
        dw_bias.reshape(1, channels),
        pw_bias.reshape(1, channels),
        lift_weight.T,
        coarse,
    )
    cells, weights, first, second, block, slab_widths = pl.pallas_call(
        pack_kernel,
        out_shape=(
            cells_shape,
            pltpu.VMEM((32, channels, tile), F32),
            strip,
            strip,
            pltpu.VMEM(coarse.shape, F32),
            pltpu.SMEM(widths.shape, jnp.int32),
        ),
        in_specs=[hbm] * 7,
        out_specs=(vmem,) * 5 + (smem,),
        scratch_shapes=[
            pltpu.VMEM(feature.shape, BF16),
            pltpu.SMEM(widths.shape, jnp.int32),
            pltpu.VMEM(dw_weight.shape, F32),
            pltpu.VMEM((1, channels), F32),
            pltpu.VMEM((1, channels), F32),
            pltpu.VMEM((parts, channels), F32),
            pltpu.VMEM(coarse.shape, F32),
            pltpu.VMEM((32, channels), F32),
            pltpu.VMEM((16, tile), F32),
            pltpu.VMEM((3, 2, channels, tile), F32),
            pltpu.SemaphoreType.DMA((channels // CHUNK,)),
            pltpu.SemaphoreType.DMA((len(small),)),
        ],
        compiler_params=params,
    )(pinned(feature), *(pinned(array) for array in small))
    second = swapped(second, "gy", 1)
    first = swapped(first, "gy", 0)
    early = SPLIT * ROWS
    cells, depth, rims, own_block = pl.pallas_call(
        conv_kernel,
        out_shape=(
            cells_shape,
            pltpu.VMEM((ZOUT, slots, early, tile), F32),
            pltpu.VMEM((ZOUT, 4, channels, tile), F32),
            pltpu.VMEM(coarse.shape, F32),
        ),
        in_specs=[smem] + [vmem] * 3,
        out_specs=(vmem,) * 4,
        input_output_aliases={3: 0},
        compiler_params=params,
        cost_estimate=pl.CostEstimate(flops=10**9, bytes_accessed=10**6, transcendentals=0),
    )(slab_widths, weights, block, cells)
    if not gathered:
        opposite = lax.ppermute(own_block, "gy", [(i, (i + 2) % 4) for i in range(4)])
    edge, far, near = pl.pallas_call(
        rim_kernel,
        out_shape=(pltpu.VMEM((2, channels, tile), F32), message, message),
        in_specs=[smem] + [vmem] * 3,
        out_specs=(vmem,) * 3,
        compiler_params=params,
    )(slab_widths, second, first, rims)
    far = swapped(far, "gx", 1)
    near = swapped(near, "gx", 0)
    blocks = (every,) if gathered else (second, first, own_block, opposite)
    ends_shape = pltpu.VMEM((ZOUT, 4 * channels, tile), F32)
    value, ends, bases, mixer = pl.pallas_call(
        functools.partial(mix_kernel, gathered),
        out_shape=(value_shape, ends_shape, ends_shape, pltpu.VMEM((4 * channels, 4 * channels), BF16)),
        in_specs=[smem] + [vmem] * (5 + len(blocks)),
        out_specs=(vmem,) * 4,
        scratch_shapes=[
            pltpu.VMEM((ZOUT, slots, channels - early, tile), F32),
            pltpu.VMEM((3, channels, tile), F32),
            pltpu.VMEM((parts, ncx, tile), F32),
        ]
        + ([] if gathered else [pltpu.VMEM((parts, ncx, ncy), F32)]),
        compiler_params=params,
        cost_estimate=pl.CostEstimate(flops=10**9, bytes_accessed=10**6, transcendentals=0),
    )(slab_widths, pw_weight, cells, weights, depth, edge, *blocks)
    out, _ = pl.pallas_call(
        finish_kernel,
        out_shape=(shape((ZOUT, channels, slots, tile), BF16), value_shape),
        in_specs=[smem] + [vmem] * 7,
        out_specs=(hbm, vmem),
        scratch_shapes=[
            pltpu.VMEM((ZOUT, channels, slots, tile), BF16),
            pltpu.SemaphoreType.DMA((channels // CHUNK, ZOUT)),
        ],
        input_output_aliases={7: 1},
        compiler_params=params,
    )(slab_widths, weights, ends, bases, mixer, far, near, value)
    return out


def solution(mesh):
    placed = (P(None, None, "gx", "gy"), P(), P(), P(), P(), P(), P(), P(None, "gy", None))
    return jax.shard_map(
        shards, mesh=mesh, in_specs=placed, out_specs=P(None, None, "gx", "gy"), check_vma=False
    )
```

```python
import functools

import jax
import jax.numpy as jnp
from jax import lax
from jax.experimental import pallas as pl
from jax.experimental.pallas import tpu as pltpu
from jax.sharding import PartitionSpec as P

XW = 16
ZOUT = 2
CF = 16
ROWS = 8
SPLIT = 5
CHUNK = 16
DW_BIAS, PW_BIAS, LIFT = 27, 28, 29
F32 = jnp.float32
BF16 = jnp.bfloat16
VMEM_BYTES = 14 * 1024 * 1024


def lane_iota(shape):
    return lax.broadcasted_iota(jnp.int32, shape, len(shape) - 1)


def row_iota(shape):
    return lax.broadcasted_iota(jnp.int32, shape, len(shape) - 2)


def tap_of(m, dx, dy):
    return 9 * m + 3 * (dx + 1) + (dy + 1)


def is_even(axis):
    return lax.rem(lax.axis_index(axis), 2) == 0


def pack_kernel(
    feature, widths_in, taps_in, dw_bias_in, pw_bias_in, lift_in, coarse_in,
    cells, weights, first, second, own_block, widths,
    planes, widths_here, taps, dw_bias, pw_bias, lift, coarse, stacked, tail, picked, sems, small_sems,
):
    count, channels, slots, tile = feature.shape
    chunks = range(0, channels, CHUNK)

    def copy_of(m):
        at = pl.ds(ZOUT * m, ZOUT)
        return pltpu.make_async_copy(feature.at[at], planes.at[at], sems.at[m])

    small = [
        pltpu.make_async_copy(source, target, small_sems.at[i])
        for i, (source, target) in enumerate(
            (
                (widths_in, widths_here),
                (taps_in, taps),
                (dw_bias_in, dw_bias),
                (pw_bias_in, pw_bias),
                (lift_in, lift),
                (coarse_in, coarse),
            )
        )
    ]
    for copy in small:
        copy.start()
    for m in range(3):
        copy_of(m).start()
    for copy in small:
        copy.wait()
    for d in range(widths.shape[0]):
        widths[d] = widths_here[d]
    width = widths_here[lax.axis_index("gx")]
    stacked[0:DW_BIAS, :] = taps[...]
    stacked[DW_BIAS : DW_BIAS + 1, :] = dw_bias[...]
    stacked[PW_BIAS : PW_BIAS + 1, :] = pw_bias[...]
    stacked[LIFT : LIFT + 3, :] = lift[...]

    own_block[...] = coarse[...]
    parts, own_rows, ncy = coarse.shape
    tail[...] = jnp.zeros_like(tail)
    if 3 * ncy <= tile:
        for k in range(parts):
            rest = coarse[k]
            for p in range(3):
                term = rest.astype(BF16).astype(F32)
                rest = rest - term
                tail[k * own_rows : (k + 1) * own_rows, p * ncy : (p + 1) * ncy] = term
    for message in (first, second):
        message[channels:, :] = tail[...].astype(BF16)

    row, along = row_iota((taps.shape[0], tile)), lane_iota((taps.shape[0], tile))
    by_side = jnp.where((along & 2) != 0, 2, 0)
    terms, rest = [], taps[...]
    for _ in range(3):
        terms.append(rest.astype(BF16))
        rest = rest - terms[-1].astype(F32)
    chosen = jnp.concatenate(
        [(row == tap_of(m, dx, -1) + by_side).astype(BF16) for m in range(3) for dx in (-1, 0, 1)], axis=1
    )
    scale = sum(lax.dot_general(term, chosen, (((0,), (0,)), ((), ())), preferred_element_type=F32) for term in terms)
    turned = jnp.transpose(stacked[...])
    for t in range(stacked.shape[0]):
        weights[t] = jnp.broadcast_to(turned[:, t : t + 1], (channels, tile))

    lane, row = lane_iota((slots, tile)), row_iota((slots, tile))
    mine = (lane >> 3) == (row & 15)
    in_even, in_odd = mine & ((lane & 4) == 0), mine & ((lane & 4) != 0)
    shape = (2 * CHUNK, CHUNK * slots)
    row, column = row_iota(shape), lane_iota(shape)
    begin = (row & (CHUNK - 1)) * slots
    low = jnp.where(row < CHUNK, begin, begin + 16)
    high = jnp.where(row < CHUNK, begin + 16, begin + slots)
    gather = ((column >= low) & (column < high)).astype(BF16)
    shape = (CHUNK, tile)
    for m in range(3):
        copy_of(m).wait()
        for c in chunks:
            rows = []
            for k in range(c, c + CHUNK):
                both = []
                for z in range(ZOUT):
                    plane = planes[ZOUT * m + z, k].astype(F32)
                    cells[ZOUT * m + z, k * slots : (k + 1) * slots, :] = plane
                    both.append(
                        jnp.concatenate(
                            [
                                pltpu.roll(plane[x : x + ROWS], (2 + 4 * z + 8 * x) % tile, 1, stride=8, stride_axis=0)
                                for x in range(0, slots, ROWS)
                            ],
                            axis=0,
                        )
                    )
                rows.append(jnp.where(in_even, both[0], jnp.where(in_odd, both[1], 0.0)))
            sums = jnp.dot(gather, jnp.concatenate(rows, axis=0).astype(BF16), preferred_element_type=F32)
            for half in range(2):
                inside = 16 * half + (lane_iota(shape) >> 3) < width
                part = sums[half * CHUNK : (half + 1) * CHUNK, :]
                picked[m, half, c : c + CHUNK, :] = jnp.where(inside, part, 0.0)

    shape = (channels, tile)
    lane = lane_iota(shape)
    on_left = (lane & 2) != 0
    packed = [None, None]
    for m in range(3):
        low, high = picked[m, 0], picked[m, 1]
        moved = {
            -1: tuple(
                pltpu.roll(jnp.where(lane < tile - 16, one, two), 16, 1) for one, two in ((low, high), (high, low))
            ),
            0: (low, high),
            1: tuple(
                pltpu.roll(jnp.where(lane >= 16, one, two), tile - 16, 1) for one, two in ((low, high), (high, low))
            ),
        }
        for dx in (-1, 0, 1):
            begin = (3 * m + dx + 1) * tile
            for half in range(2):
                term = scale[:, begin : begin + tile] * moved[dx][half]
                packed[half] = term if packed[half] is None else packed[half] + term
    left = jnp.where(on_left, packed[0], pltpu.roll(packed[1], tile - 2, 1))
    right = jnp.where(on_left, pltpu.roll(packed[1], 2, 1), packed[0])
    even = is_even("gy")
    first[0:channels, :] = jnp.where(even, right, left).astype(BF16)
    second[0:channels, :] = jnp.where(even, left, right).astype(BF16)


def shifted_sum(before, centre, after):
    lane = lane_iota(centre.shape)
    tile = centre.shape[-1]
    before = jnp.where(lane < 2, 0.0, pltpu.roll(before, 2, 1))
    after = jnp.where(lane >= tile - 2, 0.0, pltpu.roll(after, tile - 2, 1))
    return centre + before + after


def convolve_block(cells, weights, depth, b, first_block):
    channels = weights.shape[1]
    slots = cells.shape[1] // channels
    at = pl.ds(pl.multiple_of(b * ROWS, ROWS), ROWS)
    to = pl.ds(pl.multiple_of((b - first_block) * ROWS, ROWS), ROWS)
    tap = [weights[t, at, :] for t in range(27)]
    for z in range(ZOUT):
        for parity in range(2):
            sums = {}
            for x in range(parity, slots, 2):
                rows = [cells[z + ZOUT * m, pl.ds(b * (ROWS * slots) + x, ROWS, stride=slots), :] for m in range(3)]
                for m in range(3):
                    for dx in (1, 0, -1):
                        out = x - 2 * dx
                        if 0 <= out < slots:
                            for dy in (-1, 0, 1):
                                term = tap[tap_of(m, dx, dy)] * rows[m]
                                key = (out, dy)
                                sums[key] = sums[key] + term if key in sums else term
                for out in [x - 2] if x + 2 < slots else [x - 2, x]:
                    if out >= 0:
                        depth[z, out, to, :] = shifted_sum(*(sums.pop((out, dy)) for dy in (-1, 0, 1)))


def conv_kernel(widths, weights, coarse, cells_in, cells, depth, rims, own_block):
    width = widths[lax.axis_index("gx")]
    channels, tile = weights.shape[1:]
    slots = cells.shape[1] // channels
    own_block[...] = coarse[...]
    for r in range(2):

        @pl.when(width + r < slots)
        def _():
            for z in range(cells.shape[0]):
                cells[z, pl.ds(width + r, channels, stride=slots), :] = jnp.zeros((channels, tile), F32)

    for b in range(channels // ROWS):
        at = slice(b * ROWS, (b + 1) * ROWS)
        for side, dx in enumerate((1, -1)):
            tap = [[weights[tap_of(m, dx, dy), at, :] for m in range(3)] for dy in (-1, 0, 1)]
            for r in range(2):
                x = r if side == 0 else width - 2 + r
                for z in range(ZOUT):
                    rows = [
                        cells[z + ZOUT * m, pl.ds(b * (ROWS * slots) + x, ROWS, stride=slots), :] for m in range(3)
                    ]
                    parts = [sum(weight * row for weight, row in zip(weights_of, rows)) for weights_of in tap]
                    rims[z, 2 * side + r, at, :] = shifted_sum(*parts)

    def convolve(b, carry):
        convolve_block(cells, weights, depth, b, 0)
        return carry

    lax.fori_loop(0, SPLIT, convolve, 0)


def edge_term(edge, z, x):
    tile = edge.shape[2]
    begin = 8 * (x & 15) + 4 * z
    cells = pltpu.roll(edge[(x >> 4) & 1], (tile - 2 - begin) & (tile - 1), 1)
    lane = lane_iota(cells.shape)
    return jnp.where((lane < 2) | (lane >= tile - 2), cells, 0.0)


def rim_kernel(widths, second, first, rims, edge, far, near):
    width = widths[lax.axis_index("gx")]
    _, _, channels, tile = rims.shape
    even = is_even("gy")
    one, two = first[0:channels, :].astype(F32), second[0:channels, :].astype(F32)
    right = jnp.where(even, one, two)
    left = jnp.where(even, two, one)
    on_left = (lane_iota((channels, tile)) & 2) != 0
    edge[0] = jnp.where(on_left, pltpu.roll(left, 2, 1), pltpu.roll(right, tile - 2, 1))
    edge[1] = jnp.where(on_left, left, right)
    even = is_even("gx")
    for z in range(ZOUT):
        for r in range(2):
            to_lower = rims[z, r] + edge_term(edge, z, r - 2)
            to_upper = rims[z, 2 + r] + edge_term(edge, z, width + r)
            at = slice((2 * z + r) * channels, (2 * z + r + 1) * channels)
            near[at, :] = jnp.where(even, to_upper, to_lower).astype(BF16)
            far[at, :] = jnp.where(even, to_lower, to_upper).astype(BF16)


def slab_start(widths):
    slab = lax.axis_index("gx")
    start = jnp.int32(0)
    for d in range(widths.shape[0]):
        start = start + jnp.where(d < slab, widths[d], 0)
    return start


def depth_row(weights, depths, edge, z, x):
    own = jnp.concatenate([depth[z, x] for depth in depths], axis=0)
    return own + weights[DW_BIAS] + edge_term(edge, z, x)


def base_row(cells, lifted, phase, z, x):
    channels = lifted.shape[1]
    slots = cells.shape[1] // channels
    return cells[2 + z, pl.ds(x, channels, stride=slots), :] + lifted[lax.div(phase + x, CF)]


def active(weights, mixed):
    mixed = mixed + weights[PW_BIAS]
    return jnp.maximum(mixed, 0.2 * mixed)


def mix_kernel(gathered, widths, mix, cells, weights, depth, edge, *refs):
    if gathered:
        coarse, value, ends, bases, mixer, rest, lifted, across = refs
        parts, ncx, ncy = coarse.shape
    else:
        second, first, own_block, opposite, value, ends, bases, mixer, rest, lifted, across, blocks = refs
        parts, own_rows, ncy = own_block.shape
        ncx = 4 * own_rows
    width = widths[lax.axis_index("gx")]
    here = lax.axis_index("gy")
    start = slab_start(widths)
    phase = lax.rem(start, CF)
    channels, tile = weights.shape[1:]
    slots = cells.shape[1] // channels

    def convolve(b, carry):
        convolve_block(cells, weights, rest, b, SPLIT)
        return carry

    lax.fori_loop(SPLIT, channels // ROWS, convolve, 0)

    if not gathered:
        even = is_even("gy")
        after, before = lax.rem(here + 1, 4), lax.rem(here + 3, 4)
        count = parts * own_rows
        for message, owner in (
            (first, jnp.where(even, after, before)),
            (second, jnp.where(even, before, after)),
        ):
            terms = message[channels:, :].astype(F32)[0:count, :]
            sums = terms[:, 0:ncy] + terms[:, ncy : 2 * ncy] + terms[:, 2 * ncy : 3 * ncy]
            for k in range(parts):
                blocks[k, pl.ds(owner * own_rows, own_rows), :] = sums[k * own_rows : (k + 1) * own_rows]
        for block, owner in ((own_block, here), (opposite, lax.rem(here + 2, 4))):
            for k in range(parts):
                blocks[k, pl.ds(owner * own_rows, own_rows), :] = block[k]
    shape = (ncy, tile)
    cell = row_iota(shape) * CF
    place = lane_iota(shape) + here * tile
    along_y = ((place >= cell) & (place < cell + CF)).astype(F32)
    for k in range(parts):
        block = coarse[k] if gathered else blocks[k]
        across[k] = jnp.dot(block, along_y, precision=lax.Precision.HIGHEST, preferred_element_type=F32)
    for i in range(3):
        cell = lax.rem(lax.div(start, CF) + i, ncx)
        total = None
        for k in range(parts):
            term = weights[LIFT + k] * across[k, pl.ds(cell, 1), :]
            total = term if total is None else total + term
        lifted[i] = total

    group = 4
    wide = jnp.concatenate([mix[...]] * group, axis=1)
    wide = jnp.concatenate([wide] * group, axis=0)
    size = group * channels
    row, column = row_iota((size, size)), lane_iota((size, size))
    same = sum(
        ((row >= i * channels) & (row < (i + 1) * channels) & (column >= i * channels) & (column < (i + 1) * channels)).astype(F32)
        for i in range(group)
    )
    mixer[...] = jnp.where(same > 0, wide.astype(F32), 0.0).astype(BF16)

    for x in range(0, slots, group):
        depths = [
            jnp.concatenate([depth_row(weights, (depth, rest), edge, z, x + i) for i in range(group)], axis=0).astype(BF16)
            for z in range(ZOUT)
        ]
        mixed = jnp.dot(mixer[...], jnp.concatenate(depths, axis=1), preferred_element_type=F32)
        for i in range(group):
            for z in range(ZOUT):
                part = mixed[i * channels : (i + 1) * channels, z * tile : (z + 1) * tile]
                part = active(weights, part) + base_row(cells, lifted, phase, z, x + i)
                value[z, pl.ds(x + i, channels, stride=slots), :] = jnp.where(x + i < width, part, 0.0)
    for z in range(ZOUT):
        for i, x in enumerate((0, 1, width - 2, width - 1)):
            ends[z, i * channels : (i + 1) * channels, :] = depth_row(weights, (depth, rest), edge, z, x)
            bases[z, i * channels : (i + 1) * channels, :] = base_row(cells, lifted, phase, z, x)


def finish_kernel(widths, weights, ends, bases, mixer, far, near, value_in, out, value, block, sems):
    width = widths[lax.axis_index("gx")]
    channels = weights.shape[1]
    slots = block.shape[2]
    even = is_even("gx")
    half = 2 * channels
    copies = []
    for z in range(ZOUT):
        at = slice(z * half, (z + 1) * half)
        one, two = far[at, :].astype(F32), near[at, :].astype(F32)
        arrived = jnp.concatenate([jnp.where(even, one, two), jnp.where(even, two, one)], axis=0)
        mixed = jnp.dot(mixer[...], (ends[z] + arrived).astype(BF16), preferred_element_type=F32)
        for i, x in enumerate((0, 1, width - 2, width - 1)):
            at = slice(i * channels, (i + 1) * channels)
            value[z, pl.ds(x, channels, stride=slots), :] = active(weights, mixed[at, :]) + bases[z, at, :]
        for part in range(channels // CHUNK):
            for o in range(part * CHUNK, (part + 1) * CHUNK):
                block[z, o] = value[z, o * slots : (o + 1) * slots, :].astype(BF16)
            part_of = pl.ds(part * CHUNK, CHUNK)
            copy = pltpu.make_async_copy(block.at[z, part_of], out.at[z, part_of], sems.at[part, z])
            copy.start()
            copies.append(copy)
    for copy in copies:
        copy.wait()


def shards(feature, widths, dw_weight, dw_bias, pw_weight, pw_bias, lift_weight, coarse):
    planes, channels, slots, tile = feature.shape
    ny = lax.axis_size("gy")
    parts, own_rows, ncy = coarse.shape
    gathered = ny != 4
    ncx = ny * own_rows
    smem = pl.BlockSpec(memory_space=pltpu.SMEM)
    vmem = pl.BlockSpec(memory_space=pltpu.VMEM)
    hbm = pl.BlockSpec(memory_space=pltpu.HBM)
    params = pltpu.CompilerParams(vmem_limit_bytes=VMEM_BYTES)
    shape = jax.ShapeDtypeStruct
    strip = shape((channels + 16, tile), BF16)
    cells_shape = pltpu.VMEM((planes, channels * slots, tile), F32)
    value_shape = pltpu.VMEM((ZOUT, channels * slots, tile), F32)
    message = shape((2 * ZOUT * channels, tile), BF16)

    def swapped(array, axis, first):
        count = lax.axis_size(axis)
        pairs = []
        for i in range(first, count + first, 2):
            a, b = i % count, (i + 1) % count
            pairs += [(a, b), (b, a)]
        return lax.ppermute(array, axis, pairs)

    def pinned(array):
        return pltpu.with_memory_space_constraint(array, pltpu.HBM)

    if gathered:
        every = lax.all_gather(coarse, "gy", axis=1, tiled=True)
    small = (
        widths,
        dw_weight,
        dw_bias.reshape(1, channels),
        pw_bias.reshape(1, channels),
        lift_weight.T,
        coarse,
    )
    cells, weights, first, second, block, slab_widths = pl.pallas_call(
        pack_kernel,
        out_shape=(
            cells_shape,
            pltpu.VMEM((32, channels, tile), F32),
            strip,
            strip,
            pltpu.VMEM(coarse.shape, F32),
            pltpu.SMEM(widths.shape, jnp.int32),
        ),
        in_specs=[hbm] * 7,
        out_specs=(vmem,) * 5 + (smem,),
        scratch_shapes=[
            pltpu.VMEM(feature.shape, BF16),
            pltpu.SMEM(widths.shape, jnp.int32),
            pltpu.VMEM(dw_weight.shape, F32),
            pltpu.VMEM((1, channels), F32),
            pltpu.VMEM((1, channels), F32),
            pltpu.VMEM((parts, channels), F32),
            pltpu.VMEM(coarse.shape, F32),
            pltpu.VMEM((32, channels), F32),
            pltpu.VMEM((16, tile), F32),
            pltpu.VMEM((3, 2, channels, tile), F32),
            pltpu.SemaphoreType.DMA((3,)),
            pltpu.SemaphoreType.DMA((len(small),)),
        ],
        compiler_params=params,
    )(pinned(feature), *(pinned(array) for array in small))
    second = swapped(second, "gy", 1)
    first = swapped(first, "gy", 0)
    early = SPLIT * ROWS
    cells, depth, rims, own_block = pl.pallas_call(
        conv_kernel,
        out_shape=(
            cells_shape,
            pltpu.VMEM((ZOUT, slots, early, tile), F32),
            pltpu.VMEM((ZOUT, 4, channels, tile), F32),
            pltpu.VMEM(coarse.shape, F32),
        ),
        in_specs=[smem] + [vmem] * 3,
        out_specs=(vmem,) * 4,
        input_output_aliases={3: 0},
        compiler_params=params,
        cost_estimate=pl.CostEstimate(flops=10**9, bytes_accessed=10**6, transcendentals=0),
    )(slab_widths, weights, block, cells)
    if not gathered:
        opposite = lax.ppermute(own_block, "gy", [(i, (i + 2) % 4) for i in range(4)])
    edge, far, near = pl.pallas_call(
        rim_kernel,
        out_shape=(pltpu.VMEM((2, channels, tile), F32), message, message),
        in_specs=[smem] + [vmem] * 3,
        out_specs=(vmem,) * 3,
        compiler_params=params,
    )(slab_widths, second, first, rims)
    far = swapped(far, "gx", 1)
    near = swapped(near, "gx", 0)
    blocks = (every,) if gathered else (second, first, own_block, opposite)
    ends_shape = pltpu.VMEM((ZOUT, 4 * channels, tile), F32)
    value, ends, bases, mixer = pl.pallas_call(
        functools.partial(mix_kernel, gathered),
        out_shape=(value_shape, ends_shape, ends_shape, pltpu.VMEM((4 * channels, 4 * channels), BF16)),
        in_specs=[smem] + [vmem] * (5 + len(blocks)),
        out_specs=(vmem,) * 4,
        scratch_shapes=[
            pltpu.VMEM((ZOUT, slots, channels - early, tile), F32),
            pltpu.VMEM((3, channels, tile), F32),
            pltpu.VMEM((parts, ncx, tile), F32),
        ]
        + ([] if gathered else [pltpu.VMEM((parts, ncx, ncy), F32)]),
        compiler_params=params,
        cost_estimate=pl.CostEstimate(flops=10**9, bytes_accessed=10**6, transcendentals=0),
    )(slab_widths, pw_weight, cells, weights, depth, edge, *blocks)
    out, _ = pl.pallas_call(
        finish_kernel,
        out_shape=(shape((ZOUT, channels, slots, tile), BF16), value_shape),
        in_specs=[smem] + [vmem] * 7,
        out_specs=(hbm, vmem),
        scratch_shapes=[
            pltpu.VMEM((ZOUT, channels, slots, tile), BF16),
            pltpu.SemaphoreType.DMA((channels // CHUNK, ZOUT)),
        ],
        input_output_aliases={7: 1},
        compiler_params=params,
    )(slab_widths, weights, ends, bases, mixer, far, near, value)
    return out


def solution(mesh):
    placed = (P(None, None, "gx", "gy"), P(), P(), P(), P(), P(), P(), P(None, "gy", None))
    return jax.shard_map(
        shards, mesh=mesh, in_specs=placed, out_specs=P(None, None, "gx", "gy"), check_vma=False
    )
```

```python
import functools

import jax
import jax.numpy as jnp
from jax import lax
from jax.experimental import pallas as pl
from jax.experimental.pallas import tpu as pltpu
from jax.sharding import PartitionSpec as P

XW = 16
ZOUT = 2
CF = 16
ROWS = 8
SPLIT = 5
CHUNK = 16
DW_BIAS, PW_BIAS, LIFT = 27, 28, 29
F32 = jnp.float32
BF16 = jnp.bfloat16
VMEM_BYTES = 14 * 1024 * 1024


def lane_iota(shape):
    return lax.broadcasted_iota(jnp.int32, shape, len(shape) - 1)


def row_iota(shape):
    return lax.broadcasted_iota(jnp.int32, shape, len(shape) - 2)


def tap_of(m, dx, dy):
    return 9 * m + 3 * (dx + 1) + (dy + 1)


def is_even(axis):
    return lax.rem(lax.axis_index(axis), 2) == 0


def pack_kernel(
    feature, widths_in, taps_in, dw_bias_in, pw_bias_in, lift_in, coarse_in,
    cells, first, second, stacked, own_block, widths,
    planes, widths_here, taps, dw_bias, pw_bias, lift, coarse, tail, picked, sems, small_sems,
):
    count, channels, slots, tile = feature.shape

    def copy_of(m):
        at = pl.ds(ZOUT * m, ZOUT)
        return pltpu.make_async_copy(feature.at[at], planes.at[at], sems.at[m])

    small = [
        pltpu.make_async_copy(source, target, small_sems.at[i])
        for i, (source, target) in enumerate(
            (
                (widths_in, widths_here),
                (taps_in, taps),
                (dw_bias_in, dw_bias),
                (pw_bias_in, pw_bias),
                (lift_in, lift),
                (coarse_in, coarse),
            )
        )
    ]
    for copy in small:
        copy.start()
    for m in range(3):
        copy_of(m).start()
    def weights_by_lane():
        for copy in small:
            copy.wait()
        for d in range(widths.shape[0]):
            widths[d] = widths_here[d]
        stacked[0:DW_BIAS, :] = taps[...]
        stacked[DW_BIAS : DW_BIAS + 1, :] = dw_bias[...]
        stacked[PW_BIAS : PW_BIAS + 1, :] = pw_bias[...]
        stacked[LIFT : LIFT + 3, :] = lift[...]

        own_block[...] = coarse[...]
        parts, own_rows, ncy = coarse.shape
        tail[...] = jnp.zeros_like(tail)
        if 3 * ncy <= tile:
            for k in range(parts):
                rest = coarse[k]
                for p in range(3):
                    term = rest.astype(BF16).astype(F32)
                    rest = rest - term
                    tail[k * own_rows : (k + 1) * own_rows, p * ncy : (p + 1) * ncy] = term
        for message in (first, second):
            message[channels:, :] = tail[...].astype(BF16)

        row, along = row_iota((taps.shape[0], tile)), lane_iota((taps.shape[0], tile))
        by_side = jnp.where((along & 2) != 0, 2, 0)
        chosen = jnp.concatenate(
            [(row == tap_of(m, dx, -1) + by_side).astype(BF16) for m in range(3) for dx in (-1, 0, 1)], axis=1
        )
        total, rest = None, taps[...]
        for _ in range(3):
            term = rest.astype(BF16)
            rest = rest - term.astype(F32)
            part = lax.dot_general(term, chosen, (((0,), (0,)), ((), ())), preferred_element_type=F32)
            total = part if total is None else total + part
        return total

    lane, row = lane_iota((slots, tile)), row_iota((slots, tile))
    mine = (lane >> 3) == (row & 15)
    in_even, in_odd = mine & ((lane & 4) == 0), mine & ((lane & 4) != 0)
    sublane = row_iota((ROWS, tile))

    def placed(m, k):
        both = []
        for z in range(ZOUT):
            plane = planes[ZOUT * m + z, k].astype(F32)
            cells[ZOUT * m + z, k * slots : (k + 1) * slots, :] = plane
            both.append(
                jnp.concatenate(
                    [
                        pltpu.roll(plane[x : x + ROWS], (2 + 4 * z + 8 * x) % tile, 1, stride=8, stride_axis=0)
                        for x in range(0, slots, ROWS)
                    ],
                    axis=0,
                )
            )
        rows = jnp.where(in_even, both[0], jnp.where(in_odd, both[1], 0.0))
        return rows[0:ROWS] + rows[ROWS : 2 * ROWS], rows[2 * ROWS :]

    def summed(m, k, step):
        if step == 0:
            return placed(m, k)
        one, two = summed(m, k, step // 2), summed(m, k + step, step // 2)
        turn = (sublane & step) != 0
        return tuple(
            jnp.where(turn, b, a) + pltpu.roll(jnp.where(turn, a, b), step, 0) for a, b in zip(one, two)
        )

    for m in range(3):
        copy_of(m).wait()
        for c in range(0, channels, ROWS):
            for half, part in enumerate(summed(m, c, ROWS // 2)):
                picked[m, half, c : c + ROWS, :] = part
        if m == 0:
            scale = weights_by_lane()
    width = widths_here[lax.axis_index("gx")]

    shape = (channels, tile)
    lane = lane_iota(shape)
    on_left = (lane & 2) != 0
    packed = [None, None]
    for m in range(3):
        low, high = (jnp.where(16 * half + (lane >> 3) < width, picked[m, half], 0.0) for half in range(2))
        moved = {
            -1: tuple(
                pltpu.roll(jnp.where(lane < tile - 16, one, two), 16, 1) for one, two in ((low, high), (high, low))
            ),
            0: (low, high),
            1: tuple(
                pltpu.roll(jnp.where(lane >= 16, one, two), tile - 16, 1) for one, two in ((low, high), (high, low))
            ),
        }
        for dx in (-1, 0, 1):
            begin = (3 * m + dx + 1) * tile
            for half in range(2):
                term = scale[:, begin : begin + tile] * moved[dx][half]
                packed[half] = term if packed[half] is None else packed[half] + term
    left = jnp.where(on_left, packed[0], pltpu.roll(packed[1], tile - 2, 1))
    right = jnp.where(on_left, pltpu.roll(packed[1], 2, 1), packed[0])
    even = is_even("gy")
    first[0:channels, :] = jnp.where(even, right, left).astype(BF16)
    second[0:channels, :] = jnp.where(even, left, right).astype(BF16)


def shifted_sum(before, centre, after):
    lane = lane_iota(centre.shape)
    tile = centre.shape[-1]
    before = jnp.where(lane < 2, 0.0, pltpu.roll(before, 2, 1))
    after = jnp.where(lane >= tile - 2, 0.0, pltpu.roll(after, tile - 2, 1))
    return centre + before + after


def convolve_block(cells, weights, depth, b, first_block):
    channels = weights.shape[1]
    slots = cells.shape[1] // channels
    at = pl.ds(pl.multiple_of(b * ROWS, ROWS), ROWS)
    to = pl.ds(pl.multiple_of((b - first_block) * ROWS, ROWS), ROWS)
    tap = [weights[t, at, :] for t in range(27)]
    for z in range(ZOUT):
        for parity in range(2):
            sums = {}
            for x in range(parity, slots, 2):
                rows = [cells[z + ZOUT * m, pl.ds(b * (ROWS * slots) + x, ROWS, stride=slots), :] for m in range(3)]
                for m in range(3):
                    for dx in (1, 0, -1):
                        out = x - 2 * dx
                        if 0 <= out < slots:
                            for dy in (-1, 0, 1):
                                term = tap[tap_of(m, dx, dy)] * rows[m]
                                key = (out, dy)
                                sums[key] = sums[key] + term if key in sums else term
                for out in [x - 2] if x + 2 < slots else [x - 2, x]:
                    if out >= 0:
                        depth[z, out, to, :] = shifted_sum(*(sums.pop((out, dy)) for dy in (-1, 0, 1)))


def conv_kernel(widths, stacked, coarse, cells_in, cells, weights, depth, rims, own_block):
    width = widths[lax.axis_index("gx")]
    channels, tile = weights.shape[1:]
    slots = cells.shape[1] // channels
    own_block[...] = coarse[...]
    turned = jnp.transpose(stacked[...])
    for t in range(stacked.shape[0]):
        weights[t] = jnp.broadcast_to(turned[:, t : t + 1], (channels, tile))
    for r in range(2):

        @pl.when(width + r < slots)
        def _():
            for z in range(cells.shape[0]):
                cells[z, pl.ds(width + r, channels, stride=slots), :] = jnp.zeros((channels, tile), F32)

    for b in range(channels // ROWS):
        at = slice(b * ROWS, (b + 1) * ROWS)
        for side, dx in enumerate((1, -1)):
            tap = [[weights[tap_of(m, dx, dy), at, :] for m in range(3)] for dy in (-1, 0, 1)]
            for r in range(2):
                x = r if side == 0 else width - 2 + r
                for z in range(ZOUT):
                    rows = [
                        cells[z + ZOUT * m, pl.ds(b * (ROWS * slots) + x, ROWS, stride=slots), :] for m in range(3)
                    ]
                    parts = [sum(weight * row for weight, row in zip(weights_of, rows)) for weights_of in tap]
                    rims[z, 2 * side + r, at, :] = shifted_sum(*parts)

    def convolve(b, carry):
        convolve_block(cells, weights, depth, b, 0)
        return carry

    lax.fori_loop(0, SPLIT, convolve, 0)


def edge_term(edge, z, x):
    tile = edge.shape[2]
    begin = 8 * (x & 15) + 4 * z
    cells = pltpu.roll(edge[(x >> 4) & 1], (tile - 2 - begin) & (tile - 1), 1)
    lane = lane_iota(cells.shape)
    return jnp.where((lane < 2) | (lane >= tile - 2), cells, 0.0)


def rim_kernel(widths, second, first, rims, edge, far, near):
    width = widths[lax.axis_index("gx")]
    _, _, channels, tile = rims.shape
    even = is_even("gy")
    one, two = first[0:channels, :].astype(F32), second[0:channels, :].astype(F32)
    right = jnp.where(even, one, two)
    left = jnp.where(even, two, one)
    on_left = (lane_iota((channels, tile)) & 2) != 0
    edge[0] = jnp.where(on_left, pltpu.roll(left, 2, 1), pltpu.roll(right, tile - 2, 1))
    edge[1] = jnp.where(on_left, left, right)
    even = is_even("gx")
    for z in range(ZOUT):
        for r in range(2):
            to_lower = rims[z, r] + edge_term(edge, z, r - 2)
            to_upper = rims[z, 2 + r] + edge_term(edge, z, width + r)
            at = slice((2 * z + r) * channels, (2 * z + r + 1) * channels)
            near[at, :] = jnp.where(even, to_upper, to_lower).astype(BF16)
            far[at, :] = jnp.where(even, to_lower, to_upper).astype(BF16)


def slab_start(widths):
    slab = lax.axis_index("gx")
    start = jnp.int32(0)
    for d in range(widths.shape[0]):
        start = start + jnp.where(d < slab, widths[d], 0)
    return start


def depth_row(weights, depths, edge, z, x):
    own = jnp.concatenate([depth[z, x] for depth in depths], axis=0)
    return own + weights[DW_BIAS] + edge_term(edge, z, x)


def base_row(cells, lifted, phase, z, x):
    channels = lifted.shape[1]
    slots = cells.shape[1] // channels
    return cells[2 + z, pl.ds(x, channels, stride=slots), :] + lifted[lax.div(phase + x, CF)]


def active(weights, mixed):
    mixed = mixed + weights[PW_BIAS]
    return jnp.maximum(mixed, 0.2 * mixed)


def mix_kernel(gathered, widths, mix, cells, weights, depth, edge, *refs):
    if gathered:
        coarse, value, ends, bases, mixer, rest, lifted, across = refs
        parts, ncx, ncy = coarse.shape
    else:
        second, first, own_block, opposite, value, ends, bases, mixer, rest, lifted, across, blocks = refs
        parts, own_rows, ncy = own_block.shape
        ncx = 4 * own_rows
    width = widths[lax.axis_index("gx")]
    here = lax.axis_index("gy")
    start = slab_start(widths)
    phase = lax.rem(start, CF)
    channels, tile = weights.shape[1:]
    slots = cells.shape[1] // channels

    def convolve(b, carry):
        convolve_block(cells, weights, rest, b, SPLIT)
        return carry

    lax.fori_loop(SPLIT, channels // ROWS, convolve, 0)

    if not gathered:
        even = is_even("gy")
        after, before = lax.rem(here + 1, 4), lax.rem(here + 3, 4)
        count = parts * own_rows
        for message, owner in (
            (first, jnp.where(even, after, before)),
            (second, jnp.where(even, before, after)),
        ):
            terms = message[channels:, :].astype(F32)[0:count, :]
            sums = terms[:, 0:ncy] + terms[:, ncy : 2 * ncy] + terms[:, 2 * ncy : 3 * ncy]
            for k in range(parts):
                blocks[k, pl.ds(owner * own_rows, own_rows), :] = sums[k * own_rows : (k + 1) * own_rows]
        for block, owner in ((own_block, here), (opposite, lax.rem(here + 2, 4))):
            for k in range(parts):
                blocks[k, pl.ds(owner * own_rows, own_rows), :] = block[k]
    shape = (ncy, tile)
    cell = row_iota(shape) * CF
    place = lane_iota(shape) + here * tile
    along_y = ((place >= cell) & (place < cell + CF)).astype(F32)
    for k in range(parts):
        block = coarse[k] if gathered else blocks[k]
        across[k] = jnp.dot(block, along_y, precision=lax.Precision.HIGHEST, preferred_element_type=F32)
    for i in range(3):
        cell = lax.rem(lax.div(start, CF) + i, ncx)
        total = None
        for k in range(parts):
            term = weights[LIFT + k] * across[k, pl.ds(cell, 1), :]
            total = term if total is None else total + term
        lifted[i] = total

    group = 4
    wide = jnp.concatenate([mix[...]] * group, axis=1)
    wide = jnp.concatenate([wide] * group, axis=0)
    size = group * channels
    row, column = row_iota((size, size)), lane_iota((size, size))
    same = sum(
        ((row >= i * channels) & (row < (i + 1) * channels) & (column >= i * channels) & (column < (i + 1) * channels)).astype(F32)
        for i in range(group)
    )
    mixer[...] = jnp.where(same > 0, wide.astype(F32), 0.0).astype(BF16)

    for x in range(0, slots, group):
        depths = [
            jnp.concatenate([depth_row(weights, (depth, rest), edge, z, x + i) for i in range(group)], axis=0).astype(BF16)
            for z in range(ZOUT)
        ]
        mixed = jnp.dot(mixer[...], jnp.concatenate(depths, axis=1), preferred_element_type=F32)
        for i in range(group):
            for z in range(ZOUT):
                part = mixed[i * channels : (i + 1) * channels, z * tile : (z + 1) * tile]
                part = active(weights, part) + base_row(cells, lifted, phase, z, x + i)
                value[z, pl.ds(x + i, channels, stride=slots), :] = jnp.where(x + i < width, part, 0.0)
    for z in range(ZOUT):
        for i, x in enumerate((0, 1, width - 2, width - 1)):
            ends[z, i * channels : (i + 1) * channels, :] = depth_row(weights, (depth, rest), edge, z, x)
            bases[z, i * channels : (i + 1) * channels, :] = base_row(cells, lifted, phase, z, x)


def finish_kernel(widths, weights, ends, bases, mixer, far, near, value_in, out, value, block, sems):
    width = widths[lax.axis_index("gx")]
    channels = weights.shape[1]
    slots = block.shape[2]
    even = is_even("gx")
    half = 2 * channels
    copies = []
    for z in range(ZOUT):
        at = slice(z * half, (z + 1) * half)
        one, two = far[at, :].astype(F32), near[at, :].astype(F32)
        arrived = jnp.concatenate([jnp.where(even, one, two), jnp.where(even, two, one)], axis=0)
        mixed = jnp.dot(mixer[...], (ends[z] + arrived).astype(BF16), preferred_element_type=F32)
        for i, x in enumerate((0, 1, width - 2, width - 1)):
            at = slice(i * channels, (i + 1) * channels)
            value[z, pl.ds(x, channels, stride=slots), :] = active(weights, mixed[at, :]) + bases[z, at, :]
        for part in range(channels // CHUNK):
            for o in range(part * CHUNK, (part + 1) * CHUNK):
                block[z, o] = value[z, o * slots : (o + 1) * slots, :].astype(BF16)
            part_of = pl.ds(part * CHUNK, CHUNK)
            copy = pltpu.make_async_copy(block.at[z, part_of], out.at[z, part_of], sems.at[part, z])
            copy.start()
            copies.append(copy)
    for copy in copies:
        copy.wait()


def shards(feature, widths, dw_weight, dw_bias, pw_weight, pw_bias, lift_weight, coarse):
    planes, channels, slots, tile = feature.shape
    ny = lax.axis_size("gy")
    parts, own_rows, ncy = coarse.shape
    gathered = ny != 4
    ncx = ny * own_rows
    smem = pl.BlockSpec(memory_space=pltpu.SMEM)
    vmem = pl.BlockSpec(memory_space=pltpu.VMEM)
    hbm = pl.BlockSpec(memory_space=pltpu.HBM)
    params = pltpu.CompilerParams(vmem_limit_bytes=VMEM_BYTES)
    shape = jax.ShapeDtypeStruct
    strip = shape((channels + 16, tile), BF16)
    cells_shape = pltpu.VMEM((planes, channels * slots, tile), F32)
    value_shape = pltpu.VMEM((ZOUT, channels * slots, tile), F32)
    message = shape((2 * ZOUT * channels, tile), BF16)

    def swapped(array, axis, first):
        count = lax.axis_size(axis)
        pairs = []
        for i in range(first, count + first, 2):
            a, b = i % count, (i + 1) % count
            pairs += [(a, b), (b, a)]
        return lax.ppermute(array, axis, pairs)

    def pinned(array):
        return pltpu.with_memory_space_constraint(array, pltpu.HBM)

    if gathered:
        every = lax.all_gather(coarse, "gy", axis=1, tiled=True)
    small = (
        widths,
        dw_weight,
        dw_bias.reshape(1, channels),
        pw_bias.reshape(1, channels),
        lift_weight.T,
        coarse,
    )
    cells, first, second, stacked, block, slab_widths = pl.pallas_call(
        pack_kernel,
        out_shape=(
            cells_shape,
            strip,
            strip,
            pltpu.VMEM((32, channels), F32),
            pltpu.VMEM(coarse.shape, F32),
            pltpu.SMEM(widths.shape, jnp.int32),
        ),
        in_specs=[hbm] * 7,
        out_specs=(vmem,) * 5 + (smem,),
        scratch_shapes=[
            pltpu.VMEM(feature.shape, BF16),
            pltpu.SMEM(widths.shape, jnp.int32),
            pltpu.VMEM(dw_weight.shape, F32),
            pltpu.VMEM((1, channels), F32),
            pltpu.VMEM((1, channels), F32),
            pltpu.VMEM((parts, channels), F32),
            pltpu.VMEM(coarse.shape, F32),
            pltpu.VMEM((16, tile), F32),
            pltpu.VMEM((3, 2, channels, tile), F32),
            pltpu.SemaphoreType.DMA((3,)),
            pltpu.SemaphoreType.DMA((len(small),)),
        ],
        compiler_params=params,
    )(pinned(feature), *(pinned(array) for array in small))
    second = swapped(second, "gy", 1)
    first = swapped(first, "gy", 0)
    early = SPLIT * ROWS
    cells, weights, depth, rims, own_block = pl.pallas_call(
        conv_kernel,
        out_shape=(
            cells_shape,
            pltpu.VMEM((32, channels, tile), F32),
            pltpu.VMEM((ZOUT, slots, early, tile), F32),
            pltpu.VMEM((ZOUT, 4, channels, tile), F32),
            pltpu.VMEM(coarse.shape, F32),
        ),
        in_specs=[smem] + [vmem] * 3,
        out_specs=(vmem,) * 5,
        input_output_aliases={3: 0},
        compiler_params=params,
        cost_estimate=pl.CostEstimate(flops=10**9, bytes_accessed=10**6, transcendentals=0),
    )(slab_widths, stacked, block, cells)
    if not gathered:
        opposite = lax.ppermute(own_block, "gy", [(i, (i + 2) % 4) for i in range(4)])
    edge, far, near = pl.pallas_call(
        rim_kernel,
        out_shape=(pltpu.VMEM((2, channels, tile), F32), message, message),
        in_specs=[smem] + [vmem] * 3,
        out_specs=(vmem,) * 3,
        compiler_params=params,
    )(slab_widths, second, first, rims)
    far = swapped(far, "gx", 1)
    near = swapped(near, "gx", 0)
    blocks = (every,) if gathered else (second, first, own_block, opposite)
    ends_shape = pltpu.VMEM((ZOUT, 4 * channels, tile), F32)
    value, ends, bases, mixer = pl.pallas_call(
        functools.partial(mix_kernel, gathered),
        out_shape=(value_shape, ends_shape, ends_shape, pltpu.VMEM((4 * channels, 4 * channels), BF16)),
        in_specs=[smem] + [vmem] * (5 + len(blocks)),
        out_specs=(vmem,) * 4,
        scratch_shapes=[
            pltpu.VMEM((ZOUT, slots, channels - early, tile), F32),
            pltpu.VMEM((3, channels, tile), F32),
            pltpu.VMEM((parts, ncx, tile), F32),
        ]
        + ([] if gathered else [pltpu.VMEM((parts, ncx, ncy), F32)]),
        compiler_params=params,
        cost_estimate=pl.CostEstimate(flops=10**9, bytes_accessed=10**6, transcendentals=0),
    )(slab_widths, pw_weight, cells, weights, depth, edge, *blocks)
    out, _ = pl.pallas_call(
        finish_kernel,
        out_shape=(shape((ZOUT, channels, slots, tile), BF16), value_shape),
        in_specs=[smem] + [vmem] * 7,
        out_specs=(hbm, vmem),
        scratch_shapes=[
            pltpu.VMEM((ZOUT, channels, slots, tile), BF16),
            pltpu.SemaphoreType.DMA((channels // CHUNK, ZOUT)),
        ],
        input_output_aliases={7: 1},
        compiler_params=params,
    )(slab_widths, weights, ends, bases, mixer, far, near, value)
    return out


def solution(mesh):
    placed = (P(None, None, "gx", "gy"), P(), P(), P(), P(), P(), P(), P(None, "gy", None))
    return jax.shard_map(
        shards, mesh=mesh, in_specs=placed, out_specs=P(None, None, "gx", "gy"), check_vma=False
    )
```

```python
import functools

import jax
import jax.numpy as jnp
from jax import lax
from jax.experimental import pallas as pl
from jax.experimental.pallas import tpu as pltpu
from jax.sharding import PartitionSpec as P

XW = 16
ZOUT = 2
CF = 16
ROWS = 8
SPLIT = 4
CHUNK = 16
DW_BIAS, PW_BIAS, LIFT = 27, 28, 29
F32 = jnp.float32
BF16 = jnp.bfloat16
VMEM_BYTES = 14 * 1024 * 1024


def lane_iota(shape):
    return lax.broadcasted_iota(jnp.int32, shape, len(shape) - 1)


def row_iota(shape):
    return lax.broadcasted_iota(jnp.int32, shape, len(shape) - 2)


def tap_of(m, dx, dy):
    return 9 * m + 3 * (dx + 1) + (dy + 1)


def is_even(axis):
    return lax.rem(lax.axis_index(axis), 2) == 0


def pack_kernel(
    feature, widths_in, taps_in, dw_bias_in, pw_bias_in, lift_in, coarse_in,
    cells, first, second, stacked, own_block, widths,
    planes, widths_here, taps, dw_bias, pw_bias, lift, coarse, tail, picked, sems, small_sems,
):
    count, channels, slots, tile = feature.shape

    def copy_of(m):
        at = pl.ds(ZOUT * m, ZOUT)
        return pltpu.make_async_copy(feature.at[at], planes.at[at], sems.at[m])

    small = [
        pltpu.make_async_copy(source, target, small_sems.at[i])
        for i, (source, target) in enumerate(
            (
                (widths_in, widths_here),
                (taps_in, taps),
                (dw_bias_in, dw_bias),
                (pw_bias_in, pw_bias),
                (lift_in, lift),
                (coarse_in, coarse),
            )
        )
    ]
    for copy in small:
        copy.start()
    for m in range(3):
        copy_of(m).start()
    def weights_by_lane():
        for copy in small:
            copy.wait()
        for d in range(widths.shape[0]):
            widths[d] = widths_here[d]
        stacked[0:DW_BIAS, :] = taps[...]
        stacked[DW_BIAS : DW_BIAS + 1, :] = dw_bias[...]
        stacked[PW_BIAS : PW_BIAS + 1, :] = pw_bias[...]
        stacked[LIFT : LIFT + 3, :] = lift[...]

        own_block[...] = coarse[...]
        parts, own_rows, ncy = coarse.shape
        tail[...] = jnp.zeros_like(tail)
        if 3 * ncy <= tile:
            for k in range(parts):
                rest = coarse[k]
                for p in range(3):
                    term = rest.astype(BF16).astype(F32)
                    rest = rest - term
                    tail[k * own_rows : (k + 1) * own_rows, p * ncy : (p + 1) * ncy] = term
        for message in (first, second):
            message[channels:, :] = tail[...].astype(BF16)

        row, along = row_iota((taps.shape[0], tile)), lane_iota((taps.shape[0], tile))
        by_side = jnp.where((along & 2) != 0, 2, 0)
        chosen = jnp.concatenate(
            [(row == tap_of(m, dx, -1) + by_side).astype(BF16) for m in range(3) for dx in (-1, 0, 1)], axis=1
        )
        total, rest = None, taps[...]
        for _ in range(3):
            term = rest.astype(BF16)
            rest = rest - term.astype(F32)
            part = lax.dot_general(term, chosen, (((0,), (0,)), ((), ())), preferred_element_type=F32)
            total = part if total is None else total + part
        return total

    lane, row = lane_iota((slots, tile)), row_iota((slots, tile))
    mine = (lane >> 3) == (row & 15)
    in_even, in_odd = mine & ((lane & 4) == 0), mine & ((lane & 4) != 0)
    sublane = row_iota((ROWS, tile))

    def placed(m, k):
        both = []
        for z in range(ZOUT):
            plane = planes[ZOUT * m + z, k].astype(F32)
            cells[ZOUT * m + z, k * slots : (k + 1) * slots, :] = plane
            both.append(
                jnp.concatenate(
                    [
                        pltpu.roll(plane[x : x + ROWS], (2 + 4 * z + 8 * x) % tile, 1, stride=8, stride_axis=0)
                        for x in range(0, slots, ROWS)
                    ],
                    axis=0,
                )
            )
        rows = jnp.where(in_even, both[0], jnp.where(in_odd, both[1], 0.0))
        return rows[0:ROWS] + rows[ROWS : 2 * ROWS], rows[2 * ROWS :]

    def summed(m, k, step):
        if step == 0:
            return placed(m, k)
        one, two = summed(m, k, step // 2), summed(m, k + step, step // 2)
        turn = (sublane & step) != 0
        return tuple(
            jnp.where(turn, b, a) + pltpu.roll(jnp.where(turn, a, b), step, 0) for a, b in zip(one, two)
        )

    for m in range(3):
        copy_of(m).wait()
        for c in range(0, channels, ROWS):
            for half, part in enumerate(summed(m, c, ROWS // 2)):
                picked[m, half, c : c + ROWS, :] = part
        if m == 0:
            scale = weights_by_lane()
    width = widths_here[lax.axis_index("gx")]

    shape = (channels, tile)
    lane = lane_iota(shape)
    on_left = (lane & 2) != 0
    packed = [None, None]
    for m in range(3):
        low, high = (jnp.where(16 * half + (lane >> 3) < width, picked[m, half], 0.0) for half in range(2))
        moved = {
            -1: tuple(
                pltpu.roll(jnp.where(lane < tile - 16, one, two), 16, 1) for one, two in ((low, high), (high, low))
            ),
            0: (low, high),
            1: tuple(
                pltpu.roll(jnp.where(lane >= 16, one, two), tile - 16, 1) for one, two in ((low, high), (high, low))
            ),
        }
        for dx in (-1, 0, 1):
            begin = (3 * m + dx + 1) * tile
            for half in range(2):
                term = scale[:, begin : begin + tile] * moved[dx][half]
                packed[half] = term if packed[half] is None else packed[half] + term
    left = jnp.where(on_left, packed[0], pltpu.roll(packed[1], tile - 2, 1))
    right = jnp.where(on_left, pltpu.roll(packed[1], 2, 1), packed[0])
    even = is_even("gy")
    first[0:channels, :] = jnp.where(even, right, left).astype(BF16)
    second[0:channels, :] = jnp.where(even, left, right).astype(BF16)


def shifted_sum(before, centre, after):
    lane = lane_iota(centre.shape)
    tile = centre.shape[-1]
    before = jnp.where(lane < 2, 0.0, pltpu.roll(before, 2, 1))
    after = jnp.where(lane >= tile - 2, 0.0, pltpu.roll(after, tile - 2, 1))
    return centre + before + after


def convolve_block(cells, weights, depth, b, first_block):
    channels = weights.shape[1]
    slots = cells.shape[1] // channels
    at = pl.ds(pl.multiple_of(b * ROWS, ROWS), ROWS)
    to = pl.ds(pl.multiple_of((b - first_block) * ROWS, ROWS), ROWS)
    tap = [weights[t, at, :] for t in range(27)]
    for z in range(ZOUT):
        for parity in range(2):
            sums = {}
            for x in range(parity, slots, 2):
                rows = [cells[z + ZOUT * m, pl.ds(b * (ROWS * slots) + x, ROWS, stride=slots), :] for m in range(3)]
                for m in range(3):
                    for dx in (1, 0, -1):
                        out = x - 2 * dx
                        if 0 <= out < slots:
                            for dy in (-1, 0, 1):
                                term = tap[tap_of(m, dx, dy)] * rows[m]
                                key = (out, dy)
                                sums[key] = sums[key] + term if key in sums else term
                for out in [x - 2] if x + 2 < slots else [x - 2, x]:
                    if out >= 0:
                        depth[z, out, to, :] = shifted_sum(*(sums.pop((out, dy)) for dy in (-1, 0, 1)))


def conv_kernel(widths, stacked, coarse, cells_in, cells, weights, depth, rims, own_block):
    width = widths[lax.axis_index("gx")]
    channels, tile = weights.shape[1:]
    slots = cells.shape[1] // channels
    own_block[...] = coarse[...]
    turned = jnp.transpose(stacked[...])
    for t in range(stacked.shape[0]):
        weights[t] = jnp.broadcast_to(turned[:, t : t + 1], (channels, tile))
    for r in range(2):

        @pl.when(width + r < slots)
        def _():
            for z in range(cells.shape[0]):
                cells[z, pl.ds(width + r, channels, stride=slots), :] = jnp.zeros((channels, tile), F32)

    for b in range(channels // ROWS):
        at = slice(b * ROWS, (b + 1) * ROWS)
        for side, dx in enumerate((1, -1)):
            tap = [[weights[tap_of(m, dx, dy), at, :] for m in range(3)] for dy in (-1, 0, 1)]
            for r in range(2):
                x = r if side == 0 else width - 2 + r
                for z in range(ZOUT):
                    rows = [
                        cells[z + ZOUT * m, pl.ds(b * (ROWS * slots) + x, ROWS, stride=slots), :] for m in range(3)
                    ]
                    parts = [sum(weight * row for weight, row in zip(weights_of, rows)) for weights_of in tap]
                    rims[z, 2 * side + r, at, :] = shifted_sum(*parts)

    def convolve(b, carry):
        convolve_block(cells, weights, depth, b, 0)
        return carry

    lax.fori_loop(0, SPLIT, convolve, 0)


def edge_term(edge, z, x):
    tile = edge.shape[2]
    begin = 8 * (x & 15) + 4 * z
    cells = pltpu.roll(edge[(x >> 4) & 1], (tile - 2 - begin) & (tile - 1), 1)
    lane = lane_iota(cells.shape)
    return jnp.where((lane < 2) | (lane >= tile - 2), cells, 0.0)


def rim_kernel(widths, second, first, rims, edge, far, near):
    width = widths[lax.axis_index("gx")]
    _, _, channels, tile = rims.shape
    even = is_even("gy")
    one, two = first[0:channels, :].astype(F32), second[0:channels, :].astype(F32)
    right = jnp.where(even, one, two)
    left = jnp.where(even, two, one)
    on_left = (lane_iota((channels, tile)) & 2) != 0
    edge[0] = jnp.where(on_left, pltpu.roll(left, 2, 1), pltpu.roll(right, tile - 2, 1))
    edge[1] = jnp.where(on_left, left, right)
    even = is_even("gx")
    for z in range(ZOUT):
        for r in range(2):
            to_lower = rims[z, r] + edge_term(edge, z, r - 2)
            to_upper = rims[z, 2 + r] + edge_term(edge, z, width + r)
            at = slice((2 * z + r) * channels, (2 * z + r + 1) * channels)
            near[at, :] = jnp.where(even, to_upper, to_lower).astype(BF16)
            far[at, :] = jnp.where(even, to_lower, to_upper).astype(BF16)


def slab_start(widths):
    slab = lax.axis_index("gx")
    start = jnp.int32(0)
    for d in range(widths.shape[0]):
        start = start + jnp.where(d < slab, widths[d], 0)
    return start


def depth_row(weights, depths, edge, z, x):
    own = jnp.concatenate([depth[z, x] for depth in depths], axis=0)
    return own + weights[DW_BIAS] + edge_term(edge, z, x)


def base_row(cells, lifted, phase, z, x):
    channels = lifted.shape[1]
    slots = cells.shape[1] // channels
    return cells[2 + z, pl.ds(x, channels, stride=slots), :] + lifted[lax.div(phase + x, CF)]


def active(weights, mixed):
    mixed = mixed + weights[PW_BIAS]
    return jnp.maximum(mixed, 0.2 * mixed)


def rest_kernel(edge, cells, weights, rest):
    def convolve(b, carry):
        convolve_block(cells, weights, rest, b, SPLIT)
        return carry

    lax.fori_loop(SPLIT, weights.shape[1] // ROWS, convolve, 0)


def mix_kernel(gathered, widths, mix, cells, weights, depth, rest, edge, *refs):
    if gathered:
        coarse, value, ends, bases, lifted, across = refs
        parts, ncx, ncy = coarse.shape
    else:
        second, first, own_block, opposite, value, ends, bases, lifted, across, blocks = refs
        parts, own_rows, ncy = own_block.shape
        ncx = 4 * own_rows
    width = widths[lax.axis_index("gx")]
    here = lax.axis_index("gy")
    start = slab_start(widths)
    phase = lax.rem(start, CF)
    channels, tile = weights.shape[1:]
    slots = cells.shape[1] // channels

    if not gathered:
        even = is_even("gy")
        after, before = lax.rem(here + 1, 4), lax.rem(here + 3, 4)
        count = parts * own_rows
        for message, owner in (
            (first, jnp.where(even, after, before)),
            (second, jnp.where(even, before, after)),
        ):
            terms = message[channels:, :].astype(F32)[0:count, :]
            sums = terms[:, 0:ncy] + terms[:, ncy : 2 * ncy] + terms[:, 2 * ncy : 3 * ncy]
            for k in range(parts):
                blocks[k, pl.ds(owner * own_rows, own_rows), :] = sums[k * own_rows : (k + 1) * own_rows]
        for block, owner in ((own_block, here), (opposite, lax.rem(here + 2, 4))):
            for k in range(parts):
                blocks[k, pl.ds(owner * own_rows, own_rows), :] = block[k]
    shape = (ncy, tile)
    cell = row_iota(shape) * CF
    place = lane_iota(shape) + here * tile
    along_y = ((place >= cell) & (place < cell + CF)).astype(F32)
    for k in range(parts):
        block = coarse[k] if gathered else blocks[k]
        across[k] = jnp.dot(block, along_y, precision=lax.Precision.HIGHEST, preferred_element_type=F32)
    for i in range(3):
        cell = lax.rem(lax.div(start, CF) + i, ncx)
        total = None
        for k in range(parts):
            term = weights[LIFT + k] * across[k, pl.ds(cell, 1), :]
            total = term if total is None else total + term
        lifted[i] = total

    group = 4
    wide = jnp.concatenate([mix[...]] * group, axis=1)
    wide = jnp.concatenate([wide] * group, axis=0)
    size = group * channels
    row, column = row_iota((size, size)), lane_iota((size, size))
    same = sum(
        ((row >= i * channels) & (row < (i + 1) * channels) & (column >= i * channels) & (column < (i + 1) * channels)).astype(F32)
        for i in range(group)
    )
    mixer = jnp.where(same > 0, wide.astype(F32), 0.0).astype(BF16)

    for x in range(0, slots, group):
        depths = [
            jnp.concatenate([depth_row(weights, (depth, rest), edge, z, x + i) for i in range(group)], axis=0).astype(BF16)
            for z in range(ZOUT)
        ]
        mixed = jnp.dot(mixer, jnp.concatenate(depths, axis=1), preferred_element_type=F32)
        for i in range(group):
            for z in range(ZOUT):
                part = mixed[i * channels : (i + 1) * channels, z * tile : (z + 1) * tile]
                part = active(weights, part) + base_row(cells, lifted, phase, z, x + i)
                value[z, pl.ds(x + i, channels, stride=slots), :] = jnp.where(x + i < width, part, 0.0)
    for z in range(ZOUT):
        for i, x in enumerate((0, 1, width - 2, width - 1)):
            ends[z, i] = depth_row(weights, (depth, rest), edge, z, x)
            bases[z, i] = base_row(cells, lifted, phase, z, x)


def finish_kernel(widths, mix, weights, ends, bases, far, near, value_in, out, value, block, sems):
    width = widths[lax.axis_index("gx")]
    channels, tile = weights.shape[1:]
    slots = block.shape[2]
    even = is_even("gx")
    mixed = []
    for z in range(ZOUT):
        sums = []
        for i in range(4):
            at = slice((2 * z + i % 2) * channels, (2 * z + i % 2 + 1) * channels)
            one, two = far[at, :].astype(F32), near[at, :].astype(F32)
            arrived = jnp.where(even, one, two) if i < 2 else jnp.where(even, two, one)
            sums.append((ends[z, i] + arrived).astype(BF16))
        mixed.append(jnp.dot(mix[...], jnp.concatenate(sums, axis=1), preferred_element_type=F32))
    copies = []
    for z in range(ZOUT):
        for i, x in enumerate((0, 1, width - 2, width - 1)):
            value[z, pl.ds(x, channels, stride=slots), :] = (
                active(weights, mixed[z][:, i * tile : (i + 1) * tile]) + bases[z, i]
            )
        for part in range(channels // CHUNK):
            for o in range(part * CHUNK, (part + 1) * CHUNK):
                block[z, o] = value[z, o * slots : (o + 1) * slots, :].astype(BF16)
            part_of = pl.ds(part * CHUNK, CHUNK)
            copy = pltpu.make_async_copy(block.at[z, part_of], out.at[z, part_of], sems.at[part, z])
            copy.start()
            copies.append(copy)
    for copy in copies:
        copy.wait()


def shards(feature, widths, dw_weight, dw_bias, pw_weight, pw_bias, lift_weight, coarse):
    planes, channels, slots, tile = feature.shape
    ny = lax.axis_size("gy")
    parts, own_rows, ncy = coarse.shape
    gathered = ny != 4
    ncx = ny * own_rows
    smem = pl.BlockSpec(memory_space=pltpu.SMEM)
    vmem = pl.BlockSpec(memory_space=pltpu.VMEM)
    hbm = pl.BlockSpec(memory_space=pltpu.HBM)
    params = pltpu.CompilerParams(vmem_limit_bytes=VMEM_BYTES)
    shape = jax.ShapeDtypeStruct
    strip = shape((channels + 16, tile), BF16)
    cells_shape = pltpu.VMEM((planes, channels * slots, tile), F32)
    value_shape = pltpu.VMEM((ZOUT, channels * slots, tile), F32)
    message = shape((2 * ZOUT * channels, tile), BF16)

    def swapped(array, axis, first):
        count = lax.axis_size(axis)
        pairs = []
        for i in range(first, count + first, 2):
            a, b = i % count, (i + 1) % count
            pairs += [(a, b), (b, a)]
        return lax.ppermute(array, axis, pairs)

    def pinned(array):
        return pltpu.with_memory_space_constraint(array, pltpu.HBM)

    if gathered:
        every = lax.all_gather(coarse, "gy", axis=1, tiled=True)
    small = (
        widths,
        dw_weight,
        dw_bias.reshape(1, channels),
        pw_bias.reshape(1, channels),
        lift_weight.T,
        coarse,
    )
    cells, first, second, stacked, block, slab_widths = pl.pallas_call(
        pack_kernel,
        out_shape=(
            cells_shape,
            strip,
            strip,
            pltpu.VMEM((32, channels), F32),
            pltpu.VMEM(coarse.shape, F32),
            pltpu.SMEM(widths.shape, jnp.int32),
        ),
        in_specs=[hbm] * 7,
        out_specs=(vmem,) * 5 + (smem,),
        scratch_shapes=[
            pltpu.VMEM(feature.shape, BF16),
            pltpu.SMEM(widths.shape, jnp.int32),
            pltpu.VMEM(dw_weight.shape, F32),
            pltpu.VMEM((1, channels), F32),
            pltpu.VMEM((1, channels), F32),
            pltpu.VMEM((parts, channels), F32),
            pltpu.VMEM(coarse.shape, F32),
            pltpu.VMEM((16, tile), F32),
            pltpu.VMEM((3, 2, channels, tile), F32),
            pltpu.SemaphoreType.DMA((3,)),
            pltpu.SemaphoreType.DMA((len(small),)),
        ],
        compiler_params=params,
    )(pinned(feature), *(pinned(array) for array in small))
    second = swapped(second, "gy", 1)
    first = swapped(first, "gy", 0)
    early = SPLIT * ROWS
    cells, weights, depth, rims, own_block = pl.pallas_call(
        conv_kernel,
        out_shape=(
            cells_shape,
            pltpu.VMEM((32, channels, tile), F32),
            pltpu.VMEM((ZOUT, slots, early, tile), F32),
            pltpu.VMEM((ZOUT, 4, channels, tile), F32),
            pltpu.VMEM(coarse.shape, F32),
        ),
        in_specs=[smem] + [vmem] * 3,
        out_specs=(vmem,) * 5,
        input_output_aliases={3: 0},
        compiler_params=params,
        cost_estimate=pl.CostEstimate(flops=10**9, bytes_accessed=10**6, transcendentals=0),
    )(slab_widths, stacked, block, cells)
    if not gathered:
        opposite = lax.ppermute(own_block, "gy", [(i, (i + 2) % 4) for i in range(4)])
    edge, far, near = pl.pallas_call(
        rim_kernel,
        out_shape=(pltpu.VMEM((2, channels, tile), F32), message, message),
        in_specs=[smem] + [vmem] * 3,
        out_specs=(vmem,) * 3,
        compiler_params=params,
    )(slab_widths, second, first, rims)
    far = swapped(far, "gx", 1)
    near = swapped(near, "gx", 0)
    blocks = (every,) if gathered else (second, first, own_block, opposite)
    rest = pl.pallas_call(
        rest_kernel,
        out_shape=pltpu.VMEM((ZOUT, slots, channels - early, tile), F32),
        in_specs=[vmem] * 3,
        out_specs=vmem,
        compiler_params=params,
        cost_estimate=pl.CostEstimate(flops=10**9, bytes_accessed=10**6, transcendentals=0),
    )(edge, cells, weights)
    ends_shape = pltpu.VMEM((ZOUT, 4, channels, tile), F32)
    value, ends, bases = pl.pallas_call(
        functools.partial(mix_kernel, gathered),
        out_shape=(value_shape, ends_shape, ends_shape),
        in_specs=[smem] + [vmem] * (6 + len(blocks)),
        out_specs=(vmem,) * 3,
        scratch_shapes=[pltpu.VMEM((3, channels, tile), F32), pltpu.VMEM((parts, ncx, tile), F32)]
        + ([] if gathered else [pltpu.VMEM((parts, ncx, ncy), F32)]),
        compiler_params=params,
        cost_estimate=pl.CostEstimate(flops=10**9, bytes_accessed=10**6, transcendentals=0),
    )(slab_widths, pw_weight, cells, weights, depth, rest, edge, *blocks)
    out, _ = pl.pallas_call(
        finish_kernel,
        out_shape=(shape((ZOUT, channels, slots, tile), BF16), value_shape),
        in_specs=[smem] + [vmem] * 7,
        out_specs=(hbm, vmem),
        scratch_shapes=[
            pltpu.VMEM((ZOUT, channels, slots, tile), BF16),
            pltpu.SemaphoreType.DMA((channels // CHUNK, ZOUT)),
        ],
        input_output_aliases={7: 1},
        compiler_params=params,
    )(slab_widths, pw_weight, weights, ends, bases, far, near, value)
    return out


def solution(mesh):
    placed = (P(None, None, "gx", "gy"), P(), P(), P(), P(), P(), P(), P(None, "gy", None))
    return jax.shard_map(
        shards, mesh=mesh, in_specs=placed, out_specs=P(None, None, "gx", "gy"), check_vma=False
    )
```

```python
import functools

import jax
import jax.numpy as jnp
from jax import lax
from jax.experimental import pallas as pl
from jax.experimental.pallas import tpu as pltpu
from jax.sharding import PartitionSpec as P

XW = 16
ZOUT = 2
CF = 16
ROWS = 8
CHUNK = 16
TAIL = 32
DW_BIAS, PW_BIAS, LIFT = 27, 28, 29
F32 = jnp.float32
BF16 = jnp.bfloat16
VMEM_BYTES = 14 * 1024 * 1024


def lane_iota(shape):
    return lax.broadcasted_iota(jnp.int32, shape, len(shape) - 1)


def row_iota(shape):
    return lax.broadcasted_iota(jnp.int32, shape, len(shape) - 2)


def tap_of(m, dx, dy):
    return 9 * m + 3 * (dx + 1) + (dy + 1)


def is_even(axis):
    return lax.rem(lax.axis_index(axis), 2) == 0


def pack_kernel(
    feature, widths_in, taps_in, dw_bias_in, pw_bias_in, lift_in, coarse_in,
    cells, packets, stacked, widths,
    planes, widths_here, taps, dw_bias, pw_bias, lift, coarse, tail, picked, sems, small_sems,
):
    count, channels, slots, tile = feature.shape

    def copy_of(m):
        at = pl.ds(ZOUT * m, ZOUT)
        return pltpu.make_async_copy(feature.at[at], planes.at[at], sems.at[m])

    small = [
        pltpu.make_async_copy(source, target, small_sems.at[i])
        for i, (source, target) in enumerate(
            (
                (widths_in, widths_here),
                (taps_in, taps),
                (dw_bias_in, dw_bias),
                (pw_bias_in, pw_bias),
                (lift_in, lift),
                (coarse_in, coarse),
            )
        )
    ]
    for copy in small:
        copy.start()
    for m in range(3):
        copy_of(m).start()
    def weights_by_lane():
        for copy in small:
            copy.wait()
        for d in range(widths.shape[0]):
            widths[d] = widths_here[d]
        stacked[0:DW_BIAS, :] = taps[...]
        stacked[DW_BIAS : DW_BIAS + 1, :] = dw_bias[...]
        stacked[PW_BIAS : PW_BIAS + 1, :] = pw_bias[...]
        stacked[LIFT : LIFT + 3, :] = lift[...]

        parts, own_rows, ncy = coarse.shape
        tail[...] = jnp.zeros_like(tail)
        for k in range(parts):
            rest = coarse[k]
            for p in range(3):
                term = rest.astype(BF16).astype(F32)
                rest = rest - term
                at = (p * parts + k) * own_rows
                tail[at : at + own_rows, 0:ncy] = term
        for begin in range(0, packets.shape[0], channels + TAIL):
            packets[begin + channels : begin + channels + TAIL, :] = tail[...].astype(BF16)

        row, along = row_iota((taps.shape[0], tile)), lane_iota((taps.shape[0], tile))
        by_side = jnp.where((along & 2) != 0, 2, 0)
        chosen = jnp.concatenate(
            [(row == tap_of(m, dx, -1) + by_side).astype(BF16) for m in range(3) for dx in (-1, 0, 1)], axis=1
        )
        total, rest = None, taps[...]
        for _ in range(3):
            term = rest.astype(BF16)
            rest = rest - term.astype(F32)
            part = lax.dot_general(term, chosen, (((0,), (0,)), ((), ())), preferred_element_type=F32)
            total = part if total is None else total + part
        return total

    lane, row = lane_iota((slots, tile)), row_iota((slots, tile))
    mine = (lane >> 3) == (row & 15)
    in_even, in_odd = mine & ((lane & 4) == 0), mine & ((lane & 4) != 0)
    sublane = row_iota((ROWS, tile))

    def placed(m, k):
        both = []
        for z in range(ZOUT):
            plane = planes[ZOUT * m + z, k].astype(F32)
            cells[ZOUT * m + z, k * slots : (k + 1) * slots, :] = plane
            both.append(
                jnp.concatenate(
                    [
                        pltpu.roll(plane[x : x + ROWS], (2 + 4 * z + 8 * x) % tile, 1, stride=8, stride_axis=0)
                        for x in range(0, slots, ROWS)
                    ],
                    axis=0,
                )
            )
        rows = jnp.where(in_even, both[0], jnp.where(in_odd, both[1], 0.0))
        return rows[0:ROWS] + rows[ROWS : 2 * ROWS], rows[2 * ROWS :]

    def summed(m, k, step):
        if step == 0:
            return placed(m, k)
        one, two = summed(m, k, step // 2), summed(m, k + step, step // 2)
        turn = (sublane & step) != 0
        return tuple(
            jnp.where(turn, b, a) + pltpu.roll(jnp.where(turn, a, b), step, 0) for a, b in zip(one, two)
        )

    for m in range(3):
        copy_of(m).wait()
        for c in range(0, channels, ROWS):
            for half, part in enumerate(summed(m, c, ROWS // 2)):
                picked[m, half, c : c + ROWS, :] = part
        if m == 0:
            scale = weights_by_lane()
    width = widths_here[lax.axis_index("gx")]

    shape = (channels, tile)
    lane = lane_iota(shape)
    on_left = (lane & 2) != 0
    packed = [None, None]
    for m in range(3):
        low, high = (jnp.where(16 * half + (lane >> 3) < width, picked[m, half], 0.0) for half in range(2))
        moved = {
            -1: tuple(
                pltpu.roll(jnp.where(lane < tile - 16, one, two), 16, 1) for one, two in ((low, high), (high, low))
            ),
            0: (low, high),
            1: tuple(
                pltpu.roll(jnp.where(lane >= 16, one, two), tile - 16, 1) for one, two in ((low, high), (high, low))
            ),
        }
        for dx in (-1, 0, 1):
            begin = (3 * m + dx + 1) * tile
            for half in range(2):
                term = scale[:, begin : begin + tile] * moved[dx][half]
                packed[half] = term if packed[half] is None else packed[half] + term
    left = jnp.where(on_left, packed[0], pltpu.roll(packed[1], tile - 2, 1))
    right = jnp.where(on_left, pltpu.roll(packed[1], 2, 1), packed[0])
    for message, by in ((left, -1), (right, 1)):
        packets[packet_rows(by, channels), :] = message.astype(BF16)


def packet_rows(by, channels):
    count = lax.axis_size("gy")
    beside = lax.rem(lax.axis_index("gy") + by + count, count)
    return pl.ds(pl.multiple_of(beside * (channels + TAIL), 16), channels)


def shifted_sum(before, centre, after):
    lane = lane_iota(centre.shape)
    tile = centre.shape[-1]
    before = jnp.where(lane < 2, 0.0, pltpu.roll(before, 2, 1))
    after = jnp.where(lane >= tile - 2, 0.0, pltpu.roll(after, tile - 2, 1))
    return centre + before + after


def outer_kernel(widths, stacked, cells_in, cells, weights, rims):
    width = widths[lax.axis_index("gx")]
    channels, tile = weights.shape[1:]
    slots = cells.shape[1] // channels
    turned = jnp.transpose(stacked[...])
    for t in range(stacked.shape[0]):
        weights[t] = jnp.broadcast_to(turned[:, t : t + 1], (channels, tile))
    for r in range(2):

        @pl.when(width + r < slots)
        def _():
            for z in range(cells.shape[0]):
                cells[z, pl.ds(width + r, channels, stride=slots), :] = jnp.zeros((channels, tile), F32)

    for b in range(channels // ROWS):
        at = slice(b * ROWS, (b + 1) * ROWS)
        for side, dx in enumerate((1, -1)):
            tap = [[weights[tap_of(m, dx, dy), at, :] for m in range(3)] for dy in (-1, 0, 1)]
            for r in range(2):
                x = r if side == 0 else width - 2 + r
                for z in range(ZOUT):
                    rows = [
                        cells[z + ZOUT * m, pl.ds(b * (ROWS * slots) + x, ROWS, stride=slots), :] for m in range(3)
                    ]
                    parts = [sum(weight * row for weight, row in zip(weights_of, rows)) for weights_of in tap]
                    rims[z, 2 * side + r, at, :] = shifted_sum(*parts)


def conv_kernel(edge, cells, weights, depth):
    channels = weights.shape[1]
    slots = cells.shape[1] // channels

    def convolve(b, carry):
        at = pl.ds(pl.multiple_of(b * ROWS, ROWS), ROWS)
        tap = [weights[t, at, :] for t in range(27)]
        for z in range(ZOUT):
            for parity in range(2):
                sums = {}
                for x in range(parity, slots, 2):
                    rows = [cells[z + ZOUT * m, pl.ds(b * (ROWS * slots) + x, ROWS, stride=slots), :] for m in range(3)]
                    for m in range(3):
                        for dx in (1, 0, -1):
                            out = x - 2 * dx
                            if 0 <= out < slots:
                                for dy in (-1, 0, 1):
                                    term = tap[tap_of(m, dx, dy)] * rows[m]
                                    key = (out, dy)
                                    sums[key] = sums[key] + term if key in sums else term
                    for out in [x - 2] if x + 2 < slots else [x - 2, x]:
                        if out >= 0:
                            depth[z, out, at, :] = shifted_sum(*(sums.pop((out, dy)) for dy in (-1, 0, 1)))
        return carry

    lax.fori_loop(0, channels // ROWS, convolve, 0)


def edge_term(edge, z, x):
    tile = edge.shape[2]
    begin = 8 * (x & 15) + 4 * z
    cells = pltpu.roll(edge[(x >> 4) & 1], (tile - 2 - begin) & (tile - 1), 1)
    lane = lane_iota(cells.shape)
    return jnp.where((lane < 2) | (lane >= tile - 2), cells, 0.0)


def rim_kernel(widths, packets, rims, edge, far, near):
    width = widths[lax.axis_index("gx")]
    _, _, channels, tile = rims.shape
    left = packets[packet_rows(-1, channels), :].astype(F32)
    right = packets[packet_rows(1, channels), :].astype(F32)
    on_left = (lane_iota((channels, tile)) & 2) != 0
    edge[0] = jnp.where(on_left, pltpu.roll(left, 2, 1), pltpu.roll(right, tile - 2, 1))
    edge[1] = jnp.where(on_left, left, right)
    even = is_even("gx")
    for z in range(ZOUT):
        for r in range(2):
            to_lower = rims[z, r] + edge_term(edge, z, r - 2)
            to_upper = rims[z, 2 + r] + edge_term(edge, z, width + r)
            at = slice((2 * z + r) * channels, (2 * z + r + 1) * channels)
            near[at, :] = jnp.where(even, to_upper, to_lower).astype(BF16)
            far[at, :] = jnp.where(even, to_lower, to_upper).astype(BF16)


def slab_start(widths):
    slab = lax.axis_index("gx")
    start = jnp.int32(0)
    for d in range(widths.shape[0]):
        start = start + jnp.where(d < slab, widths[d], 0)
    return start


def depth_row(weights, depth, edge, z, x):
    return depth[z, x] + weights[DW_BIAS] + edge_term(edge, z, x)


def base_row(cells, lifted, phase, z, x):
    channels = lifted.shape[1]
    slots = cells.shape[1] // channels
    return cells[2 + z, pl.ds(x, channels, stride=slots), :] + lifted[lax.div(phase + x, CF)]


def active(weights, mixed):
    mixed = mixed + weights[PW_BIAS]
    return jnp.maximum(mixed, 0.2 * mixed)


def mix_kernel(grid, widths, mix, packets, cells, weights, depth, edge, value, ends, bases, lifted, across, blocks):
    parts, own_rows, ncy = grid
    ncx = blocks.shape[1]
    width = widths[lax.axis_index("gx")]
    here = lax.axis_index("gy")
    start = slab_start(widths)
    phase = lax.rem(start, CF)
    channels, tile = weights.shape[1:]
    slots = cells.shape[1] // channels
    count = parts * own_rows
    for owner in range(ncx // own_rows):
        begin = owner * (channels + TAIL) + channels
        terms = packets[begin : begin + TAIL, :].astype(F32)
        sums = terms[0:count] + terms[count : 2 * count] + terms[2 * count : 3 * count]
        for k in range(parts):
            blocks[k, owner * own_rows : (owner + 1) * own_rows, :] = sums[k * own_rows : (k + 1) * own_rows, 0:ncy]
    shape = (ncy, tile)
    cell = row_iota(shape) * CF
    place = lane_iota(shape) + here * tile
    along_y = ((place >= cell) & (place < cell + CF)).astype(F32)
    for k in range(parts):
        across[k] = jnp.dot(blocks[k], along_y, precision=lax.Precision.HIGHEST, preferred_element_type=F32)
    for i in range(3):
        cell = lax.rem(lax.div(start, CF) + i, ncx)
        total = None
        for k in range(parts):
            term = weights[LIFT + k] * across[k, pl.ds(cell, 1), :]
            total = term if total is None else total + term
        lifted[i] = total

    group = 4
    wide = jnp.concatenate([mix[...]] * group, axis=1)
    wide = jnp.concatenate([wide] * group, axis=0)
    size = group * channels
    row, column = row_iota((size, size)), lane_iota((size, size))
    same = sum(
        ((row >= i * channels) & (row < (i + 1) * channels) & (column >= i * channels) & (column < (i + 1) * channels)).astype(F32)
        for i in range(group)
    )
    mixer = jnp.where(same > 0, wide.astype(F32), 0.0).astype(BF16)

    for x in range(0, slots, group):
        depths = [
            jnp.concatenate([depth_row(weights, depth, edge, z, x + i) for i in range(group)], axis=0).astype(BF16)
            for z in range(ZOUT)
        ]
        mixed = jnp.dot(mixer, jnp.concatenate(depths, axis=1), preferred_element_type=F32)
        for i in range(group):
            for z in range(ZOUT):
                part = mixed[i * channels : (i + 1) * channels, z * tile : (z + 1) * tile]
                part = active(weights, part) + base_row(cells, lifted, phase, z, x + i)
                value[z, pl.ds(x + i, channels, stride=slots), :] = jnp.where(x + i < width, part, 0.0)
    for z in range(ZOUT):
        for i, x in enumerate((0, 1, width - 2, width - 1)):
            ends[z, i] = depth_row(weights, depth, edge, z, x)
            bases[z, i] = base_row(cells, lifted, phase, z, x)


def finish_kernel(widths, mix, weights, ends, bases, far, near, value_in, out, value, block, sems):
    width = widths[lax.axis_index("gx")]
    channels, tile = weights.shape[1:]
    slots = block.shape[2]
    even = is_even("gx")
    mixed = []
    for z in range(ZOUT):
        sums = []
        for i in range(4):
            at = slice((2 * z + i % 2) * channels, (2 * z + i % 2 + 1) * channels)
            one, two = far[at, :].astype(F32), near[at, :].astype(F32)
            arrived = jnp.where(even, one, two) if i < 2 else jnp.where(even, two, one)
            sums.append((ends[z, i] + arrived).astype(BF16))
        mixed.append(jnp.dot(mix[...], jnp.concatenate(sums, axis=1), preferred_element_type=F32))
    copies = []
    for z in range(ZOUT):
        for i, x in enumerate((0, 1, width - 2, width - 1)):
            value[z, pl.ds(x, channels, stride=slots), :] = (
                active(weights, mixed[z][:, i * tile : (i + 1) * tile]) + bases[z, i]
            )
        for part in range(channels // CHUNK):
            for o in range(part * CHUNK, (part + 1) * CHUNK):
                block[z, o] = value[z, o * slots : (o + 1) * slots, :].astype(BF16)
            part_of = pl.ds(part * CHUNK, CHUNK)
            copy = pltpu.make_async_copy(block.at[z, part_of], out.at[z, part_of], sems.at[part, z])
            copy.start()
            copies.append(copy)
    for copy in copies:
        copy.wait()


def shards(feature, widths, dw_weight, dw_bias, pw_weight, pw_bias, lift_weight, coarse):
    planes, channels, slots, tile = feature.shape
    ny = lax.axis_size("gy")
    parts, own_rows, ncy = coarse.shape
    ncx = ny * own_rows
    smem = pl.BlockSpec(memory_space=pltpu.SMEM)
    vmem = pl.BlockSpec(memory_space=pltpu.VMEM)
    hbm = pl.BlockSpec(memory_space=pltpu.HBM)
    params = pltpu.CompilerParams(vmem_limit_bytes=VMEM_BYTES)
    shape = jax.ShapeDtypeStruct
    cells_shape = pltpu.VMEM((planes, channels * slots, tile), F32)
    value_shape = pltpu.VMEM((ZOUT, channels * slots, tile), F32)
    message = shape((2 * ZOUT * channels, tile), BF16)

    def swapped(array, axis, first):
        count = lax.axis_size(axis)
        pairs = []
        for i in range(first, count + first, 2):
            a, b = i % count, (i + 1) % count
            pairs += [(a, b), (b, a)]
        return lax.ppermute(array, axis, pairs)

    def pinned(array):
        return pltpu.with_memory_space_constraint(array, pltpu.HBM)

    small = (
        widths,
        dw_weight,
        dw_bias.reshape(1, channels),
        pw_bias.reshape(1, channels),
        lift_weight.T,
        coarse,
    )
    cells, packets, stacked, slab_widths = pl.pallas_call(
        pack_kernel,
        out_shape=(
            cells_shape,
            shape((ny * (channels + TAIL), tile), BF16),
            pltpu.VMEM((32, channels), F32),
            pltpu.SMEM(widths.shape, jnp.int32),
        ),
        in_specs=[hbm] * 7,
        out_specs=(vmem,) * 3 + (smem,),
        scratch_shapes=[
            pltpu.VMEM(feature.shape, BF16),
            pltpu.SMEM(widths.shape, jnp.int32),
            pltpu.VMEM(dw_weight.shape, F32),
            pltpu.VMEM((1, channels), F32),
            pltpu.VMEM((1, channels), F32),
            pltpu.VMEM((parts, channels), F32),
            pltpu.VMEM(coarse.shape, F32),
            pltpu.VMEM((TAIL, tile), F32),
            pltpu.VMEM((3, 2, channels, tile), F32),
            pltpu.SemaphoreType.DMA((3,)),
            pltpu.SemaphoreType.DMA((len(small),)),
        ],
        compiler_params=params,
    )(pinned(feature), *(pinned(array) for array in small))
    packets = lax.all_to_all(packets, "gy", split_axis=0, concat_axis=0, tiled=True)
    cells, weights, rims = pl.pallas_call(
        outer_kernel,
        out_shape=(
            cells_shape,
            pltpu.VMEM((32, channels, tile), F32),
            pltpu.VMEM((ZOUT, 4, channels, tile), F32),
        ),
        in_specs=[smem] + [vmem] * 2,
        out_specs=(vmem,) * 3,
        input_output_aliases={2: 0},
        compiler_params=params,
        cost_estimate=pl.CostEstimate(flops=10**9, bytes_accessed=10**6, transcendentals=0),
    )(slab_widths, stacked, cells)
    edge, far, near = pl.pallas_call(
        rim_kernel,
        out_shape=(pltpu.VMEM((2, channels, tile), F32), message, message),
        in_specs=[smem] + [vmem] * 2,
        out_specs=(vmem,) * 3,
        compiler_params=params,
    )(slab_widths, packets, rims)
    far = swapped(far, "gx", 1)
    near = swapped(near, "gx", 0)
    depth = pl.pallas_call(
        conv_kernel,
        out_shape=pltpu.VMEM((ZOUT, slots, channels, tile), F32),
        in_specs=[vmem] * 3,
        out_specs=vmem,
        compiler_params=params,
        cost_estimate=pl.CostEstimate(flops=10**9, bytes_accessed=10**6, transcendentals=0),
    )(edge, cells, weights)
    ends_shape = pltpu.VMEM((ZOUT, 4, channels, tile), F32)
    value, ends, bases = pl.pallas_call(
        functools.partial(mix_kernel, coarse.shape),
        out_shape=(value_shape, ends_shape, ends_shape),
        in_specs=[smem] + [vmem] * 6,
        out_specs=(vmem,) * 3,
        scratch_shapes=[
            pltpu.VMEM((3, channels, tile), F32),
            pltpu.VMEM((parts, ncx, tile), F32),
            pltpu.VMEM((parts, ncx, ncy), F32),
        ],
        compiler_params=params,
        cost_estimate=pl.CostEstimate(flops=10**9, bytes_accessed=10**6, transcendentals=0),
    )(slab_widths, pw_weight, packets, cells, weights, depth, edge)
    out, _ = pl.pallas_call(
        finish_kernel,
        out_shape=(shape((ZOUT, channels, slots, tile), BF16), value_shape),
        in_specs=[smem] + [vmem] * 7,
        out_specs=(hbm, vmem),
        scratch_shapes=[
            pltpu.VMEM((ZOUT, channels, slots, tile), BF16),
            pltpu.SemaphoreType.DMA((channels // CHUNK, ZOUT)),
        ],
        input_output_aliases={7: 1},
        compiler_params=params,
    )(slab_widths, pw_weight, weights, ends, bases, far, near, value)
    return out


def solution(mesh):
    placed = (P(None, None, "gx", "gy"), P(), P(), P(), P(), P(), P(), P(None, "gy", None))
    return jax.shard_map(
        shards, mesh=mesh, in_specs=placed, out_specs=P(None, None, "gx", "gy"), check_vma=False
    )
```

```python
import functools

import jax
import jax.numpy as jnp
from jax import lax
from jax.experimental import pallas as pl
from jax.experimental.pallas import tpu as pltpu
from jax.sharding import PartitionSpec as P

XW = 16
ZOUT = 2
CF = 16
ROWS = 8
SPLIT = 4
CHUNK = 16
DW_BIAS, PW_BIAS, LIFT = 27, 28, 29
F32 = jnp.float32
BF16 = jnp.bfloat16
VMEM_BYTES = 14 * 1024 * 1024


def lane_iota(shape):
    return lax.broadcasted_iota(jnp.int32, shape, len(shape) - 1)


def row_iota(shape):
    return lax.broadcasted_iota(jnp.int32, shape, len(shape) - 2)


def tap_of(m, dx, dy):
    return 9 * m + 3 * (dx + 1) + (dy + 1)


def is_even(axis):
    return lax.rem(lax.axis_index(axis), 2) == 0


def pack_kernel(
    feature, widths_in, taps_in, dw_bias_in, pw_bias_in, lift_in, coarse_in,
    cells, first, second, stacked, own_block, widths,
    planes, widths_here, taps, dw_bias, pw_bias, lift, coarse, tail, picked, sems, small_sems,
):
    count, channels, slots, tile = feature.shape

    def copy_of(m):
        at = pl.ds(ZOUT * m, ZOUT)
        return pltpu.make_async_copy(feature.at[at], planes.at[at], sems.at[m])

    small = [
        pltpu.make_async_copy(source, target, small_sems.at[i])
        for i, (source, target) in enumerate(
            (
                (widths_in, widths_here),
                (taps_in, taps),
                (dw_bias_in, dw_bias),
                (pw_bias_in, pw_bias),
                (lift_in, lift),
                (coarse_in, coarse),
            )
        )
    ]
    for copy in small:
        copy.start()
    for m in range(3):
        copy_of(m).start()
    def weights_by_lane():
        for copy in small:
            copy.wait()
        for d in range(widths.shape[0]):
            widths[d] = widths_here[d]
        stacked[0:DW_BIAS, :] = taps[...]
        stacked[DW_BIAS : DW_BIAS + 1, :] = dw_bias[...]
        stacked[PW_BIAS : PW_BIAS + 1, :] = pw_bias[...]
        stacked[LIFT : LIFT + 3, :] = lift[...]

        own_block[...] = coarse[...]
        parts, own_rows, ncy = coarse.shape
        tail[...] = jnp.zeros_like(tail)
        if 3 * ncy <= tile:
            for k in range(parts):
                rest = coarse[k]
                for p in range(3):
                    term = rest.astype(BF16).astype(F32)
                    rest = rest - term
                    tail[k * own_rows : (k + 1) * own_rows, p * ncy : (p + 1) * ncy] = term
        for message in (first, second):
            message[channels:, :] = tail[...].astype(BF16)

        row, along = row_iota((taps.shape[0], tile)), lane_iota((taps.shape[0], tile))
        by_side = jnp.where((along & 2) != 0, 2, 0)
        chosen = jnp.concatenate(
            [(row == tap_of(m, dx, -1) + by_side).astype(BF16) for m in range(3) for dx in (-1, 0, 1)], axis=1
        )
        total, rest = None, taps[...]
        for _ in range(3):
            term = rest.astype(BF16)
            rest = rest - term.astype(F32)
            part = lax.dot_general(term, chosen, (((0,), (0,)), ((), ())), preferred_element_type=F32)
            total = part if total is None else total + part
        return total

    lane, row = lane_iota((slots, tile)), row_iota((slots, tile))
    mine = (lane >> 3) == (row & 15)
    in_even, in_odd = mine & ((lane & 4) == 0), mine & ((lane & 4) != 0)
    sublane = row_iota((ROWS, tile))

    def placed(m, k):
        both = []
        for z in range(ZOUT):
            plane = planes[ZOUT * m + z, k].astype(F32)
            cells[ZOUT * m + z, k * slots : (k + 1) * slots, :] = plane
            both.append(
                jnp.concatenate(
                    [
                        pltpu.roll(plane[x : x + ROWS], (2 + 4 * z + 8 * x) % tile, 1, stride=8, stride_axis=0)
                        for x in range(0, slots, ROWS)
                    ],
                    axis=0,
                )
            )
        rows = jnp.where(in_even, both[0], jnp.where(in_odd, both[1], 0.0))
        return rows[0:ROWS] + rows[ROWS : 2 * ROWS], rows[2 * ROWS :]

    def summed(m, k, step):
        if step == 0:
            return placed(m, k)
        one, two = summed(m, k, step // 2), summed(m, k + step, step // 2)
        turn = (sublane & step) != 0
        return tuple(
            jnp.where(turn, b, a) + pltpu.roll(jnp.where(turn, a, b), step, 0) for a, b in zip(one, two)
        )

    for m in range(3):
        copy_of(m).wait()
        for c in range(0, channels, ROWS):
            for half, part in enumerate(summed(m, c, ROWS // 2)):
                picked[m, half, c : c + ROWS, :] = part
        if m == 0:
            scale = weights_by_lane()
    width = widths_here[lax.axis_index("gx")]

    shape = (channels, tile)
    lane = lane_iota(shape)
    on_left = (lane & 2) != 0
    packed = [None, None]
    for m in range(3):
        low, high = (jnp.where(16 * half + (lane >> 3) < width, picked[m, half], 0.0) for half in range(2))
        moved = {
            -1: tuple(
                pltpu.roll(jnp.where(lane < tile - 16, one, two), 16, 1) for one, two in ((low, high), (high, low))
            ),
            0: (low, high),
            1: tuple(
                pltpu.roll(jnp.where(lane >= 16, one, two), tile - 16, 1) for one, two in ((low, high), (high, low))
            ),
        }
        for dx in (-1, 0, 1):
            begin = (3 * m + dx + 1) * tile
            for half in range(2):
                term = scale[:, begin : begin + tile] * moved[dx][half]
                packed[half] = term if packed[half] is None else packed[half] + term
    left = jnp.where(on_left, packed[0], pltpu.roll(packed[1], tile - 2, 1))
    right = jnp.where(on_left, pltpu.roll(packed[1], 2, 1), packed[0])
    first[0:channels, :] = right.astype(BF16)
    second[0:channels, :] = left.astype(BF16)


def shifted_sum(before, centre, after):
    lane = lane_iota(centre.shape)
    tile = centre.shape[-1]
    before = jnp.where(lane < 2, 0.0, pltpu.roll(before, 2, 1))
    after = jnp.where(lane >= tile - 2, 0.0, pltpu.roll(after, tile - 2, 1))
    return centre + before + after


def convolve_block(cells, weights, depth, b, first_block):
    channels = weights.shape[1]
    slots = cells.shape[1] // channels
    at = pl.ds(pl.multiple_of(b * ROWS, ROWS), ROWS)
    to = pl.ds(pl.multiple_of((b - first_block) * ROWS, ROWS), ROWS)
    tap = [weights[t, at, :] for t in range(27)]
    for z in range(ZOUT):
        for parity in range(2):
            sums = {}
            for x in range(parity, slots, 2):
                rows = [cells[z + ZOUT * m, pl.ds(b * (ROWS * slots) + x, ROWS, stride=slots), :] for m in range(3)]
                for m in range(3):
                    for dx in (1, 0, -1):
                        out = x - 2 * dx
                        if 0 <= out < slots:
                            for dy in (-1, 0, 1):
                                term = tap[tap_of(m, dx, dy)] * rows[m]
                                key = (out, dy)
                                sums[key] = sums[key] + term if key in sums else term
                for out in [x - 2] if x + 2 < slots else [x - 2, x]:
                    if out >= 0:
                        depth[z, out, to, :] = shifted_sum(*(sums.pop((out, dy)) for dy in (-1, 0, 1)))


def conv_kernel(widths, stacked, coarse, cells_in, cells, weights, depth, rims, own_block):
    width = widths[lax.axis_index("gx")]
    channels, tile = weights.shape[1:]
    slots = cells.shape[1] // channels
    own_block[...] = coarse[...]
    turned = jnp.transpose(stacked[...])
    for t in range(stacked.shape[0]):
        weights[t] = jnp.broadcast_to(turned[:, t : t + 1], (channels, tile))
    for r in range(2):

        @pl.when(width + r < slots)
        def _():
            for z in range(cells.shape[0]):
                cells[z, pl.ds(width + r, channels, stride=slots), :] = jnp.zeros((channels, tile), F32)

    for b in range(channels // ROWS):
        at = slice(b * ROWS, (b + 1) * ROWS)
        for side, dx in enumerate((1, -1)):
            tap = [[weights[tap_of(m, dx, dy), at, :] for m in range(3)] for dy in (-1, 0, 1)]
            for r in range(2):
                x = r if side == 0 else width - 2 + r
                for z in range(ZOUT):
                    rows = [
                        cells[z + ZOUT * m, pl.ds(b * (ROWS * slots) + x, ROWS, stride=slots), :] for m in range(3)
                    ]
                    parts = [sum(weight * row for weight, row in zip(weights_of, rows)) for weights_of in tap]
                    rims[z, 2 * side + r, at, :] = shifted_sum(*parts)

    def convolve(b, carry):
        convolve_block(cells, weights, depth, b, 0)
        return carry

    lax.fori_loop(0, SPLIT, convolve, 0)


def edge_term(edge, z, x):
    tile = edge.shape[2]
    begin = 8 * (x & 15) + 4 * z
    cells = pltpu.roll(edge[(x >> 4) & 1], (tile - 2 - begin) & (tile - 1), 1)
    lane = lane_iota(cells.shape)
    return jnp.where((lane < 2) | (lane >= tile - 2), cells, 0.0)


def rim_kernel(widths, first, second, rims, edge, far, near):
    width = widths[lax.axis_index("gx")]
    _, _, channels, tile = rims.shape
    left, right = first[0:channels, :].astype(F32), second[0:channels, :].astype(F32)
    on_left = (lane_iota((channels, tile)) & 2) != 0
    edge[0] = jnp.where(on_left, pltpu.roll(left, 2, 1), pltpu.roll(right, tile - 2, 1))
    edge[1] = jnp.where(on_left, left, right)
    even = is_even("gx")
    for z in range(ZOUT):
        for r in range(2):
            to_lower = rims[z, r] + edge_term(edge, z, r - 2)
            to_upper = rims[z, 2 + r] + edge_term(edge, z, width + r)
            at = slice((2 * z + r) * channels, (2 * z + r + 1) * channels)
            near[at, :] = jnp.where(even, to_upper, to_lower).astype(BF16)
            far[at, :] = jnp.where(even, to_lower, to_upper).astype(BF16)


def slab_start(widths):
    slab = lax.axis_index("gx")
    start = jnp.int32(0)
    for d in range(widths.shape[0]):
        start = start + jnp.where(d < slab, widths[d], 0)
    return start


def depth_row(weights, depths, edge, z, x):
    own = jnp.concatenate([depth[z, x] for depth in depths], axis=0)
    return own + weights[DW_BIAS] + edge_term(edge, z, x)


def base_row(cells, lifted, phase, z, x):
    channels = lifted.shape[1]
    slots = cells.shape[1] // channels
    return cells[2 + z, pl.ds(x, channels, stride=slots), :] + lifted[lax.div(phase + x, CF)]


def active(weights, mixed):
    mixed = mixed + weights[PW_BIAS]
    return jnp.maximum(mixed, 0.2 * mixed)


def rest_kernel(edge, cells, weights, rest):
    def convolve(b, carry):
        convolve_block(cells, weights, rest, b, SPLIT)
        return carry

    lax.fori_loop(SPLIT, weights.shape[1] // ROWS, convolve, 0)


def mix_kernel(gathered, widths, mix, cells, weights, depth, rest, edge, *refs):
    if gathered:
        coarse, value, ends, bases, lifted, across = refs
        parts, ncx, ncy = coarse.shape
    else:
        first, second, own_block, opposite, value, ends, bases, lifted, across, blocks = refs
        parts, own_rows, ncy = own_block.shape
        ncx = 4 * own_rows
    width = widths[lax.axis_index("gx")]
    here = lax.axis_index("gy")
    start = slab_start(widths)
    phase = lax.rem(start, CF)
    channels, tile = weights.shape[1:]
    slots = cells.shape[1] // channels

    if not gathered:
        count = parts * own_rows
        for message, owner in ((first, lax.rem(here + 3, 4)), (second, lax.rem(here + 1, 4))):
            terms = message[channels:, :].astype(F32)[0:count, :]
            sums = terms[:, 0:ncy] + terms[:, ncy : 2 * ncy] + terms[:, 2 * ncy : 3 * ncy]
            for k in range(parts):
                blocks[k, pl.ds(owner * own_rows, own_rows), :] = sums[k * own_rows : (k + 1) * own_rows]
        for block, owner in ((own_block, here), (opposite, lax.rem(here + 2, 4))):
            for k in range(parts):
                blocks[k, pl.ds(owner * own_rows, own_rows), :] = block[k]
    shape = (ncy, tile)
    cell = row_iota(shape) * CF
    place = lane_iota(shape) + here * tile
    along_y = ((place >= cell) & (place < cell + CF)).astype(F32)
    for k in range(parts):
        block = coarse[k] if gathered else blocks[k]
        across[k] = jnp.dot(block, along_y, precision=lax.Precision.HIGHEST, preferred_element_type=F32)
    for i in range(3):
        cell = lax.rem(lax.div(start, CF) + i, ncx)
        total = None
        for k in range(parts):
            term = weights[LIFT + k] * across[k, pl.ds(cell, 1), :]
            total = term if total is None else total + term
        lifted[i] = total

    group = 4
    wide = jnp.concatenate([mix[...]] * group, axis=1)
    wide = jnp.concatenate([wide] * group, axis=0)
    size = group * channels
    row, column = row_iota((size, size)), lane_iota((size, size))
    same = sum(
        ((row >= i * channels) & (row < (i + 1) * channels) & (column >= i * channels) & (column < (i + 1) * channels)).astype(F32)
        for i in range(group)
    )
    mixer = jnp.where(same > 0, wide.astype(F32), 0.0).astype(BF16)

    for x in range(0, slots, group):
        depths = [
            jnp.concatenate([depth_row(weights, (depth, rest), edge, z, x + i) for i in range(group)], axis=0).astype(BF16)
            for z in range(ZOUT)
        ]
        mixed = jnp.dot(mixer, jnp.concatenate(depths, axis=1), preferred_element_type=F32)
        for i in range(group):
            for z in range(ZOUT):
                part = mixed[i * channels : (i + 1) * channels, z * tile : (z + 1) * tile]
                part = active(weights, part) + base_row(cells, lifted, phase, z, x + i)
                value[z, pl.ds(x + i, channels, stride=slots), :] = jnp.where(x + i < width, part, 0.0)
    for z in range(ZOUT):
        for i, x in enumerate((0, 1, width - 2, width - 1)):
            ends[z, i] = depth_row(weights, (depth, rest), edge, z, x)
            bases[z, i] = base_row(cells, lifted, phase, z, x)


def finish_kernel(widths, mix, weights, ends, bases, far, near, value_in, out, value, block, sems):
    width = widths[lax.axis_index("gx")]
    channels, tile = weights.shape[1:]
    slots = block.shape[2]
    even = is_even("gx")
    mixed = []
    for z in range(ZOUT):
        sums = []
        for i in range(4):
            at = slice((2 * z + i % 2) * channels, (2 * z + i % 2 + 1) * channels)
            one, two = far[at, :].astype(F32), near[at, :].astype(F32)
            arrived = jnp.where(even, one, two) if i < 2 else jnp.where(even, two, one)
            sums.append((ends[z, i] + arrived).astype(BF16))
        mixed.append(jnp.dot(mix[...], jnp.concatenate(sums, axis=1), preferred_element_type=F32))
    copies = []
    for z in range(ZOUT):
        for i, x in enumerate((0, 1, width - 2, width - 1)):
            value[z, pl.ds(x, channels, stride=slots), :] = (
                active(weights, mixed[z][:, i * tile : (i + 1) * tile]) + bases[z, i]
            )
        for part in range(channels // CHUNK):
            for o in range(part * CHUNK, (part + 1) * CHUNK):
                block[z, o] = value[z, o * slots : (o + 1) * slots, :].astype(BF16)
            part_of = pl.ds(part * CHUNK, CHUNK)
            copy = pltpu.make_async_copy(block.at[z, part_of], out.at[z, part_of], sems.at[part, z])
            copy.start()
            copies.append(copy)
    for copy in copies:
        copy.wait()


def shards(feature, widths, dw_weight, dw_bias, pw_weight, pw_bias, lift_weight, coarse):
    planes, channels, slots, tile = feature.shape
    ny = lax.axis_size("gy")
    parts, own_rows, ncy = coarse.shape
    gathered = ny != 4
    ncx = ny * own_rows
    smem = pl.BlockSpec(memory_space=pltpu.SMEM)
    vmem = pl.BlockSpec(memory_space=pltpu.VMEM)
    hbm = pl.BlockSpec(memory_space=pltpu.HBM)
    params = pltpu.CompilerParams(vmem_limit_bytes=VMEM_BYTES)
    shape = jax.ShapeDtypeStruct
    strip = shape((channels + 16, tile), BF16)
    cells_shape = pltpu.VMEM((planes, channels * slots, tile), F32)
    value_shape = pltpu.VMEM((ZOUT, channels * slots, tile), F32)
    message = shape((2 * ZOUT * channels, tile), BF16)

    def swapped(array, axis, first):
        count = lax.axis_size(axis)
        pairs = []
        for i in range(first, count + first, 2):
            a, b = i % count, (i + 1) % count
            pairs += [(a, b), (b, a)]
        return lax.ppermute(array, axis, pairs)

    def pinned(array):
        return pltpu.with_memory_space_constraint(array, pltpu.HBM)

    if gathered:
        every = lax.all_gather(coarse, "gy", axis=1, tiled=True)
    small = (
        widths,
        dw_weight,
        dw_bias.reshape(1, channels),
        pw_bias.reshape(1, channels),
        lift_weight.T,
        coarse,
    )
    cells, first, second, stacked, block, slab_widths = pl.pallas_call(
        pack_kernel,
        out_shape=(
            cells_shape,
            strip,
            strip,
            pltpu.VMEM((32, channels), F32),
            pltpu.VMEM(coarse.shape, F32),
            pltpu.SMEM(widths.shape, jnp.int32),
        ),
        in_specs=[hbm] * 7,
        out_specs=(vmem,) * 5 + (smem,),
        scratch_shapes=[
            pltpu.VMEM(feature.shape, BF16),
            pltpu.SMEM(widths.shape, jnp.int32),
            pltpu.VMEM(dw_weight.shape, F32),
            pltpu.VMEM((1, channels), F32),
            pltpu.VMEM((1, channels), F32),
            pltpu.VMEM((parts, channels), F32),
            pltpu.VMEM(coarse.shape, F32),
            pltpu.VMEM((16, tile), F32),
            pltpu.VMEM((3, 2, channels, tile), F32),
            pltpu.SemaphoreType.DMA((3,)),
            pltpu.SemaphoreType.DMA((len(small),)),
        ],
        compiler_params=params,
    )(pinned(feature), *(pinned(array) for array in small))
    first = lax.ppermute(first, "gy", [(i, (i + 1) % ny) for i in range(ny)])
    second = lax.ppermute(second, "gy", [((i + 1) % ny, i) for i in range(ny)])
    early = SPLIT * ROWS
    cells, weights, depth, rims, own_block = pl.pallas_call(
        conv_kernel,
        out_shape=(
            cells_shape,
            pltpu.VMEM((32, channels, tile), F32),
            pltpu.VMEM((ZOUT, slots, early, tile), F32),
            pltpu.VMEM((ZOUT, 4, channels, tile), F32),
            pltpu.VMEM(coarse.shape, F32),
        ),
        in_specs=[smem] + [vmem] * 3,
        out_specs=(vmem,) * 5,
        input_output_aliases={3: 0},
        compiler_params=params,
        cost_estimate=pl.CostEstimate(flops=10**9, bytes_accessed=10**6, transcendentals=0),
    )(slab_widths, stacked, block, cells)
    if not gathered:
        opposite = lax.ppermute(own_block, "gy", [(i, (i + 2) % 4) for i in range(4)])
    edge, far, near = pl.pallas_call(
        rim_kernel,
        out_shape=(pltpu.VMEM((2, channels, tile), F32), message, message),
        in_specs=[smem] + [vmem] * 3,
        out_specs=(vmem,) * 3,
        compiler_params=params,
    )(slab_widths, first, second, rims)
    far = swapped(far, "gx", 1)
    near = swapped(near, "gx", 0)
    blocks = (every,) if gathered else (first, second, own_block, opposite)
    rest = pl.pallas_call(
        rest_kernel,
        out_shape=pltpu.VMEM((ZOUT, slots, channels - early, tile), F32),
        in_specs=[vmem] * 3,
        out_specs=vmem,
        compiler_params=params,
        cost_estimate=pl.CostEstimate(flops=10**9, bytes_accessed=10**6, transcendentals=0),
    )(edge, cells, weights)
    ends_shape = pltpu.VMEM((ZOUT, 4, channels, tile), F32)
    value, ends, bases = pl.pallas_call(
        functools.partial(mix_kernel, gathered),
        out_shape=(value_shape, ends_shape, ends_shape),
        in_specs=[smem] + [vmem] * (6 + len(blocks)),
        out_specs=(vmem,) * 3,
        scratch_shapes=[pltpu.VMEM((3, channels, tile), F32), pltpu.VMEM((parts, ncx, tile), F32)]
        + ([] if gathered else [pltpu.VMEM((parts, ncx, ncy), F32)]),
        compiler_params=params,
        cost_estimate=pl.CostEstimate(flops=10**9, bytes_accessed=10**6, transcendentals=0),
    )(slab_widths, pw_weight, cells, weights, depth, rest, edge, *blocks)
    out, _ = pl.pallas_call(
        finish_kernel,
        out_shape=(shape((ZOUT, channels, slots, tile), BF16), value_shape),
        in_specs=[smem] + [vmem] * 7,
        out_specs=(hbm, vmem),
        scratch_shapes=[
            pltpu.VMEM((ZOUT, channels, slots, tile), BF16),
            pltpu.SemaphoreType.DMA((channels // CHUNK, ZOUT)),
        ],
        input_output_aliases={7: 1},
        compiler_params=params,
    )(slab_widths, pw_weight, weights, ends, bases, far, near, value)
    return out


def solution(mesh):
    placed = (P(None, None, "gx", "gy"), P(), P(), P(), P(), P(), P(), P(None, "gy", None))
    return jax.shard_map(
        shards, mesh=mesh, in_specs=placed, out_specs=P(None, None, "gx", "gy"), check_vma=False
    )
```

```python
import functools

import jax
import jax.numpy as jnp
from jax import lax
from jax.experimental import pallas as pl
from jax.experimental.pallas import tpu as pltpu
from jax.sharding import PartitionSpec as P

XW = 16
ZOUT = 2
CF = 16
ROWS = 8
SPLIT = 2
CHUNK = 16
DW_BIAS, PW_BIAS, LIFT = 27, 28, 29
F32 = jnp.float32
BF16 = jnp.bfloat16
VMEM_BYTES = 14 * 1024 * 1024


def lane_iota(shape):
    return lax.broadcasted_iota(jnp.int32, shape, len(shape) - 1)


def row_iota(shape):
    return lax.broadcasted_iota(jnp.int32, shape, len(shape) - 2)


def tap_of(m, dx, dy):
    return 9 * m + 3 * (dx + 1) + (dy + 1)


def is_even(axis):
    return lax.rem(lax.axis_index(axis), 2) == 0


def pack_kernel(
    feature, widths_in, taps_in, dw_bias_in, pw_bias_in, lift_in, coarse_in,
    cells, first, second, stacked, own_block, widths,
    planes, widths_here, taps, dw_bias, pw_bias, lift, coarse, tail, picked, sems, small_sems,
):
    count, channels, slots, tile = feature.shape

    half_of = channels // 2

    def copy_of(m, part):
        at = (pl.ds(ZOUT * m, ZOUT), pl.ds(part * half_of, half_of))
        return pltpu.make_async_copy(feature.at[at], planes.at[at], sems.at[m, part])

    small = [
        pltpu.make_async_copy(source, target, small_sems.at[i])
        for i, (source, target) in enumerate(
            (
                (widths_in, widths_here),
                (taps_in, taps),
                (dw_bias_in, dw_bias),
                (pw_bias_in, pw_bias),
                (lift_in, lift),
                (coarse_in, coarse),
            )
        )
    ]
    for copy in small:
        copy.start()
    for m in range(3):
        for part in range(2):
            copy_of(m, part).start()
    def weights_by_lane():
        for copy in small:
            copy.wait()
        for d in range(widths.shape[0]):
            widths[d] = widths_here[d]
        stacked[0:DW_BIAS, :] = taps[...]
        stacked[DW_BIAS : DW_BIAS + 1, :] = dw_bias[...]
        stacked[PW_BIAS : PW_BIAS + 1, :] = pw_bias[...]
        stacked[LIFT : LIFT + 3, :] = lift[...]

        own_block[...] = coarse[...]
        parts, own_rows, ncy = coarse.shape
        tail[...] = jnp.zeros_like(tail)
        if 3 * ncy <= tile:
            for k in range(parts):
                rest = coarse[k]
                for p in range(3):
                    term = rest.astype(BF16).astype(F32)
                    rest = rest - term
                    tail[k * own_rows : (k + 1) * own_rows, p * ncy : (p + 1) * ncy] = term
        for message in (first, second):
            message[channels:, :] = tail[...].astype(BF16)

        row, along = row_iota((taps.shape[0], tile)), lane_iota((taps.shape[0], tile))
        by_side = jnp.where((along & 2) != 0, 2, 0)
        chosen = jnp.concatenate(
            [(row == tap_of(m, dx, -1) + by_side).astype(BF16) for m in range(3) for dx in (-1, 0, 1)], axis=1
        )
        total, rest = None, taps[...]
        for _ in range(3):
            term = rest.astype(BF16)
            rest = rest - term.astype(F32)
            part = lax.dot_general(term, chosen, (((0,), (0,)), ((), ())), preferred_element_type=F32)
            total = part if total is None else total + part
        return total

    lane, row = lane_iota((slots, tile)), row_iota((slots, tile))
    mine = (lane >> 3) == (row & 15)
    in_even, in_odd = mine & ((lane & 4) == 0), mine & ((lane & 4) != 0)
    sublane = row_iota((ROWS, tile))

    def placed(m, k):
        both = []
        for z in range(ZOUT):
            plane = planes[ZOUT * m + z, k].astype(F32)
            cells[ZOUT * m + z, k * slots : (k + 1) * slots, :] = plane
            both.append(
                jnp.concatenate(
                    [
                        pltpu.roll(plane[x : x + ROWS], (2 + 4 * z + 8 * x) % tile, 1, stride=8, stride_axis=0)
                        for x in range(0, slots, ROWS)
                    ],
                    axis=0,
                )
            )
        rows = jnp.where(in_even, both[0], jnp.where(in_odd, both[1], 0.0))
        return rows[0:ROWS] + rows[ROWS : 2 * ROWS], rows[2 * ROWS :]

    def summed(m, k, step):
        if step == 0:
            return placed(m, k)
        one, two = summed(m, k, step // 2), summed(m, k + step, step // 2)
        turn = (sublane & step) != 0
        return tuple(
            jnp.where(turn, b, a) + pltpu.roll(jnp.where(turn, a, b), step, 0) for a, b in zip(one, two)
        )

    for m in range(3):
        for part in range(2):
            copy_of(m, part).wait()
            for c in range(part * half_of, (part + 1) * half_of, ROWS):
                for half, total in enumerate(summed(m, c, ROWS // 2)):
                    picked[m, half, c : c + ROWS, :] = total
        if m == 0:
            scale = weights_by_lane()
    width = widths_here[lax.axis_index("gx")]

    shape = (channels, tile)
    lane = lane_iota(shape)
    on_left = (lane & 2) != 0
    packed = [None, None]
    for m in range(3):
        low, high = (jnp.where(16 * half + (lane >> 3) < width, picked[m, half], 0.0) for half in range(2))
        moved = {
            -1: tuple(
                pltpu.roll(jnp.where(lane < tile - 16, one, two), 16, 1) for one, two in ((low, high), (high, low))
            ),
            0: (low, high),
            1: tuple(
                pltpu.roll(jnp.where(lane >= 16, one, two), tile - 16, 1) for one, two in ((low, high), (high, low))
            ),
        }
        for dx in (-1, 0, 1):
            begin = (3 * m + dx + 1) * tile
            for half in range(2):
                term = scale[:, begin : begin + tile] * moved[dx][half]
                packed[half] = term if packed[half] is None else packed[half] + term
    left = jnp.where(on_left, packed[0], pltpu.roll(packed[1], tile - 2, 1))
    right = jnp.where(on_left, pltpu.roll(packed[1], 2, 1), packed[0])
    first[0:channels, :] = right.astype(BF16)
    second[0:channels, :] = left.astype(BF16)


def shifted_sum(before, centre, after):
    lane = lane_iota(centre.shape)
    tile = centre.shape[-1]
    before = jnp.where(lane < 2, 0.0, pltpu.roll(before, 2, 1))
    after = jnp.where(lane >= tile - 2, 0.0, pltpu.roll(after, tile - 2, 1))
    return centre + before + after


def convolve_block(cells, weights, depth, b, first_block):
    channels = weights.shape[1]
    slots = cells.shape[1] // channels
    at = pl.ds(pl.multiple_of(b * ROWS, ROWS), ROWS)
    to = pl.ds(pl.multiple_of((b - first_block) * ROWS, ROWS), ROWS)
    tap = [weights[t, at, :] for t in range(27)]
    for z in range(ZOUT):
        for parity in range(2):
            sums = {}
            for x in range(parity, slots, 2):
                rows = [cells[z + ZOUT * m, pl.ds(b * (ROWS * slots) + x, ROWS, stride=slots), :] for m in range(3)]
                for m in range(3):
                    for dx in (1, 0, -1):
                        out = x - 2 * dx
                        if 0 <= out < slots:
                            for dy in (-1, 0, 1):
                                term = tap[tap_of(m, dx, dy)] * rows[m]
                                key = (out, dy)
                                sums[key] = sums[key] + term if key in sums else term
                for out in [x - 2] if x + 2 < slots else [x - 2, x]:
                    if out >= 0:
                        depth[z, out, to, :] = shifted_sum(*(sums.pop((out, dy)) for dy in (-1, 0, 1)))


def spread_kernel(widths, stacked, coarse, cells_in, cells, weights, own_block):
    width = widths[lax.axis_index("gx")]
    channels, tile = weights.shape[1:]
    slots = cells.shape[1] // channels
    own_block[...] = coarse[...]
    turned = jnp.transpose(stacked[...])
    for t in range(stacked.shape[0]):
        weights[t] = jnp.broadcast_to(turned[:, t : t + 1], (channels, tile))
    for r in range(2):

        @pl.when(width + r < slots)
        def _():
            for z in range(cells.shape[0]):
                cells[z, pl.ds(width + r, channels, stride=slots), :] = jnp.zeros((channels, tile), F32)


def conv_kernel(widths, cells, weights, depth, rims):
    width = widths[lax.axis_index("gx")]
    channels, tile = weights.shape[1:]
    slots = cells.shape[1] // channels
    for b in range(channels // ROWS):
        at = slice(b * ROWS, (b + 1) * ROWS)
        for side, dx in enumerate((1, -1)):
            tap = [[weights[tap_of(m, dx, dy), at, :] for m in range(3)] for dy in (-1, 0, 1)]
            for r in range(2):
                x = r if side == 0 else width - 2 + r
                for z in range(ZOUT):
                    rows = [
                        cells[z + ZOUT * m, pl.ds(b * (ROWS * slots) + x, ROWS, stride=slots), :] for m in range(3)
                    ]
                    parts = [sum(weight * row for weight, row in zip(weights_of, rows)) for weights_of in tap]
                    rims[z, 2 * side + r, at, :] = shifted_sum(*parts)

    def convolve(b, carry):
        convolve_block(cells, weights, depth, b, 0)
        return carry

    lax.fori_loop(0, SPLIT, convolve, 0)


def edge_term(edge, z, x):
    tile = edge.shape[2]
    begin = 8 * (x & 15) + 4 * z
    cells = pltpu.roll(edge[(x >> 4) & 1], (tile - 2 - begin) & (tile - 1), 1)
    lane = lane_iota(cells.shape)
    return jnp.where((lane < 2) | (lane >= tile - 2), cells, 0.0)


def rim_kernel(widths, first, second, rims, edge, far, near):
    width = widths[lax.axis_index("gx")]
    _, _, channels, tile = rims.shape
    left, right = first[0:channels, :].astype(F32), second[0:channels, :].astype(F32)
    on_left = (lane_iota((channels, tile)) & 2) != 0
    edge[0] = jnp.where(on_left, pltpu.roll(left, 2, 1), pltpu.roll(right, tile - 2, 1))
    edge[1] = jnp.where(on_left, left, right)
    even = is_even("gx")
    for z in range(ZOUT):
        for r in range(2):
            to_lower = rims[z, r] + edge_term(edge, z, r - 2)
            to_upper = rims[z, 2 + r] + edge_term(edge, z, width + r)
            at = slice((2 * z + r) * channels, (2 * z + r + 1) * channels)
            near[at, :] = jnp.where(even, to_upper, to_lower).astype(BF16)
            far[at, :] = jnp.where(even, to_lower, to_upper).astype(BF16)


def slab_start(widths):
    slab = lax.axis_index("gx")
    start = jnp.int32(0)
    for d in range(widths.shape[0]):
        start = start + jnp.where(d < slab, widths[d], 0)
    return start


def depth_row(weights, depths, edge, z, x):
    own = jnp.concatenate([depth[z, x] for depth in depths], axis=0)
    return own + weights[DW_BIAS] + edge_term(edge, z, x)


def base_row(cells, lifted, phase, z, x):
    channels = lifted.shape[1]
    slots = cells.shape[1] // channels
    return cells[2 + z, pl.ds(x, channels, stride=slots), :] + lifted[lax.div(phase + x, CF)]


def active(weights, mixed):
    mixed = mixed + weights[PW_BIAS]
    return jnp.maximum(mixed, 0.2 * mixed)


def rest_kernel(edge, cells, weights, rest):
    def convolve(b, carry):
        convolve_block(cells, weights, rest, b, SPLIT)
        return carry

    lax.fori_loop(SPLIT, weights.shape[1] // ROWS, convolve, 0)


def mix_kernel(gathered, widths, mix, cells, weights, depth, rest, edge, *refs):
    if gathered:
        coarse, value, ends, bases, lifted, across = refs
        parts, ncx, ncy = coarse.shape
    else:
        first, second, own_block, opposite, value, ends, bases, lifted, across, blocks = refs
        parts, own_rows, ncy = own_block.shape
        ncx = 4 * own_rows
    width = widths[lax.axis_index("gx")]
    here = lax.axis_index("gy")
    start = slab_start(widths)
    phase = lax.rem(start, CF)
    channels, tile = weights.shape[1:]
    slots = cells.shape[1] // channels

    if not gathered:
        count = parts * own_rows
        for message, owner in ((first, lax.rem(here + 3, 4)), (second, lax.rem(here + 1, 4))):
            terms = message[channels:, :].astype(F32)[0:count, :]
            sums = terms[:, 0:ncy] + terms[:, ncy : 2 * ncy] + terms[:, 2 * ncy : 3 * ncy]
            for k in range(parts):
                blocks[k, pl.ds(owner * own_rows, own_rows), :] = sums[k * own_rows : (k + 1) * own_rows]
        for block, owner in ((own_block, here), (opposite, lax.rem(here + 2, 4))):
            for k in range(parts):
                blocks[k, pl.ds(owner * own_rows, own_rows), :] = block[k]
    shape = (ncy, tile)
    cell = row_iota(shape) * CF
    place = lane_iota(shape) + here * tile
    along_y = ((place >= cell) & (place < cell + CF)).astype(F32)
    for k in range(parts):
        block = coarse[k] if gathered else blocks[k]
        across[k] = jnp.dot(block, along_y, precision=lax.Precision.HIGHEST, preferred_element_type=F32)
    for i in range(3):
        cell = lax.rem(lax.div(start, CF) + i, ncx)
        total = None
        for k in range(parts):
            term = weights[LIFT + k] * across[k, pl.ds(cell, 1), :]
            total = term if total is None else total + term
        lifted[i] = total

    group = 4
    wide = jnp.concatenate([mix[...]] * group, axis=1)
    wide = jnp.concatenate([wide] * group, axis=0)
    size = group * channels
    row, column = row_iota((size, size)), lane_iota((size, size))
    same = sum(
        ((row >= i * channels) & (row < (i + 1) * channels) & (column >= i * channels) & (column < (i + 1) * channels)).astype(F32)
        for i in range(group)
    )
    mixer = jnp.where(same > 0, wide.astype(F32), 0.0).astype(BF16)

    for x in range(0, slots, group):
        depths = [
            jnp.concatenate([depth_row(weights, (depth, rest), edge, z, x + i) for i in range(group)], axis=0).astype(BF16)
            for z in range(ZOUT)
        ]
        mixed = jnp.dot(mixer, jnp.concatenate(depths, axis=1), preferred_element_type=F32)
        for i in range(group):
            for z in range(ZOUT):
                part = mixed[i * channels : (i + 1) * channels, z * tile : (z + 1) * tile]
                part = active(weights, part) + base_row(cells, lifted, phase, z, x + i)
                value[z, pl.ds(x + i, channels, stride=slots), :] = jnp.where(x + i < width, part, 0.0)
    for z in range(ZOUT):
        for i, x in enumerate((0, 1, width - 2, width - 1)):
            ends[z, i] = depth_row(weights, (depth, rest), edge, z, x)
            bases[z, i] = base_row(cells, lifted, phase, z, x)


def finish_kernel(widths, mix, weights, ends, bases, far, near, value_in, out, value, block, sems):
    width = widths[lax.axis_index("gx")]
    channels, tile = weights.shape[1:]
    slots = block.shape[2]
    even = is_even("gx")
    mixed = []
    for z in range(ZOUT):
        sums = []
        for i in range(4):
            at = slice((2 * z + i % 2) * channels, (2 * z + i % 2 + 1) * channels)
            one, two = far[at, :].astype(F32), near[at, :].astype(F32)
            arrived = jnp.where(even, one, two) if i < 2 else jnp.where(even, two, one)
            sums.append((ends[z, i] + arrived).astype(BF16))
        mixed.append(jnp.dot(mix[...], jnp.concatenate(sums, axis=1), preferred_element_type=F32))
    copies = []
    for z in range(ZOUT):
        for i, x in enumerate((0, 1, width - 2, width - 1)):
            value[z, pl.ds(x, channels, stride=slots), :] = (
                active(weights, mixed[z][:, i * tile : (i + 1) * tile]) + bases[z, i]
            )
        for part in range(channels // CHUNK):
            for o in range(part * CHUNK, (part + 1) * CHUNK):
                block[z, o] = value[z, o * slots : (o + 1) * slots, :].astype(BF16)
            part_of = pl.ds(part * CHUNK, CHUNK)
            copy = pltpu.make_async_copy(block.at[z, part_of], out.at[z, part_of], sems.at[part, z])
            copy.start()
            copies.append(copy)
    for copy in copies:
        copy.wait()


def shards(feature, widths, dw_weight, dw_bias, pw_weight, pw_bias, lift_weight, coarse):
    planes, channels, slots, tile = feature.shape
    ny = lax.axis_size("gy")
    parts, own_rows, ncy = coarse.shape
    gathered = ny != 4
    ncx = ny * own_rows
    smem = pl.BlockSpec(memory_space=pltpu.SMEM)
    vmem = pl.BlockSpec(memory_space=pltpu.VMEM)
    hbm = pl.BlockSpec(memory_space=pltpu.HBM)
    params = pltpu.CompilerParams(vmem_limit_bytes=VMEM_BYTES)
    shape = jax.ShapeDtypeStruct
    strip = shape((channels + 16, tile), BF16)
    cells_shape = pltpu.VMEM((planes, channels * slots, tile), F32)
    value_shape = pltpu.VMEM((ZOUT, channels * slots, tile), F32)
    message = shape((2 * ZOUT * channels, tile), BF16)

    def swapped(array, axis, first):
        count = lax.axis_size(axis)
        pairs = []
        for i in range(first, count + first, 2):
            a, b = i % count, (i + 1) % count
            pairs += [(a, b), (b, a)]
        return lax.ppermute(array, axis, pairs)

    def pinned(array):
        return pltpu.with_memory_space_constraint(array, pltpu.HBM)

    if gathered:
        every = lax.all_gather(coarse, "gy", axis=1, tiled=True)
    small = (
        widths,
        dw_weight,
        dw_bias.reshape(1, channels),
        pw_bias.reshape(1, channels),
        lift_weight.T,
        coarse,
    )
    cells, first, second, stacked, block, slab_widths = pl.pallas_call(
        pack_kernel,
        out_shape=(
            cells_shape,
            strip,
            strip,
            pltpu.VMEM((32, channels), F32),
            pltpu.VMEM(coarse.shape, F32),
            pltpu.SMEM(widths.shape, jnp.int32),
        ),
        in_specs=[hbm] * 7,
        out_specs=(vmem,) * 5 + (smem,),
        scratch_shapes=[
            pltpu.VMEM(feature.shape, BF16),
            pltpu.SMEM(widths.shape, jnp.int32),
            pltpu.VMEM(dw_weight.shape, F32),
            pltpu.VMEM((1, channels), F32),
            pltpu.VMEM((1, channels), F32),
            pltpu.VMEM((parts, channels), F32),
            pltpu.VMEM(coarse.shape, F32),
            pltpu.VMEM((16, tile), F32),
            pltpu.VMEM((3, 2, channels, tile), F32),
            pltpu.SemaphoreType.DMA((3, 2)),
            pltpu.SemaphoreType.DMA((len(small),)),
        ],
        compiler_params=params,
    )(pinned(feature), *(pinned(array) for array in small))
    first = lax.ppermute(first, "gy", [(i, (i + 1) % ny) for i in range(ny)])
    second = lax.ppermute(second, "gy", [((i + 1) % ny, i) for i in range(ny)])
    early = SPLIT * ROWS
    cells, weights, own_block = pl.pallas_call(
        spread_kernel,
        out_shape=(cells_shape, pltpu.VMEM((32, channels, tile), F32), pltpu.VMEM(coarse.shape, F32)),
        in_specs=[smem] + [vmem] * 3,
        out_specs=(vmem,) * 3,
        input_output_aliases={3: 0},
        compiler_params=params,
        cost_estimate=pl.CostEstimate(flops=10**8, bytes_accessed=10**6, transcendentals=0),
    )(slab_widths, stacked, block, cells)
    if not gathered:
        opposite = lax.ppermute(own_block, "gy", [(i, (i + 2) % 4) for i in range(4)])
    depth, rims = pl.pallas_call(
        conv_kernel,
        out_shape=(
            pltpu.VMEM((ZOUT, slots, early, tile), F32),
            pltpu.VMEM((ZOUT, 4, channels, tile), F32),
        ),
        in_specs=[smem] + [vmem] * 2,
        out_specs=(vmem,) * 2,
        compiler_params=params,
        cost_estimate=pl.CostEstimate(flops=10**9, bytes_accessed=10**6, transcendentals=0),
    )(slab_widths, cells, weights)
    edge, far, near = pl.pallas_call(
        rim_kernel,
        out_shape=(pltpu.VMEM((2, channels, tile), F32), message, message),
        in_specs=[smem] + [vmem] * 3,
        out_specs=(vmem,) * 3,
        compiler_params=params,
    )(slab_widths, first, second, rims)
    far = swapped(far, "gx", 1)
    near = swapped(near, "gx", 0)
    blocks = (every,) if gathered else (first, second, own_block, opposite)
    rest = pl.pallas_call(
        rest_kernel,
        out_shape=pltpu.VMEM((ZOUT, slots, channels - early, tile), F32),
        in_specs=[vmem] * 3,
        out_specs=vmem,
        compiler_params=params,
        cost_estimate=pl.CostEstimate(flops=10**9, bytes_accessed=10**6, transcendentals=0),
    )(edge, cells, weights)
    ends_shape = pltpu.VMEM((ZOUT, 4, channels, tile), F32)
    value, ends, bases = pl.pallas_call(
        functools.partial(mix_kernel, gathered),
        out_shape=(value_shape, ends_shape, ends_shape),
        in_specs=[smem] + [vmem] * (6 + len(blocks)),
        out_specs=(vmem,) * 3,
        scratch_shapes=[pltpu.VMEM((3, channels, tile), F32), pltpu.VMEM((parts, ncx, tile), F32)]
        + ([] if gathered else [pltpu.VMEM((parts, ncx, ncy), F32)]),
        compiler_params=params,
        cost_estimate=pl.CostEstimate(flops=10**9, bytes_accessed=10**6, transcendentals=0),
    )(slab_widths, pw_weight, cells, weights, depth, rest, edge, *blocks)
    out, _ = pl.pallas_call(
        finish_kernel,
        out_shape=(shape((ZOUT, channels, slots, tile), BF16), value_shape),
        in_specs=[smem] + [vmem] * 7,
        out_specs=(hbm, vmem),
        scratch_shapes=[
            pltpu.VMEM((ZOUT, channels, slots, tile), BF16),
            pltpu.SemaphoreType.DMA((channels // CHUNK, ZOUT)),
        ],
        input_output_aliases={7: 1},
        compiler_params=params,
    )(slab_widths, pw_weight, weights, ends, bases, far, near, value)
    return out


def solution(mesh):
    placed = (P(None, None, "gx", "gy"), P(), P(), P(), P(), P(), P(), P(None, "gy", None))
    return jax.shard_map(
        shards, mesh=mesh, in_specs=placed, out_specs=P(None, None, "gx", "gy"), check_vma=False
    )
```

```python
import functools

import jax
import jax.numpy as jnp
from jax import lax
from jax.experimental import pallas as pl
from jax.experimental.pallas import tpu as pltpu
from jax.sharding import PartitionSpec as P

XW = 16
ZOUT = 2
CF = 16
ROWS = 8
SPLIT = 2
CHUNK = 16
DW_BIAS, PW_BIAS, LIFT = 27, 28, 29
F32 = jnp.float32
BF16 = jnp.bfloat16
VMEM_BYTES = 14 * 1024 * 1024


def lane_iota(shape):
    return lax.broadcasted_iota(jnp.int32, shape, len(shape) - 1)


def row_iota(shape):
    return lax.broadcasted_iota(jnp.int32, shape, len(shape) - 2)


def tap_of(m, dx, dy):
    return 9 * m + 3 * (dx + 1) + (dy + 1)


def is_even(axis):
    return lax.rem(lax.axis_index(axis), 2) == 0


def pack_kernel(
    feature, widths_in, taps_in, dw_bias_in, pw_bias_in, lift_in, coarse_in,
    cells, weights, first, second, own_block, widths,
    planes, widths_here, taps, dw_bias, pw_bias, lift, coarse, stacked, tail, picked, sems, small_sems,
):
    count, channels, slots, tile = feature.shape

    half_of = channels // 2

    def copy_of(m, part):
        at = (pl.ds(ZOUT * m, ZOUT), pl.ds(part * half_of, half_of))
        return pltpu.make_async_copy(feature.at[at], planes.at[at], sems.at[m, part])

    small = [
        pltpu.make_async_copy(source, target, small_sems.at[i])
        for i, (source, target) in enumerate(
            (
                (widths_in, widths_here),
                (taps_in, taps),
                (dw_bias_in, dw_bias),
                (pw_bias_in, pw_bias),
                (lift_in, lift),
                (coarse_in, coarse),
            )
        )
    ]
    for copy in small:
        copy.start()
    for m in range(3):
        for part in range(2):
            copy_of(m, part).start()
    def weights_by_lane():
        for copy in small:
            copy.wait()
        for d in range(widths.shape[0]):
            widths[d] = widths_here[d]
        stacked[0:DW_BIAS, :] = taps[...]
        stacked[DW_BIAS : DW_BIAS + 1, :] = dw_bias[...]
        stacked[PW_BIAS : PW_BIAS + 1, :] = pw_bias[...]
        stacked[LIFT : LIFT + 3, :] = lift[...]
        turned = jnp.transpose(stacked[...])
        for t in range(stacked.shape[0]):
            weights[t] = jnp.broadcast_to(turned[:, t : t + 1], (channels, tile))

        own_block[...] = coarse[...]
        parts, own_rows, ncy = coarse.shape
        tail[...] = jnp.zeros_like(tail)
        if 3 * ncy <= tile:
            for k in range(parts):
                rest = coarse[k]
                for p in range(3):
                    term = rest.astype(BF16).astype(F32)
                    rest = rest - term
                    tail[k * own_rows : (k + 1) * own_rows, p * ncy : (p + 1) * ncy] = term
        for message in (first, second):
            message[channels:, :] = tail[...].astype(BF16)

        row, along = row_iota((taps.shape[0], tile)), lane_iota((taps.shape[0], tile))
        by_side = jnp.where((along & 2) != 0, 2, 0)
        chosen = jnp.concatenate(
            [(row == tap_of(m, dx, -1) + by_side).astype(BF16) for m in range(3) for dx in (-1, 0, 1)], axis=1
        )
        total, rest = None, taps[...]
        for _ in range(3):
            term = rest.astype(BF16)
            rest = rest - term.astype(F32)
            part = lax.dot_general(term, chosen, (((0,), (0,)), ((), ())), preferred_element_type=F32)
            total = part if total is None else total + part
        return total

    lane, row = lane_iota((slots, tile)), row_iota((slots, tile))
    mine = (lane >> 3) == (row & 15)
    in_even, in_odd = mine & ((lane & 4) == 0), mine & ((lane & 4) != 0)
    sublane = row_iota((ROWS, tile))

    def placed(m, k):
        both = []
        for z in range(ZOUT):
            plane = planes[ZOUT * m + z, k].astype(F32)
            cells[ZOUT * m + z, k * slots : (k + 1) * slots, :] = plane
            both.append(
                jnp.concatenate(
                    [
                        pltpu.roll(plane[x : x + ROWS], (2 + 4 * z + 8 * x) % tile, 1, stride=8, stride_axis=0)
                        for x in range(0, slots, ROWS)
                    ],
                    axis=0,
                )
            )
        rows = jnp.where(in_even, both[0], jnp.where(in_odd, both[1], 0.0))
        return rows[0:ROWS] + rows[ROWS : 2 * ROWS], rows[2 * ROWS :]

    def summed(m, k, step):
        if step == 0:
            return placed(m, k)
        one, two = summed(m, k, step // 2), summed(m, k + step, step // 2)
        turn = (sublane & step) != 0
        return tuple(
            jnp.where(turn, b, a) + pltpu.roll(jnp.where(turn, a, b), step, 0) for a, b in zip(one, two)
        )

    for m in range(3):
        for part in range(2):
            copy_of(m, part).wait()
            for c in range(part * half_of, (part + 1) * half_of, ROWS):
                for half, total in enumerate(summed(m, c, ROWS // 2)):
                    picked[m, half, c : c + ROWS, :] = total
        if m == 0:
            scale = weights_by_lane()
    width = widths_here[lax.axis_index("gx")]

    shape = (channels, tile)
    lane = lane_iota(shape)
    on_left = (lane & 2) != 0
    packed = [None, None]
    for m in range(3):
        low, high = (jnp.where(16 * half + (lane >> 3) < width, picked[m, half], 0.0) for half in range(2))
        moved = {
            -1: tuple(
                pltpu.roll(jnp.where(lane < tile - 16, one, two), 16, 1) for one, two in ((low, high), (high, low))
            ),
            0: (low, high),
            1: tuple(
                pltpu.roll(jnp.where(lane >= 16, one, two), tile - 16, 1) for one, two in ((low, high), (high, low))
            ),
        }
        for dx in (-1, 0, 1):
            begin = (3 * m + dx + 1) * tile
            for half in range(2):
                term = scale[:, begin : begin + tile] * moved[dx][half]
                packed[half] = term if packed[half] is None else packed[half] + term
    left = jnp.where(on_left, packed[0], pltpu.roll(packed[1], tile - 2, 1))
    right = jnp.where(on_left, pltpu.roll(packed[1], 2, 1), packed[0])
    first[0:channels, :] = right.astype(BF16)
    second[0:channels, :] = left.astype(BF16)


def shifted_sum(before, centre, after):
    lane = lane_iota(centre.shape)
    tile = centre.shape[-1]
    before = jnp.where(lane < 2, 0.0, pltpu.roll(before, 2, 1))
    after = jnp.where(lane >= tile - 2, 0.0, pltpu.roll(after, tile - 2, 1))
    return centre + before + after


def convolve_block(cells, weights, depth, b, first_block):
    channels = weights.shape[1]
    slots = cells.shape[1] // channels
    at = pl.ds(pl.multiple_of(b * ROWS, ROWS), ROWS)
    to = pl.ds(pl.multiple_of((b - first_block) * ROWS, ROWS), ROWS)
    tap = [weights[t, at, :] for t in range(27)]
    for z in range(ZOUT):
        for parity in range(2):
            sums = {}
            for x in range(parity, slots, 2):
                rows = [cells[z + ZOUT * m, pl.ds(b * (ROWS * slots) + x, ROWS, stride=slots), :] for m in range(3)]
                for m in range(3):
                    for dx in (1, 0, -1):
                        out = x - 2 * dx
                        if 0 <= out < slots:
                            for dy in (-1, 0, 1):
                                term = tap[tap_of(m, dx, dy)] * rows[m]
                                key = (out, dy)
                                sums[key] = sums[key] + term if key in sums else term
                for out in [x - 2] if x + 2 < slots else [x - 2, x]:
                    if out >= 0:
                        depth[z, out, to, :] = shifted_sum(*(sums.pop((out, dy)) for dy in (-1, 0, 1)))


def outer_kernel(widths, weights, coarse, cells_in, cells, rims, own_block):
    width = widths[lax.axis_index("gx")]
    channels, tile = weights.shape[1:]
    slots = cells.shape[1] // channels
    own_block[...] = coarse[...]
    for b in range(channels // ROWS):
        at = slice(b * ROWS, (b + 1) * ROWS)
        for side, dx in enumerate((1, -1)):
            tap = [[weights[tap_of(m, dx, dy), at, :] for m in range(3)] for dy in (-1, 0, 1)]
            for r in range(2):
                x = r if side == 0 else width - 2 + r
                for z in range(ZOUT):
                    rows = [
                        cells[z + ZOUT * m, pl.ds(b * (ROWS * slots) + x, ROWS, stride=slots), :] for m in range(3)
                    ]
                    parts = [sum(weight * row for weight, row in zip(weights_of, rows)) for weights_of in tap]
                    rims[z, 2 * side + r, at, :] = shifted_sum(*parts)
    for r in range(2):

        @pl.when(width + r < slots)
        def _():
            for z in range(cells.shape[0]):
                cells[z, pl.ds(width + r, channels, stride=slots), :] = jnp.zeros((channels, tile), F32)


def conv_kernel(cells, weights, depth):
    def convolve(b, carry):
        convolve_block(cells, weights, depth, b, 0)
        return carry

    lax.fori_loop(0, SPLIT, convolve, 0)


def edge_term(edge, z, x):
    tile = edge.shape[2]
    begin = 8 * (x & 15) + 4 * z
    cells = pltpu.roll(edge[(x >> 4) & 1], (tile - 2 - begin) & (tile - 1), 1)
    lane = lane_iota(cells.shape)
    return jnp.where((lane < 2) | (lane >= tile - 2), cells, 0.0)


def rim_kernel(widths, first, second, rims, edge, far, near):
    width = widths[lax.axis_index("gx")]
    _, _, channels, tile = rims.shape
    left, right = first[0:channels, :].astype(F32), second[0:channels, :].astype(F32)
    on_left = (lane_iota((channels, tile)) & 2) != 0
    edge[0] = jnp.where(on_left, pltpu.roll(left, 2, 1), pltpu.roll(right, tile - 2, 1))
    edge[1] = jnp.where(on_left, left, right)
    even = is_even("gx")
    for z in range(ZOUT):
        for r in range(2):
            to_lower = rims[z, r] + edge_term(edge, z, r - 2)
            to_upper = rims[z, 2 + r] + edge_term(edge, z, width + r)
            at = slice((2 * z + r) * channels, (2 * z + r + 1) * channels)
            near[at, :] = jnp.where(even, to_upper, to_lower).astype(BF16)
            far[at, :] = jnp.where(even, to_lower, to_upper).astype(BF16)


def slab_start(widths):
    slab = lax.axis_index("gx")
    start = jnp.int32(0)
    for d in range(widths.shape[0]):
        start = start + jnp.where(d < slab, widths[d], 0)
    return start


def depth_row(weights, depths, edge, z, x):
    own = jnp.concatenate([depth[z, x] for depth in depths], axis=0)
    return own + weights[DW_BIAS] + edge_term(edge, z, x)


def base_row(cells, lifted, phase, z, x):
    channels = lifted.shape[1]
    slots = cells.shape[1] // channels
    return cells[2 + z, pl.ds(x, channels, stride=slots), :] + lifted[lax.div(phase + x, CF)]


def active(weights, mixed):
    mixed = mixed + weights[PW_BIAS]
    return jnp.maximum(mixed, 0.2 * mixed)


def rest_kernel(edge, cells, weights, rest):
    def convolve(b, carry):
        convolve_block(cells, weights, rest, b, SPLIT)
        return carry

    lax.fori_loop(SPLIT, weights.shape[1] // ROWS, convolve, 0)


def mix_kernel(gathered, widths, mix, cells, weights, depth, rest, edge, *refs):
    if gathered:
        coarse, value, ends, bases, lifted, across = refs
        parts, ncx, ncy = coarse.shape
    else:
        first, second, own_block, opposite, value, ends, bases, lifted, across, blocks = refs
        parts, own_rows, ncy = own_block.shape
        ncx = 4 * own_rows
    width = widths[lax.axis_index("gx")]
    here = lax.axis_index("gy")
    start = slab_start(widths)
    phase = lax.rem(start, CF)
    channels, tile = weights.shape[1:]
    slots = cells.shape[1] // channels

    if not gathered:
        count = parts * own_rows
        for message, owner in ((first, lax.rem(here + 3, 4)), (second, lax.rem(here + 1, 4))):
            terms = message[channels:, :].astype(F32)[0:count, :]
            sums = terms[:, 0:ncy] + terms[:, ncy : 2 * ncy] + terms[:, 2 * ncy : 3 * ncy]
            for k in range(parts):
                blocks[k, pl.ds(owner * own_rows, own_rows), :] = sums[k * own_rows : (k + 1) * own_rows]
        for block, owner in ((own_block, here), (opposite, lax.rem(here + 2, 4))):
            for k in range(parts):
                blocks[k, pl.ds(owner * own_rows, own_rows), :] = block[k]
    shape = (ncy, tile)
    cell = row_iota(shape) * CF
    place = lane_iota(shape) + here * tile
    along_y = ((place >= cell) & (place < cell + CF)).astype(F32)
    for k in range(parts):
        block = coarse[k] if gathered else blocks[k]
        across[k] = jnp.dot(block, along_y, precision=lax.Precision.HIGHEST, preferred_element_type=F32)
    for i in range(3):
        cell = lax.rem(lax.div(start, CF) + i, ncx)
        total = None
        for k in range(parts):
            term = weights[LIFT + k] * across[k, pl.ds(cell, 1), :]
            total = term if total is None else total + term
        lifted[i] = total

    group = 4
    wide = jnp.concatenate([mix[...]] * group, axis=1)
    wide = jnp.concatenate([wide] * group, axis=0)
    size = group * channels
    row, column = row_iota((size, size)), lane_iota((size, size))
    same = sum(
        ((row >= i * channels) & (row < (i + 1) * channels) & (column >= i * channels) & (column < (i + 1) * channels)).astype(F32)
        for i in range(group)
    )
    mixer = jnp.where(same > 0, wide.astype(F32), 0.0).astype(BF16)

    for x in range(0, slots, group):
        depths = [
            jnp.concatenate([depth_row(weights, (depth, rest), edge, z, x + i) for i in range(group)], axis=0).astype(BF16)
            for z in range(ZOUT)
        ]
        mixed = jnp.dot(mixer, jnp.concatenate(depths, axis=1), preferred_element_type=F32)
        for i in range(group):
            for z in range(ZOUT):
                part = mixed[i * channels : (i + 1) * channels, z * tile : (z + 1) * tile]
                part = active(weights, part) + base_row(cells, lifted, phase, z, x + i)
                value[z, pl.ds(x + i, channels, stride=slots), :] = jnp.where(x + i < width, part, 0.0)
    for z in range(ZOUT):
        for i, x in enumerate((0, 1, width - 2, width - 1)):
            ends[z, i] = depth_row(weights, (depth, rest), edge, z, x)
            bases[z, i] = base_row(cells, lifted, phase, z, x)


def finish_kernel(widths, mix, weights, ends, bases, far, near, value_in, out, value, block, sems):
    width = widths[lax.axis_index("gx")]
    channels, tile = weights.shape[1:]
    slots = block.shape[2]
    even = is_even("gx")
    mixed = []
    for z in range(ZOUT):
        sums = []
        for i in range(4):
            at = slice((2 * z + i % 2) * channels, (2 * z + i % 2 + 1) * channels)
            one, two = far[at, :].astype(F32), near[at, :].astype(F32)
            arrived = jnp.where(even, one, two) if i < 2 else jnp.where(even, two, one)
            sums.append((ends[z, i] + arrived).astype(BF16))
        mixed.append(jnp.dot(mix[...], jnp.concatenate(sums, axis=1), preferred_element_type=F32))
    copies = []
    for z in range(ZOUT):
        for i, x in enumerate((0, 1, width - 2, width - 1)):
            value[z, pl.ds(x, channels, stride=slots), :] = (
                active(weights, mixed[z][:, i * tile : (i + 1) * tile]) + bases[z, i]
            )
        for part in range(channels // CHUNK):
            for o in range(part * CHUNK, (part + 1) * CHUNK):
                block[z, o] = value[z, o * slots : (o + 1) * slots, :].astype(BF16)
            part_of = pl.ds(part * CHUNK, CHUNK)
            copy = pltpu.make_async_copy(block.at[z, part_of], out.at[z, part_of], sems.at[part, z])
            copy.start()
            copies.append(copy)
    for copy in copies:
        copy.wait()


def shards(feature, widths, dw_weight, dw_bias, pw_weight, pw_bias, lift_weight, coarse):
    planes, channels, slots, tile = feature.shape
    ny = lax.axis_size("gy")
    parts, own_rows, ncy = coarse.shape
    gathered = ny != 4
    ncx = ny * own_rows
    smem = pl.BlockSpec(memory_space=pltpu.SMEM)
    vmem = pl.BlockSpec(memory_space=pltpu.VMEM)
    hbm = pl.BlockSpec(memory_space=pltpu.HBM)
    params = pltpu.CompilerParams(vmem_limit_bytes=VMEM_BYTES)
    shape = jax.ShapeDtypeStruct
    strip = shape((channels + 16, tile), BF16)
    cells_shape = pltpu.VMEM((planes, channels * slots, tile), F32)
    value_shape = pltpu.VMEM((ZOUT, channels * slots, tile), F32)
    message = shape((2 * ZOUT * channels, tile), BF16)

    def swapped(array, axis, first):
        count = lax.axis_size(axis)
        pairs = []
        for i in range(first, count + first, 2):
            a, b = i % count, (i + 1) % count
            pairs += [(a, b), (b, a)]
        return lax.ppermute(array, axis, pairs)

    def pinned(array):
        return pltpu.with_memory_space_constraint(array, pltpu.HBM)

    if gathered:
        every = lax.all_gather(coarse, "gy", axis=1, tiled=True)
    small = (
        widths,
        dw_weight,
        dw_bias.reshape(1, channels),
        pw_bias.reshape(1, channels),
        lift_weight.T,
        coarse,
    )
    cells, weights, first, second, block, slab_widths = pl.pallas_call(
        pack_kernel,
        out_shape=(
            cells_shape,
            pltpu.VMEM((32, channels, tile), F32),
            strip,
            strip,
            pltpu.VMEM(coarse.shape, F32),
            pltpu.SMEM(widths.shape, jnp.int32),
        ),
        in_specs=[hbm] * 7,
        out_specs=(vmem,) * 5 + (smem,),
        scratch_shapes=[
            pltpu.VMEM(feature.shape, BF16),
            pltpu.SMEM(widths.shape, jnp.int32),
            pltpu.VMEM(dw_weight.shape, F32),
            pltpu.VMEM((1, channels), F32),
            pltpu.VMEM((1, channels), F32),
            pltpu.VMEM((parts, channels), F32),
            pltpu.VMEM(coarse.shape, F32),
            pltpu.VMEM((32, channels), F32),
            pltpu.VMEM((16, tile), F32),
            pltpu.VMEM((3, 2, channels, tile), F32),
            pltpu.SemaphoreType.DMA((3, 2)),
            pltpu.SemaphoreType.DMA((len(small),)),
        ],
        compiler_params=params,
    )(pinned(feature), *(pinned(array) for array in small))
    first = lax.ppermute(first, "gy", [(i, (i + 1) % ny) for i in range(ny)])
    second = lax.ppermute(second, "gy", [((i + 1) % ny, i) for i in range(ny)])
    early = SPLIT * ROWS
    cells, rims, own_block = pl.pallas_call(
        outer_kernel,
        out_shape=(
            cells_shape,
            pltpu.VMEM((ZOUT, 4, channels, tile), F32),
            pltpu.VMEM(coarse.shape, F32),
        ),
        in_specs=[smem] + [vmem] * 3,
        out_specs=(vmem,) * 3,
        input_output_aliases={3: 0},
        compiler_params=params,
        cost_estimate=pl.CostEstimate(flops=10**8, bytes_accessed=10**6, transcendentals=0),
    )(slab_widths, weights, block, cells)
    if not gathered:
        opposite = lax.ppermute(own_block, "gy", [(i, (i + 2) % 4) for i in range(4)])
    depth = pl.pallas_call(
        conv_kernel,
        out_shape=pltpu.VMEM((ZOUT, slots, early, tile), F32),
        in_specs=[vmem] * 2,
        out_specs=vmem,
        compiler_params=params,
        cost_estimate=pl.CostEstimate(flops=10**9, bytes_accessed=10**6, transcendentals=0),
    )(cells, weights)
    edge, far, near = pl.pallas_call(
        rim_kernel,
        out_shape=(pltpu.VMEM((2, channels, tile), F32), message, message),
        in_specs=[smem] + [vmem] * 3,
        out_specs=(vmem,) * 3,
        compiler_params=params,
    )(slab_widths, first, second, rims)
    far = swapped(far, "gx", 1)
    near = swapped(near, "gx", 0)
    blocks = (every,) if gathered else (first, second, own_block, opposite)
    rest = pl.pallas_call(
        rest_kernel,
        out_shape=pltpu.VMEM((ZOUT, slots, channels - early, tile), F32),
        in_specs=[vmem] * 3,
        out_specs=vmem,
        compiler_params=params,
        cost_estimate=pl.CostEstimate(flops=10**9, bytes_accessed=10**6, transcendentals=0),
    )(edge, cells, weights)
    ends_shape = pltpu.VMEM((ZOUT, 4, channels, tile), F32)
    value, ends, bases = pl.pallas_call(
        functools.partial(mix_kernel, gathered),
        out_shape=(value_shape, ends_shape, ends_shape),
        in_specs=[smem] + [vmem] * (6 + len(blocks)),
        out_specs=(vmem,) * 3,
        scratch_shapes=[pltpu.VMEM((3, channels, tile), F32), pltpu.VMEM((parts, ncx, tile), F32)]
        + ([] if gathered else [pltpu.VMEM((parts, ncx, ncy), F32)]),
        compiler_params=params,
        cost_estimate=pl.CostEstimate(flops=10**9, bytes_accessed=10**6, transcendentals=0),
    )(slab_widths, pw_weight, cells, weights, depth, rest, edge, *blocks)
    out, _ = pl.pallas_call(
        finish_kernel,
        out_shape=(shape((ZOUT, channels, slots, tile), BF16), value_shape),
        in_specs=[smem] + [vmem] * 7,
        out_specs=(hbm, vmem),
        scratch_shapes=[
            pltpu.VMEM((ZOUT, channels, slots, tile), BF16),
            pltpu.SemaphoreType.DMA((channels // CHUNK, ZOUT)),
        ],
        input_output_aliases={7: 1},
        compiler_params=params,
    )(slab_widths, pw_weight, weights, ends, bases, far, near, value)
    return out


def solution(mesh):
    placed = (P(None, None, "gx", "gy"), P(), P(), P(), P(), P(), P(), P(None, "gy", None))
    return jax.shard_map(
        shards, mesh=mesh, in_specs=placed, out_specs=P(None, None, "gx", "gy"), check_vma=False
    )
```

```python
import functools

import jax
import jax.numpy as jnp
from jax import lax
from jax.experimental import pallas as pl
from jax.experimental.pallas import tpu as pltpu
from jax.sharding import PartitionSpec as P

XW = 16
ZOUT = 2
CF = 16
ROWS = 8
SPLIT = 1
CHUNK = 16
DW_BIAS, PW_BIAS, LIFT = 27, 28, 29
F32 = jnp.float32
BF16 = jnp.bfloat16
VMEM_BYTES = 14 * 1024 * 1024


def lane_iota(shape):
    return lax.broadcasted_iota(jnp.int32, shape, len(shape) - 1)


def row_iota(shape):
    return lax.broadcasted_iota(jnp.int32, shape, len(shape) - 2)


def tap_of(m, dx, dy):
    return 9 * m + 3 * (dx + 1) + (dy + 1)


def is_even(axis):
    return lax.rem(lax.axis_index(axis), 2) == 0


def pack_kernel(
    feature, widths_in, taps_in, dw_bias_in, pw_bias_in, lift_in, coarse_in,
    cells, weights, first, second, own_block, widths,
    planes, widths_here, taps, dw_bias, pw_bias, lift, coarse, stacked, tail, picked, sems, small_sems,
):
    count, channels, slots, tile = feature.shape

    half_of = channels // 2

    def copy_of(m, part):
        at = (pl.ds(ZOUT * m, ZOUT), pl.ds(part * half_of, half_of))
        return pltpu.make_async_copy(feature.at[at], planes.at[at], sems.at[m, part])

    small = [
        pltpu.make_async_copy(source, target, small_sems.at[i])
        for i, (source, target) in enumerate(
            (
                (widths_in, widths_here),
                (taps_in, taps),
                (dw_bias_in, dw_bias),
                (pw_bias_in, pw_bias),
                (lift_in, lift),
                (coarse_in, coarse),
            )
        )
    ]
    for copy in small:
        copy.start()
    for m in range(3):
        for part in range(2):
            copy_of(m, part).start()
    def weights_by_lane():
        for copy in small:
            copy.wait()
        for d in range(widths.shape[0]):
            widths[d] = widths_here[d]
        stacked[0:DW_BIAS, :] = taps[...]
        stacked[DW_BIAS : DW_BIAS + 1, :] = dw_bias[...]
        stacked[PW_BIAS : PW_BIAS + 1, :] = pw_bias[...]
        stacked[LIFT : LIFT + 3, :] = lift[...]
        turned = jnp.transpose(stacked[...])
        for t in range(stacked.shape[0]):
            weights[t] = jnp.broadcast_to(turned[:, t : t + 1], (channels, tile))

        own_block[...] = coarse[...]
        parts, own_rows, ncy = coarse.shape
        tail[...] = jnp.zeros_like(tail)
        if 3 * ncy <= tile:
            for k in range(parts):
                rest = coarse[k]
                for p in range(3):
                    term = rest.astype(BF16).astype(F32)
                    rest = rest - term
                    tail[k * own_rows : (k + 1) * own_rows, p * ncy : (p + 1) * ncy] = term
        for message in (first, second):
            message[channels:, :] = tail[...].astype(BF16)

        row, along = row_iota((taps.shape[0], tile)), lane_iota((taps.shape[0], tile))
        by_side = jnp.where((along & 2) != 0, 2, 0)
        chosen = jnp.concatenate(
            [(row == tap_of(m, dx, -1) + by_side).astype(BF16) for m in range(3) for dx in (-1, 0, 1)], axis=1
        )
        total, rest = None, taps[...]
        for _ in range(3):
            term = rest.astype(BF16)
            rest = rest - term.astype(F32)
            part = lax.dot_general(term, chosen, (((0,), (0,)), ((), ())), preferred_element_type=F32)
            total = part if total is None else total + part
        return total

    shape = (ZOUT * tile, tile)
    row, lane = row_iota(shape), lane_iota(shape)
    column = jnp.where((lane & 3) < 2, tile - 2 + (lane & 3), (lane & 3) - 2)
    picks = (row == jnp.where((lane & 4) != 0, tile + column, column)).astype(BF16)
    mine = (lane_iota((slots, tile)) >> 3) == (row_iota((slots, tile)) & 15)
    sublane = row_iota((ROWS, tile))

    def summed(placed, step):
        if step == 0:
            rows = jnp.where(mine, placed, 0.0)
            return rows[0:ROWS] + rows[ROWS : 2 * ROWS], rows[2 * ROWS :]
        one, two = summed(placed[: step * slots], step // 2), summed(placed[step * slots :], step // 2)
        turn = (sublane & step) != 0
        return tuple(
            jnp.where(turn, b, a) + pltpu.roll(jnp.where(turn, a, b), step, 0) for a, b in zip(one, two)
        )

    for m in range(3):
        for part in range(2):
            copy_of(m, part).wait()
            for c in range(part * half_of, (part + 1) * half_of, CHUNK):
                rows = [planes[ZOUT * m + z, c : c + CHUNK].reshape(CHUNK * slots, tile) for z in range(ZOUT)]
                for z in range(ZOUT):
                    cells[ZOUT * m + z, c * slots : (c + CHUNK) * slots, :] = rows[z].astype(F32)
                placed = jnp.dot(jnp.concatenate(rows, axis=1), picks, preferred_element_type=F32)
                for k in range(0, CHUNK, ROWS):
                    for half, total in enumerate(summed(placed[k * slots : (k + ROWS) * slots], ROWS // 2)):
                        picked[m, half, c + k : c + k + ROWS, :] = total
        if m == 0:
            scale = weights_by_lane()
    width = widths_here[lax.axis_index("gx")]

    shape = (channels, tile)
    lane = lane_iota(shape)
    on_left = (lane & 2) != 0
    packed = [None, None]
    for m in range(3):
        low, high = (jnp.where(16 * half + (lane >> 3) < width, picked[m, half], 0.0) for half in range(2))
        moved = {
            -1: tuple(
                pltpu.roll(jnp.where(lane < tile - 16, one, two), 16, 1) for one, two in ((low, high), (high, low))
            ),
            0: (low, high),
            1: tuple(
                pltpu.roll(jnp.where(lane >= 16, one, two), tile - 16, 1) for one, two in ((low, high), (high, low))
            ),
        }
        for dx in (-1, 0, 1):
            begin = (3 * m + dx + 1) * tile
            for half in range(2):
                term = scale[:, begin : begin + tile] * moved[dx][half]
                packed[half] = term if packed[half] is None else packed[half] + term
    left = jnp.where(on_left, packed[0], pltpu.roll(packed[1], tile - 2, 1))
    right = jnp.where(on_left, pltpu.roll(packed[1], 2, 1), packed[0])
    first[0:channels, :] = right.astype(BF16)
    second[0:channels, :] = left.astype(BF16)


def shifted_sum(before, centre, after):
    lane = lane_iota(centre.shape)
    tile = centre.shape[-1]
    before = jnp.where(lane < 2, 0.0, pltpu.roll(before, 2, 1))
    after = jnp.where(lane >= tile - 2, 0.0, pltpu.roll(after, tile - 2, 1))
    return centre + before + after


def convolve_block(cells, weights, depth, b, first_block):
    channels = weights.shape[1]
    slots = cells.shape[1] // channels
    at = pl.ds(pl.multiple_of(b * ROWS, ROWS), ROWS)
    to = pl.ds(pl.multiple_of((b - first_block) * ROWS, ROWS), ROWS)
    tap = [weights[t, at, :] for t in range(27)]
    for z in range(ZOUT):
        for parity in range(2):
            sums = {}
            for x in range(parity, slots, 2):
                rows = [cells[z + ZOUT * m, pl.ds(b * (ROWS * slots) + x, ROWS, stride=slots), :] for m in range(3)]
                for m in range(3):
                    for dx in (1, 0, -1):
                        out = x - 2 * dx
                        if 0 <= out < slots:
                            for dy in (-1, 0, 1):
                                term = tap[tap_of(m, dx, dy)] * rows[m]
                                key = (out, dy)
                                sums[key] = sums[key] + term if key in sums else term
                for out in [x - 2] if x + 2 < slots else [x - 2, x]:
                    if out >= 0:
                        depth[z, out, to, :] = shifted_sum(*(sums.pop((out, dy)) for dy in (-1, 0, 1)))


def outer_kernel(widths, weights, coarse, cells_in, cells, rims, own_block):
    width = widths[lax.axis_index("gx")]
    channels, tile = weights.shape[1:]
    slots = cells.shape[1] // channels
    own_block[...] = coarse[...]
    for b in range(channels // ROWS):
        at = slice(b * ROWS, (b + 1) * ROWS)
        for side, dx in enumerate((1, -1)):
            tap = [[weights[tap_of(m, dx, dy), at, :] for m in range(3)] for dy in (-1, 0, 1)]
            for r in range(2):
                x = r if side == 0 else width - 2 + r
                for z in range(ZOUT):
                    rows = [
                        cells[z + ZOUT * m, pl.ds(b * (ROWS * slots) + x, ROWS, stride=slots), :] for m in range(3)
                    ]
                    parts = [sum(weight * row for weight, row in zip(weights_of, rows)) for weights_of in tap]
                    rims[z, 2 * side + r, at, :] = shifted_sum(*parts)
    for r in range(2):

        @pl.when(width + r < slots)
        def _():
            for z in range(cells.shape[0]):
                cells[z, pl.ds(width + r, channels, stride=slots), :] = jnp.zeros((channels, tile), F32)


def conv_kernel(cells, weights, depth):
    def convolve(b, carry):
        convolve_block(cells, weights, depth, b, 0)
        return carry

    lax.fori_loop(0, SPLIT, convolve, 0)


def edge_term(edge, z, x):
    tile = edge.shape[2]
    begin = 8 * (x & 15) + 4 * z
    cells = pltpu.roll(edge[(x >> 4) & 1], (tile - 2 - begin) & (tile - 1), 1)
    lane = lane_iota(cells.shape)
    return jnp.where((lane < 2) | (lane >= tile - 2), cells, 0.0)


def rim_kernel(widths, first, second, rims, edge, far, near):
    width = widths[lax.axis_index("gx")]
    _, _, channels, tile = rims.shape
    left, right = first[0:channels, :].astype(F32), second[0:channels, :].astype(F32)
    on_left = (lane_iota((channels, tile)) & 2) != 0
    edge[0] = jnp.where(on_left, pltpu.roll(left, 2, 1), pltpu.roll(right, tile - 2, 1))
    edge[1] = jnp.where(on_left, left, right)
    even = is_even("gx")
    for z in range(ZOUT):
        for r in range(2):
            to_lower = rims[z, r] + edge_term(edge, z, r - 2)
            to_upper = rims[z, 2 + r] + edge_term(edge, z, width + r)
            at = slice((2 * z + r) * channels, (2 * z + r + 1) * channels)
            near[at, :] = jnp.where(even, to_upper, to_lower).astype(BF16)
            far[at, :] = jnp.where(even, to_lower, to_upper).astype(BF16)


def slab_start(widths):
    slab = lax.axis_index("gx")
    start = jnp.int32(0)
    for d in range(widths.shape[0]):
        start = start + jnp.where(d < slab, widths[d], 0)
    return start


def depth_row(weights, depths, edge, z, x):
    own = jnp.concatenate([depth[z, x] for depth in depths], axis=0)
    return own + weights[DW_BIAS] + edge_term(edge, z, x)


def base_row(cells, lifted, phase, z, x):
    channels = lifted.shape[1]
    slots = cells.shape[1] // channels
    return cells[2 + z, pl.ds(x, channels, stride=slots), :] + lifted[lax.div(phase + x, CF)]


def active(weights, mixed):
    mixed = mixed + weights[PW_BIAS]
    return jnp.maximum(mixed, 0.2 * mixed)


def rest_kernel(edge, cells, weights, rest):
    def convolve(b, carry):
        convolve_block(cells, weights, rest, b, SPLIT)
        return carry

    lax.fori_loop(SPLIT, weights.shape[1] // ROWS, convolve, 0)


def mix_kernel(gathered, widths, mix, cells, weights, depth, rest, edge, *refs):
    if gathered:
        coarse, value, ends, bases, lifted, across = refs
        parts, ncx, ncy = coarse.shape
    else:
        first, second, own_block, opposite, value, ends, bases, lifted, across, blocks = refs
        parts, own_rows, ncy = own_block.shape
        ncx = 4 * own_rows
    width = widths[lax.axis_index("gx")]
    here = lax.axis_index("gy")
    start = slab_start(widths)
    phase = lax.rem(start, CF)
    channels, tile = weights.shape[1:]
    slots = cells.shape[1] // channels

    if not gathered:
        count = parts * own_rows
        for message, owner in ((first, lax.rem(here + 3, 4)), (second, lax.rem(here + 1, 4))):
            terms = message[channels:, :].astype(F32)[0:count, :]
            sums = terms[:, 0:ncy] + terms[:, ncy : 2 * ncy] + terms[:, 2 * ncy : 3 * ncy]
            for k in range(parts):
                blocks[k, pl.ds(owner * own_rows, own_rows), :] = sums[k * own_rows : (k + 1) * own_rows]
        for block, owner in ((own_block, here), (opposite, lax.rem(here + 2, 4))):
            for k in range(parts):
                blocks[k, pl.ds(owner * own_rows, own_rows), :] = block[k]
    shape = (ncy, tile)
    cell = row_iota(shape) * CF
    place = lane_iota(shape) + here * tile
    along_y = ((place >= cell) & (place < cell + CF)).astype(F32)
    for k in range(parts):
        block = coarse[k] if gathered else blocks[k]
        across[k] = jnp.dot(block, along_y, precision=lax.Precision.HIGHEST, preferred_element_type=F32)
    for i in range(3):
        cell = lax.rem(lax.div(start, CF) + i, ncx)
        total = None
        for k in range(parts):
            term = weights[LIFT + k] * across[k, pl.ds(cell, 1), :]
            total = term if total is None else total + term
        lifted[i] = total

    group = 4
    wide = jnp.concatenate([mix[...]] * group, axis=1)
    wide = jnp.concatenate([wide] * group, axis=0)
    size = group * channels
    row, column = row_iota((size, size)), lane_iota((size, size))
    same = sum(
        ((row >= i * channels) & (row < (i + 1) * channels) & (column >= i * channels) & (column < (i + 1) * channels)).astype(F32)
        for i in range(group)
    )
    mixer = jnp.where(same > 0, wide.astype(F32), 0.0).astype(BF16)

    for x in range(0, slots, group):
        depths = [
            jnp.concatenate([depth_row(weights, (depth, rest), edge, z, x + i) for i in range(group)], axis=0).astype(BF16)
            for z in range(ZOUT)
        ]
        mixed = jnp.dot(mixer, jnp.concatenate(depths, axis=1), preferred_element_type=F32)
        for i in range(group):
            for z in range(ZOUT):
                part = mixed[i * channels : (i + 1) * channels, z * tile : (z + 1) * tile]
                part = active(weights, part) + base_row(cells, lifted, phase, z, x + i)
                value[z, pl.ds(x + i, channels, stride=slots), :] = jnp.where(x + i < width, part, 0.0)
    for z in range(ZOUT):
        for i, x in enumerate((0, 1, width - 2, width - 1)):
            ends[z, i] = depth_row(weights, (depth, rest), edge, z, x)
            bases[z, i] = base_row(cells, lifted, phase, z, x)


def finish_kernel(widths, mix, weights, ends, bases, far, near, value_in, out, value, block, sems):
    width = widths[lax.axis_index("gx")]
    channels, tile = weights.shape[1:]
    slots = block.shape[2]
    even = is_even("gx")
    mixed = []
    for z in range(ZOUT):
        sums = []
        for i in range(4):
            at = slice((2 * z + i % 2) * channels, (2 * z + i % 2 + 1) * channels)
            one, two = far[at, :].astype(F32), near[at, :].astype(F32)
            arrived = jnp.where(even, one, two) if i < 2 else jnp.where(even, two, one)
            sums.append((ends[z, i] + arrived).astype(BF16))
        mixed.append(jnp.dot(mix[...], jnp.concatenate(sums, axis=1), preferred_element_type=F32))
    copies = []
    for z in range(ZOUT):
        for i, x in enumerate((0, 1, width - 2, width - 1)):
            value[z, pl.ds(x, channels, stride=slots), :] = (
                active(weights, mixed[z][:, i * tile : (i + 1) * tile]) + bases[z, i]
            )
        for part in range(channels // CHUNK):
            for o in range(part * CHUNK, (part + 1) * CHUNK):
                block[z, o] = value[z, o * slots : (o + 1) * slots, :].astype(BF16)
            part_of = pl.ds(part * CHUNK, CHUNK)
            copy = pltpu.make_async_copy(block.at[z, part_of], out.at[z, part_of], sems.at[part, z])
            copy.start()
            copies.append(copy)
    for copy in copies:
        copy.wait()


def shards(feature, widths, dw_weight, dw_bias, pw_weight, pw_bias, lift_weight, coarse):
    planes, channels, slots, tile = feature.shape
    ny = lax.axis_size("gy")
    parts, own_rows, ncy = coarse.shape
    gathered = ny != 4
    ncx = ny * own_rows
    smem = pl.BlockSpec(memory_space=pltpu.SMEM)
    vmem = pl.BlockSpec(memory_space=pltpu.VMEM)
    hbm = pl.BlockSpec(memory_space=pltpu.HBM)
    params = pltpu.CompilerParams(vmem_limit_bytes=VMEM_BYTES)
    shape = jax.ShapeDtypeStruct
    strip = shape((channels + 16, tile), BF16)
    cells_shape = pltpu.VMEM((planes, channels * slots, tile), F32)
    value_shape = pltpu.VMEM((ZOUT, channels * slots, tile), F32)
    message = shape((2 * ZOUT * channels, tile), BF16)

    def swapped(array, axis, first):
        count = lax.axis_size(axis)
        pairs = []
        for i in range(first, count + first, 2):
            a, b = i % count, (i + 1) % count
            pairs += [(a, b), (b, a)]
        return lax.ppermute(array, axis, pairs)

    def pinned(array):
        return pltpu.with_memory_space_constraint(array, pltpu.HBM)

    if gathered:
        every = lax.all_gather(coarse, "gy", axis=1, tiled=True)
    small = (
        widths,
        dw_weight,
        dw_bias.reshape(1, channels),
        pw_bias.reshape(1, channels),
        lift_weight.T,
        coarse,
    )
    cells, weights, first, second, block, slab_widths = pl.pallas_call(
        pack_kernel,
        out_shape=(
            cells_shape,
            pltpu.VMEM((32, channels, tile), F32),
            strip,
            strip,
            pltpu.VMEM(coarse.shape, F32),
            pltpu.SMEM(widths.shape, jnp.int32),
        ),
        in_specs=[hbm] * 7,
        out_specs=(vmem,) * 5 + (smem,),
        scratch_shapes=[
            pltpu.VMEM(feature.shape, BF16),
            pltpu.SMEM(widths.shape, jnp.int32),
            pltpu.VMEM(dw_weight.shape, F32),
            pltpu.VMEM((1, channels), F32),
            pltpu.VMEM((1, channels), F32),
            pltpu.VMEM((parts, channels), F32),
            pltpu.VMEM(coarse.shape, F32),
            pltpu.VMEM((32, channels), F32),
            pltpu.VMEM((16, tile), F32),
            pltpu.VMEM((3, 2, channels, tile), F32),
            pltpu.SemaphoreType.DMA((3, 2)),
            pltpu.SemaphoreType.DMA((len(small),)),
        ],
        compiler_params=params,
    )(pinned(feature), *(pinned(array) for array in small))
    first = lax.ppermute(first, "gy", [(i, (i + 1) % ny) for i in range(ny)])
    second = lax.ppermute(second, "gy", [((i + 1) % ny, i) for i in range(ny)])
    early = SPLIT * ROWS
    cells, rims, own_block = pl.pallas_call(
        outer_kernel,
        out_shape=(
            cells_shape,
            pltpu.VMEM((ZOUT, 4, channels, tile), F32),
            pltpu.VMEM(coarse.shape, F32),
        ),
        in_specs=[smem] + [vmem] * 3,
        out_specs=(vmem,) * 3,
        input_output_aliases={3: 0},
        compiler_params=params,
        cost_estimate=pl.CostEstimate(flops=10**8, bytes_accessed=10**6, transcendentals=0),
    )(slab_widths, weights, block, cells)
    if not gathered:
        opposite = lax.ppermute(own_block, "gy", [(i, (i + 2) % 4) for i in range(4)])
    depth = pl.pallas_call(
        conv_kernel,
        out_shape=pltpu.VMEM((ZOUT, slots, early, tile), F32),
        in_specs=[vmem] * 2,
        out_specs=vmem,
        compiler_params=params,
        cost_estimate=pl.CostEstimate(flops=10**9, bytes_accessed=10**6, transcendentals=0),
    )(cells, weights)
    edge, far, near = pl.pallas_call(
        rim_kernel,
        out_shape=(pltpu.VMEM((2, channels, tile), F32), message, message),
        in_specs=[smem] + [vmem] * 3,
        out_specs=(vmem,) * 3,
        compiler_params=params,
    )(slab_widths, first, second, rims)
    far = swapped(far, "gx", 1)
    near = swapped(near, "gx", 0)
    blocks = (every,) if gathered else (first, second, own_block, opposite)
    rest = pl.pallas_call(
        rest_kernel,
        out_shape=pltpu.VMEM((ZOUT, slots, channels - early, tile), F32),
        in_specs=[vmem] * 3,
        out_specs=vmem,
        compiler_params=params,
        cost_estimate=pl.CostEstimate(flops=10**9, bytes_accessed=10**6, transcendentals=0),
    )(edge, cells, weights)
    ends_shape = pltpu.VMEM((ZOUT, 4, channels, tile), F32)
    value, ends, bases = pl.pallas_call(
        functools.partial(mix_kernel, gathered),
        out_shape=(value_shape, ends_shape, ends_shape),
        in_specs=[smem] + [vmem] * (6 + len(blocks)),
        out_specs=(vmem,) * 3,
        scratch_shapes=[pltpu.VMEM((3, channels, tile), F32), pltpu.VMEM((parts, ncx, tile), F32)]
        + ([] if gathered else [pltpu.VMEM((parts, ncx, ncy), F32)]),
        compiler_params=params,
        cost_estimate=pl.CostEstimate(flops=10**9, bytes_accessed=10**6, transcendentals=0),
    )(slab_widths, pw_weight, cells, weights, depth, rest, edge, *blocks)
    out, _ = pl.pallas_call(
        finish_kernel,
        out_shape=(shape((ZOUT, channels, slots, tile), BF16), value_shape),
        in_specs=[smem] + [vmem] * 7,
        out_specs=(hbm, vmem),
        scratch_shapes=[
            pltpu.VMEM((ZOUT, channels, slots, tile), BF16),
            pltpu.SemaphoreType.DMA((channels // CHUNK, ZOUT)),
        ],
        input_output_aliases={7: 1},
        compiler_params=params,
    )(slab_widths, pw_weight, weights, ends, bases, far, near, value)
    return out


def solution(mesh):
    placed = (P(None, None, "gx", "gy"), P(), P(), P(), P(), P(), P(), P(None, "gy", None))
    return jax.shard_map(
        shards, mesh=mesh, in_specs=placed, out_specs=P(None, None, "gx", "gy"), check_vma=False
    )
```

```python
import functools

import jax
import jax.numpy as jnp
from jax import lax
from jax.experimental import pallas as pl
from jax.experimental.pallas import tpu as pltpu
from jax.sharding import PartitionSpec as P

XW = 16
ZOUT = 2
CF = 16
ROWS = 8
SPLIT = 1
CHUNK = 16
DW_BIAS, PW_BIAS, LIFT = 27, 28, 29
F32 = jnp.float32
BF16 = jnp.bfloat16
VMEM_BYTES = 14 * 1024 * 1024


def lane_iota(shape):
    return lax.broadcasted_iota(jnp.int32, shape, len(shape) - 1)


def row_iota(shape):
    return lax.broadcasted_iota(jnp.int32, shape, len(shape) - 2)


def tap_of(m, dx, dy):
    return 9 * m + 3 * (dx + 1) + (dy + 1)


def is_even(axis):
    return lax.rem(lax.axis_index(axis), 2) == 0


def pack_kernel(
    feature, widths_in, taps_in, dw_bias_in, pw_bias_in, lift_in, coarse_in,
    cells, weights, first, second, own_block, widths,
    planes, widths_here, taps, dw_bias, pw_bias, lift, coarse, stacked, tail, picked, sems, small_sems,
):
    count, channels, slots, tile = feature.shape

    half_of = channels // 2

    def copy_of(m, part):
        at = (pl.ds(ZOUT * m, ZOUT), pl.ds(part * half_of, half_of))
        return pltpu.make_async_copy(feature.at[at], planes.at[at], sems.at[m, part])

    small = [
        pltpu.make_async_copy(source, target, small_sems.at[i])
        for i, (source, target) in enumerate(
            (
                (widths_in, widths_here),
                (taps_in, taps),
                (dw_bias_in, dw_bias),
                (pw_bias_in, pw_bias),
                (lift_in, lift),
                (coarse_in, coarse),
            )
        )
    ]
    for copy in small:
        copy.start()
    for m in range(3):
        for part in range(2):
            copy_of(m, part).start()
    def take_small():
        for copy in small:
            copy.wait()
        for d in range(widths.shape[0]):
            widths[d] = widths_here[d]
        stacked[0:DW_BIAS, :] = taps[...]
        stacked[DW_BIAS : DW_BIAS + 1, :] = dw_bias[...]
        stacked[PW_BIAS : PW_BIAS + 1, :] = pw_bias[...]
        stacked[LIFT : LIFT + 3, :] = lift[...]
        turned = jnp.transpose(stacked[...])
        for t in range(stacked.shape[0]):
            weights[t] = jnp.broadcast_to(turned[:, t : t + 1], (channels, tile))

        own_block[...] = coarse[...]
        parts, own_rows, ncy = coarse.shape
        tail[...] = jnp.zeros_like(tail)
        if 3 * ncy <= tile:
            for k in range(parts):
                rest = coarse[k]
                for p in range(3):
                    term = rest.astype(BF16).astype(F32)
                    rest = rest - term
                    tail[k * own_rows : (k + 1) * own_rows, p * ncy : (p + 1) * ncy] = term
        for message in (first, second):
            message[channels:, :] = tail[...].astype(BF16)

    lane, row = lane_iota((slots, tile)), row_iota((slots, tile))
    mine = (lane >> 3) == (row & 15)
    in_even, in_odd = mine & ((lane & 4) == 0), mine & ((lane & 4) != 0)
    sublane = row_iota((ROWS, tile))

    def placed(m, k):
        both = []
        for z in range(ZOUT):
            plane = planes[ZOUT * m + z, k].astype(F32)
            cells[ZOUT * m + z, k * slots : (k + 1) * slots, :] = plane
            both.append(
                jnp.concatenate(
                    [
                        pltpu.roll(plane[x : x + ROWS], (2 + 4 * z + 8 * x) % tile, 1, stride=8, stride_axis=0)
                        for x in range(0, slots, ROWS)
                    ],
                    axis=0,
                )
            )
        rows = jnp.where(in_even, both[0], jnp.where(in_odd, both[1], 0.0))
        return rows[0:ROWS] + rows[ROWS : 2 * ROWS], rows[2 * ROWS :]

    def summed(m, k, step):
        if step == 0:
            return placed(m, k)
        one, two = summed(m, k, step // 2), summed(m, k + step, step // 2)
        turn = (sublane & step) != 0
        return tuple(
            jnp.where(turn, b, a) + pltpu.roll(jnp.where(turn, a, b), step, 0) for a, b in zip(one, two)
        )

    for m in range(3):
        for part in range(2):
            copy_of(m, part).wait()
            for c in range(part * half_of, (part + 1) * half_of, ROWS):
                for half, total in enumerate(summed(m, c, ROWS // 2)):
                    picked[m, half, c : c + ROWS, :] = total
        if m == 0:
            take_small()
    width = widths_here[lax.axis_index("gx")]

    shape = (channels, tile)
    lane = lane_iota(shape)
    on_left = (lane & 2) != 0
    packed = [None, None]
    for m in range(3):
        low, high = (jnp.where(16 * half + (lane >> 3) < width, picked[m, half], 0.0) for half in range(2))
        moved = {
            -1: tuple(
                pltpu.roll(jnp.where(lane < tile - 16, one, two), 16, 1) for one, two in ((low, high), (high, low))
            ),
            0: (low, high),
            1: tuple(
                pltpu.roll(jnp.where(lane >= 16, one, two), tile - 16, 1) for one, two in ((low, high), (high, low))
            ),
        }
        for dx in (-1, 0, 1):
            weight = jnp.where(on_left, weights[tap_of(m, dx, 1)], weights[tap_of(m, dx, -1)])
            for half in range(2):
                term = weight * moved[dx][half]
                packed[half] = term if packed[half] is None else packed[half] + term
    left = jnp.where(on_left, packed[0], pltpu.roll(packed[1], tile - 2, 1))
    right = jnp.where(on_left, pltpu.roll(packed[1], 2, 1), packed[0])
    first[0:channels, :] = right.astype(BF16)
    second[0:channels, :] = left.astype(BF16)


def shifted_sum(before, centre, after):
    lane = lane_iota(centre.shape)
    tile = centre.shape[-1]
    before = jnp.where(lane < 2, 0.0, pltpu.roll(before, 2, 1))
    after = jnp.where(lane >= tile - 2, 0.0, pltpu.roll(after, tile - 2, 1))
    return centre + before + after


def convolve_block(cells, weights, depth, b, first_block):
    channels = weights.shape[1]
    slots = cells.shape[1] // channels
    at = pl.ds(pl.multiple_of(b * ROWS, ROWS), ROWS)
    to = pl.ds(pl.multiple_of((b - first_block) * ROWS, ROWS), ROWS)
    tap = [weights[t, at, :] for t in range(27)]
    for z in range(ZOUT):
        for parity in range(2):
            sums = {}
            for x in range(parity, slots, 2):
                rows = [cells[z + ZOUT * m, pl.ds(b * (ROWS * slots) + x, ROWS, stride=slots), :] for m in range(3)]
                for m in range(3):
                    for dx in (1, 0, -1):
                        out = x - 2 * dx
                        if 0 <= out < slots:
                            for dy in (-1, 0, 1):
                                term = tap[tap_of(m, dx, dy)] * rows[m]
                                key = (out, dy)
                                sums[key] = sums[key] + term if key in sums else term
                for out in [x - 2] if x + 2 < slots else [x - 2, x]:
                    if out >= 0:
                        depth[z, out, to, :] = shifted_sum(*(sums.pop((out, dy)) for dy in (-1, 0, 1)))


def outer_kernel(widths, weights, coarse, cells_in, cells, rims, own_block):
    width = widths[lax.axis_index("gx")]
    channels, tile = weights.shape[1:]
    slots = cells.shape[1] // channels
    own_block[...] = coarse[...]
    for b in range(channels // ROWS):
        at = slice(b * ROWS, (b + 1) * ROWS)
        for side, dx in enumerate((1, -1)):
            tap = [[weights[tap_of(m, dx, dy), at, :] for m in range(3)] for dy in (-1, 0, 1)]
            for r in range(2):
                x = r if side == 0 else width - 2 + r
                for z in range(ZOUT):
                    rows = [
                        cells[z + ZOUT * m, pl.ds(b * (ROWS * slots) + x, ROWS, stride=slots), :] for m in range(3)
                    ]
                    parts = [sum(weight * row for weight, row in zip(weights_of, rows)) for weights_of in tap]
                    rims[z, 2 * side + r, at, :] = shifted_sum(*parts)
    for r in range(2):

        @pl.when(width + r < slots)
        def _():
            for z in range(cells.shape[0]):
                cells[z, pl.ds(width + r, channels, stride=slots), :] = jnp.zeros((channels, tile), F32)


def conv_kernel(cells, weights, depth):
    def convolve(b, carry):
        convolve_block(cells, weights, depth, b, 0)
        return carry

    lax.fori_loop(0, SPLIT, convolve, 0)


def edge_term(edge, z, x):
    tile = edge.shape[2]
    begin = 8 * (x & 15) + 4 * z
    cells = pltpu.roll(edge[(x >> 4) & 1], (tile - 2 - begin) & (tile - 1), 1)
    lane = lane_iota(cells.shape)
    return jnp.where((lane < 2) | (lane >= tile - 2), cells, 0.0)


def rim_kernel(widths, first, second, rims, edge, far, near):
    width = widths[lax.axis_index("gx")]
    _, _, channels, tile = rims.shape
    left, right = first[0:channels, :].astype(F32), second[0:channels, :].astype(F32)
    on_left = (lane_iota((channels, tile)) & 2) != 0
    edge[0] = jnp.where(on_left, pltpu.roll(left, 2, 1), pltpu.roll(right, tile - 2, 1))
    edge[1] = jnp.where(on_left, left, right)
    even = is_even("gx")
    for z in range(ZOUT):
        for r in range(2):
            to_lower = rims[z, r] + edge_term(edge, z, r - 2)
            to_upper = rims[z, 2 + r] + edge_term(edge, z, width + r)
            at = slice((2 * z + r) * channels, (2 * z + r + 1) * channels)
            near[at, :] = jnp.where(even, to_upper, to_lower).astype(BF16)
            far[at, :] = jnp.where(even, to_lower, to_upper).astype(BF16)


def slab_start(widths):
    slab = lax.axis_index("gx")
    start = jnp.int32(0)
    for d in range(widths.shape[0]):
        start = start + jnp.where(d < slab, widths[d], 0)
    return start


def depth_row(weights, depths, edge, z, x):
    own = jnp.concatenate([depth[z, x] for depth in depths], axis=0)
    return own + weights[DW_BIAS] + edge_term(edge, z, x)


def base_row(cells, lifted, phase, z, x):
    channels = lifted.shape[1]
    slots = cells.shape[1] // channels
    return cells[2 + z, pl.ds(x, channels, stride=slots), :] + lifted[lax.div(phase + x, CF)]


def active(weights, mixed):
    mixed = mixed + weights[PW_BIAS]
    return jnp.maximum(mixed, 0.2 * mixed)


def rest_kernel(edge, cells, weights, rest):
    def convolve(b, carry):
        convolve_block(cells, weights, rest, b, SPLIT)
        return carry

    lax.fori_loop(SPLIT, weights.shape[1] // ROWS, convolve, 0)


def mix_kernel(gathered, widths, mix, cells, weights, depth, rest, edge, *refs):
    if gathered:
        coarse, value, ends, bases, lifted, across = refs
        parts, ncx, ncy = coarse.shape
    else:
        first, second, own_block, opposite, value, ends, bases, lifted, across, blocks = refs
        parts, own_rows, ncy = own_block.shape
        ncx = 4 * own_rows
    width = widths[lax.axis_index("gx")]
    here = lax.axis_index("gy")
    start = slab_start(widths)
    phase = lax.rem(start, CF)
    channels, tile = weights.shape[1:]
    slots = cells.shape[1] // channels

    if not gathered:
        count = parts * own_rows
        for message, owner in ((first, lax.rem(here + 3, 4)), (second, lax.rem(here + 1, 4))):
            terms = message[channels:, :].astype(F32)[0:count, :]
            sums = terms[:, 0:ncy] + terms[:, ncy : 2 * ncy] + terms[:, 2 * ncy : 3 * ncy]
            for k in range(parts):
                blocks[k, pl.ds(owner * own_rows, own_rows), :] = sums[k * own_rows : (k + 1) * own_rows]
        for block, owner in ((own_block, here), (opposite, lax.rem(here + 2, 4))):
            for k in range(parts):
                blocks[k, pl.ds(owner * own_rows, own_rows), :] = block[k]
    shape = (ncy, tile)
    cell = row_iota(shape) * CF
    place = lane_iota(shape) + here * tile
    along_y = ((place >= cell) & (place < cell + CF)).astype(F32)
    for k in range(parts):
        block = coarse[k] if gathered else blocks[k]
        across[k] = jnp.dot(block, along_y, precision=lax.Precision.HIGHEST, preferred_element_type=F32)
    for i in range(3):
        cell = lax.rem(lax.div(start, CF) + i, ncx)
        total = None
        for k in range(parts):
            term = weights[LIFT + k] * across[k, pl.ds(cell, 1), :]
            total = term if total is None else total + term
        lifted[i] = total

    group = 4
    wide = jnp.concatenate([mix[...]] * group, axis=1)
    wide = jnp.concatenate([wide] * group, axis=0)
    size = group * channels
    row, column = row_iota((size, size)), lane_iota((size, size))
    same = sum(
        ((row >= i * channels) & (row < (i + 1) * channels) & (column >= i * channels) & (column < (i + 1) * channels)).astype(F32)
        for i in range(group)
    )
    mixer = jnp.where(same > 0, wide.astype(F32), 0.0).astype(BF16)

    for x in range(0, slots, group):
        depths = [
            jnp.concatenate([depth_row(weights, (depth, rest), edge, z, x + i) for i in range(group)], axis=0).astype(BF16)
            for z in range(ZOUT)
        ]
        mixed = jnp.dot(mixer, jnp.concatenate(depths, axis=1), preferred_element_type=F32)
        for i in range(group):
            for z in range(ZOUT):
                part = mixed[i * channels : (i + 1) * channels, z * tile : (z + 1) * tile]
                part = active(weights, part) + base_row(cells, lifted, phase, z, x + i)
                value[z, pl.ds(x + i, channels, stride=slots), :] = jnp.where(x + i < width, part, 0.0)
    for z in range(ZOUT):
        for i, x in enumerate((0, 1, width - 2, width - 1)):
            ends[z, i] = depth_row(weights, (depth, rest), edge, z, x)
            bases[z, i] = base_row(cells, lifted, phase, z, x)


def finish_kernel(widths, mix, weights, ends, bases, far, near, value_in, out, value, block, sems):
    width = widths[lax.axis_index("gx")]
    channels, tile = weights.shape[1:]
    slots = block.shape[2]
    even = is_even("gx")
    mixed = []
    for z in range(ZOUT):
        sums = []
        for i in range(4):
            at = slice((2 * z + i % 2) * channels, (2 * z + i % 2 + 1) * channels)
            one, two = far[at, :].astype(F32), near[at, :].astype(F32)
            arrived = jnp.where(even, one, two) if i < 2 else jnp.where(even, two, one)
            sums.append((ends[z, i] + arrived).astype(BF16))
        mixed.append(jnp.dot(mix[...], jnp.concatenate(sums, axis=1), preferred_element_type=F32))
    copies = []
    for z in range(ZOUT):
        for i, x in enumerate((0, 1, width - 2, width - 1)):
            value[z, pl.ds(x, channels, stride=slots), :] = (
                active(weights, mixed[z][:, i * tile : (i + 1) * tile]) + bases[z, i]
            )
        for part in range(channels // CHUNK):
            for o in range(part * CHUNK, (part + 1) * CHUNK):
                block[z, o] = value[z, o * slots : (o + 1) * slots, :].astype(BF16)
            part_of = pl.ds(part * CHUNK, CHUNK)
            copy = pltpu.make_async_copy(block.at[z, part_of], out.at[z, part_of], sems.at[part, z])
            copy.start()
            copies.append(copy)
    for copy in copies:
        copy.wait()


def shards(feature, widths, dw_weight, dw_bias, pw_weight, pw_bias, lift_weight, coarse):
    planes, channels, slots, tile = feature.shape
    ny = lax.axis_size("gy")
    parts, own_rows, ncy = coarse.shape
    gathered = ny != 4
    ncx = ny * own_rows
    smem = pl.BlockSpec(memory_space=pltpu.SMEM)
    vmem = pl.BlockSpec(memory_space=pltpu.VMEM)
    hbm = pl.BlockSpec(memory_space=pltpu.HBM)
    params = pltpu.CompilerParams(vmem_limit_bytes=VMEM_BYTES)
    shape = jax.ShapeDtypeStruct
    strip = shape((channels + 16, tile), BF16)
    cells_shape = pltpu.VMEM((planes, channels * slots, tile), F32)
    value_shape = pltpu.VMEM((ZOUT, channels * slots, tile), F32)
    message = shape((2 * ZOUT * channels, tile), BF16)

    def swapped(array, axis, first):
        count = lax.axis_size(axis)
        pairs = []
        for i in range(first, count + first, 2):
            a, b = i % count, (i + 1) % count
            pairs += [(a, b), (b, a)]
        return lax.ppermute(array, axis, pairs)

    def pinned(array):
        return pltpu.with_memory_space_constraint(array, pltpu.HBM)

    if gathered:
        every = lax.all_gather(coarse, "gy", axis=1, tiled=True)
    small = (
        widths,
        dw_weight,
        dw_bias.reshape(1, channels),
        pw_bias.reshape(1, channels),
        lift_weight.T,
        coarse,
    )
    cells, weights, first, second, block, slab_widths = pl.pallas_call(
        pack_kernel,
        out_shape=(
            cells_shape,
            pltpu.VMEM((32, channels, tile), F32),
            strip,
            strip,
            pltpu.VMEM(coarse.shape, F32),
            pltpu.SMEM(widths.shape, jnp.int32),
        ),
        in_specs=[hbm] * 7,
        out_specs=(vmem,) * 5 + (smem,),
        scratch_shapes=[
            pltpu.VMEM(feature.shape, BF16),
            pltpu.SMEM(widths.shape, jnp.int32),
            pltpu.VMEM(dw_weight.shape, F32),
            pltpu.VMEM((1, channels), F32),
            pltpu.VMEM((1, channels), F32),
            pltpu.VMEM((parts, channels), F32),
            pltpu.VMEM(coarse.shape, F32),
            pltpu.VMEM((32, channels), F32),
            pltpu.VMEM((16, tile), F32),
            pltpu.VMEM((3, 2, channels, tile), F32),
            pltpu.SemaphoreType.DMA((3, 2)),
            pltpu.SemaphoreType.DMA((len(small),)),
        ],
        compiler_params=params,
    )(pinned(feature), *(pinned(array) for array in small))
    first = lax.ppermute(first, "gy", [(i, (i + 1) % ny) for i in range(ny)])
    second = lax.ppermute(second, "gy", [((i + 1) % ny, i) for i in range(ny)])
    early = SPLIT * ROWS
    cells, rims, own_block = pl.pallas_call(
        outer_kernel,
        out_shape=(
            cells_shape,
            pltpu.VMEM((ZOUT, 4, channels, tile), F32),
            pltpu.VMEM(coarse.shape, F32),
        ),
        in_specs=[smem] + [vmem] * 3,
        out_specs=(vmem,) * 3,
        input_output_aliases={3: 0},
        compiler_params=params,
        cost_estimate=pl.CostEstimate(flops=10**8, bytes_accessed=10**6, transcendentals=0),
    )(slab_widths, weights, block, cells)
    if not gathered:
        opposite = lax.ppermute(own_block, "gy", [(i, (i + 2) % 4) for i in range(4)])
    depth = pl.pallas_call(
        conv_kernel,
        out_shape=pltpu.VMEM((ZOUT, slots, early, tile), F32),
        in_specs=[vmem] * 2,
        out_specs=vmem,
        compiler_params=params,
        cost_estimate=pl.CostEstimate(flops=10**9, bytes_accessed=10**6, transcendentals=0),
    )(cells, weights)
    edge, far, near = pl.pallas_call(
        rim_kernel,
        out_shape=(pltpu.VMEM((2, channels, tile), F32), message, message),
        in_specs=[smem] + [vmem] * 3,
        out_specs=(vmem,) * 3,
        compiler_params=params,
    )(slab_widths, first, second, rims)
    far = swapped(far, "gx", 1)
    near = swapped(near, "gx", 0)
    blocks = (every,) if gathered else (first, second, own_block, opposite)
    rest = pl.pallas_call(
        rest_kernel,
        out_shape=pltpu.VMEM((ZOUT, slots, channels - early, tile), F32),
        in_specs=[vmem] * 3,
        out_specs=vmem,
        compiler_params=params,
        cost_estimate=pl.CostEstimate(flops=10**9, bytes_accessed=10**6, transcendentals=0),
    )(edge, cells, weights)
    ends_shape = pltpu.VMEM((ZOUT, 4, channels, tile), F32)
    value, ends, bases = pl.pallas_call(
        functools.partial(mix_kernel, gathered),
        out_shape=(value_shape, ends_shape, ends_shape),
        in_specs=[smem] + [vmem] * (6 + len(blocks)),
        out_specs=(vmem,) * 3,
        scratch_shapes=[pltpu.VMEM((3, channels, tile), F32), pltpu.VMEM((parts, ncx, tile), F32)]
        + ([] if gathered else [pltpu.VMEM((parts, ncx, ncy), F32)]),
        compiler_params=params,
        cost_estimate=pl.CostEstimate(flops=10**9, bytes_accessed=10**6, transcendentals=0),
    )(slab_widths, pw_weight, cells, weights, depth, rest, edge, *blocks)
    out, _ = pl.pallas_call(
        finish_kernel,
        out_shape=(shape((ZOUT, channels, slots, tile), BF16), value_shape),
        in_specs=[smem] + [vmem] * 7,
        out_specs=(hbm, vmem),
        scratch_shapes=[
            pltpu.VMEM((ZOUT, channels, slots, tile), BF16),
            pltpu.SemaphoreType.DMA((channels // CHUNK, ZOUT)),
        ],
        input_output_aliases={7: 1},
        compiler_params=params,
    )(slab_widths, pw_weight, weights, ends, bases, far, near, value)
    return out


def solution(mesh):
    placed = (P(None, None, "gx", "gy"), P(), P(), P(), P(), P(), P(), P(None, "gy", None))
    return jax.shard_map(
        shards, mesh=mesh, in_specs=placed, out_specs=P(None, None, "gx", "gy"), check_vma=False
    )
```

```python
import functools

import jax
import jax.numpy as jnp
from jax import lax
from jax.experimental import pallas as pl
from jax.experimental.pallas import tpu as pltpu
from jax.sharding import PartitionSpec as P

XW = 16
ZOUT = 2
CF = 16
ROWS = 8
CHUNK = 16
DW_BIAS, PW_BIAS, LIFT = 27, 28, 29
F32 = jnp.float32
BF16 = jnp.bfloat16
VMEM_BYTES = 14 * 1024 * 1024


def lane_iota(shape):
    return lax.broadcasted_iota(jnp.int32, shape, len(shape) - 1)


def row_iota(shape):
    return lax.broadcasted_iota(jnp.int32, shape, len(shape) - 2)


def tap_of(m, dx, dy):
    return 9 * m + 3 * (dx + 1) + (dy + 1)


def is_even(axis):
    return lax.rem(lax.axis_index(axis), 2) == 0


def pack_kernel(
    feature, widths_in, taps_in, dw_bias_in, pw_bias_in, lift_in, coarse_in,
    cells, weights, first, second, own_block, widths,
    planes, widths_here, taps, dw_bias, pw_bias, lift, coarse, stacked, tail, picked, sems, small_sems,
):
    count, channels, slots, tile = feature.shape

    half_of = channels // 2

    def copy_of(m, part):
        at = (pl.ds(ZOUT * m, ZOUT), pl.ds(part * half_of, half_of))
        return pltpu.make_async_copy(feature.at[at], planes.at[at], sems.at[m, part])

    small = [
        pltpu.make_async_copy(source, target, small_sems.at[i])
        for i, (source, target) in enumerate(
            (
                (widths_in, widths_here),
                (taps_in, taps),
                (dw_bias_in, dw_bias),
                (pw_bias_in, pw_bias),
                (lift_in, lift),
                (coarse_in, coarse),
            )
        )
    ]
    for copy in small:
        copy.start()
    for m in range(3):
        for part in range(2):
            copy_of(m, part).start()
    def take_small():
        for copy in small:
            copy.wait()
        for d in range(widths.shape[0]):
            widths[d] = widths_here[d]
        stacked[0:DW_BIAS, :] = taps[...]
        stacked[DW_BIAS : DW_BIAS + 1, :] = dw_bias[...]
        stacked[PW_BIAS : PW_BIAS + 1, :] = pw_bias[...]
        stacked[LIFT : LIFT + 3, :] = lift[...]
        turned = jnp.transpose(stacked[...])
        for t in range(stacked.shape[0]):
            weights[t] = jnp.broadcast_to(turned[:, t : t + 1], (channels, tile))

        own_block[...] = coarse[...]
        parts, own_rows, ncy = coarse.shape
        tail[...] = jnp.zeros_like(tail)
        if 3 * ncy <= tile:
            for k in range(parts):
                rest = coarse[k]
                for p in range(3):
                    term = rest.astype(BF16).astype(F32)
                    rest = rest - term
                    tail[k * own_rows : (k + 1) * own_rows, p * ncy : (p + 1) * ncy] = term
        for message in (first, second):
            message[channels:, :] = tail[...].astype(BF16)

    lane, row = lane_iota((slots, tile)), row_iota((slots, tile))
    mine = (lane >> 3) == (row & 15)
    in_even, in_odd = mine & ((lane & 4) == 0), mine & ((lane & 4) != 0)
    sublane = row_iota((ROWS, tile))

    def placed(m, k):
        both = []
        for z in range(ZOUT):
            plane = planes[ZOUT * m + z, k].astype(F32)
            cells[ZOUT * m + z, k * slots : (k + 1) * slots, :] = plane
            both.append(
                jnp.concatenate(
                    [
                        pltpu.roll(plane[x : x + ROWS], (2 + 4 * z + 8 * x) % tile, 1, stride=8, stride_axis=0)
                        for x in range(0, slots, ROWS)
                    ],
                    axis=0,
                )
            )
        rows = jnp.where(in_even, both[0], jnp.where(in_odd, both[1], 0.0))
        return rows[0:ROWS] + rows[ROWS : 2 * ROWS], rows[2 * ROWS :]

    def summed(m, k, step):
        if step == 0:
            return placed(m, k)
        one, two = summed(m, k, step // 2), summed(m, k + step, step // 2)
        turn = (sublane & step) != 0
        return tuple(
            jnp.where(turn, b, a) + pltpu.roll(jnp.where(turn, a, b), step, 0) for a, b in zip(one, two)
        )

    for m in range(3):
        for part in range(2):
            copy_of(m, part).wait()
            for c in range(part * half_of, (part + 1) * half_of, ROWS):
                for half, total in enumerate(summed(m, c, ROWS // 2)):
                    picked[m, half, c : c + ROWS, :] = total
        if m == 0:
            take_small()
    width = widths_here[lax.axis_index("gx")]

    shape = (channels, tile)
    lane = lane_iota(shape)
    on_left = (lane & 2) != 0
    packed = [None, None]
    for m in range(3):
        low, high = (jnp.where(16 * half + (lane >> 3) < width, picked[m, half], 0.0) for half in range(2))
        moved = {
            -1: tuple(
                pltpu.roll(jnp.where(lane < tile - 16, one, two), 16, 1) for one, two in ((low, high), (high, low))
            ),
            0: (low, high),
            1: tuple(
                pltpu.roll(jnp.where(lane >= 16, one, two), tile - 16, 1) for one, two in ((low, high), (high, low))
            ),
        }
        for dx in (-1, 0, 1):
            weight = jnp.where(on_left, weights[tap_of(m, dx, 1)], weights[tap_of(m, dx, -1)])
            for half in range(2):
                term = weight * moved[dx][half]
                packed[half] = term if packed[half] is None else packed[half] + term
    left = jnp.where(on_left, packed[0], pltpu.roll(packed[1], tile - 2, 1))
    right = jnp.where(on_left, pltpu.roll(packed[1], 2, 1), packed[0])
    first[0:channels, :] = right.astype(BF16)
    second[0:channels, :] = left.astype(BF16)


def shifted_sum(before, centre, after):
    lane = lane_iota(centre.shape)
    tile = centre.shape[-1]
    before = jnp.where(lane < 2, 0.0, pltpu.roll(before, 2, 1))
    after = jnp.where(lane >= tile - 2, 0.0, pltpu.roll(after, tile - 2, 1))
    return centre + before + after


def convolve_block(cells, weights, depth, b, limit):
    channels = weights.shape[1]
    slots = cells.shape[1] // channels
    at = pl.ds(pl.multiple_of(b * ROWS, ROWS), ROWS)
    tap = [weights[t, at, :] for t in range(27)]
    for z in range(ZOUT):
        for parity in range(2):
            sums = {}
            for x in range(parity, limit, 2):
                rows = [cells[z + ZOUT * m, pl.ds(b * (ROWS * slots) + x, ROWS, stride=slots), :] for m in range(3)]
                for m in range(3):
                    for dx in (1, 0, -1):
                        out = x - 2 * dx
                        if 0 <= out < limit:
                            for dy in (-1, 0, 1):
                                term = tap[tap_of(m, dx, dy)] * rows[m]
                                key = (out, dy)
                                sums[key] = sums[key] + term if key in sums else term
                for out in [x - 2] if x + 2 < limit else [x - 2, x]:
                    if out >= 0:
                        depth[z, out, at, :] = shifted_sum(*(sums.pop((out, dy)) for dy in (-1, 0, 1)))


def outer_kernel(widths, weights, coarse, cells_in, cells, rims, own_block):
    width = widths[lax.axis_index("gx")]
    channels, tile = weights.shape[1:]
    slots = cells.shape[1] // channels
    own_block[...] = coarse[...]
    for b in range(channels // ROWS):
        at = slice(b * ROWS, (b + 1) * ROWS)
        for side, dx in enumerate((1, -1)):
            tap = [[weights[tap_of(m, dx, dy), at, :] for m in range(3)] for dy in (-1, 0, 1)]
            for r in range(2):
                x = r if side == 0 else width - 2 + r
                for z in range(ZOUT):
                    rows = [
                        cells[z + ZOUT * m, pl.ds(b * (ROWS * slots) + x, ROWS, stride=slots), :] for m in range(3)
                    ]
                    parts = [sum(weight * row for weight, row in zip(weights_of, rows)) for weights_of in tap]
                    rims[z, 2 * side + r, at, :] = shifted_sum(*parts)
    for r in range(2):

        @pl.when(width + r < slots)
        def _():
            for z in range(cells.shape[0]):
                cells[z, pl.ds(width + r, channels, stride=slots), :] = jnp.zeros((channels, tile), F32)


def conv_kernel(widths, edge, cells, weights, depth):
    width = widths[lax.axis_index("gx")]
    channels = weights.shape[1]
    slots = cells.shape[1] // channels
    for limit in range(ROWS, slots + 1, ROWS):

        @pl.when((width > limit - ROWS) & (width <= limit))
        def _():
            def convolve(b, carry):
                convolve_block(cells, weights, depth, b, limit)
                return carry

            lax.fori_loop(0, channels // ROWS, convolve, 0)


def edge_term(edge, z, x):
    tile = edge.shape[2]
    begin = 8 * (x & 15) + 4 * z
    cells = pltpu.roll(edge[(x >> 4) & 1], (tile - 2 - begin) & (tile - 1), 1)
    lane = lane_iota(cells.shape)
    return jnp.where((lane < 2) | (lane >= tile - 2), cells, 0.0)


def rim_kernel(widths, first, second, rims, edge, far, near):
    width = widths[lax.axis_index("gx")]
    _, _, channels, tile = rims.shape
    left, right = first[0:channels, :].astype(F32), second[0:channels, :].astype(F32)
    on_left = (lane_iota((channels, tile)) & 2) != 0
    edge[0] = jnp.where(on_left, pltpu.roll(left, 2, 1), pltpu.roll(right, tile - 2, 1))
    edge[1] = jnp.where(on_left, left, right)
    even = is_even("gx")
    for z in range(ZOUT):
        for r in range(2):
            to_lower = rims[z, r] + edge_term(edge, z, r - 2)
            to_upper = rims[z, 2 + r] + edge_term(edge, z, width + r)
            at = slice((2 * z + r) * channels, (2 * z + r + 1) * channels)
            near[at, :] = jnp.where(even, to_upper, to_lower).astype(BF16)
            far[at, :] = jnp.where(even, to_lower, to_upper).astype(BF16)


def slab_start(widths):
    slab = lax.axis_index("gx")
    start = jnp.int32(0)
    for d in range(widths.shape[0]):
        start = start + jnp.where(d < slab, widths[d], 0)
    return start


def depth_row(weights, depth, edge, z, x):
    return depth[z, x] + weights[DW_BIAS] + edge_term(edge, z, x)


def base_row(cells, lifted, phase, z, x):
    channels = lifted.shape[1]
    slots = cells.shape[1] // channels
    return cells[2 + z, pl.ds(x, channels, stride=slots), :] + lifted[lax.div(phase + x, CF)]


def active(weights, mixed):
    mixed = mixed + weights[PW_BIAS]
    return jnp.maximum(mixed, 0.2 * mixed)


def mix_kernel(gathered, widths, mix, cells, weights, depth, edge, *refs):
    if gathered:
        coarse, value, ends, bases, lifted, across = refs
        parts, ncx, ncy = coarse.shape
    else:
        first, second, own_block, opposite, value, ends, bases, lifted, across, blocks = refs
        parts, own_rows, ncy = own_block.shape
        ncx = 4 * own_rows
    width = widths[lax.axis_index("gx")]
    here = lax.axis_index("gy")
    start = slab_start(widths)
    phase = lax.rem(start, CF)
    channels, tile = weights.shape[1:]
    slots = cells.shape[1] // channels

    if not gathered:
        count = parts * own_rows
        for message, owner in ((first, lax.rem(here + 3, 4)), (second, lax.rem(here + 1, 4))):
            terms = message[channels:, :].astype(F32)[0:count, :]
            sums = terms[:, 0:ncy] + terms[:, ncy : 2 * ncy] + terms[:, 2 * ncy : 3 * ncy]
            for k in range(parts):
                blocks[k, pl.ds(owner * own_rows, own_rows), :] = sums[k * own_rows : (k + 1) * own_rows]
        for block, owner in ((own_block, here), (opposite, lax.rem(here + 2, 4))):
            for k in range(parts):
                blocks[k, pl.ds(owner * own_rows, own_rows), :] = block[k]
    shape = (ncy, tile)
    cell = row_iota(shape) * CF
    place = lane_iota(shape) + here * tile
    along_y = ((place >= cell) & (place < cell + CF)).astype(F32)
    for k in range(parts):
        block = coarse[k] if gathered else blocks[k]
        across[k] = jnp.dot(block, along_y, precision=lax.Precision.HIGHEST, preferred_element_type=F32)
    for i in range(3):
        cell = lax.rem(lax.div(start, CF) + i, ncx)
        total = None
        for k in range(parts):
            term = weights[LIFT + k] * across[k, pl.ds(cell, 1), :]
            total = term if total is None else total + term
        lifted[i] = total

    group = 4
    wide = jnp.concatenate([mix[...]] * group, axis=1)
    wide = jnp.concatenate([wide] * group, axis=0)
    size = group * channels
    row, column = row_iota((size, size)), lane_iota((size, size))
    same = sum(
        ((row >= i * channels) & (row < (i + 1) * channels) & (column >= i * channels) & (column < (i + 1) * channels)).astype(F32)
        for i in range(group)
    )
    mixer = jnp.where(same > 0, wide.astype(F32), 0.0).astype(BF16)

    def mix_rows(begin):
        for x in range(begin, begin + ROWS, group):
            depths = [
                jnp.concatenate([depth_row(weights, depth, edge, z, x + i) for i in range(group)], axis=0)
                for z in range(ZOUT)
            ]
            mixed = jnp.dot(mixer, jnp.concatenate(depths, axis=1).astype(BF16), preferred_element_type=F32)
            for i in range(group):
                for z in range(ZOUT):
                    part = mixed[i * channels : (i + 1) * channels, z * tile : (z + 1) * tile]
                    part = active(weights, part) + base_row(cells, lifted, phase, z, x + i)
                    value[z, pl.ds(x + i, channels, stride=slots), :] = jnp.where(x + i < width, part, 0.0)

    def no_rows(begin):
        for x in range(begin, begin + ROWS):
            for z in range(ZOUT):
                value[z, pl.ds(x, channels, stride=slots), :] = jnp.zeros((channels, tile), F32)

    mix_rows(0)
    for begin in range(ROWS, slots, ROWS):
        pl.when(width > begin)(lambda begin=begin: mix_rows(begin))
        pl.when(width <= begin)(lambda begin=begin: no_rows(begin))
    for z in range(ZOUT):
        for i, x in enumerate((0, 1, width - 2, width - 1)):
            ends[z, i] = depth_row(weights, depth, edge, z, x)
            bases[z, i] = base_row(cells, lifted, phase, z, x)


def finish_kernel(widths, mix, weights, ends, bases, far, near, value_in, out, value, block, sems):
    width = widths[lax.axis_index("gx")]
    channels, tile = weights.shape[1:]
    slots = block.shape[2]
    even = is_even("gx")
    mixed = []
    for z in range(ZOUT):
        sums = []
        for i in range(4):
            at = slice((2 * z + i % 2) * channels, (2 * z + i % 2 + 1) * channels)
            one, two = far[at, :].astype(F32), near[at, :].astype(F32)
            arrived = jnp.where(even, one, two) if i < 2 else jnp.where(even, two, one)
            sums.append((ends[z, i] + arrived).astype(BF16))
        mixed.append(jnp.dot(mix[...], jnp.concatenate(sums, axis=1), preferred_element_type=F32))
    copies = []
    for z in range(ZOUT):
        for part in range(channels // CHUNK):
            at = slice(part * CHUNK, (part + 1) * CHUNK)
            for i, x in enumerate((0, 1, width - 2, width - 1)):
                rows = mixed[z][at, i * tile : (i + 1) * tile] + weights[PW_BIAS, at, :]
                rows = jnp.maximum(rows, 0.2 * rows) + bases[z, i, at, :]
                value[z, pl.ds(part * CHUNK * slots + x, CHUNK, stride=slots), :] = rows
            for o in range(part * CHUNK, (part + 1) * CHUNK):
                block[z, o] = value[z, o * slots : (o + 1) * slots, :].astype(BF16)
            part_of = pl.ds(part * CHUNK, CHUNK)
            copy = pltpu.make_async_copy(block.at[z, part_of], out.at[z, part_of], sems.at[part, z])
            copy.start()
            copies.append(copy)
    for copy in copies:
        copy.wait()


def shards(feature, widths, dw_weight, dw_bias, pw_weight, pw_bias, lift_weight, coarse):
    planes, channels, slots, tile = feature.shape
    ny = lax.axis_size("gy")
    parts, own_rows, ncy = coarse.shape
    gathered = ny != 4
    ncx = ny * own_rows
    smem = pl.BlockSpec(memory_space=pltpu.SMEM)
    vmem = pl.BlockSpec(memory_space=pltpu.VMEM)
    hbm = pl.BlockSpec(memory_space=pltpu.HBM)
    params = pltpu.CompilerParams(vmem_limit_bytes=VMEM_BYTES)
    shape = jax.ShapeDtypeStruct
    strip = shape((channels + 16, tile), BF16)
    cells_shape = pltpu.VMEM((planes, channels * slots, tile), F32)
    value_shape = pltpu.VMEM((ZOUT, channels * slots, tile), F32)
    message = shape((2 * ZOUT * channels, tile), BF16)

    def swapped(array, axis, first):
        count = lax.axis_size(axis)
        pairs = []
        for i in range(first, count + first, 2):
            a, b = i % count, (i + 1) % count
            pairs += [(a, b), (b, a)]
        return lax.ppermute(array, axis, pairs)

    def pinned(array):
        return pltpu.with_memory_space_constraint(array, pltpu.HBM)

    if gathered:
        every = lax.all_gather(coarse, "gy", axis=1, tiled=True)
    small = (
        widths,
        dw_weight,
        dw_bias.reshape(1, channels),
        pw_bias.reshape(1, channels),
        lift_weight.T,
        coarse,
    )
    cells, weights, first, second, block, slab_widths = pl.pallas_call(
        pack_kernel,
        out_shape=(
            cells_shape,
            pltpu.VMEM((32, channels, tile), F32),
            strip,
            strip,
            pltpu.VMEM(coarse.shape, F32),
            pltpu.SMEM(widths.shape, jnp.int32),
        ),
        in_specs=[hbm] * 7,
        out_specs=(vmem,) * 5 + (smem,),
        scratch_shapes=[
            pltpu.VMEM(feature.shape, BF16),
            pltpu.SMEM(widths.shape, jnp.int32),
            pltpu.VMEM(dw_weight.shape, F32),
            pltpu.VMEM((1, channels), F32),
            pltpu.VMEM((1, channels), F32),
            pltpu.VMEM((parts, channels), F32),
            pltpu.VMEM(coarse.shape, F32),
            pltpu.VMEM((32, channels), F32),
            pltpu.VMEM((16, tile), F32),
            pltpu.VMEM((3, 2, channels, tile), F32),
            pltpu.SemaphoreType.DMA((3, 2)),
            pltpu.SemaphoreType.DMA((len(small),)),
        ],
        compiler_params=params,
    )(pinned(feature), *(pinned(array) for array in small))
    first = lax.ppermute(first, "gy", [(i, (i + 1) % ny) for i in range(ny)])
    second = lax.ppermute(second, "gy", [((i + 1) % ny, i) for i in range(ny)])
    cells, rims, own_block = pl.pallas_call(
        outer_kernel,
        out_shape=(
            cells_shape,
            pltpu.VMEM((ZOUT, 4, channels, tile), F32),
            pltpu.VMEM(coarse.shape, F32),
        ),
        in_specs=[smem] + [vmem] * 3,
        out_specs=(vmem,) * 3,
        input_output_aliases={3: 0},
        compiler_params=params,
        cost_estimate=pl.CostEstimate(flops=10**8, bytes_accessed=10**6, transcendentals=0),
    )(slab_widths, weights, block, cells)
    if not gathered:
        opposite = lax.ppermute(own_block, "gy", [(i, (i + 2) % 4) for i in range(4)])
    edge, far, near = pl.pallas_call(
        rim_kernel,
        out_shape=(pltpu.VMEM((2, channels, tile), F32), message, message),
        in_specs=[smem] + [vmem] * 3,
        out_specs=(vmem,) * 3,
        compiler_params=params,
    )(slab_widths, first, second, rims)
    far = swapped(far, "gx", 1)
    near = swapped(near, "gx", 0)
    blocks = (every,) if gathered else (first, second, own_block, opposite)
    depth = pl.pallas_call(
        conv_kernel,
        out_shape=pltpu.VMEM((ZOUT, slots, channels, tile), F32),
        in_specs=[smem] + [vmem] * 3,
        out_specs=vmem,
        compiler_params=params,
        cost_estimate=pl.CostEstimate(flops=10**9, bytes_accessed=10**6, transcendentals=0),
    )(slab_widths, edge, cells, weights)
    ends_shape = pltpu.VMEM((ZOUT, 4, channels, tile), F32)
    value, ends, bases = pl.pallas_call(
        functools.partial(mix_kernel, gathered),
        out_shape=(value_shape, ends_shape, ends_shape),
        in_specs=[smem] + [vmem] * (5 + len(blocks)),
        out_specs=(vmem,) * 3,
        scratch_shapes=[pltpu.VMEM((3, channels, tile), F32), pltpu.VMEM((parts, ncx, tile), F32)]
        + ([] if gathered else [pltpu.VMEM((parts, ncx, ncy), F32)]),
        compiler_params=params,
        cost_estimate=pl.CostEstimate(flops=10**9, bytes_accessed=10**6, transcendentals=0),
    )(slab_widths, pw_weight, cells, weights, depth, edge, *blocks)
    out, _ = pl.pallas_call(
        finish_kernel,
        out_shape=(shape((ZOUT, channels, slots, tile), BF16), value_shape),
        in_specs=[smem] + [vmem] * 7,
        out_specs=(hbm, vmem),
        scratch_shapes=[
            pltpu.VMEM((ZOUT, channels, slots, tile), BF16),
            pltpu.SemaphoreType.DMA((channels // CHUNK, ZOUT)),
        ],
        input_output_aliases={7: 1},
        compiler_params=params,
    )(slab_widths, pw_weight, weights, ends, bases, far, near, value)
    return out


def solution(mesh):
    placed = (P(None, None, "gx", "gy"), P(), P(), P(), P(), P(), P(), P(None, "gy", None))
    return jax.shard_map(
        shards, mesh=mesh, in_specs=placed, out_specs=P(None, None, "gx", "gy"), check_vma=False
    )
```

```python
import functools

import jax
import jax.numpy as jnp
from jax import lax
from jax.experimental import pallas as pl
from jax.experimental.pallas import tpu as pltpu
from jax.sharding import PartitionSpec as P

XW = 16
ZOUT = 2
CF = 16
ROWS = 8
CHUNK = 16
DW_BIAS, PW_BIAS, LIFT = 27, 28, 29
F32 = jnp.float32
BF16 = jnp.bfloat16
VMEM_BYTES = 14 * 1024 * 1024


def lane_iota(shape):
    return lax.broadcasted_iota(jnp.int32, shape, len(shape) - 1)


def row_iota(shape):
    return lax.broadcasted_iota(jnp.int32, shape, len(shape) - 2)


def tap_of(m, dx, dy):
    return 9 * m + 3 * (dx + 1) + (dy + 1)


def is_even(axis):
    return lax.rem(lax.axis_index(axis), 2) == 0


def pack_kernel(
    feature, widths_in, taps_in, dw_bias_in, pw_bias_in, lift_in, coarse_in,
    cells, weights, first, second, own_block, widths,
    planes, widths_here, taps, dw_bias, pw_bias, lift, coarse, stacked, tail, picked, sems, small_sems,
):
    count, channels, slots, tile = feature.shape

    half_of = channels // 2

    def copy_of(m, part):
        at = (pl.ds(ZOUT * m, ZOUT), pl.ds(part * half_of, half_of))
        return pltpu.make_async_copy(feature.at[at], planes.at[at], sems.at[m, part])

    small = [
        pltpu.make_async_copy(source, target, small_sems.at[i])
        for i, (source, target) in enumerate(
            (
                (widths_in, widths_here),
                (taps_in, taps),
                (dw_bias_in, dw_bias),
                (pw_bias_in, pw_bias),
                (lift_in, lift),
                (coarse_in, coarse),
            )
        )
    ]
    for copy in small:
        copy.start()
    for m in range(3):
        for part in range(2):
            copy_of(m, part).start()
    def take_small():
        for copy in small:
            copy.wait()
        for d in range(widths.shape[0]):
            widths[d] = widths_here[d]
        stacked[0:DW_BIAS, :] = taps[...]
        stacked[DW_BIAS : DW_BIAS + 1, :] = dw_bias[...]
        stacked[PW_BIAS : PW_BIAS + 1, :] = pw_bias[...]
        stacked[LIFT : LIFT + 3, :] = lift[...]
        turned = jnp.transpose(stacked[...])
        for t in range(stacked.shape[0]):
            weights[t] = jnp.broadcast_to(turned[:, t : t + 1], (channels, tile))

        own_block[...] = coarse[...]
        parts, own_rows, ncy = coarse.shape
        tail[...] = jnp.zeros_like(tail)
        if 3 * ncy <= tile:
            for k in range(parts):
                rest = coarse[k]
                for p in range(3):
                    term = rest.astype(BF16).astype(F32)
                    rest = rest - term
                    tail[k * own_rows : (k + 1) * own_rows, p * ncy : (p + 1) * ncy] = term
        for message in (first, second):
            message[channels:, :] = tail[...].astype(BF16)

    lane, row = lane_iota((slots, tile)), row_iota((slots, tile))
    mine = (lane >> 3) == (row & 15)
    in_even, in_odd = mine & ((lane & 4) == 0), mine & ((lane & 4) != 0)
    sublane = row_iota((ROWS, tile))

    def placed(m, k):
        both = []
        for z in range(ZOUT):
            plane = planes[ZOUT * m + z, k].astype(F32)
            cells[ZOUT * m + z, k * slots : (k + 1) * slots, :] = plane
            both.append(
                jnp.concatenate(
                    [
                        pltpu.roll(plane[x : x + ROWS], (2 + 4 * z + 8 * x) % tile, 1, stride=8, stride_axis=0)
                        for x in range(0, slots, ROWS)
                    ],
                    axis=0,
                )
            )
        rows = jnp.where(in_even, both[0], jnp.where(in_odd, both[1], 0.0))
        return rows[0:ROWS] + rows[ROWS : 2 * ROWS], rows[2 * ROWS :]

    def summed(m, k, step):
        if step == 0:
            return placed(m, k)
        one, two = summed(m, k, step // 2), summed(m, k + step, step // 2)
        turn = (sublane & step) != 0
        return tuple(
            jnp.where(turn, b, a) + pltpu.roll(jnp.where(turn, a, b), step, 0) for a, b in zip(one, two)
        )

    for m in range(3):
        for part in range(2):
            copy_of(m, part).wait()
            for c in range(part * half_of, (part + 1) * half_of, ROWS):
                for half, total in enumerate(summed(m, c, ROWS // 2)):
                    picked[m, half, c : c + ROWS, :] = total
        if m == 0:
            take_small()
    width = widths_here[lax.axis_index("gx")]

    shape = (channels, tile)
    lane = lane_iota(shape)
    on_left = (lane & 2) != 0
    packed = [None, None]
    for m in range(3):
        low, high = (jnp.where(16 * half + (lane >> 3) < width, picked[m, half], 0.0) for half in range(2))
        moved = {
            -1: tuple(
                pltpu.roll(jnp.where(lane < tile - 16, one, two), 16, 1) for one, two in ((low, high), (high, low))
            ),
            0: (low, high),
            1: tuple(
                pltpu.roll(jnp.where(lane >= 16, one, two), tile - 16, 1) for one, two in ((low, high), (high, low))
            ),
        }
        for dx in (-1, 0, 1):
            weight = jnp.where(on_left, weights[tap_of(m, dx, 1)], weights[tap_of(m, dx, -1)])
            for half in range(2):
                term = weight * moved[dx][half]
                packed[half] = term if packed[half] is None else packed[half] + term
    left = jnp.where(on_left, packed[0], pltpu.roll(packed[1], tile - 2, 1))
    right = jnp.where(on_left, pltpu.roll(packed[1], 2, 1), packed[0])
    first[0:channels, :] = right.astype(BF16)
    second[0:channels, :] = left.astype(BF16)


def shifted_sum(before, centre, after):
    lane = lane_iota(centre.shape)
    tile = centre.shape[-1]
    before = jnp.where(lane < 2, 0.0, pltpu.roll(before, 2, 1))
    after = jnp.where(lane >= tile - 2, 0.0, pltpu.roll(after, tile - 2, 1))
    return centre + before + after


def convolve_block(cells, weights, depth, b, limit):
    channels = weights.shape[1]
    slots = cells.shape[1] // channels
    at = pl.ds(pl.multiple_of(b * ROWS, ROWS), ROWS)
    tap = [weights[t, at, :] for t in range(27)]
    for z in range(ZOUT):
        for parity in range(2):
            sums = {}
            for x in range(parity, limit, 2):
                rows = [cells[z + ZOUT * m, pl.ds(b * (ROWS * slots) + x, ROWS, stride=slots), :] for m in range(3)]
                for m in range(3):
                    for dx in (1, 0, -1):
                        out = x - 2 * dx
                        if 0 <= out < limit:
                            for dy in (-1, 0, 1):
                                term = tap[tap_of(m, dx, dy)] * rows[m]
                                key = (out, dy)
                                sums[key] = sums[key] + term if key in sums else term
                for out in [x - 2] if x + 2 < limit else [x - 2, x]:
                    if out >= 0:
                        depth[z, out, at, :] = shifted_sum(*(sums.pop((out, dy)) for dy in (-1, 0, 1)))


def outer_kernel(widths, weights, coarse, cells_in, cells, rims, own_block):
    width = widths[lax.axis_index("gx")]
    channels, tile = weights.shape[1:]
    slots = cells.shape[1] // channels
    own_block[...] = coarse[...]
    for b in range(channels // ROWS):
        at = slice(b * ROWS, (b + 1) * ROWS)
        for side, dx in enumerate((1, -1)):
            tap = [[weights[tap_of(m, dx, dy), at, :] for m in range(3)] for dy in (-1, 0, 1)]
            for r in range(2):
                x = r if side == 0 else width - 2 + r
                for z in range(ZOUT):
                    rows = [
                        cells[z + ZOUT * m, pl.ds(b * (ROWS * slots) + x, ROWS, stride=slots), :] for m in range(3)
                    ]
                    parts = [sum(weight * row for weight, row in zip(weights_of, rows)) for weights_of in tap]
                    rims[z, 2 * side + r, at, :] = shifted_sum(*parts)
    for r in range(2):

        @pl.when(width + r < slots)
        def _():
            for z in range(cells.shape[0]):
                cells[z, pl.ds(width + r, channels, stride=slots), :] = jnp.zeros((channels, tile), F32)


def conv_kernel(widths, edge, cells, weights, depth):
    width = widths[lax.axis_index("gx")]
    channels = weights.shape[1]
    slots = cells.shape[1] // channels
    for limit in range(ROWS, slots + 1, ROWS):

        @pl.when((width > limit - ROWS) & (width <= limit))
        def _():
            def convolve(b, carry):
                convolve_block(cells, weights, depth, b, limit)
                return carry

            lax.fori_loop(0, channels // ROWS, convolve, 0)


def edge_term(edge, z, x):
    tile = edge.shape[2]
    begin = 8 * (x & 15) + 4 * z
    cells = pltpu.roll(edge[(x >> 4) & 1], (tile - 2 - begin) & (tile - 1), 1)
    lane = lane_iota(cells.shape)
    return jnp.where((lane < 2) | (lane >= tile - 2), cells, 0.0)


def rim_kernel(widths, first, second, rims, edge, far, near):
    width = widths[lax.axis_index("gx")]
    _, _, channels, tile = rims.shape
    left, right = first[0:channels, :].astype(F32), second[0:channels, :].astype(F32)
    on_left = (lane_iota((channels, tile)) & 2) != 0
    edge[0] = jnp.where(on_left, pltpu.roll(left, 2, 1), pltpu.roll(right, tile - 2, 1))
    edge[1] = jnp.where(on_left, left, right)
    even = is_even("gx")
    for z in range(ZOUT):
        for r in range(2):
            to_lower = rims[z, r] + edge_term(edge, z, r - 2)
            to_upper = rims[z, 2 + r] + edge_term(edge, z, width + r)
            at = slice((2 * z + r) * channels, (2 * z + r + 1) * channels)
            near[at, :] = jnp.where(even, to_upper, to_lower).astype(BF16)
            far[at, :] = jnp.where(even, to_lower, to_upper).astype(BF16)


def slab_start(widths):
    slab = lax.axis_index("gx")
    start = jnp.int32(0)
    for d in range(widths.shape[0]):
        start = start + jnp.where(d < slab, widths[d], 0)
    return start


def depth_row(weights, depth, edge, z, x):
    return depth[z, x] + weights[DW_BIAS] + edge_term(edge, z, x)


def base_row(cells, lifted, phase, z, x):
    channels = lifted.shape[1]
    slots = cells.shape[1] // channels
    return cells[2 + z, pl.ds(x, channels, stride=slots), :] + lifted[lax.div(phase + x, CF)]


def active(weights, mixed):
    mixed = mixed + weights[PW_BIAS]
    return jnp.maximum(mixed, 0.2 * mixed)


def mix_kernel(gathered, widths, mix, cells, weights, depth, edge, *refs):
    if gathered:
        coarse, value, ends, bases, lifted, across, mixer = refs
        parts, ncx, ncy = coarse.shape
    else:
        first, second, own_block, opposite, value, ends, bases, lifted, across, mixer, blocks = refs
        parts, own_rows, ncy = own_block.shape
        ncx = 4 * own_rows
    width = widths[lax.axis_index("gx")]
    here = lax.axis_index("gy")
    start = slab_start(widths)
    phase = lax.rem(start, CF)
    channels, tile = weights.shape[1:]
    slots = cells.shape[1] // channels

    if not gathered:
        count = parts * own_rows
        for message, owner in ((first, lax.rem(here + 3, 4)), (second, lax.rem(here + 1, 4))):
            terms = message[channels:, :].astype(F32)[0:count, :]
            sums = terms[:, 0:ncy] + terms[:, ncy : 2 * ncy] + terms[:, 2 * ncy : 3 * ncy]
            for k in range(parts):
                blocks[k, pl.ds(owner * own_rows, own_rows), :] = sums[k * own_rows : (k + 1) * own_rows]
        for block, owner in ((own_block, here), (opposite, lax.rem(here + 2, 4))):
            for k in range(parts):
                blocks[k, pl.ds(owner * own_rows, own_rows), :] = block[k]
    shape = (ncy, tile)
    cell = row_iota(shape) * CF
    place = lane_iota(shape) + here * tile
    along_y = ((place >= cell) & (place < cell + CF)).astype(F32)
    for k in range(parts):
        block = coarse[k] if gathered else blocks[k]
        across[k] = jnp.dot(block, along_y, precision=lax.Precision.HIGHEST, preferred_element_type=F32)
    for i in range(3):
        cell = lax.rem(lax.div(start, CF) + i, ncx)
        total = None
        for k in range(parts):
            term = weights[LIFT + k] * across[k, pl.ds(cell, 1), :]
            total = term if total is None else total + term
        lifted[i] = total

    group = 4
    wide = jnp.concatenate([mix[...]] * group, axis=1)
    wide = jnp.concatenate([wide] * group, axis=0)
    size = group * channels
    row, column = row_iota((size, size)), lane_iota((size, size))
    same = sum(
        ((row >= i * channels) & (row < (i + 1) * channels) & (column >= i * channels) & (column < (i + 1) * channels)).astype(F32)
        for i in range(group)
    )
    mixer[...] = jnp.where(same > 0, wide.astype(F32), 0.0).astype(BF16)

    def mix_rows(limit):
        for x in range(0, limit, group):
            depths = [
                jnp.concatenate([depth_row(weights, depth, edge, z, x + i) for i in range(group)], axis=0)
                for z in range(ZOUT)
            ]
            mixed = jnp.dot(mixer[...], jnp.concatenate(depths, axis=1).astype(BF16), preferred_element_type=F32)
            for i in range(group):
                for z in range(ZOUT):
                    part = mixed[i * channels : (i + 1) * channels, z * tile : (z + 1) * tile]
                    part = active(weights, part) + base_row(cells, lifted, phase, z, x + i)
                    if x + i >= limit - ROWS:
                        part = jnp.where(x + i < width, part, 0.0)
                    value[z, pl.ds(x + i, channels, stride=slots), :] = part
        for x in range(limit, slots):
            for z in range(ZOUT):
                value[z, pl.ds(x, channels, stride=slots), :] = jnp.zeros((channels, tile), F32)
        for z in range(ZOUT):
            for i, x in enumerate((0, 1, width - 2, width - 1)):
                ends[z, i] = depth_row(weights, depth, edge, z, x)
                bases[z, i] = base_row(cells, lifted, phase, z, x)

    for limit in range(ROWS, slots + 1, ROWS):
        pl.when((width > limit - ROWS) & (width <= limit))(lambda limit=limit: mix_rows(limit))


def finish_kernel(widths, mix, weights, ends, bases, far, near, value_in, out, value, block, sems):
    width = widths[lax.axis_index("gx")]
    channels, tile = weights.shape[1:]
    slots = block.shape[2]
    even = is_even("gx")
    mixed = []
    for z in range(ZOUT):
        sums = []
        for i in range(4):
            at = slice((2 * z + i % 2) * channels, (2 * z + i % 2 + 1) * channels)
            one, two = far[at, :].astype(F32), near[at, :].astype(F32)
            arrived = jnp.where(even, one, two) if i < 2 else jnp.where(even, two, one)
            sums.append((ends[z, i] + arrived).astype(BF16))
        mixed.append(jnp.dot(mix[...], jnp.concatenate(sums, axis=1), preferred_element_type=F32))
    copies = []
    for z in range(ZOUT):
        for part in range(channels // CHUNK):
            at = slice(part * CHUNK, (part + 1) * CHUNK)
            for i, x in enumerate((0, 1, width - 2, width - 1)):
                rows = mixed[z][at, i * tile : (i + 1) * tile] + weights[PW_BIAS, at, :]
                rows = jnp.maximum(rows, 0.2 * rows) + bases[z, i, at, :]
                value[z, pl.ds(part * CHUNK * slots + x, CHUNK, stride=slots), :] = rows
            for o in range(part * CHUNK, (part + 1) * CHUNK):
                block[z, o] = value[z, o * slots : (o + 1) * slots, :].astype(BF16)
            part_of = pl.ds(part * CHUNK, CHUNK)
            copy = pltpu.make_async_copy(block.at[z, part_of], out.at[z, part_of], sems.at[part, z])
            copy.start()
            copies.append(copy)
    for copy in copies:
        copy.wait()


def shards(feature, widths, dw_weight, dw_bias, pw_weight, pw_bias, lift_weight, coarse):
    planes, channels, slots, tile = feature.shape
    ny = lax.axis_size("gy")
    parts, own_rows, ncy = coarse.shape
    gathered = ny != 4
    ncx = ny * own_rows
    smem = pl.BlockSpec(memory_space=pltpu.SMEM)
    vmem = pl.BlockSpec(memory_space=pltpu.VMEM)
    hbm = pl.BlockSpec(memory_space=pltpu.HBM)
    params = pltpu.CompilerParams(vmem_limit_bytes=VMEM_BYTES)
    shape = jax.ShapeDtypeStruct
    strip = shape((channels + 16, tile), BF16)
    cells_shape = pltpu.VMEM((planes, channels * slots, tile), F32)
    value_shape = pltpu.VMEM((ZOUT, channels * slots, tile), F32)
    message = shape((2 * ZOUT * channels, tile), BF16)

    def swapped(array, axis, first):
        count = lax.axis_size(axis)
        pairs = []
        for i in range(first, count + first, 2):
            a, b = i % count, (i + 1) % count
            pairs += [(a, b), (b, a)]
        return lax.ppermute(array, axis, pairs)

    def pinned(array):
        return pltpu.with_memory_space_constraint(array, pltpu.HBM)

    if gathered:
        every = lax.all_gather(coarse, "gy", axis=1, tiled=True)
    small = (
        widths,
        dw_weight,
        dw_bias.reshape(1, channels),
        pw_bias.reshape(1, channels),
        lift_weight.T,
        coarse,
    )
    cells, weights, first, second, block, slab_widths = pl.pallas_call(
        pack_kernel,
        out_shape=(
            cells_shape,
            pltpu.VMEM((32, channels, tile), F32),
            strip,
            strip,
            pltpu.VMEM(coarse.shape, F32),
            pltpu.SMEM(widths.shape, jnp.int32),
        ),
        in_specs=[hbm] * 7,
        out_specs=(vmem,) * 5 + (smem,),
        scratch_shapes=[
            pltpu.VMEM(feature.shape, BF16),
            pltpu.SMEM(widths.shape, jnp.int32),
            pltpu.VMEM(dw_weight.shape, F32),
            pltpu.VMEM((1, channels), F32),
            pltpu.VMEM((1, channels), F32),
            pltpu.VMEM((parts, channels), F32),
            pltpu.VMEM(coarse.shape, F32),
            pltpu.VMEM((32, channels), F32),
            pltpu.VMEM((16, tile), F32),
            pltpu.VMEM((3, 2, channels, tile), F32),
            pltpu.SemaphoreType.DMA((3, 2)),
            pltpu.SemaphoreType.DMA((len(small),)),
        ],
        compiler_params=params,
    )(pinned(feature), *(pinned(array) for array in small))
    first = lax.ppermute(first, "gy", [(i, (i + 1) % ny) for i in range(ny)])
    second = lax.ppermute(second, "gy", [((i + 1) % ny, i) for i in range(ny)])
    cells, rims, own_block = pl.pallas_call(
        outer_kernel,
        out_shape=(
            cells_shape,
            pltpu.VMEM((ZOUT, 4, channels, tile), F32),
            pltpu.VMEM(coarse.shape, F32),
        ),
        in_specs=[smem] + [vmem] * 3,
        out_specs=(vmem,) * 3,
        input_output_aliases={3: 0},
        compiler_params=params,
        cost_estimate=pl.CostEstimate(flops=10**8, bytes_accessed=10**6, transcendentals=0),
    )(slab_widths, weights, block, cells)
    if not gathered:
        opposite = lax.ppermute(own_block, "gy", [(i, (i + 2) % 4) for i in range(4)])
    edge, far, near = pl.pallas_call(
        rim_kernel,
        out_shape=(pltpu.VMEM((2, channels, tile), F32), message, message),
        in_specs=[smem] + [vmem] * 3,
        out_specs=(vmem,) * 3,
        compiler_params=params,
    )(slab_widths, first, second, rims)
    far = swapped(far, "gx", 1)
    near = swapped(near, "gx", 0)
    blocks = (every,) if gathered else (first, second, own_block, opposite)
    depth = pl.pallas_call(
        conv_kernel,
        out_shape=pltpu.VMEM((ZOUT, slots, channels, tile), F32),
        in_specs=[smem] + [vmem] * 3,
        out_specs=vmem,
        compiler_params=params,
        cost_estimate=pl.CostEstimate(flops=10**9, bytes_accessed=10**6, transcendentals=0),
    )(slab_widths, edge, cells, weights)
    ends_shape = pltpu.VMEM((ZOUT, 4, channels, tile), F32)
    value, ends, bases = pl.pallas_call(
        functools.partial(mix_kernel, gathered),
        out_shape=(value_shape, ends_shape, ends_shape),
        in_specs=[smem] + [vmem] * (5 + len(blocks)),
        out_specs=(vmem,) * 3,
        scratch_shapes=[
            pltpu.VMEM((3, channels, tile), F32),
            pltpu.VMEM((parts, ncx, tile), F32),
            pltpu.VMEM((4 * channels, 4 * channels), BF16),
        ]
        + ([] if gathered else [pltpu.VMEM((parts, ncx, ncy), F32)]),
        compiler_params=params,
        cost_estimate=pl.CostEstimate(flops=10**9, bytes_accessed=10**6, transcendentals=0),
    )(slab_widths, pw_weight, cells, weights, depth, edge, *blocks)
    out, _ = pl.pallas_call(
        finish_kernel,
        out_shape=(shape((ZOUT, channels, slots, tile), BF16), value_shape),
        in_specs=[smem] + [vmem] * 7,
        out_specs=(hbm, vmem),
        scratch_shapes=[
            pltpu.VMEM((ZOUT, channels, slots, tile), BF16),
            pltpu.SemaphoreType.DMA((channels // CHUNK, ZOUT)),
        ],
        input_output_aliases={7: 1},
        compiler_params=params,
    )(slab_widths, pw_weight, weights, ends, bases, far, near, value)
    return out


def solution(mesh):
    placed = (P(None, None, "gx", "gy"), P(), P(), P(), P(), P(), P(), P(None, "gy", None))
    return jax.shard_map(
        shards, mesh=mesh, in_specs=placed, out_specs=P(None, None, "gx", "gy"), check_vma=False
    )
```

```python
import functools

import jax
import jax.numpy as jnp
from jax import lax
from jax.experimental import pallas as pl
from jax.experimental.pallas import tpu as pltpu
from jax.sharding import PartitionSpec as P

XW = 16
ZOUT = 2
CF = 16
ROWS = 8
SPLIT = 1
CHUNK = 16
DW_BIAS, PW_BIAS, LIFT = 27, 28, 29
F32 = jnp.float32
BF16 = jnp.bfloat16
VMEM_BYTES = 14 * 1024 * 1024


def lane_iota(shape):
    return lax.broadcasted_iota(jnp.int32, shape, len(shape) - 1)


def row_iota(shape):
    return lax.broadcasted_iota(jnp.int32, shape, len(shape) - 2)


def tap_of(m, dx, dy):
    return 9 * m + 3 * (dx + 1) + (dy + 1)


def is_even(axis):
    return lax.rem(lax.axis_index(axis), 2) == 0


def pack_kernel(
    feature, widths_in, taps_in, dw_bias_in, pw_bias_in, lift_in, coarse_in,
    cells, weights, first, second, own_block, widths,
    planes, widths_here, taps, dw_bias, pw_bias, lift, coarse, stacked, tail, picked, sems, small_sems,
):
    count, channels, slots, tile = feature.shape

    half_of = channels // 2

    def copy_of(m, part):
        at = (pl.ds(ZOUT * m, ZOUT), pl.ds(part * half_of, half_of))
        return pltpu.make_async_copy(feature.at[at], planes.at[at], sems.at[m, part])

    small = [
        pltpu.make_async_copy(source, target, small_sems.at[i])
        for i, (source, target) in enumerate(
            (
                (widths_in, widths_here),
                (taps_in, taps),
                (dw_bias_in, dw_bias),
                (pw_bias_in, pw_bias),
                (lift_in, lift),
                (coarse_in, coarse),
            )
        )
    ]
    for copy in small:
        copy.start()
    for m in range(3):
        for part in range(2):
            copy_of(m, part).start()
    def take_small():
        for copy in small:
            copy.wait()
        for d in range(widths.shape[0]):
            widths[d] = widths_here[d]
        stacked[0:DW_BIAS, :] = taps[...]
        stacked[DW_BIAS : DW_BIAS + 1, :] = dw_bias[...]
        stacked[PW_BIAS : PW_BIAS + 1, :] = pw_bias[...]
        stacked[LIFT : LIFT + 3, :] = lift[...]
        turned = jnp.transpose(stacked[...])
        for t in range(stacked.shape[0]):
            weights[t] = jnp.broadcast_to(turned[:, t : t + 1], (channels, tile))

        own_block[...] = coarse[...]
        parts, own_rows, ncy = coarse.shape
        tail[...] = jnp.zeros_like(tail)
        if 3 * ncy <= tile:
            for k in range(parts):
                rest = coarse[k]
                for p in range(3):
                    term = rest.astype(BF16).astype(F32)
                    rest = rest - term
                    tail[k * own_rows : (k + 1) * own_rows, p * ncy : (p + 1) * ncy] = term
        for message in (first, second):
            message[channels:, :] = tail[...].astype(BF16)

    lane, row = lane_iota((slots, tile)), row_iota((slots, tile))
    mine = (lane >> 3) == (row & 15)
    in_even, in_odd = mine & ((lane & 4) == 0), mine & ((lane & 4) != 0)
    sublane = row_iota((ROWS, tile))

    def placed(m, k):
        both = []
        for z in range(ZOUT):
            plane = planes[ZOUT * m + z, k].astype(F32)
            cells[ZOUT * m + z, k * slots : (k + 1) * slots, :] = plane
            both.append(
                jnp.concatenate(
                    [
                        pltpu.roll(plane[x : x + ROWS], (2 + 4 * z + 8 * x) % tile, 1, stride=8, stride_axis=0)
                        for x in range(0, slots, ROWS)
                    ],
                    axis=0,
                )
            )
        rows = jnp.where(in_even, both[0], jnp.where(in_odd, both[1], 0.0))
        return rows[0:ROWS] + rows[ROWS : 2 * ROWS], rows[2 * ROWS :]

    def summed(m, k, step):
        if step == 0:
            return placed(m, k)
        one, two = summed(m, k, step // 2), summed(m, k + step, step // 2)
        turn = (sublane & step) != 0
        return tuple(
            jnp.where(turn, b, a) + pltpu.roll(jnp.where(turn, a, b), step, 0) for a, b in zip(one, two)
        )

    for m in range(3):
        for part in range(2):
            copy_of(m, part).wait()
            for c in range(part * half_of, (part + 1) * half_of, ROWS):
                for half, total in enumerate(summed(m, c, ROWS // 2)):
                    picked[m, half, c : c + ROWS, :] = total
        if m == 0:
            take_small()
    width = widths_here[lax.axis_index("gx")]

    shape = (channels, tile)
    lane = lane_iota(shape)
    on_left = (lane & 2) != 0
    packed = [None, None]
    for m in range(3):
        low, high = (jnp.where(16 * half + (lane >> 3) < width, picked[m, half], 0.0) for half in range(2))
        moved = {
            -1: tuple(
                pltpu.roll(jnp.where(lane < tile - 16, one, two), 16, 1) for one, two in ((low, high), (high, low))
            ),
            0: (low, high),
            1: tuple(
                pltpu.roll(jnp.where(lane >= 16, one, two), tile - 16, 1) for one, two in ((low, high), (high, low))
            ),
        }
        for dx in (-1, 0, 1):
            weight = jnp.where(on_left, weights[tap_of(m, dx, 1)], weights[tap_of(m, dx, -1)])
            for half in range(2):
                term = weight * moved[dx][half]
                packed[half] = term if packed[half] is None else packed[half] + term
    left = jnp.where(on_left, packed[0], pltpu.roll(packed[1], tile - 2, 1))
    right = jnp.where(on_left, pltpu.roll(packed[1], 2, 1), packed[0])
    first[0:channels, :] = right.astype(BF16)
    second[0:channels, :] = left.astype(BF16)


def shifted_sum(before, centre, after):
    lane = lane_iota(centre.shape)
    tile = centre.shape[-1]
    before = jnp.where(lane < 2, 0.0, pltpu.roll(before, 2, 1))
    after = jnp.where(lane >= tile - 2, 0.0, pltpu.roll(after, tile - 2, 1))
    return centre + before + after


def convolve_block(cells, weights, depth, b, first, limit):
    channels = weights.shape[1]
    slots = cells.shape[1] // channels
    at = pl.ds(pl.multiple_of(b * ROWS, ROWS), ROWS)
    to = pl.ds(pl.multiple_of((b - first) * ROWS, ROWS), ROWS)
    tap = [weights[t, at, :] for t in range(27)]
    for z in range(ZOUT):
        for parity in range(2):
            sums = {}
            for x in range(parity, limit, 2):
                rows = [cells[z + ZOUT * m, pl.ds(b * (ROWS * slots) + x, ROWS, stride=slots), :] for m in range(3)]
                for m in range(3):
                    for dx in (1, 0, -1):
                        out = x - 2 * dx
                        if 0 <= out < limit:
                            for dy in (-1, 0, 1):
                                term = tap[tap_of(m, dx, dy)] * rows[m]
                                key = (out, dy)
                                sums[key] = sums[key] + term if key in sums else term
                for out in [x - 2] if x + 2 < limit else [x - 2, x]:
                    if out >= 0:
                        depth[z, out, to, :] = shifted_sum(*(sums.pop((out, dy)) for dy in (-1, 0, 1)))


def outer_kernel(widths, weights, coarse, cells_in, cells, rims, own_block):
    width = widths[lax.axis_index("gx")]
    channels, tile = weights.shape[1:]
    slots = cells.shape[1] // channels
    own_block[...] = coarse[...]
    for b in range(channels // ROWS):
        at = slice(b * ROWS, (b + 1) * ROWS)
        for side, dx in enumerate((1, -1)):
            tap = [[weights[tap_of(m, dx, dy), at, :] for m in range(3)] for dy in (-1, 0, 1)]
            for r in range(2):
                x = r if side == 0 else width - 2 + r
                for z in range(ZOUT):
                    rows = [
                        cells[z + ZOUT * m, pl.ds(b * (ROWS * slots) + x, ROWS, stride=slots), :] for m in range(3)
                    ]
                    parts = [sum(weight * row for weight, row in zip(weights_of, rows)) for weights_of in tap]
                    rims[z, 2 * side + r, at, :] = shifted_sum(*parts)
    for r in range(2):

        @pl.when(width + r < slots)
        def _():
            for z in range(cells.shape[0]):
                cells[z, pl.ds(width + r, channels, stride=slots), :] = jnp.zeros((channels, tile), F32)


def convolve_blocks(widths, cells, weights, depth, first, last):
    width = widths[lax.axis_index("gx")]
    slots = cells.shape[1] // weights.shape[1]
    for limit in range(ROWS, slots + 1, ROWS):

        @pl.when((width > limit - ROWS) & (width <= limit))
        def _():
            def convolve(b, carry):
                convolve_block(cells, weights, depth, b, first, limit)
                return carry

            lax.fori_loop(first, last, convolve, 0)


def early_kernel(widths, cells, weights, depth):
    convolve_blocks(widths, cells, weights, depth, 0, SPLIT)


def rest_kernel(widths, edge, cells, weights, depth):
    convolve_blocks(widths, cells, weights, depth, SPLIT, weights.shape[1] // ROWS)


def edge_term(edge, z, x):
    tile = edge.shape[2]
    begin = 8 * (x & 15) + 4 * z
    cells = pltpu.roll(edge[(x >> 4) & 1], (tile - 2 - begin) & (tile - 1), 1)
    lane = lane_iota(cells.shape)
    return jnp.where((lane < 2) | (lane >= tile - 2), cells, 0.0)


def rim_kernel(widths, first, second, rims, edge, far, near):
    width = widths[lax.axis_index("gx")]
    _, _, channels, tile = rims.shape
    left, right = first[0:channels, :].astype(F32), second[0:channels, :].astype(F32)
    on_left = (lane_iota((channels, tile)) & 2) != 0
    edge[0] = jnp.where(on_left, pltpu.roll(left, 2, 1), pltpu.roll(right, tile - 2, 1))
    edge[1] = jnp.where(on_left, left, right)
    even = is_even("gx")
    for z in range(ZOUT):
        for r in range(2):
            to_lower = rims[z, r] + edge_term(edge, z, r - 2)
            to_upper = rims[z, 2 + r] + edge_term(edge, z, width + r)
            at = slice((2 * z + r) * channels, (2 * z + r + 1) * channels)
            near[at, :] = jnp.where(even, to_upper, to_lower).astype(BF16)
            far[at, :] = jnp.where(even, to_lower, to_upper).astype(BF16)


def slab_start(widths):
    slab = lax.axis_index("gx")
    start = jnp.int32(0)
    for d in range(widths.shape[0]):
        start = start + jnp.where(d < slab, widths[d], 0)
    return start


def depth_row(weights, depths, edge, z, x):
    own = jnp.concatenate([depth[z, x] for depth in depths], axis=0)
    return own + weights[DW_BIAS] + edge_term(edge, z, x)


def base_row(cells, lifted, phase, z, x):
    channels = lifted.shape[1]
    slots = cells.shape[1] // channels
    return cells[2 + z, pl.ds(x, channels, stride=slots), :] + lifted[lax.div(phase + x, CF)]


def active(weights, mixed):
    mixed = mixed + weights[PW_BIAS]
    return jnp.maximum(mixed, 0.2 * mixed)


def mix_kernel(gathered, widths, mix, cells, weights, depth, rest, edge, *refs):
    if gathered:
        coarse, value, ends, bases, lifted, across, mixer = refs
        parts, ncx, ncy = coarse.shape
    else:
        first, second, own_block, opposite, value, ends, bases, lifted, across, mixer, blocks = refs
        parts, own_rows, ncy = own_block.shape
        ncx = 4 * own_rows
    width = widths[lax.axis_index("gx")]
    here = lax.axis_index("gy")
    start = slab_start(widths)
    phase = lax.rem(start, CF)
    channels, tile = weights.shape[1:]
    slots = cells.shape[1] // channels

    if not gathered:
        count = parts * own_rows
        for message, owner in ((first, lax.rem(here + 3, 4)), (second, lax.rem(here + 1, 4))):
            terms = message[channels:, :].astype(F32)[0:count, :]
            sums = terms[:, 0:ncy] + terms[:, ncy : 2 * ncy] + terms[:, 2 * ncy : 3 * ncy]
            for k in range(parts):
                blocks[k, pl.ds(owner * own_rows, own_rows), :] = sums[k * own_rows : (k + 1) * own_rows]
        for block, owner in ((own_block, here), (opposite, lax.rem(here + 2, 4))):
            for k in range(parts):
                blocks[k, pl.ds(owner * own_rows, own_rows), :] = block[k]
    shape = (ncy, tile)
    cell = row_iota(shape) * CF
    place = lane_iota(shape) + here * tile
    along_y = ((place >= cell) & (place < cell + CF)).astype(F32)
    for k in range(parts):
        block = coarse[k] if gathered else blocks[k]
        across[k] = jnp.dot(block, along_y, precision=lax.Precision.HIGHEST, preferred_element_type=F32)
    for i in range(3):
        cell = lax.rem(lax.div(start, CF) + i, ncx)
        total = None
        for k in range(parts):
            term = weights[LIFT + k] * across[k, pl.ds(cell, 1), :]
            total = term if total is None else total + term
        lifted[i] = total

    group = 4
    wide = jnp.concatenate([mix[...]] * group, axis=1)
    wide = jnp.concatenate([wide] * group, axis=0)
    size = group * channels
    row, column = row_iota((size, size)), lane_iota((size, size))
    same = sum(
        ((row >= i * channels) & (row < (i + 1) * channels) & (column >= i * channels) & (column < (i + 1) * channels)).astype(F32)
        for i in range(group)
    )
    mixer[...] = jnp.where(same > 0, wide.astype(F32), 0.0).astype(BF16)

    def mix_rows(begin, end):
        for x in range(begin, end, group):
            depths = [
                jnp.concatenate([depth_row(weights, (depth, rest), edge, z, x + i) for i in range(group)], axis=0)
                for z in range(ZOUT)
            ]
            mixed = jnp.dot(mixer[...], jnp.concatenate(depths, axis=1).astype(BF16), preferred_element_type=F32)
            for i in range(group):
                for z in range(ZOUT):
                    part = mixed[i * channels : (i + 1) * channels, z * tile : (z + 1) * tile]
                    part = active(weights, part) + base_row(cells, lifted, phase, z, x + i)
                    if x + i >= end - ROWS and begin:
                        part = jnp.where(x + i < width, part, 0.0)
                    value[z, pl.ds(x + i, channels, stride=slots), :] = part

    mix_rows(0, ROWS)
    for z in range(ZOUT):
        for i, x in enumerate((0, 1, width - 2, width - 1)):
            ends[z, i] = depth_row(weights, (depth, rest), edge, z, x)
            bases[z, i] = base_row(cells, lifted, phase, z, x)

    def further_rows(limit):
        mix_rows(ROWS, limit)
        for x in range(limit, slots):
            for z in range(ZOUT):
                value[z, pl.ds(x, channels, stride=slots), :] = jnp.zeros((channels, tile), F32)

    for limit in range(ROWS, slots + 1, ROWS):
        pl.when((width > limit - ROWS) & (width <= limit))(lambda limit=limit: further_rows(limit))


def finish_kernel(widths, mix, weights, ends, bases, far, near, value_in, out, value, block, sems):
    width = widths[lax.axis_index("gx")]
    channels, tile = weights.shape[1:]
    slots = block.shape[2]
    even = is_even("gx")
    mixed = []
    for z in range(ZOUT):
        sums = []
        for i in range(4):
            at = slice((2 * z + i % 2) * channels, (2 * z + i % 2 + 1) * channels)
            one, two = far[at, :].astype(F32), near[at, :].astype(F32)
            arrived = jnp.where(even, one, two) if i < 2 else jnp.where(even, two, one)
            sums.append((ends[z, i] + arrived).astype(BF16))
        mixed.append(jnp.dot(mix[...], jnp.concatenate(sums, axis=1), preferred_element_type=F32))
    copies = []
    for z in range(ZOUT):
        for part in range(channels // CHUNK):
            at = slice(part * CHUNK, (part + 1) * CHUNK)
            for i, x in enumerate((0, 1, width - 2, width - 1)):
                rows = mixed[z][at, i * tile : (i + 1) * tile] + weights[PW_BIAS, at, :]
                rows = jnp.maximum(rows, 0.2 * rows) + bases[z, i, at, :]
                value[z, pl.ds(part * CHUNK * slots + x, CHUNK, stride=slots), :] = rows
            for o in range(part * CHUNK, (part + 1) * CHUNK):
                block[z, o] = value[z, o * slots : (o + 1) * slots, :].astype(BF16)
            part_of = pl.ds(part * CHUNK, CHUNK)
            copy = pltpu.make_async_copy(block.at[z, part_of], out.at[z, part_of], sems.at[part, z])
            copy.start()
            copies.append(copy)
    for copy in copies:
        copy.wait()


def shards(feature, widths, dw_weight, dw_bias, pw_weight, pw_bias, lift_weight, coarse):
    planes, channels, slots, tile = feature.shape
    ny = lax.axis_size("gy")
    parts, own_rows, ncy = coarse.shape
    gathered = ny != 4
    ncx = ny * own_rows
    smem = pl.BlockSpec(memory_space=pltpu.SMEM)
    vmem = pl.BlockSpec(memory_space=pltpu.VMEM)
    hbm = pl.BlockSpec(memory_space=pltpu.HBM)
    params = pltpu.CompilerParams(vmem_limit_bytes=VMEM_BYTES)
    shape = jax.ShapeDtypeStruct
    strip = shape((channels + 16, tile), BF16)
    cells_shape = pltpu.VMEM((planes, channels * slots, tile), F32)
    value_shape = pltpu.VMEM((ZOUT, channels * slots, tile), F32)
    message = shape((2 * ZOUT * channels, tile), BF16)

    def swapped(array, axis, first):
        count = lax.axis_size(axis)
        pairs = []
        for i in range(first, count + first, 2):
            a, b = i % count, (i + 1) % count
            pairs += [(a, b), (b, a)]
        return lax.ppermute(array, axis, pairs)

    def pinned(array):
        return pltpu.with_memory_space_constraint(array, pltpu.HBM)

    if gathered:
        every = lax.all_gather(coarse, "gy", axis=1, tiled=True)
    small = (
        widths,
        dw_weight,
        dw_bias.reshape(1, channels),
        pw_bias.reshape(1, channels),
        lift_weight.T,
        coarse,
    )
    cells, weights, first, second, block, slab_widths = pl.pallas_call(
        pack_kernel,
        out_shape=(
            cells_shape,
            pltpu.VMEM((32, channels, tile), F32),
            strip,
            strip,
            pltpu.VMEM(coarse.shape, F32),
            pltpu.SMEM(widths.shape, jnp.int32),
        ),
        in_specs=[hbm] * 7,
        out_specs=(vmem,) * 5 + (smem,),
        scratch_shapes=[
            pltpu.VMEM(feature.shape, BF16),
            pltpu.SMEM(widths.shape, jnp.int32),
            pltpu.VMEM(dw_weight.shape, F32),
            pltpu.VMEM((1, channels), F32),
            pltpu.VMEM((1, channels), F32),
            pltpu.VMEM((parts, channels), F32),
            pltpu.VMEM(coarse.shape, F32),
            pltpu.VMEM((32, channels), F32),
            pltpu.VMEM((16, tile), F32),
            pltpu.VMEM((3, 2, channels, tile), F32),
            pltpu.SemaphoreType.DMA((3, 2)),
            pltpu.SemaphoreType.DMA((len(small),)),
        ],
        compiler_params=params,
    )(pinned(feature), *(pinned(array) for array in small))
    first = lax.ppermute(first, "gy", [(i, (i + 1) % ny) for i in range(ny)])
    second = lax.ppermute(second, "gy", [((i + 1) % ny, i) for i in range(ny)])
    cells, rims, own_block = pl.pallas_call(
        outer_kernel,
        out_shape=(
            cells_shape,
            pltpu.VMEM((ZOUT, 4, channels, tile), F32),
            pltpu.VMEM(coarse.shape, F32),
        ),
        in_specs=[smem] + [vmem] * 3,
        out_specs=(vmem,) * 3,
        input_output_aliases={3: 0},
        compiler_params=params,
        cost_estimate=pl.CostEstimate(flops=10**8, bytes_accessed=10**6, transcendentals=0),
    )(slab_widths, weights, block, cells)
    if not gathered:
        opposite = lax.ppermute(own_block, "gy", [(i, (i + 2) % 4) for i in range(4)])
    early = SPLIT * ROWS
    depth = pl.pallas_call(
        early_kernel,
        out_shape=pltpu.VMEM((ZOUT, slots, early, tile), F32),
        in_specs=[smem] + [vmem] * 2,
        out_specs=vmem,
        compiler_params=params,
        cost_estimate=pl.CostEstimate(flops=10**9, bytes_accessed=10**6, transcendentals=0),
    )(slab_widths, cells, weights)
    edge, far, near = pl.pallas_call(
        rim_kernel,
        out_shape=(pltpu.VMEM((2, channels, tile), F32), message, message),
        in_specs=[smem] + [vmem] * 3,
        out_specs=(vmem,) * 3,
        compiler_params=params,
    )(slab_widths, first, second, rims)
    far = swapped(far, "gx", 1)
    near = swapped(near, "gx", 0)
    blocks = (every,) if gathered else (first, second, own_block, opposite)
    rest = pl.pallas_call(
        rest_kernel,
        out_shape=pltpu.VMEM((ZOUT, slots, channels - early, tile), F32),
        in_specs=[smem] + [vmem] * 3,
        out_specs=vmem,
        compiler_params=params,
        cost_estimate=pl.CostEstimate(flops=10**9, bytes_accessed=10**6, transcendentals=0),
    )(slab_widths, edge, cells, weights)
    ends_shape = pltpu.VMEM((ZOUT, 4, channels, tile), F32)
    value, ends, bases = pl.pallas_call(
        functools.partial(mix_kernel, gathered),
        out_shape=(value_shape, ends_shape, ends_shape),
        in_specs=[smem] + [vmem] * (6 + len(blocks)),
        out_specs=(vmem,) * 3,
        scratch_shapes=[
            pltpu.VMEM((3, channels, tile), F32),
            pltpu.VMEM((parts, ncx, tile), F32),
            pltpu.VMEM((4 * channels, 4 * channels), BF16),
        ]
        + ([] if gathered else [pltpu.VMEM((parts, ncx, ncy), F32)]),
        compiler_params=params,
        cost_estimate=pl.CostEstimate(flops=10**9, bytes_accessed=10**6, transcendentals=0),
    )(slab_widths, pw_weight, cells, weights, depth, rest, edge, *blocks)
    out, _ = pl.pallas_call(
        finish_kernel,
        out_shape=(shape((ZOUT, channels, slots, tile), BF16), value_shape),
        in_specs=[smem] + [vmem] * 7,
        out_specs=(hbm, vmem),
        scratch_shapes=[
            pltpu.VMEM((ZOUT, channels, slots, tile), BF16),
            pltpu.SemaphoreType.DMA((channels // CHUNK, ZOUT)),
        ],
        input_output_aliases={7: 1},
        compiler_params=params,
    )(slab_widths, pw_weight, weights, ends, bases, far, near, value)
    return out


def solution(mesh):
    placed = (P(None, None, "gx", "gy"), P(), P(), P(), P(), P(), P(), P(None, "gy", None))
    return jax.shard_map(
        shards, mesh=mesh, in_specs=placed, out_specs=P(None, None, "gx", "gy"), check_vma=False
    )
```

```python
import functools

import jax
import jax.numpy as jnp
from jax import lax
from jax.experimental import pallas as pl
from jax.experimental.pallas import tpu as pltpu
from jax.sharding import PartitionSpec as P

XW = 16
ZOUT = 2
CF = 16
ROWS = 8
SPLIT = 1
STORED = 32
DW_BIAS, PW_BIAS, LIFT = 0, 1, 2
F32 = jnp.float32
BF16 = jnp.bfloat16
VMEM_BYTES = 14 * 1024 * 1024


def lane_iota(shape):
    return lax.broadcasted_iota(jnp.int32, shape, len(shape) - 1)


def row_iota(shape):
    return lax.broadcasted_iota(jnp.int32, shape, len(shape) - 2)


def tap_of(m, dx, dy):
    return 9 * m + 3 * (dx + 1) + (dy + 1)


def is_even(axis):
    return lax.rem(lax.axis_index(axis), 2) == 0


def pack_kernel(
    feature, widths_in, taps_in, coarse_in,
    cells, weights, first, second, own_block, widths,
    planes, widths_here, taps, coarse, tail, picked, sems, small_sems,
):
    count, channels, slots, tile = feature.shape

    def copy_of(m):
        at = pl.ds(ZOUT * m, ZOUT)
        return pltpu.make_async_copy(feature.at[at], planes.at[at], sems.at[m])

    small = [
        pltpu.make_async_copy(source, target, small_sems.at[i])
        for i, (source, target) in enumerate(
            (
                (widths_in, widths_here),
                (taps_in, taps),
                (coarse_in, coarse),
            )
        )
    ]
    copy_of(0).start()
    for copy in small:
        copy.start()
    for m in range(1, 3):
        copy_of(m).start()
    def take_small():
        for copy in small:
            copy.wait()
        for d in range(widths.shape[0]):
            widths[d] = widths_here[d]
        turned = jnp.transpose(taps[...])
        for t in range(weights.shape[0]):
            weights[t] = jnp.broadcast_to(turned[:, t : t + 1], (channels, tile))

        own_block[...] = coarse[...]
        parts, own_rows, ncy = coarse.shape
        tail[...] = jnp.zeros_like(tail)
        if 3 * ncy <= tile:
            for k in range(parts):
                rest = coarse[k]
                for p in range(3):
                    term = rest.astype(BF16).astype(F32)
                    rest = rest - term
                    tail[k * own_rows : (k + 1) * own_rows, p * ncy : (p + 1) * ncy] = term
        for message in (first, second):
            message[channels:, :] = tail[...].astype(BF16)

    lane, row = lane_iota((slots, tile)), row_iota((slots, tile))
    mine = (lane >> 3) == (row & 15)
    in_even, in_odd = mine & ((lane & 4) == 0), mine & ((lane & 4) != 0)
    sublane = row_iota((ROWS, tile))

    def placed(m, k):
        both = []
        for z in range(ZOUT):
            plane = planes[ZOUT * m + z, k].astype(F32)
            cells[ZOUT * m + z, k * slots : (k + 1) * slots, :] = plane
            both.append(
                jnp.concatenate(
                    [
                        pltpu.roll(plane[x : x + ROWS], (2 + 4 * z + 8 * x) % tile, 1, stride=8, stride_axis=0)
                        for x in range(0, slots, ROWS)
                    ],
                    axis=0,
                )
            )
        rows = jnp.where(in_even, both[0], jnp.where(in_odd, both[1], 0.0))
        return rows[0:ROWS] + rows[ROWS : 2 * ROWS], rows[2 * ROWS :]

    def summed(m, k, step):
        if step == 0:
            return placed(m, k)
        one, two = summed(m, k, step // 2), summed(m, k + step, step // 2)
        turn = (sublane & step) != 0
        return tuple(
            jnp.where(turn, b, a) + pltpu.roll(jnp.where(turn, a, b), step, 0) for a, b in zip(one, two)
        )

    for m in range(3):
        copy_of(m).wait()
        for c in range(0, channels, ROWS):
            for half, total in enumerate(summed(m, c, ROWS // 2)):
                picked[m, half, c : c + ROWS, :] = total
        if m == 0:
            take_small()
    width = widths_here[lax.axis_index("gx")]

    shape = (channels, tile)
    lane = lane_iota(shape)
    on_left = (lane & 2) != 0
    packed = [None, None]
    for m in range(3):
        low, high = (jnp.where(16 * half + (lane >> 3) < width, picked[m, half], 0.0) for half in range(2))
        moved = {
            -1: tuple(
                pltpu.roll(jnp.where(lane < tile - 16, one, two), 16, 1) for one, two in ((low, high), (high, low))
            ),
            0: (low, high),
            1: tuple(
                pltpu.roll(jnp.where(lane >= 16, one, two), tile - 16, 1) for one, two in ((low, high), (high, low))
            ),
        }
        for dx in (-1, 0, 1):
            weight = jnp.where(on_left, weights[tap_of(m, dx, 1)], weights[tap_of(m, dx, -1)])
            for half in range(2):
                term = weight * moved[dx][half]
                packed[half] = term if packed[half] is None else packed[half] + term
    left = jnp.where(on_left, packed[0], pltpu.roll(packed[1], tile - 2, 1))
    right = jnp.where(on_left, pltpu.roll(packed[1], 2, 1), packed[0])
    first[0:channels, :] = right.astype(BF16)
    second[0:channels, :] = left.astype(BF16)


def shifted_sum(before, centre, after):
    lane = lane_iota(centre.shape)
    tile = centre.shape[-1]
    before = jnp.where(lane < 2, 0.0, pltpu.roll(before, 2, 1))
    after = jnp.where(lane >= tile - 2, 0.0, pltpu.roll(after, tile - 2, 1))
    return centre + before + after


def convolve_block(cells, weights, depth, b, first, limit):
    channels = weights.shape[1]
    slots = cells.shape[1] // channels
    at = pl.ds(pl.multiple_of(b * ROWS, ROWS), ROWS)
    to = pl.ds(pl.multiple_of((b - first) * ROWS, ROWS), ROWS)
    tap = [weights[t, at, :] for t in range(27)]
    for z in range(ZOUT):
        for parity in range(2):
            sums = {}
            for x in range(parity, limit, 2):
                rows = [cells[z + ZOUT * m, pl.ds(b * (ROWS * slots) + x, ROWS, stride=slots), :] for m in range(3)]
                for m in range(3):
                    for dx in (1, 0, -1):
                        out = x - 2 * dx
                        if 0 <= out < limit:
                            for dy in (-1, 0, 1):
                                term = tap[tap_of(m, dx, dy)] * rows[m]
                                key = (out, dy)
                                sums[key] = sums[key] + term if key in sums else term
                for out in [x - 2] if x + 2 < limit else [x - 2, x]:
                    if out >= 0:
                        depth[z, out, to, :] = shifted_sum(*(sums.pop((out, dy)) for dy in (-1, 0, 1)))


def outer_kernel(widths, weights, dw_bias, pw_bias, lift, coarse, cells_in, cells, extras, rims, own_block, stacked):
    width = widths[lax.axis_index("gx")]
    channels, tile = weights.shape[1:]
    slots = cells.shape[1] // channels
    own_block[...] = coarse[...]
    stacked[DW_BIAS : DW_BIAS + 1, :] = dw_bias[...]
    stacked[PW_BIAS : PW_BIAS + 1, :] = pw_bias[...]
    stacked[LIFT : LIFT + 3, :] = lift[...]
    turned = jnp.transpose(stacked[...])
    for t in range(extras.shape[0]):
        extras[t] = jnp.broadcast_to(turned[:, t : t + 1], (channels, tile))
    for b in range(channels // ROWS):
        at = slice(b * ROWS, (b + 1) * ROWS)
        for side, dx in enumerate((1, -1)):
            tap = [[weights[tap_of(m, dx, dy), at, :] for m in range(3)] for dy in (-1, 0, 1)]
            for r in range(2):
                x = r if side == 0 else width - 2 + r
                for z in range(ZOUT):
                    rows = [
                        cells[z + ZOUT * m, pl.ds(b * (ROWS * slots) + x, ROWS, stride=slots), :] for m in range(3)
                    ]
                    parts = [sum(weight * row for weight, row in zip(weights_of, rows)) for weights_of in tap]
                    rims[z, 2 * side + r, at, :] = shifted_sum(*parts)
    for r in range(2):

        @pl.when(width + r < slots)
        def _():
            for z in range(cells.shape[0]):
                cells[z, pl.ds(width + r, channels, stride=slots), :] = jnp.zeros((channels, tile), F32)


def convolve_blocks(widths, cells, weights, depth, first, last):
    width = widths[lax.axis_index("gx")]
    slots = cells.shape[1] // weights.shape[1]
    for limit in range(ROWS, slots + 1, ROWS):

        @pl.when((width > limit - ROWS) & (width <= limit))
        def _():
            def convolve(b, carry):
                convolve_block(cells, weights, depth, b, first, limit)
                return carry

            lax.fori_loop(first, last, convolve, 0)


def early_kernel(widths, cells, weights, depth):
    convolve_blocks(widths, cells, weights, depth, 0, SPLIT)


def rest_kernel(widths, edge, cells, weights, depth):
    convolve_blocks(widths, cells, weights, depth, SPLIT, weights.shape[1] // ROWS)


def edge_term(edge, z, x):
    tile = edge.shape[2]
    begin = 8 * (x & 15) + 4 * z
    cells = pltpu.roll(edge[(x >> 4) & 1], (tile - 2 - begin) & (tile - 1), 1)
    lane = lane_iota(cells.shape)
    return jnp.where((lane < 2) | (lane >= tile - 2), cells, 0.0)


def rim_kernel(widths, first, second, rims, edge, far, near):
    width = widths[lax.axis_index("gx")]
    _, _, channels, tile = rims.shape
    left, right = first[0:channels, :].astype(F32), second[0:channels, :].astype(F32)
    on_left = (lane_iota((channels, tile)) & 2) != 0
    edge[0] = jnp.where(on_left, pltpu.roll(left, 2, 1), pltpu.roll(right, tile - 2, 1))
    edge[1] = jnp.where(on_left, left, right)
    even = is_even("gx")
    for z in range(ZOUT):
        for r in range(2):
            to_lower = rims[z, r] + edge_term(edge, z, r - 2)
            to_upper = rims[z, 2 + r] + edge_term(edge, z, width + r)
            at = slice((2 * z + r) * channels, (2 * z + r + 1) * channels)
            near[at, :] = jnp.where(even, to_upper, to_lower).astype(BF16)
            far[at, :] = jnp.where(even, to_lower, to_upper).astype(BF16)


def slab_start(widths):
    slab = lax.axis_index("gx")
    start = jnp.int32(0)
    for d in range(widths.shape[0]):
        start = start + jnp.where(d < slab, widths[d], 0)
    return start


def depth_row(extras, depths, edge, z, x):
    own = jnp.concatenate([depth[z, x] for depth in depths], axis=0)
    return own + extras[DW_BIAS] + edge_term(edge, z, x)


def base_row(cells, lifted, phase, z, x):
    channels = lifted.shape[1]
    slots = cells.shape[1] // channels
    return cells[2 + z, pl.ds(x, channels, stride=slots), :] + lifted[lax.div(phase + x, CF)]


def active(extras, mixed):
    mixed = mixed + extras[PW_BIAS]
    return jnp.maximum(mixed, 0.2 * mixed)


def mix_kernel(gathered, widths, mix, cells, extras, depth, rest, edge, *refs):
    if gathered:
        coarse, value, ends, bases, lifted, across, mixer = refs
        parts, ncx, ncy = coarse.shape
    else:
        first, second, own_block, opposite, value, ends, bases, lifted, across, mixer, blocks = refs
        parts, own_rows, ncy = own_block.shape
        ncx = 4 * own_rows
    width = widths[lax.axis_index("gx")]
    here = lax.axis_index("gy")
    start = slab_start(widths)
    phase = lax.rem(start, CF)
    channels, tile = extras.shape[1:]
    slots = cells.shape[1] // channels

    if not gathered:
        count = parts * own_rows
        for message, owner in ((first, lax.rem(here + 3, 4)), (second, lax.rem(here + 1, 4))):
            terms = message[channels:, :].astype(F32)[0:count, :]
            sums = terms[:, 0:ncy] + terms[:, ncy : 2 * ncy] + terms[:, 2 * ncy : 3 * ncy]
            for k in range(parts):
                blocks[k, pl.ds(owner * own_rows, own_rows), :] = sums[k * own_rows : (k + 1) * own_rows]
        for block, owner in ((own_block, here), (opposite, lax.rem(here + 2, 4))):
            for k in range(parts):
                blocks[k, pl.ds(owner * own_rows, own_rows), :] = block[k]
    shape = (ncy, tile)
    cell = row_iota(shape) * CF
    place = lane_iota(shape) + here * tile
    along_y = ((place >= cell) & (place < cell + CF)).astype(F32)
    for k in range(parts):
        block = coarse[k] if gathered else blocks[k]
        across[k] = jnp.dot(block, along_y, precision=lax.Precision.HIGHEST, preferred_element_type=F32)
    for i in range(3):
        cell = lax.rem(lax.div(start, CF) + i, ncx)
        total = None
        for k in range(parts):
            term = extras[LIFT + k] * across[k, pl.ds(cell, 1), :]
            total = term if total is None else total + term
        lifted[i] = total

    group = 4
    wide = jnp.concatenate([mix[...]] * group, axis=1)
    wide = jnp.concatenate([wide] * group, axis=0)
    size = group * channels
    row, column = row_iota((size, size)), lane_iota((size, size))
    same = sum(
        ((row >= i * channels) & (row < (i + 1) * channels) & (column >= i * channels) & (column < (i + 1) * channels)).astype(F32)
        for i in range(group)
    )
    mixer[...] = jnp.where(same > 0, wide.astype(F32), 0.0).astype(BF16)

    def mix_rows(begin, end):
        for x in range(begin, end, group):
            depths = [
                jnp.concatenate([depth_row(extras, (depth, rest), edge, z, x + i) for i in range(group)], axis=0)
                for z in range(ZOUT)
            ]
            mixed = jnp.dot(mixer[...], jnp.concatenate(depths, axis=1).astype(BF16), preferred_element_type=F32)
            for i in range(group):
                for z in range(ZOUT):
                    part = mixed[i * channels : (i + 1) * channels, z * tile : (z + 1) * tile]
                    part = active(extras, part) + base_row(cells, lifted, phase, z, x + i)
                    if x + i >= end - ROWS and begin:
                        part = jnp.where(x + i < width, part, 0.0)
                    value[z, pl.ds(x + i, channels, stride=slots), :] = part

    mix_rows(0, ROWS)
    for z in range(ZOUT):
        for i, x in enumerate((0, 1, width - 2, width - 1)):
            ends[z, i] = depth_row(extras, (depth, rest), edge, z, x)
            bases[z, i] = base_row(cells, lifted, phase, z, x)

    def further_rows(limit):
        mix_rows(ROWS, limit)
        for x in range(limit, slots):
            for z in range(ZOUT):
                value[z, pl.ds(x, channels, stride=slots), :] = jnp.zeros((channels, tile), F32)

    for limit in range(ROWS, slots + 1, ROWS):
        pl.when((width > limit - ROWS) & (width <= limit))(lambda limit=limit: further_rows(limit))


def finish_kernel(widths, mix, extras, ends, bases, far, near, value_in, out, value, block, sems):
    width = widths[lax.axis_index("gx")]
    channels, tile = extras.shape[1:]
    slots = block.shape[2]
    even = is_even("gx")
    mixed = []
    for z in range(ZOUT):
        sums = []
        for i in range(4):
            at = slice((2 * z + i % 2) * channels, (2 * z + i % 2 + 1) * channels)
            one, two = far[at, :].astype(F32), near[at, :].astype(F32)
            arrived = jnp.where(even, one, two) if i < 2 else jnp.where(even, two, one)
            sums.append((ends[z, i] + arrived).astype(BF16))
        mixed.append(jnp.dot(mix[...], jnp.concatenate(sums, axis=1), preferred_element_type=F32))
    copies = []
    for z in range(ZOUT):
        for part in range(channels // STORED):
            at = slice(part * STORED, (part + 1) * STORED)
            for i, x in enumerate((0, 1, width - 2, width - 1)):
                rows = mixed[z][at, i * tile : (i + 1) * tile] + extras[PW_BIAS, at, :]
                rows = jnp.maximum(rows, 0.2 * rows) + bases[z, i, at, :]
                value[z, pl.ds(part * STORED * slots + x, STORED, stride=slots), :] = rows
            for o in range(part * STORED, (part + 1) * STORED):
                block[z, o] = value[z, o * slots : (o + 1) * slots, :].astype(BF16)
            part_of = pl.ds(part * STORED, STORED)
            copy = pltpu.make_async_copy(block.at[z, part_of], out.at[z, part_of], sems.at[part, z])
            copy.start()
            copies.append(copy)
    for copy in copies:
        copy.wait()


def shards(feature, widths, dw_weight, dw_bias, pw_weight, pw_bias, lift_weight, coarse):
    planes, channels, slots, tile = feature.shape
    ny = lax.axis_size("gy")
    parts, own_rows, ncy = coarse.shape
    gathered = ny != 4
    ncx = ny * own_rows
    smem = pl.BlockSpec(memory_space=pltpu.SMEM)
    vmem = pl.BlockSpec(memory_space=pltpu.VMEM)
    hbm = pl.BlockSpec(memory_space=pltpu.HBM)
    params = pltpu.CompilerParams(vmem_limit_bytes=VMEM_BYTES)
    shape = jax.ShapeDtypeStruct
    strip = shape((channels + 16, tile), BF16)
    cells_shape = pltpu.VMEM((planes, channels * slots, tile), F32)
    value_shape = pltpu.VMEM((ZOUT, channels * slots, tile), F32)
    message = shape((2 * ZOUT * channels, tile), BF16)

    def swapped(array, axis, first):
        count = lax.axis_size(axis)
        pairs = []
        for i in range(first, count + first, 2):
            a, b = i % count, (i + 1) % count
            pairs += [(a, b), (b, a)]
        return lax.ppermute(array, axis, pairs)

    def pinned(array):
        return pltpu.with_memory_space_constraint(array, pltpu.HBM)

    if gathered:
        every = lax.all_gather(coarse, "gy", axis=1, tiled=True)
    small = (widths, dw_weight, coarse)
    cells, weights, first, second, block, slab_widths = pl.pallas_call(
        pack_kernel,
        out_shape=(
            cells_shape,
            pltpu.VMEM((27, channels, tile), F32),
            strip,
            strip,
            pltpu.VMEM(coarse.shape, F32),
            pltpu.SMEM(widths.shape, jnp.int32),
        ),
        in_specs=[hbm] * 4,
        out_specs=(vmem,) * 5 + (smem,),
        scratch_shapes=[
            pltpu.VMEM(feature.shape, BF16),
            pltpu.SMEM(widths.shape, jnp.int32),
            pltpu.VMEM(dw_weight.shape, F32),
            pltpu.VMEM(coarse.shape, F32),
            pltpu.VMEM((16, tile), F32),
            pltpu.VMEM((3, 2, channels, tile), F32),
            pltpu.SemaphoreType.DMA((3,)),
            pltpu.SemaphoreType.DMA((len(small),)),
        ],
        compiler_params=params,
    )(pinned(feature), *(pinned(array) for array in small))
    first = lax.ppermute(first, "gy", [(i, (i + 1) % ny) for i in range(ny)])
    second = lax.ppermute(second, "gy", [((i + 1) % ny, i) for i in range(ny)])
    cells, extras, rims, own_block = pl.pallas_call(
        outer_kernel,
        out_shape=(
            cells_shape,
            pltpu.VMEM((5, channels, tile), F32),
            pltpu.VMEM((ZOUT, 4, channels, tile), F32),
            pltpu.VMEM(coarse.shape, F32),
        ),
        in_specs=[smem] + [vmem] * 6,
        out_specs=(vmem,) * 4,
        scratch_shapes=[pltpu.VMEM((8, channels), F32)],
        input_output_aliases={6: 0},
        compiler_params=params,
        cost_estimate=pl.CostEstimate(flops=10**8, bytes_accessed=10**6, transcendentals=0),
    )(
        slab_widths, weights, dw_bias.reshape(1, channels), pw_bias.reshape(1, channels), lift_weight.T, block, cells
    )
    if not gathered:
        opposite = lax.ppermute(own_block, "gy", [(i, (i + 2) % 4) for i in range(4)])
    early = SPLIT * ROWS
    depth = pl.pallas_call(
        early_kernel,
        out_shape=pltpu.VMEM((ZOUT, slots, early, tile), F32),
        in_specs=[smem] + [vmem] * 2,
        out_specs=vmem,
        compiler_params=params,
        cost_estimate=pl.CostEstimate(flops=10**9, bytes_accessed=10**6, transcendentals=0),
    )(slab_widths, cells, weights)
    edge, far, near = pl.pallas_call(
        rim_kernel,
        out_shape=(pltpu.VMEM((2, channels, tile), F32), message, message),
        in_specs=[smem] + [vmem] * 3,
        out_specs=(vmem,) * 3,
        compiler_params=params,
    )(slab_widths, first, second, rims)
    far = swapped(far, "gx", 1)
    near = swapped(near, "gx", 0)
    blocks = (every,) if gathered else (first, second, own_block, opposite)
    rest = pl.pallas_call(
        rest_kernel,
        out_shape=pltpu.VMEM((ZOUT, slots, channels - early, tile), F32),
        in_specs=[smem] + [vmem] * 3,
        out_specs=vmem,
        compiler_params=params,
        cost_estimate=pl.CostEstimate(flops=10**9, bytes_accessed=10**6, transcendentals=0),
    )(slab_widths, edge, cells, weights)
    ends_shape = pltpu.VMEM((ZOUT, 4, channels, tile), F32)
    value, ends, bases = pl.pallas_call(
        functools.partial(mix_kernel, gathered),
        out_shape=(value_shape, ends_shape, ends_shape),
        in_specs=[smem] + [vmem] * (6 + len(blocks)),
        out_specs=(vmem,) * 3,
        scratch_shapes=[
            pltpu.VMEM((3, channels, tile), F32),
            pltpu.VMEM((parts, ncx, tile), F32),
            pltpu.VMEM((4 * channels, 4 * channels), BF16),
        ]
        + ([] if gathered else [pltpu.VMEM((parts, ncx, ncy), F32)]),
        compiler_params=params,
        cost_estimate=pl.CostEstimate(flops=10**9, bytes_accessed=10**6, transcendentals=0),
    )(slab_widths, pw_weight, cells, extras, depth, rest, edge, *blocks)
    out, _ = pl.pallas_call(
        finish_kernel,
        out_shape=(shape((ZOUT, channels, slots, tile), BF16), value_shape),
        in_specs=[smem] + [vmem] * 7,
        out_specs=(hbm, vmem),
        scratch_shapes=[
            pltpu.VMEM((ZOUT, channels, slots, tile), BF16),
            pltpu.SemaphoreType.DMA((channels // STORED, ZOUT)),
        ],
        input_output_aliases={7: 1},
        compiler_params=params,
    )(slab_widths, pw_weight, extras, ends, bases, far, near, value)
    return out


def solution(mesh):
    placed = (P(None, None, "gx", "gy"), P(), P(), P(), P(), P(), P(), P(None, "gy", None))
    return jax.shard_map(
        shards, mesh=mesh, in_specs=placed, out_specs=P(None, None, "gx", "gy"), check_vma=False
    )
```

```python
import functools

import jax
import jax.numpy as jnp
from jax import lax
from jax.experimental import pallas as pl
from jax.experimental.pallas import tpu as pltpu
from jax.sharding import PartitionSpec as P

XW = 16
ZOUT = 2
CF = 16
ROWS = 8
EARLY, EARLY_WIDE = 1, 3
STORED = 32
DW_BIAS, PW_BIAS, LIFT = 0, 1, 2
F32 = jnp.float32
BF16 = jnp.bfloat16
VMEM_BYTES = 14 * 1024 * 1024


def lane_iota(shape):
    return lax.broadcasted_iota(jnp.int32, shape, len(shape) - 1)


def row_iota(shape):
    return lax.broadcasted_iota(jnp.int32, shape, len(shape) - 2)


def tap_of(m, dx, dy):
    return 9 * m + 3 * (dx + 1) + (dy + 1)


def is_even(axis):
    return lax.rem(lax.axis_index(axis), 2) == 0


def pack_kernel(
    feature, widths_in, taps_in, coarse_in,
    cells, weights, first, second, own_block, widths,
    planes, widths_here, taps, coarse, tail, picked, sems, small_sems,
):
    count, channels, slots, tile = feature.shape

    def copy_of(m):
        at = pl.ds(ZOUT * m, ZOUT)
        return pltpu.make_async_copy(feature.at[at], planes.at[at], sems.at[m])

    small = [
        pltpu.make_async_copy(source, target, small_sems.at[i])
        for i, (source, target) in enumerate(
            (
                (widths_in, widths_here),
                (taps_in, taps),
                (coarse_in, coarse),
            )
        )
    ]
    copy_of(0).start()
    for copy in small:
        copy.start()
    for m in range(1, 3):
        copy_of(m).start()
    def take_small():
        for copy in small:
            copy.wait()
        for d in range(widths.shape[0]):
            widths[d] = widths_here[d]
        turned = jnp.transpose(taps[...])
        for t in range(weights.shape[0]):
            weights[t] = jnp.broadcast_to(turned[:, t : t + 1], (channels, tile))

        own_block[...] = coarse[...]
        parts, own_rows, ncy = coarse.shape
        tail[...] = jnp.zeros_like(tail)
        if 3 * ncy <= tile:
            for k in range(parts):
                rest = coarse[k]
                for p in range(3):
                    term = rest.astype(BF16).astype(F32)
                    rest = rest - term
                    tail[k * own_rows : (k + 1) * own_rows, p * ncy : (p + 1) * ncy] = term
        for message in (first, second):
            message[channels:, :] = tail[...].astype(BF16)

    lane, row = lane_iota((slots, tile)), row_iota((slots, tile))
    mine = (lane >> 3) == (row & 15)
    lane = lane_iota((ROWS * slots, tile))
    of_second = (lane >= 2) & (lane < 6)
    sublane = row_iota((ROWS, tile))

    def merged(m, c):
        rows = [planes[ZOUT * m + z, c : c + ROWS].reshape(ROWS * slots, tile) for z in range(ZOUT)]
        for z in range(ZOUT):
            cells[ZOUT * m + z, c * slots : (c + ROWS) * slots, :] = rows[z].astype(F32)
        return jnp.where(of_second, pltpu.roll(rows[1], 4, 1), rows[0]).astype(F32)

    def summed(rows, step):
        if step == 0:
            placed = jnp.concatenate(
                [
                    pltpu.roll(rows[x : x + ROWS], (2 + 8 * x) % tile, 1, stride=8, stride_axis=0)
                    for x in range(0, slots, ROWS)
                ],
                axis=0,
            )
            placed = jnp.where(mine, placed, 0.0)
            return placed[0:ROWS] + placed[ROWS : 2 * ROWS], placed[2 * ROWS :]
        one, two = summed(rows[: step * slots], step // 2), summed(rows[step * slots :], step // 2)
        turn = (sublane & step) != 0
        return tuple(
            jnp.where(turn, b, a) + pltpu.roll(jnp.where(turn, a, b), step, 0) for a, b in zip(one, two)
        )

    for m in range(3):
        copy_of(m).wait()
        for c in range(0, channels, ROWS):
            for half, total in enumerate(summed(merged(m, c), ROWS // 2)):
                picked[m, half, c : c + ROWS, :] = total
        if m == 0:
            take_small()
    width = widths_here[lax.axis_index("gx")]

    shape = (channels, tile)
    lane = lane_iota(shape)
    on_left = (lane & 2) != 0
    packed = [None, None]
    for m in range(3):
        low, high = (jnp.where(16 * half + (lane >> 3) < width, picked[m, half], 0.0) for half in range(2))
        moved = {
            -1: tuple(
                pltpu.roll(jnp.where(lane < tile - 16, one, two), 16, 1) for one, two in ((low, high), (high, low))
            ),
            0: (low, high),
            1: tuple(
                pltpu.roll(jnp.where(lane >= 16, one, two), tile - 16, 1) for one, two in ((low, high), (high, low))
            ),
        }
        for dx in (-1, 0, 1):
            weight = jnp.where(on_left, weights[tap_of(m, dx, 1)], weights[tap_of(m, dx, -1)])
            for half in range(2):
                term = weight * moved[dx][half]
                packed[half] = term if packed[half] is None else packed[half] + term
    left = jnp.where(on_left, packed[0], pltpu.roll(packed[1], tile - 2, 1))
    right = jnp.where(on_left, pltpu.roll(packed[1], 2, 1), packed[0])
    first[0:channels, :] = right.astype(BF16)
    second[0:channels, :] = left.astype(BF16)


def shifted_sum(before, centre, after):
    lane = lane_iota(centre.shape)
    tile = centre.shape[-1]
    before = jnp.where(lane < 2, 0.0, pltpu.roll(before, 2, 1))
    after = jnp.where(lane >= tile - 2, 0.0, pltpu.roll(after, tile - 2, 1))
    return centre + before + after


def convolve_block(cells, weights, depth, b, limit):
    channels = weights.shape[1]
    slots = cells.shape[1] // channels
    at = pl.ds(pl.multiple_of(b * ROWS, ROWS), ROWS)
    tap = [weights[t, at, :] for t in range(27)]
    for z in range(ZOUT):
        for parity in range(2):
            sums = {}
            for x in range(parity, limit, 2):
                rows = [cells[z + ZOUT * m, pl.ds(b * (ROWS * slots) + x, ROWS, stride=slots), :] for m in range(3)]
                for m in range(3):
                    for dx in (1, 0, -1):
                        out = x - 2 * dx
                        if 0 <= out < limit:
                            for dy in (-1, 0, 1):
                                term = tap[tap_of(m, dx, dy)] * rows[m]
                                key = (out, dy)
                                sums[key] = sums[key] + term if key in sums else term
                for out in [x - 2] if x + 2 < limit else [x - 2, x]:
                    if out >= 0:
                        depth[z, out, at, :] = shifted_sum(*(sums.pop((out, dy)) for dy in (-1, 0, 1)))


def outer_kernel(widths, weights, dw_bias, pw_bias, lift, coarse, cells_in, cells, extras, rims, own_block, stacked):
    width = widths[lax.axis_index("gx")]
    channels, tile = weights.shape[1:]
    slots = cells.shape[1] // channels
    own_block[...] = coarse[...]
    stacked[DW_BIAS : DW_BIAS + 1, :] = dw_bias[...]
    stacked[PW_BIAS : PW_BIAS + 1, :] = pw_bias[...]
    stacked[LIFT : LIFT + 3, :] = lift[...]
    turned = jnp.transpose(stacked[...])
    for t in range(extras.shape[0]):
        extras[t] = jnp.broadcast_to(turned[:, t : t + 1], (channels, tile))
    for b in range(channels // ROWS):
        at = slice(b * ROWS, (b + 1) * ROWS)
        for side, dx in enumerate((1, -1)):
            tap = [[weights[tap_of(m, dx, dy), at, :] for m in range(3)] for dy in (-1, 0, 1)]
            for r in range(2):
                x = r if side == 0 else width - 2 + r
                for z in range(ZOUT):
                    rows = [
                        cells[z + ZOUT * m, pl.ds(b * (ROWS * slots) + x, ROWS, stride=slots), :] for m in range(3)
                    ]
                    parts = [sum(weight * row for weight, row in zip(weights_of, rows)) for weights_of in tap]
                    rims[z, 2 * side + r, at, :] = shifted_sum(*parts)
    for r in range(2):

        @pl.when(width + r < slots)
        def _():
            for z in range(cells.shape[0]):
                cells[z, pl.ds(width + r, channels, stride=slots), :] = jnp.zeros((channels, tile), F32)


def convolve_blocks(widths, cells, weights, depth, first, last):
    width = widths[lax.axis_index("gx")]
    slots = cells.shape[1] // weights.shape[1]
    for limit in range(ROWS, slots + 1, ROWS):

        @pl.when((width > limit - ROWS) & (width <= limit))
        def _():
            def convolve(b, carry):
                convolve_block(cells, weights, depth, b, limit)
                return carry

            lax.fori_loop(first, last, convolve, 0)


def early_blocks(widths, slots):
    wide = widths[lax.axis_index("gx")] > slots - ROWS
    return jnp.where(wide & jnp.logical_not(is_even("gx")), EARLY_WIDE, EARLY)


def early_kernel(widths, cells, weights, depth):
    slots = cells.shape[1] // weights.shape[1]
    convolve_blocks(widths, cells, weights, depth, 0, early_blocks(widths, slots))


def rest_kernel(widths, edge, cells, weights, depth_in, depth):
    channels = weights.shape[1]
    first = early_blocks(widths, cells.shape[1] // channels)
    convolve_blocks(widths, cells, weights, depth, first, channels // ROWS)


def edge_term(edge, z, x):
    tile = edge.shape[2]
    begin = 8 * (x & 15) + 4 * z
    cells = pltpu.roll(edge[(x >> 4) & 1], (tile - 2 - begin) & (tile - 1), 1)
    lane = lane_iota(cells.shape)
    return jnp.where((lane < 2) | (lane >= tile - 2), cells, 0.0)


def rim_kernel(widths, first, second, rims, edge, far, near):
    width = widths[lax.axis_index("gx")]
    _, _, channels, tile = rims.shape
    left, right = first[0:channels, :].astype(F32), second[0:channels, :].astype(F32)
    on_left = (lane_iota((channels, tile)) & 2) != 0
    edge[0] = jnp.where(on_left, pltpu.roll(left, 2, 1), pltpu.roll(right, tile - 2, 1))
    edge[1] = jnp.where(on_left, left, right)
    even = is_even("gx")
    for z in range(ZOUT):
        for r in range(2):
            to_lower = rims[z, r] + edge_term(edge, z, r - 2)
            to_upper = rims[z, 2 + r] + edge_term(edge, z, width + r)
            at = slice((2 * z + r) * channels, (2 * z + r + 1) * channels)
            near[at, :] = jnp.where(even, to_upper, to_lower).astype(BF16)
            far[at, :] = jnp.where(even, to_lower, to_upper).astype(BF16)


def slab_start(widths):
    slab = lax.axis_index("gx")
    start = jnp.int32(0)
    for d in range(widths.shape[0]):
        start = start + jnp.where(d < slab, widths[d], 0)
    return start


def depth_row(extras, depth, edge, z, x):
    return depth[z, x] + extras[DW_BIAS] + edge_term(edge, z, x)


def base_row(cells, lifted, phase, z, x):
    channels = lifted.shape[1]
    slots = cells.shape[1] // channels
    return cells[2 + z, pl.ds(x, channels, stride=slots), :] + lifted[lax.div(phase + x, CF)]


def active(extras, mixed):
    mixed = mixed + extras[PW_BIAS]
    return jnp.maximum(mixed, 0.2 * mixed)


def mix_kernel(gathered, widths, mix, cells, extras, depth, edge, *refs):
    if gathered:
        coarse, value, ends, bases, lifted, across, mixer = refs
        parts, ncx, ncy = coarse.shape
    else:
        first, second, own_block, opposite, value, ends, bases, lifted, across, mixer, blocks = refs
        parts, own_rows, ncy = own_block.shape
        ncx = 4 * own_rows
    width = widths[lax.axis_index("gx")]
    here = lax.axis_index("gy")
    start = slab_start(widths)
    phase = lax.rem(start, CF)
    channels, tile = extras.shape[1:]
    slots = cells.shape[1] // channels

    if not gathered:
        count = parts * own_rows
        for message, owner in ((first, lax.rem(here + 3, 4)), (second, lax.rem(here + 1, 4))):
            terms = message[channels:, :].astype(F32)[0:count, :]
            sums = terms[:, 0:ncy] + terms[:, ncy : 2 * ncy] + terms[:, 2 * ncy : 3 * ncy]
            for k in range(parts):
                blocks[k, pl.ds(owner * own_rows, own_rows), :] = sums[k * own_rows : (k + 1) * own_rows]
        for block, owner in ((own_block, here), (opposite, lax.rem(here + 2, 4))):
            for k in range(parts):
                blocks[k, pl.ds(owner * own_rows, own_rows), :] = block[k]
    shape = (ncy, tile)
    cell = row_iota(shape) * CF
    place = lane_iota(shape) + here * tile
    along_y = ((place >= cell) & (place < cell + CF)).astype(F32)
    for k in range(parts):
        block = coarse[k] if gathered else blocks[k]
        across[k] = jnp.dot(block, along_y, precision=lax.Precision.HIGHEST, preferred_element_type=F32)
    for i in range(3):
        cell = lax.rem(lax.div(start, CF) + i, ncx)
        total = None
        for k in range(parts):
            term = extras[LIFT + k] * across[k, pl.ds(cell, 1), :]
            total = term if total is None else total + term
        lifted[i] = total

    group = 4
    wide = jnp.concatenate([mix[...]] * group, axis=1)
    wide = jnp.concatenate([wide] * group, axis=0)
    size = group * channels
    row, column = row_iota((size, size)), lane_iota((size, size))
    same = sum(
        ((row >= i * channels) & (row < (i + 1) * channels) & (column >= i * channels) & (column < (i + 1) * channels)).astype(F32)
        for i in range(group)
    )
    mixer[...] = jnp.where(same > 0, wide.astype(F32), 0.0).astype(BF16)

    def mix_rows(begin, end):
        for x in range(begin, end, group):
            depths = [
                jnp.concatenate([depth_row(extras, depth, edge, z, x + i) for i in range(group)], axis=0)
                for z in range(ZOUT)
            ]
            mixed = jnp.dot(mixer[...], jnp.concatenate(depths, axis=1).astype(BF16), preferred_element_type=F32)
            for i in range(group):
                for z in range(ZOUT):
                    part = mixed[i * channels : (i + 1) * channels, z * tile : (z + 1) * tile]
                    part = active(extras, part) + base_row(cells, lifted, phase, z, x + i)
                    if x + i >= end - ROWS and begin:
                        part = jnp.where(x + i < width, part, 0.0)
                    value[z, pl.ds(x + i, channels, stride=slots), :] = part

    mix_rows(0, ROWS)
    for z in range(ZOUT):
        for i, x in enumerate((0, 1, width - 2, width - 1)):
            ends[z, i] = depth_row(extras, depth, edge, z, x)
            bases[z, i] = base_row(cells, lifted, phase, z, x)

    def further_rows(limit):
        mix_rows(ROWS, limit)
        for x in range(limit, slots):
            for z in range(ZOUT):
                value[z, pl.ds(x, channels, stride=slots), :] = jnp.zeros((channels, tile), F32)

    for limit in range(ROWS, slots + 1, ROWS):
        pl.when((width > limit - ROWS) & (width <= limit))(lambda limit=limit: further_rows(limit))


def finish_kernel(widths, mix, extras, ends, bases, far, near, value_in, out, value, block, sems):
    width = widths[lax.axis_index("gx")]
    channels, tile = extras.shape[1:]
    slots = block.shape[2]
    even = is_even("gx")
    mixed = []
    for z in range(ZOUT):
        sums = []
        for i in range(4):
            at = slice((2 * z + i % 2) * channels, (2 * z + i % 2 + 1) * channels)
            one, two = far[at, :].astype(F32), near[at, :].astype(F32)
            arrived = jnp.where(even, one, two) if i < 2 else jnp.where(even, two, one)
            sums.append((ends[z, i] + arrived).astype(BF16))
        mixed.append(jnp.dot(mix[...], jnp.concatenate(sums, axis=1), preferred_element_type=F32))
    copies = []
    for z in range(ZOUT):
        for part in range(channels // STORED):
            at = slice(part * STORED, (part + 1) * STORED)
            for i, x in enumerate((0, 1, width - 2, width - 1)):
                rows = mixed[z][at, i * tile : (i + 1) * tile] + extras[PW_BIAS, at, :]
                rows = jnp.maximum(rows, 0.2 * rows) + bases[z, i, at, :]
                value[z, pl.ds(part * STORED * slots + x, STORED, stride=slots), :] = rows
            for o in range(part * STORED, (part + 1) * STORED):
                block[z, o] = value[z, o * slots : (o + 1) * slots, :].astype(BF16)
            part_of = pl.ds(part * STORED, STORED)
            copy = pltpu.make_async_copy(block.at[z, part_of], out.at[z, part_of], sems.at[part, z])
            copy.start()
            copies.append(copy)
    for copy in copies:
        copy.wait()


def shards(feature, widths, dw_weight, dw_bias, pw_weight, pw_bias, lift_weight, coarse):
    planes, channels, slots, tile = feature.shape
    ny = lax.axis_size("gy")
    parts, own_rows, ncy = coarse.shape
    gathered = ny != 4
    ncx = ny * own_rows
    smem = pl.BlockSpec(memory_space=pltpu.SMEM)
    vmem = pl.BlockSpec(memory_space=pltpu.VMEM)
    hbm = pl.BlockSpec(memory_space=pltpu.HBM)
    params = pltpu.CompilerParams(vmem_limit_bytes=VMEM_BYTES)
    shape = jax.ShapeDtypeStruct
    strip = shape((channels + 16, tile), BF16)
    cells_shape = pltpu.VMEM((planes, channels * slots, tile), F32)
    value_shape = pltpu.VMEM((ZOUT, channels * slots, tile), F32)
    message = shape((2 * ZOUT * channels, tile), BF16)

    def swapped(array, axis, first):
        count = lax.axis_size(axis)
        pairs = []
        for i in range(first, count + first, 2):
            a, b = i % count, (i + 1) % count
            pairs += [(a, b), (b, a)]
        return lax.ppermute(array, axis, pairs)

    def pinned(array):
        return pltpu.with_memory_space_constraint(array, pltpu.HBM)

    if gathered:
        every = lax.all_gather(coarse, "gy", axis=1, tiled=True)
    small = (widths, dw_weight, coarse)
    cells, weights, first, second, block, slab_widths = pl.pallas_call(
        pack_kernel,
        out_shape=(
            cells_shape,
            pltpu.VMEM((27, channels, tile), F32),
            strip,
            strip,
            pltpu.VMEM(coarse.shape, F32),
            pltpu.SMEM(widths.shape, jnp.int32),
        ),
        in_specs=[hbm] * 4,
        out_specs=(vmem,) * 5 + (smem,),
        scratch_shapes=[
            pltpu.VMEM(feature.shape, BF16),
            pltpu.SMEM(widths.shape, jnp.int32),
            pltpu.VMEM(dw_weight.shape, F32),
            pltpu.VMEM(coarse.shape, F32),
            pltpu.VMEM((16, tile), F32),
            pltpu.VMEM((3, 2, channels, tile), F32),
            pltpu.SemaphoreType.DMA((3,)),
            pltpu.SemaphoreType.DMA((len(small),)),
        ],
        compiler_params=params,
    )(pinned(feature), *(pinned(array) for array in small))
    first = lax.ppermute(first, "gy", [(i, (i + 1) % ny) for i in range(ny)])
    second = lax.ppermute(second, "gy", [((i + 1) % ny, i) for i in range(ny)])
    cells, extras, rims, own_block = pl.pallas_call(
        outer_kernel,
        out_shape=(
            cells_shape,
            pltpu.VMEM((5, channels, tile), F32),
            pltpu.VMEM((ZOUT, 4, channels, tile), F32),
            pltpu.VMEM(coarse.shape, F32),
        ),
        in_specs=[smem] + [vmem] * 6,
        out_specs=(vmem,) * 4,
        scratch_shapes=[pltpu.VMEM((8, channels), F32)],
        input_output_aliases={6: 0},
        compiler_params=params,
        cost_estimate=pl.CostEstimate(flops=10**8, bytes_accessed=10**6, transcendentals=0),
    )(
        slab_widths, weights, dw_bias.reshape(1, channels), pw_bias.reshape(1, channels), lift_weight.T, block, cells
    )
    if not gathered:
        opposite = lax.ppermute(own_block, "gy", [(i, (i + 2) % 4) for i in range(4)])
    depth_shape = pltpu.VMEM((ZOUT, slots, channels, tile), F32)
    depth = pl.pallas_call(
        early_kernel,
        out_shape=depth_shape,
        in_specs=[smem] + [vmem] * 2,
        out_specs=vmem,
        compiler_params=params,
        cost_estimate=pl.CostEstimate(flops=10**9, bytes_accessed=10**6, transcendentals=0),
    )(slab_widths, cells, weights)
    edge, far, near = pl.pallas_call(
        rim_kernel,
        out_shape=(pltpu.VMEM((2, channels, tile), F32), message, message),
        in_specs=[smem] + [vmem] * 3,
        out_specs=(vmem,) * 3,
        compiler_params=params,
    )(slab_widths, first, second, rims)
    far = swapped(far, "gx", 1)
    near = swapped(near, "gx", 0)
    blocks = (every,) if gathered else (first, second, own_block, opposite)
    depth = pl.pallas_call(
        rest_kernel,
        out_shape=depth_shape,
        in_specs=[smem] + [vmem] * 4,
        out_specs=vmem,
        input_output_aliases={4: 0},
        compiler_params=params,
        cost_estimate=pl.CostEstimate(flops=10**9, bytes_accessed=10**6, transcendentals=0),
    )(slab_widths, edge, cells, weights, depth)
    ends_shape = pltpu.VMEM((ZOUT, 4, channels, tile), F32)
    value, ends, bases = pl.pallas_call(
        functools.partial(mix_kernel, gathered),
        out_shape=(value_shape, ends_shape, ends_shape),
        in_specs=[smem] + [vmem] * (5 + len(blocks)),
        out_specs=(vmem,) * 3,
        scratch_shapes=[
            pltpu.VMEM((3, channels, tile), F32),
            pltpu.VMEM((parts, ncx, tile), F32),
            pltpu.VMEM((4 * channels, 4 * channels), BF16),
        ]
        + ([] if gathered else [pltpu.VMEM((parts, ncx, ncy), F32)]),
        compiler_params=params,
        cost_estimate=pl.CostEstimate(flops=10**9, bytes_accessed=10**6, transcendentals=0),
    )(slab_widths, pw_weight, cells, extras, depth, edge, *blocks)
    out, _ = pl.pallas_call(
        finish_kernel,
        out_shape=(shape((ZOUT, channels, slots, tile), BF16), value_shape),
        in_specs=[smem] + [vmem] * 7,
        out_specs=(hbm, vmem),
        scratch_shapes=[
            pltpu.VMEM((ZOUT, channels, slots, tile), BF16),
            pltpu.SemaphoreType.DMA((channels // STORED, ZOUT)),
        ],
        input_output_aliases={7: 1},
        compiler_params=params,
    )(slab_widths, pw_weight, extras, ends, bases, far, near, value)
    return out


def solution(mesh):
    placed = (P(None, None, "gx", "gy"), P(), P(), P(), P(), P(), P(), P(None, "gy", None))
    return jax.shard_map(
        shards, mesh=mesh, in_specs=placed, out_specs=P(None, None, "gx", "gy"), check_vma=False
    )
```

```python
import functools

import jax
import jax.numpy as jnp
from jax import lax
from jax.experimental import pallas as pl
from jax.experimental.pallas import tpu as pltpu
from jax.sharding import PartitionSpec as P

XW = 16
ZOUT = 2
CF = 16
ROWS = 8
GROUP = 4
SPLIT = 1
STORED = 32
DW_BIAS, PW_BIAS, LIFT = 0, 1, 2
F32 = jnp.float32
BF16 = jnp.bfloat16
VMEM_BYTES = 14 * 1024 * 1024


def lane_iota(shape):
    return lax.broadcasted_iota(jnp.int32, shape, len(shape) - 1)


def row_iota(shape):
    return lax.broadcasted_iota(jnp.int32, shape, len(shape) - 2)


def tap_of(m, dx, dy):
    return 9 * m + 3 * (dx + 1) + (dy + 1)


def is_even(axis):
    return lax.rem(lax.axis_index(axis), 2) == 0


def pack_kernel(
    feature, widths_in, taps_in, coarse_in,
    cells, weights, first, second, own_block, widths,
    planes, widths_here, taps, coarse, tail, picked, sems, small_sems,
):
    count, channels, slots, tile = feature.shape

    def copy_of(m):
        at = pl.ds(ZOUT * m, ZOUT)
        return pltpu.make_async_copy(feature.at[at], planes.at[at], sems.at[m])

    small = [
        pltpu.make_async_copy(source, target, small_sems.at[i])
        for i, (source, target) in enumerate(
            (
                (widths_in, widths_here),
                (taps_in, taps),
                (coarse_in, coarse),
            )
        )
    ]
    copy_of(0).start()
    for copy in small:
        copy.start()
    for m in range(1, 3):
        copy_of(m).start()
    def take_small():
        for copy in small:
            copy.wait()
        for d in range(widths.shape[0]):
            widths[d] = widths_here[d]
        turned = jnp.transpose(taps[...])
        for t in range(weights.shape[0]):
            weights[t] = jnp.broadcast_to(turned[:, t : t + 1], (channels, tile))

        own_block[...] = coarse[...]
        parts, own_rows, ncy = coarse.shape
        tail[...] = jnp.zeros_like(tail)
        if 3 * ncy <= tile:
            for k in range(parts):
                rest = coarse[k]
                for p in range(3):
                    term = rest.astype(BF16).astype(F32)
                    rest = rest - term
                    tail[k * own_rows : (k + 1) * own_rows, p * ncy : (p + 1) * ncy] = term
        for message in (first, second):
            message[channels:, :] = tail[...].astype(BF16)

    lane, row = lane_iota((slots, tile)), row_iota((slots, tile))
    mine = (lane >> 3) == (row & 15)
    in_even, in_odd = mine & ((lane & 4) == 0), mine & ((lane & 4) != 0)
    sublane = row_iota((ROWS, tile))

    def placed(m, k):
        both = []
        for z in range(ZOUT):
            plane = planes[ZOUT * m + z, k].astype(F32)
            cells[ZOUT * m + z, k * slots : (k + 1) * slots, :] = plane
            both.append(
                jnp.concatenate(
                    [
                        pltpu.roll(plane[x : x + ROWS], (2 + 4 * z + 8 * x) % tile, 1, stride=8, stride_axis=0)
                        for x in range(0, slots, ROWS)
                    ],
                    axis=0,
                )
            )
        rows = jnp.where(in_even, both[0], jnp.where(in_odd, both[1], 0.0))
        return rows[0:ROWS] + rows[ROWS : 2 * ROWS], rows[2 * ROWS :]

    def summed(m, k, step):
        if step == 0:
            return placed(m, k)
        one, two = summed(m, k, step // 2), summed(m, k + step, step // 2)
        turn = (sublane & step) != 0
        return tuple(
            jnp.where(turn, b, a) + pltpu.roll(jnp.where(turn, a, b), step, 0) for a, b in zip(one, two)
        )

    for m in range(3):
        copy_of(m).wait()
        for c in range(0, channels, ROWS):
            for half, total in enumerate(summed(m, c, ROWS // 2)):
                picked[m, half, c : c + ROWS, :] = total
        if m == 0:
            take_small()
    width = widths_here[lax.axis_index("gx")]

    shape = (channels, tile)
    lane = lane_iota(shape)
    on_left = (lane & 2) != 0
    packed = [None, None]
    for m in range(3):
        low, high = (jnp.where(16 * half + (lane >> 3) < width, picked[m, half], 0.0) for half in range(2))
        moved = {
            -1: tuple(
                pltpu.roll(jnp.where(lane < tile - 16, one, two), 16, 1) for one, two in ((low, high), (high, low))
            ),
            0: (low, high),
            1: tuple(
                pltpu.roll(jnp.where(lane >= 16, one, two), tile - 16, 1) for one, two in ((low, high), (high, low))
            ),
        }
        for dx in (-1, 0, 1):
            weight = jnp.where(on_left, weights[tap_of(m, dx, 1)], weights[tap_of(m, dx, -1)])
            for half in range(2):
                term = weight * moved[dx][half]
                packed[half] = term if packed[half] is None else packed[half] + term
    left = jnp.where(on_left, packed[0], pltpu.roll(packed[1], tile - 2, 1))
    right = jnp.where(on_left, pltpu.roll(packed[1], 2, 1), packed[0])
    first[0:channels, :] = right.astype(BF16)
    second[0:channels, :] = left.astype(BF16)


def shifted_sum(before, centre, after):
    lane = lane_iota(centre.shape)
    tile = centre.shape[-1]
    before = jnp.where(lane < 2, 0.0, pltpu.roll(before, 2, 1))
    after = jnp.where(lane >= tile - 2, 0.0, pltpu.roll(after, tile - 2, 1))
    return centre + before + after


def convolve_block(cells, weights, depth, b, first, limit):
    channels = weights.shape[1]
    slots = cells.shape[1] // channels
    at = pl.ds(pl.multiple_of(b * ROWS, ROWS), ROWS)
    to = pl.ds(pl.multiple_of((b - first) * ROWS, ROWS), ROWS)
    tap = [weights[t, at, :] for t in range(27)]
    for z in range(ZOUT):
        for parity in range(2):
            sums = {}
            for x in range(parity, limit, 2):
                rows = [cells[z + ZOUT * m, pl.ds(b * (ROWS * slots) + x, ROWS, stride=slots), :] for m in range(3)]
                for m in range(3):
                    for dx in (1, 0, -1):
                        out = x - 2 * dx
                        if 0 <= out < limit:
                            for dy in (-1, 0, 1):
                                term = tap[tap_of(m, dx, dy)] * rows[m]
                                key = (out, dy)
                                sums[key] = sums[key] + term if key in sums else term
                for out in [x - 2] if x + 2 < limit else [x - 2, x]:
                    if out >= 0:
                        depth[z, out, to, :] = shifted_sum(*(sums.pop((out, dy)) for dy in (-1, 0, 1)))


def outer_kernel(
    widths, weights, dw_bias, pw_bias, lift, mix, coarse, cells_in, cells, extras, rims, own_block, mixer, stacked
):
    width = widths[lax.axis_index("gx")]
    channels, tile = weights.shape[1:]
    slots = cells.shape[1] // channels
    own_block[...] = coarse[...]
    stacked[DW_BIAS : DW_BIAS + 1, :] = dw_bias[...]
    stacked[PW_BIAS : PW_BIAS + 1, :] = pw_bias[...]
    stacked[LIFT : LIFT + 3, :] = lift[...]
    turned = jnp.transpose(stacked[...])
    for t in range(extras.shape[0]):
        extras[t] = jnp.broadcast_to(turned[:, t : t + 1], (channels, tile))
    for b in range(channels // ROWS):
        at = slice(b * ROWS, (b + 1) * ROWS)
        for side, dx in enumerate((1, -1)):
            tap = [[weights[tap_of(m, dx, dy), at, :] for m in range(3)] for dy in (-1, 0, 1)]
            for r in range(2):
                x = r if side == 0 else width - 2 + r
                for z in range(ZOUT):
                    rows = [
                        cells[z + ZOUT * m, pl.ds(b * (ROWS * slots) + x, ROWS, stride=slots), :] for m in range(3)
                    ]
                    parts = [sum(weight * row for weight, row in zip(weights_of, rows)) for weights_of in tap]
                    rims[z, 2 * side + r, at, :] = shifted_sum(*parts)
    wide = jnp.concatenate([mix[...]] * GROUP, axis=1)
    wide = jnp.concatenate([wide] * GROUP, axis=0)
    size = GROUP * channels
    row, column = row_iota((size, size)), lane_iota((size, size))
    same = sum(
        ((row >= i * channels) & (row < (i + 1) * channels) & (column >= i * channels) & (column < (i + 1) * channels)).astype(F32)
        for i in range(GROUP)
    )
    mixer[...] = jnp.where(same > 0, wide.astype(F32), 0.0).astype(BF16)
    for r in range(2):

        @pl.when(width + r < slots)
        def _():
            for z in range(cells.shape[0]):
                cells[z, pl.ds(width + r, channels, stride=slots), :] = jnp.zeros((channels, tile), F32)


def convolve_blocks(widths, cells, weights, depth, first, last):
    width = widths[lax.axis_index("gx")]
    slots = cells.shape[1] // weights.shape[1]
    for limit in range(ROWS, slots + 1, GROUP):

        @pl.when((width > limit - GROUP) & (width <= limit))
        def _():
            def convolve(b, carry):
                convolve_block(cells, weights, depth, b, first, limit)
                return carry

            lax.fori_loop(first, last, convolve, 0)


def early_kernel(widths, cells, weights, depth):
    convolve_blocks(widths, cells, weights, depth, 0, SPLIT)


def rest_kernel(widths, edge, cells, weights, depth):
    convolve_blocks(widths, cells, weights, depth, SPLIT, weights.shape[1] // ROWS)


def edge_term(edge, z, x):
    tile = edge.shape[2]
    begin = 8 * (x & 15) + 4 * z
    cells = pltpu.roll(edge[(x >> 4) & 1], (tile - 2 - begin) & (tile - 1), 1)
    lane = lane_iota(cells.shape)
    return jnp.where((lane < 2) | (lane >= tile - 2), cells, 0.0)


def rim_kernel(widths, first, second, rims, edge, far, near):
    width = widths[lax.axis_index("gx")]
    _, _, channels, tile = rims.shape
    left, right = first[0:channels, :].astype(F32), second[0:channels, :].astype(F32)
    on_left = (lane_iota((channels, tile)) & 2) != 0
    edge[0] = jnp.where(on_left, pltpu.roll(left, 2, 1), pltpu.roll(right, tile - 2, 1))
    edge[1] = jnp.where(on_left, left, right)
    even = is_even("gx")
    for z in range(ZOUT):
        for r in range(2):
            to_lower = rims[z, r] + edge_term(edge, z, r - 2)
            to_upper = rims[z, 2 + r] + edge_term(edge, z, width + r)
            at = slice((2 * z + r) * channels, (2 * z + r + 1) * channels)
            near[at, :] = jnp.where(even, to_upper, to_lower).astype(BF16)
            far[at, :] = jnp.where(even, to_lower, to_upper).astype(BF16)


def slab_start(widths):
    slab = lax.axis_index("gx")
    start = jnp.int32(0)
    for d in range(widths.shape[0]):
        start = start + jnp.where(d < slab, widths[d], 0)
    return start


def depth_row(extras, depths, edge, z, x):
    own = jnp.concatenate([depth[z, x] for depth in depths], axis=0)
    return own + extras[DW_BIAS] + edge_term(edge, z, x)


def base_row(cells, lifted, phase, z, x):
    channels = lifted.shape[1]
    slots = cells.shape[1] // channels
    return cells[2 + z, pl.ds(x, channels, stride=slots), :] + lifted[lax.div(phase + x, CF)]


def active(extras, mixed):
    mixed = mixed + extras[PW_BIAS]
    return jnp.maximum(mixed, 0.2 * mixed)


def mix_kernel(gathered, widths, mixer, cells, extras, depth, rest, edge, *refs):
    if gathered:
        coarse, value, ends, bases, lifted, across = refs
        parts, ncx, ncy = coarse.shape
    else:
        first, second, own_block, opposite, value, ends, bases, lifted, across, blocks = refs
        parts, own_rows, ncy = own_block.shape
        ncx = 4 * own_rows
    width = widths[lax.axis_index("gx")]
    here = lax.axis_index("gy")
    start = slab_start(widths)
    phase = lax.rem(start, CF)
    channels, tile = extras.shape[1:]
    slots = cells.shape[1] // channels

    if not gathered:
        count = parts * own_rows
        for message, owner in ((first, lax.rem(here + 3, 4)), (second, lax.rem(here + 1, 4))):
            terms = message[channels:, :].astype(F32)[0:count, :]
            sums = terms[:, 0:ncy] + terms[:, ncy : 2 * ncy] + terms[:, 2 * ncy : 3 * ncy]
            for k in range(parts):
                blocks[k, pl.ds(owner * own_rows, own_rows), :] = sums[k * own_rows : (k + 1) * own_rows]
        for block, owner in ((own_block, here), (opposite, lax.rem(here + 2, 4))):
            for k in range(parts):
                blocks[k, pl.ds(owner * own_rows, own_rows), :] = block[k]
    shape = (ncy, tile)
    cell = row_iota(shape) * CF
    place = lane_iota(shape) + here * tile
    along_y = ((place >= cell) & (place < cell + CF)).astype(F32)
    for k in range(parts):
        block = coarse[k] if gathered else blocks[k]
        across[k] = jnp.dot(block, along_y, precision=lax.Precision.HIGHEST, preferred_element_type=F32)
    for i in range(3):
        cell = lax.rem(lax.div(start, CF) + i, ncx)
        total = None
        for k in range(parts):
            term = extras[LIFT + k] * across[k, pl.ds(cell, 1), :]
            total = term if total is None else total + term
        lifted[i] = total

    group = GROUP

    def mix_rows(begin, end):
        for x in range(begin, end, group):
            depths = [
                jnp.concatenate([depth_row(extras, (depth, rest), edge, z, x + i) for i in range(group)], axis=0)
                for z in range(ZOUT)
            ]
            mixed = jnp.dot(mixer[...], jnp.concatenate(depths, axis=1).astype(BF16), preferred_element_type=F32)
            for i in range(group):
                for z in range(ZOUT):
                    part = mixed[i * channels : (i + 1) * channels, z * tile : (z + 1) * tile]
                    part = active(extras, part) + base_row(cells, lifted, phase, z, x + i)
                    if x + i >= end - GROUP and begin:
                        part = jnp.where(x + i < width, part, 0.0)
                    value[z, pl.ds(x + i, channels, stride=slots), :] = part

    mix_rows(0, ROWS)
    for z in range(ZOUT):
        for i, x in enumerate((0, 1, width - 2, width - 1)):
            ends[z, i] = depth_row(extras, (depth, rest), edge, z, x)
            bases[z, i] = base_row(cells, lifted, phase, z, x)

    def further_rows(limit):
        mix_rows(ROWS, limit)
        for x in range(limit, slots):
            for z in range(ZOUT):
                value[z, pl.ds(x, channels, stride=slots), :] = jnp.zeros((channels, tile), F32)

    for limit in range(ROWS, slots + 1, GROUP):
        pl.when((width > limit - GROUP) & (width <= limit))(lambda limit=limit: further_rows(limit))


def finish_kernel(widths, mix, extras, ends, bases, far, near, value_in, out, value, block, sems):
    width = widths[lax.axis_index("gx")]
    channels, tile = extras.shape[1:]
    slots = block.shape[2]
    even = is_even("gx")
    mixed = []
    for z in range(ZOUT):
        sums = []
        for i in range(4):
            at = slice((2 * z + i % 2) * channels, (2 * z + i % 2 + 1) * channels)
            one, two = far[at, :].astype(F32), near[at, :].astype(F32)
            arrived = jnp.where(even, one, two) if i < 2 else jnp.where(even, two, one)
            sums.append((ends[z, i] + arrived).astype(BF16))
        mixed.append(jnp.dot(mix[...], jnp.concatenate(sums, axis=1), preferred_element_type=F32))
    copies = []
    for z in range(ZOUT):
        for part in range(channels // STORED):
            at = slice(part * STORED, (part + 1) * STORED)
            for i, x in enumerate((0, 1, width - 2, width - 1)):
                rows = mixed[z][at, i * tile : (i + 1) * tile] + extras[PW_BIAS, at, :]
                rows = jnp.maximum(rows, 0.2 * rows) + bases[z, i, at, :]
                value[z, pl.ds(part * STORED * slots + x, STORED, stride=slots), :] = rows
            for o in range(part * STORED, (part + 1) * STORED):
                block[z, o] = value[z, o * slots : (o + 1) * slots, :].astype(BF16)
            part_of = pl.ds(part * STORED, STORED)
            copy = pltpu.make_async_copy(block.at[z, part_of], out.at[z, part_of], sems.at[part, z])
            copy.start()
            copies.append(copy)
    for copy in copies:
        copy.wait()


def shards(feature, widths, dw_weight, dw_bias, pw_weight, pw_bias, lift_weight, coarse):
    planes, channels, slots, tile = feature.shape
    ny = lax.axis_size("gy")
    parts, own_rows, ncy = coarse.shape
    gathered = ny != 4
    ncx = ny * own_rows
    smem = pl.BlockSpec(memory_space=pltpu.SMEM)
    vmem = pl.BlockSpec(memory_space=pltpu.VMEM)
    hbm = pl.BlockSpec(memory_space=pltpu.HBM)
    params = pltpu.CompilerParams(vmem_limit_bytes=VMEM_BYTES)
    shape = jax.ShapeDtypeStruct
    strip = shape((channels + 16, tile), BF16)
    cells_shape = pltpu.VMEM((planes, channels * slots, tile), F32)
    value_shape = pltpu.VMEM((ZOUT, channels * slots, tile), F32)
    message = shape((2 * ZOUT * channels, tile), BF16)

    def swapped(array, axis, first):
        count = lax.axis_size(axis)
        pairs = []
        for i in range(first, count + first, 2):
            a, b = i % count, (i + 1) % count
            pairs += [(a, b), (b, a)]
        return lax.ppermute(array, axis, pairs)

    def pinned(array):
        return pltpu.with_memory_space_constraint(array, pltpu.HBM)

    if gathered:
        every = lax.all_gather(coarse, "gy", axis=1, tiled=True)
    small = (widths, dw_weight, coarse)
    cells, weights, first, second, block, slab_widths = pl.pallas_call(
        pack_kernel,
        out_shape=(
            cells_shape,
            pltpu.VMEM((27, channels, tile), F32),
            strip,
            strip,
            pltpu.VMEM(coarse.shape, F32),
            pltpu.SMEM(widths.shape, jnp.int32),
        ),
        in_specs=[hbm] * 4,
        out_specs=(vmem,) * 5 + (smem,),
        scratch_shapes=[
            pltpu.VMEM(feature.shape, BF16),
            pltpu.SMEM(widths.shape, jnp.int32),
            pltpu.VMEM(dw_weight.shape, F32),
            pltpu.VMEM(coarse.shape, F32),
            pltpu.VMEM((16, tile), F32),
            pltpu.VMEM((3, 2, channels, tile), F32),
            pltpu.SemaphoreType.DMA((3,)),
            pltpu.SemaphoreType.DMA((len(small),)),
        ],
        compiler_params=params,
    )(pinned(feature), *(pinned(array) for array in small))
    first = lax.ppermute(first, "gy", [(i, (i + 1) % ny) for i in range(ny)])
    second = lax.ppermute(second, "gy", [((i + 1) % ny, i) for i in range(ny)])
    cells, extras, rims, own_block, mixer = pl.pallas_call(
        outer_kernel,
        out_shape=(
            cells_shape,
            pltpu.VMEM((5, channels, tile), F32),
            pltpu.VMEM((ZOUT, 4, channels, tile), F32),
            pltpu.VMEM(coarse.shape, F32),
            pltpu.VMEM((GROUP * channels, GROUP * channels), BF16),
        ),
        in_specs=[smem] + [vmem] * 7,
        out_specs=(vmem,) * 5,
        scratch_shapes=[pltpu.VMEM((8, channels), F32)],
        input_output_aliases={7: 0},
        compiler_params=params,
        cost_estimate=pl.CostEstimate(flops=10**8, bytes_accessed=10**6, transcendentals=0),
    )(
        slab_widths, weights, dw_bias.reshape(1, channels), pw_bias.reshape(1, channels), lift_weight.T, pw_weight,
        block, cells,
    )
    if not gathered:
        opposite = lax.ppermute(own_block, "gy", [(i, (i + 2) % 4) for i in range(4)])
    early = SPLIT * ROWS
    depth = pl.pallas_call(
        early_kernel,
        out_shape=pltpu.VMEM((ZOUT, slots, early, tile), F32),
        in_specs=[smem] + [vmem] * 2,
        out_specs=vmem,
        compiler_params=params,
        cost_estimate=pl.CostEstimate(flops=10**9, bytes_accessed=10**6, transcendentals=0),
    )(slab_widths, cells, weights)
    edge, far, near = pl.pallas_call(
        rim_kernel,
        out_shape=(pltpu.VMEM((2, channels, tile), F32), message, message),
        in_specs=[smem] + [vmem] * 3,
        out_specs=(vmem,) * 3,
        compiler_params=params,
    )(slab_widths, first, second, rims)
    far = swapped(far, "gx", 1)
    near = swapped(near, "gx", 0)
    blocks = (every,) if gathered else (first, second, own_block, opposite)
    rest = pl.pallas_call(
        rest_kernel,
        out_shape=pltpu.VMEM((ZOUT, slots, channels - early, tile), F32),
        in_specs=[smem] + [vmem] * 3,
        out_specs=vmem,
        compiler_params=params,
        cost_estimate=pl.CostEstimate(flops=10**9, bytes_accessed=10**6, transcendentals=0),
    )(slab_widths, edge, cells, weights)
    ends_shape = pltpu.VMEM((ZOUT, 4, channels, tile), F32)
    value, ends, bases = pl.pallas_call(
        functools.partial(mix_kernel, gathered),
        out_shape=(value_shape, ends_shape, ends_shape),
        in_specs=[smem] + [vmem] * (6 + len(blocks)),
        out_specs=(vmem,) * 3,
        scratch_shapes=[
            pltpu.VMEM((3, channels, tile), F32),
            pltpu.VMEM((parts, ncx, tile), F32),
        ]
        + ([] if gathered else [pltpu.VMEM((parts, ncx, ncy), F32)]),
        compiler_params=params,
        cost_estimate=pl.CostEstimate(flops=10**9, bytes_accessed=10**6, transcendentals=0),
    )(slab_widths, mixer, cells, extras, depth, rest, edge, *blocks)
    out, _ = pl.pallas_call(
        finish_kernel,
        out_shape=(shape((ZOUT, channels, slots, tile), BF16), value_shape),
        in_specs=[smem] + [vmem] * 7,
        out_specs=(hbm, vmem),
        scratch_shapes=[
            pltpu.VMEM((ZOUT, channels, slots, tile), BF16),
            pltpu.SemaphoreType.DMA((channels // STORED, ZOUT)),
        ],
        input_output_aliases={7: 1},
        compiler_params=params,
    )(slab_widths, pw_weight, extras, ends, bases, far, near, value)
    return out


def solution(mesh):
    placed = (P(None, None, "gx", "gy"), P(), P(), P(), P(), P(), P(), P(None, "gy", None))
    return jax.shard_map(
        shards, mesh=mesh, in_specs=placed, out_specs=P(None, None, "gx", "gy"), check_vma=False
    )
```

```python
import functools

import jax
import jax.numpy as jnp
from jax import lax
from jax.experimental import pallas as pl
from jax.experimental.pallas import tpu as pltpu
from jax.sharding import PartitionSpec as P

XW = 16
ZOUT = 2
CF = 16
ROWS = 8
GROUP = 4
SPLIT = 1
STORED = 32
DW_BIAS, PW_BIAS, LIFT = 0, 1, 2
F32 = jnp.float32
BF16 = jnp.bfloat16
VMEM_BYTES = 14 * 1024 * 1024


def lane_iota(shape):
    return lax.broadcasted_iota(jnp.int32, shape, len(shape) - 1)


def row_iota(shape):
    return lax.broadcasted_iota(jnp.int32, shape, len(shape) - 2)


def tap_of(m, dx, dy):
    return 9 * m + 3 * (dx + 1) + (dy + 1)


def is_even(axis):
    return lax.rem(lax.axis_index(axis), 2) == 0


def pack_kernel(
    feature, widths_in, taps_in, coarse_in,
    cells, weights, first, second, own_block, widths,
    planes, widths_here, taps, coarse, tail, picked, sems, small_sems,
):
    count, channels, slots, tile = feature.shape

    def copy_of(m):
        at = pl.ds(ZOUT * m, ZOUT)
        return pltpu.make_async_copy(feature.at[at], planes.at[at], sems.at[m])

    small = [
        pltpu.make_async_copy(source, target, small_sems.at[i])
        for i, (source, target) in enumerate(
            (
                (widths_in, widths_here),
                (taps_in, taps),
                (coarse_in, coarse),
            )
        )
    ]
    for copy in small:
        copy.start()
    for m in range(3):
        copy_of(m).start()
    def take_small():
        for copy in small:
            copy.wait()
        for d in range(widths.shape[0]):
            widths[d] = widths_here[d]
        turned = jnp.transpose(taps[...])
        for t in range(weights.shape[0]):
            weights[t] = jnp.broadcast_to(turned[:, t : t + 1], (channels, tile))

        own_block[...] = coarse[...]
        parts, own_rows, ncy = coarse.shape
        tail[...] = jnp.zeros_like(tail)
        if 3 * ncy <= tile:
            for k in range(parts):
                rest = coarse[k]
                for p in range(3):
                    term = rest.astype(BF16).astype(F32)
                    rest = rest - term
                    tail[k * own_rows : (k + 1) * own_rows, p * ncy : (p + 1) * ncy] = term
        for message in (first, second):
            message[channels:, :] = tail[...].astype(BF16)

    lane, row = lane_iota((slots, tile)), row_iota((slots, tile))
    mine = (lane >> 3) == (row & 15)
    in_even, in_odd = mine & ((lane & 4) == 0), mine & ((lane & 4) != 0)
    sublane = row_iota((ROWS, tile))

    def placed(m, k):
        both = []
        for z in range(ZOUT):
            plane = planes[ZOUT * m + z, k].astype(F32)
            cells[ZOUT * m + z, k * slots : (k + 1) * slots, :] = plane
            both.append(
                jnp.concatenate(
                    [
                        pltpu.roll(plane[x : x + ROWS], (2 + 4 * z + 8 * x) % tile, 1, stride=8, stride_axis=0)
                        for x in range(0, slots, ROWS)
                    ],
                    axis=0,
                )
            )
        rows = jnp.where(in_even, both[0], jnp.where(in_odd, both[1], 0.0))
        return rows[0:ROWS] + rows[ROWS : 2 * ROWS], rows[2 * ROWS :]

    def summed(m, k, step):
        if step == 0:
            return placed(m, k)
        one, two = summed(m, k, step // 2), summed(m, k + step, step // 2)
        turn = (sublane & step) != 0
        return tuple(
            jnp.where(turn, b, a) + pltpu.roll(jnp.where(turn, a, b), step, 0) for a, b in zip(one, two)
        )

    take_small()
    for m in range(3):
        copy_of(m).wait()
        for c in range(0, channels, ROWS):
            for half, total in enumerate(summed(m, c, ROWS // 2)):
                picked[m, half, c : c + ROWS, :] = total
    width = widths_here[lax.axis_index("gx")]

    shape = (channels, tile)
    lane = lane_iota(shape)
    on_left = (lane & 2) != 0
    packed = [None, None]
    for m in range(3):
        low, high = (jnp.where(16 * half + (lane >> 3) < width, picked[m, half], 0.0) for half in range(2))
        moved = {
            -1: tuple(
                pltpu.roll(jnp.where(lane < tile - 16, one, two), 16, 1) for one, two in ((low, high), (high, low))
            ),
            0: (low, high),
            1: tuple(
                pltpu.roll(jnp.where(lane >= 16, one, two), tile - 16, 1) for one, two in ((low, high), (high, low))
            ),
        }
        for dx in (-1, 0, 1):
            weight = jnp.where(on_left, weights[tap_of(m, dx, 1)], weights[tap_of(m, dx, -1)])
            for half in range(2):
                term = weight * moved[dx][half]
                packed[half] = term if packed[half] is None else packed[half] + term
    left = jnp.where(on_left, packed[0], pltpu.roll(packed[1], tile - 2, 1))
    right = jnp.where(on_left, pltpu.roll(packed[1], 2, 1), packed[0])
    first[0:channels, :] = right.astype(BF16)
    second[0:channels, :] = left.astype(BF16)


def shifted_sum(before, centre, after):
    lane = lane_iota(centre.shape)
    tile = centre.shape[-1]
    before = jnp.where(lane < 2, 0.0, pltpu.roll(before, 2, 1))
    after = jnp.where(lane >= tile - 2, 0.0, pltpu.roll(after, tile - 2, 1))
    return centre + before + after


def convolve_block(cells, weights, depth, b, first, limit):
    channels = weights.shape[1]
    slots = cells.shape[1] // channels
    at = pl.ds(pl.multiple_of(b * ROWS, ROWS), ROWS)
    to = pl.ds(pl.multiple_of((b - first) * ROWS, ROWS), ROWS)
    tap = [weights[t, at, :] for t in range(27)]
    for z in range(ZOUT):
        for parity in range(2):
            sums = {}
            for x in range(parity, limit, 2):
                rows = [cells[z + ZOUT * m, pl.ds(b * (ROWS * slots) + x, ROWS, stride=slots), :] for m in range(3)]
                for m in range(3):
                    for dx in (1, 0, -1):
                        out = x - 2 * dx
                        if 0 <= out < limit:
                            for dy in (-1, 0, 1):
                                term = tap[tap_of(m, dx, dy)] * rows[m]
                                key = (out, dy)
                                sums[key] = sums[key] + term if key in sums else term
                for out in [x - 2] if x + 2 < limit else [x - 2, x]:
                    if out >= 0:
                        depth[z, out, to, :] = shifted_sum(*(sums.pop((out, dy)) for dy in (-1, 0, 1)))


def outer_kernel(
    widths, weights, dw_bias, pw_bias, lift, mix, coarse, cells_in, cells, extras, rims, own_block, mixer, stacked
):
    width = widths[lax.axis_index("gx")]
    channels, tile = weights.shape[1:]
    slots = cells.shape[1] // channels
    own_block[...] = coarse[...]
    stacked[DW_BIAS : DW_BIAS + 1, :] = dw_bias[...]
    stacked[PW_BIAS : PW_BIAS + 1, :] = pw_bias[...]
    stacked[LIFT : LIFT + 3, :] = lift[...]
    turned = jnp.transpose(stacked[...])
    for t in range(extras.shape[0]):
        extras[t] = jnp.broadcast_to(turned[:, t : t + 1], (channels, tile))
    for b in range(channels // ROWS):
        at = slice(b * ROWS, (b + 1) * ROWS)
        for side, dx in enumerate((1, -1)):
            tap = [[weights[tap_of(m, dx, dy), at, :] for m in range(3)] for dy in (-1, 0, 1)]
            for r in range(2):
                x = r if side == 0 else width - 2 + r
                for z in range(ZOUT):
                    rows = [
                        cells[z + ZOUT * m, pl.ds(b * (ROWS * slots) + x, ROWS, stride=slots), :] for m in range(3)
                    ]
                    parts = [sum(weight * row for weight, row in zip(weights_of, rows)) for weights_of in tap]
                    rims[z, 2 * side + r, at, :] = shifted_sum(*parts)
    wide = jnp.concatenate([mix[...]] * GROUP, axis=1)
    wide = jnp.concatenate([wide] * GROUP, axis=0)
    size = GROUP * channels
    row, column = row_iota((size, size)), lane_iota((size, size))
    same = sum(
        ((row >= i * channels) & (row < (i + 1) * channels) & (column >= i * channels) & (column < (i + 1) * channels)).astype(F32)
        for i in range(GROUP)
    )
    mixer[...] = jnp.where(same > 0, wide.astype(F32), 0.0).astype(BF16)
    for r in range(2):

        @pl.when(width + r < slots)
        def _():
            for z in range(cells.shape[0]):
                cells[z, pl.ds(width + r, channels, stride=slots), :] = jnp.zeros((channels, tile), F32)


def convolve_blocks(widths, cells, weights, depth, first, last):
    width = widths[lax.axis_index("gx")]
    slots = cells.shape[1] // weights.shape[1]
    for limit in range(ROWS, slots + 1, GROUP):

        @pl.when((width > limit - GROUP) & (width <= limit))
        def _():
            def convolve(b, carry):
                convolve_block(cells, weights, depth, b, first, limit)
                return carry

            lax.fori_loop(first, last, convolve, 0)


def early_kernel(widths, cells, weights, depth):
    convolve_blocks(widths, cells, weights, depth, 0, SPLIT)


def rest_kernel(widths, edge, cells, weights, depth):
    convolve_blocks(widths, cells, weights, depth, SPLIT, weights.shape[1] // ROWS)


def edge_term(edge, z, x):
    tile = edge.shape[2]
    begin = 8 * (x & 15) + 4 * z
    cells = pltpu.roll(edge[(x >> 4) & 1], (tile - 2 - begin) & (tile - 1), 1)
    lane = lane_iota(cells.shape)
    return jnp.where((lane < 2) | (lane >= tile - 2), cells, 0.0)


def rim_kernel(widths, first, second, rims, edge, far, near):
    width = widths[lax.axis_index("gx")]
    _, _, channels, tile = rims.shape
    left, right = first[0:channels, :].astype(F32), second[0:channels, :].astype(F32)
    on_left = (lane_iota((channels, tile)) & 2) != 0
    edge[0] = jnp.where(on_left, pltpu.roll(left, 2, 1), pltpu.roll(right, tile - 2, 1))
    edge[1] = jnp.where(on_left, left, right)
    even = is_even("gx")
    for z in range(ZOUT):
        for r in range(2):
            to_lower = rims[z, r] + edge_term(edge, z, r - 2)
            to_upper = rims[z, 2 + r] + edge_term(edge, z, width + r)
            at = slice((2 * z + r) * channels, (2 * z + r + 1) * channels)
            near[at, :] = jnp.where(even, to_upper, to_lower).astype(BF16)
            far[at, :] = jnp.where(even, to_lower, to_upper).astype(BF16)


def slab_start(widths):
    slab = lax.axis_index("gx")
    start = jnp.int32(0)
    for d in range(widths.shape[0]):
        start = start + jnp.where(d < slab, widths[d], 0)
    return start


def depth_row(extras, depths, edge, z, x):
    own = jnp.concatenate([depth[z, x] for depth in depths], axis=0)
    return own + extras[DW_BIAS] + edge_term(edge, z, x)


def base_row(cells, lifted, phase, z, x):
    channels = lifted.shape[1]
    slots = cells.shape[1] // channels
    return cells[2 + z, pl.ds(x, channels, stride=slots), :] + lifted[lax.div(phase + x, CF)]


def active(extras, mixed):
    mixed = mixed + extras[PW_BIAS]
    return jnp.maximum(mixed, 0.2 * mixed)


def mix_kernel(gathered, widths, mixer, cells, extras, depth, rest, edge, *refs):
    if gathered:
        coarse, value, ends, bases, lifted, across = refs
        parts, ncx, ncy = coarse.shape
    else:
        first, second, own_block, opposite, value, ends, bases, lifted, across, blocks = refs
        parts, own_rows, ncy = own_block.shape
        ncx = 4 * own_rows
    width = widths[lax.axis_index("gx")]
    here = lax.axis_index("gy")
    start = slab_start(widths)
    phase = lax.rem(start, CF)
    channels, tile = extras.shape[1:]
    slots = cells.shape[1] // channels

    if not gathered:
        count = parts * own_rows
        for message, owner in ((first, lax.rem(here + 3, 4)), (second, lax.rem(here + 1, 4))):
            terms = message[channels:, :].astype(F32)[0:count, :]
            sums = terms[:, 0:ncy] + terms[:, ncy : 2 * ncy] + terms[:, 2 * ncy : 3 * ncy]
            for k in range(parts):
                blocks[k, pl.ds(owner * own_rows, own_rows), :] = sums[k * own_rows : (k + 1) * own_rows]
        for block, owner in ((own_block, here), (opposite, lax.rem(here + 2, 4))):
            for k in range(parts):
                blocks[k, pl.ds(owner * own_rows, own_rows), :] = block[k]
    shape = (ncy, tile)
    cell = row_iota(shape) * CF
    place = lane_iota(shape) + here * tile
    along_y = ((place >= cell) & (place < cell + CF)).astype(F32)
    for k in range(parts):
        block = coarse[k] if gathered else blocks[k]
        across[k] = jnp.dot(block, along_y, precision=lax.Precision.HIGHEST, preferred_element_type=F32)
    for i in range(3):
        cell = lax.rem(lax.div(start, CF) + i, ncx)
        total = None
        for k in range(parts):
            term = extras[LIFT + k] * across[k, pl.ds(cell, 1), :]
            total = term if total is None else total + term
        lifted[i] = total

    group = GROUP

    def mix_rows(begin, end):
        for x in range(begin, end, group):
            depths = [
                jnp.concatenate([depth_row(extras, (depth, rest), edge, z, x + i) for i in range(group)], axis=0)
                for z in range(ZOUT)
            ]
            mixed = jnp.dot(mixer[...], jnp.concatenate(depths, axis=1).astype(BF16), preferred_element_type=F32)
            for i in range(group):
                for z in range(ZOUT):
                    part = mixed[i * channels : (i + 1) * channels, z * tile : (z + 1) * tile]
                    part = active(extras, part) + base_row(cells, lifted, phase, z, x + i)
                    if x + i >= end - GROUP and begin:
                        part = jnp.where(x + i < width, part, 0.0)
                    value[z, pl.ds(x + i, channels, stride=slots), :] = part

    mix_rows(0, ROWS)
    for z in range(ZOUT):
        for i, x in enumerate((0, 1, width - 2, width - 1)):
            ends[z, i] = depth_row(extras, (depth, rest), edge, z, x)
            bases[z, i] = base_row(cells, lifted, phase, z, x)

    def further_rows(limit):
        mix_rows(ROWS, limit)
        for x in range(limit, slots):
            for z in range(ZOUT):
                value[z, pl.ds(x, channels, stride=slots), :] = jnp.zeros((channels, tile), F32)

    for limit in range(ROWS, slots + 1, GROUP):
        pl.when((width > limit - GROUP) & (width <= limit))(lambda limit=limit: further_rows(limit))


def finish_kernel(widths, mix, extras, ends, bases, far, near, value_in, out, value, block, sems):
    width = widths[lax.axis_index("gx")]
    channels, tile = extras.shape[1:]
    slots = block.shape[2]
    even = is_even("gx")
    mixed = []
    for z in range(ZOUT):
        sums = []
        for i in range(4):
            at = slice((2 * z + i % 2) * channels, (2 * z + i % 2 + 1) * channels)
            one, two = far[at, :].astype(F32), near[at, :].astype(F32)
            arrived = jnp.where(even, one, two) if i < 2 else jnp.where(even, two, one)
            sums.append((ends[z, i] + arrived).astype(BF16))
        mixed.append(jnp.dot(mix[...], jnp.concatenate(sums, axis=1), preferred_element_type=F32))
    copies = []
    for z in range(ZOUT):
        for part in range(channels // STORED):
            at = slice(part * STORED, (part + 1) * STORED)
            for i, x in enumerate((0, 1, width - 2, width - 1)):
                rows = mixed[z][at, i * tile : (i + 1) * tile] + extras[PW_BIAS, at, :]
                rows = jnp.maximum(rows, 0.2 * rows) + bases[z, i, at, :]
                value[z, pl.ds(part * STORED * slots + x, STORED, stride=slots), :] = rows
            for o in range(part * STORED, (part + 1) * STORED):
                block[z, o] = value[z, o * slots : (o + 1) * slots, :].astype(BF16)
            part_of = pl.ds(part * STORED, STORED)
            copy = pltpu.make_async_copy(block.at[z, part_of], out.at[z, part_of], sems.at[part, z])
            copy.start()
            copies.append(copy)
    for copy in copies:
        copy.wait()


def shards(feature, widths, dw_weight, dw_bias, pw_weight, pw_bias, lift_weight, coarse):
    planes, channels, slots, tile = feature.shape
    ny = lax.axis_size("gy")
    parts, own_rows, ncy = coarse.shape
    gathered = ny != 4
    ncx = ny * own_rows
    smem = pl.BlockSpec(memory_space=pltpu.SMEM)
    vmem = pl.BlockSpec(memory_space=pltpu.VMEM)
    hbm = pl.BlockSpec(memory_space=pltpu.HBM)
    params = pltpu.CompilerParams(vmem_limit_bytes=VMEM_BYTES)
    shape = jax.ShapeDtypeStruct
    strip = shape((channels + 16, tile), BF16)
    cells_shape = pltpu.VMEM((planes, channels * slots, tile), F32)
    value_shape = pltpu.VMEM((ZOUT, channels * slots, tile), F32)
    message = shape((2 * ZOUT * channels, tile), BF16)

    def swapped(array, axis, first):
        count = lax.axis_size(axis)
        pairs = []
        for i in range(first, count + first, 2):
            a, b = i % count, (i + 1) % count
            pairs += [(a, b), (b, a)]
        return lax.ppermute(array, axis, pairs)

    def pinned(array):
        return pltpu.with_memory_space_constraint(array, pltpu.HBM)

    if gathered:
        every = lax.all_gather(coarse, "gy", axis=1, tiled=True)
    small = (widths, dw_weight, coarse)
    cells, weights, first, second, block, slab_widths = pl.pallas_call(
        pack_kernel,
        out_shape=(
            cells_shape,
            pltpu.VMEM((27, channels, tile), F32),
            strip,
            strip,
            pltpu.VMEM(coarse.shape, F32),
            pltpu.SMEM(widths.shape, jnp.int32),
        ),
        in_specs=[hbm] * 4,
        out_specs=(vmem,) * 5 + (smem,),
        scratch_shapes=[
            pltpu.VMEM(feature.shape, BF16),
            pltpu.SMEM(widths.shape, jnp.int32),
            pltpu.VMEM(dw_weight.shape, F32),
            pltpu.VMEM(coarse.shape, F32),
            pltpu.VMEM((16, tile), F32),
            pltpu.VMEM((3, 2, channels, tile), F32),
            pltpu.SemaphoreType.DMA((3,)),
            pltpu.SemaphoreType.DMA((len(small),)),
        ],
        compiler_params=params,
    )(pinned(feature), *(pinned(array) for array in small))
    first = lax.ppermute(first, "gy", [(i, (i + 1) % ny) for i in range(ny)])
    second = lax.ppermute(second, "gy", [((i + 1) % ny, i) for i in range(ny)])
    cells, extras, rims, own_block, mixer = pl.pallas_call(
        outer_kernel,
        out_shape=(
            cells_shape,
            pltpu.VMEM((5, channels, tile), F32),
            pltpu.VMEM((ZOUT, 4, channels, tile), F32),
            pltpu.VMEM(coarse.shape, F32),
            pltpu.VMEM((GROUP * channels, GROUP * channels), BF16),
        ),
        in_specs=[smem] + [vmem] * 7,
        out_specs=(vmem,) * 5,
        scratch_shapes=[pltpu.VMEM((8, channels), F32)],
        input_output_aliases={7: 0},
        compiler_params=params,
        cost_estimate=pl.CostEstimate(flops=10**8, bytes_accessed=10**6, transcendentals=0),
    )(
        slab_widths, weights, dw_bias.reshape(1, channels), pw_bias.reshape(1, channels), lift_weight.T, pw_weight,
        block, cells,
    )
    if not gathered:
        opposite = lax.ppermute(own_block, "gy", [(i, (i + 2) % 4) for i in range(4)])
    early = SPLIT * ROWS
    depth = pl.pallas_call(
        early_kernel,
        out_shape=pltpu.VMEM((ZOUT, slots, early, tile), F32),
        in_specs=[smem] + [vmem] * 2,
        out_specs=vmem,
        compiler_params=params,
        cost_estimate=pl.CostEstimate(flops=10**9, bytes_accessed=10**6, transcendentals=0),
    )(slab_widths, cells, weights)
    edge, far, near = pl.pallas_call(
        rim_kernel,
        out_shape=(pltpu.VMEM((2, channels, tile), F32), message, message),
        in_specs=[smem] + [vmem] * 3,
        out_specs=(vmem,) * 3,
        compiler_params=params,
    )(slab_widths, first, second, rims)
    far = swapped(far, "gx", 1)
    near = swapped(near, "gx", 0)
    blocks = (every,) if gathered else (first, second, own_block, opposite)
    rest = pl.pallas_call(
        rest_kernel,
        out_shape=pltpu.VMEM((ZOUT, slots, channels - early, tile), F32),
        in_specs=[smem] + [vmem] * 3,
        out_specs=vmem,
        compiler_params=params,
        cost_estimate=pl.CostEstimate(flops=10**9, bytes_accessed=10**6, transcendentals=0),
    )(slab_widths, edge, cells, weights)
    ends_shape = pltpu.VMEM((ZOUT, 4, channels, tile), F32)
    value, ends, bases = pl.pallas_call(
        functools.partial(mix_kernel, gathered),
        out_shape=(value_shape, ends_shape, ends_shape),
        in_specs=[smem] + [vmem] * (6 + len(blocks)),
        out_specs=(vmem,) * 3,
        scratch_shapes=[
            pltpu.VMEM((3, channels, tile), F32),
            pltpu.VMEM((parts, ncx, tile), F32),
        ]
        + ([] if gathered else [pltpu.VMEM((parts, ncx, ncy), F32)]),
        compiler_params=params,
        cost_estimate=pl.CostEstimate(flops=10**9, bytes_accessed=10**6, transcendentals=0),
    )(slab_widths, mixer, cells, extras, depth, rest, edge, *blocks)
    out, _ = pl.pallas_call(
        finish_kernel,
        out_shape=(shape((ZOUT, channels, slots, tile), BF16), value_shape),
        in_specs=[smem] + [vmem] * 7,
        out_specs=(hbm, vmem),
        scratch_shapes=[
            pltpu.VMEM((ZOUT, channels, slots, tile), BF16),
            pltpu.SemaphoreType.DMA((channels // STORED, ZOUT)),
        ],
        input_output_aliases={7: 1},
        compiler_params=params,
    )(slab_widths, pw_weight, extras, ends, bases, far, near, value)
    return out


def solution(mesh):
    placed = (P(None, None, "gx", "gy"), P(), P(), P(), P(), P(), P(), P(None, "gy", None))
    return jax.shard_map(
        shards, mesh=mesh, in_specs=placed, out_specs=P(None, None, "gx", "gy"), check_vma=False
    )
```
